32 devices in a mesh: dp: 2 (over core), row: 4 (over y, x), col: 4 (over z).
Axes of the slice: x: 2, y: 2, z: 4, core: 2. Of those that a mesh axis runs over, the one named last changes fastest.
Arguments:
- tokens: bfloat16 [2, 64, 64, 768], P('dp', 'row', 'col'), may hold values from -8 to 8
- ln1_gain: bfloat16 [768], replicated, may hold values from 0.5 to 1.5
- ln1_bias: bfloat16 [768], replicated, may hold values from -1 to 1
- qkv_weight: bfloat16 [768, 2304], P('dp', ('row', 'col')), may hold values from -1 to 1
- query_bias: bfloat16 [768], replicated, may hold values from -1 to 1
- value_bias: bfloat16 [768], replicated, may hold values from -1 to 1
- rel_rows: bfloat16 [27, 64], replicated, may hold values from -0.75 to 0.75
- rel_cols: bfloat16 [27, 64], replicated, may hold values from -0.75 to 0.75
- proj_weight: bfloat16 [768, 768], P('dp', ('row', 'col')), may hold values from -0.875 to 0.875
- proj_bias: bfloat16 [768], replicated, may hold values from -1 to 1
- ln2_gain: bfloat16 [768], replicated, may hold values from 0.5 to 1.5
- ln2_bias: bfloat16 [768], replicated, may hold values from -1 to 1
- fc1_weight: bfloat16 [768, 3072], P('dp', ('row', 'col')), may hold values from -1 to 1
- fc1_bias: bfloat16 [3072], replicated, may hold values from -1 to 1
- fc2_weight: bfloat16 [3072, 768], P('dp', ('row', 'col')), may hold values from -0.109375 to 0.109375
- fc2_bias: bfloat16 [768], replicated, may hold values from -1 to 1
- cotangent: bfloat16 [2, 64, 64, 768], P('dp', 'row', 'col'), may hold values from -6 to 6
Outputs:
- output: bfloat16 [2, 64, 64, 768], P('dp', 'row', 'col')
- input_grad: bfloat16 [2, 64, 64, 768], P('dp', 'row', 'col')
- grad_ln1_gain: float32 [768], replicated
- grad_ln1_bias: float32 [768], replicated
- grad_qkv_weight: float32 [768, 2304], P('dp', ('row', 'col'))
- grad_query_bias: float32 [768], replicated
- grad_value_bias: float32 [768], replicated
- grad_rel_rows: float32 [27, 64], replicated
- grad_rel_cols: float32 [27, 64], replicated
- grad_proj_weight: float32 [768, 768], P('dp', ('row', 'col'))
- grad_proj_bias: float32 [768], replicated
- grad_ln2_gain: float32 [768], replicated
- grad_ln2_bias: float32 [768], replicated
- grad_fc1_weight: float32 [768, 3072], P('dp', ('row', 'col'))
- grad_fc1_bias: float32 [3072], replicated
- grad_fc2_weight: float32 [3072, 768], P('dp', ('row', 'col'))
- grad_fc2_bias: float32 [768], replicated
- statistics: float32 [2, 5], P('dp')
The draws below stay inside these ranges and needn't reach their ends.
All inputs are finite; a program needn't handle non-finite values.
Results may differ from the reference program's by a relative error of at most 0.019.
Values may be sent and summed in bfloat16 or wider, within the bound.
A program may use at most 192 MiB of HBM per device.

```python
import jax
import jax.numpy as jnp
from jax import lax

D = 768
HEADS = 12
HEAD = 64
FF = 3072
GRID = 64
WIN = 14
IMAGES = 2
NWIN = 5
REL = 27


def draw_tokens(key, part):
    places = jnp.arange(GRID, dtype=jnp.float32)
    level = (places[:, None] + places[None, :]) / (2.0 * (GRID - 1))
    base = jax.random.truncated_normal(key, -4.0, 4.0, (IMAGES, GRID, GRID, D), jnp.float32)
    spread_scale = 0.6 * 3.0 ** level
    return (base * spread_scale[None, :, :, None]).astype(jnp.bfloat16)


def column_weight(key, row_count, column_count):
    entries = jax.random.truncated_normal(jax.random.fold_in(key, 11), -4.0, 4.0, (row_count, column_count), jnp.float32)
    column_part = jax.random.truncated_normal(jax.random.fold_in(key, 23), -3.0, 3.0, (1, column_count), jnp.float32)
    return ((entries + 0.5 * column_part) * row_count ** (-0.5)).astype(jnp.bfloat16)


def draw_qkv_weight(key, part):
    return column_weight(key, D, 3 * D)


def draw_fc1_weight(key, part):
    return column_weight(key, D, FF)


def steps_of(rng, dims, pieces, smallest, largest):
    level = 1.0
    for position, blocks in pieces:
        steps = jax.random.uniform(jax.random.fold_in(jax.random.fold_in(rng, 6), position), (blocks,), jnp.float32, smallest / len(pieces), largest / len(pieces))
        level = level * jnp.repeat(jnp.exp(steps), dims[position] // blocks).reshape((-1,) + (1,) * (len(dims) - 1 - position))
    return level


def scatter_about(own_key, shape, width, bound, shards=(), held_as=jnp.bfloat16):
    values = width * jax.random.normal(own_key, shape, jnp.float32)
    if shards:
        values = values * steps_of(own_key, shape, shards, -0.22, 0.18)
    return jnp.clip(values, -bound, bound).astype(held_as)


def setup_inputs(seed: int = 0) -> dict:
    streams_of = jax.random.split(jax.random.key(seed), 18)
    return {
        "tokens": draw_tokens(jax.random.fold_in(streams_of[17], 71), 0),
        "ln1_gain": jnp.clip(1.0 + 0.1 * jax.random.normal(streams_of[1], (D,), jnp.float32), 0.5, 1.5).astype(jnp.bfloat16),
        "ln1_bias": scatter_about(streams_of[2], (D,), 0.2, 1.0),
        "qkv_weight": draw_qkv_weight(jax.random.fold_in(streams_of[17], 71), 0),
        "query_bias": scatter_about(streams_of[4], (D,), 0.2, 1.0),
        "value_bias": scatter_about(streams_of[5], (D,), 0.2, 1.0),
        "rel_rows": scatter_about(streams_of[6], (REL, HEAD), 0.15, 0.75),
        "rel_cols": scatter_about(streams_of[7], (REL, HEAD), 0.15, 0.75),
        "proj_weight": scatter_about(streams_of[8], (D, D), (D // WIN) ** -0.5, 0.875, ((0, 2), (1, 16))),
        "proj_bias": scatter_about(streams_of[9], (D,), 0.2, 1.0),
        "ln2_gain": jnp.clip(1.0 + 0.1 * jax.random.normal(streams_of[10], (D,), jnp.float32), 0.5, 1.5).astype(jnp.bfloat16),
        "ln2_bias": scatter_about(streams_of[11], (D,), 0.2, 1.0),
        "fc1_weight": draw_fc1_weight(jax.random.fold_in(streams_of[17], 71), 0),
        "fc1_bias": scatter_about(streams_of[13], (FF,), 0.2, 1.0),
        "fc2_weight": scatter_about(streams_of[14], (FF, D), FF ** -0.5, 0.109375, ((0, 2), (1, 16))),
        "fc2_bias": scatter_about(streams_of[15], (D,), 0.2, 1.0),
        "cotangent": scatter_about(streams_of[16], (IMAGES, GRID, GRID, D), 1.0, 6.0, ((0, 2), (1, 4), (2, 4))),
    }


TOP_PRECISION = lax.Precision.HIGHEST
NORM_EPSILON = 1e-06

@jax.custom_vjp
def low(v):
    return lax.optimization_barrier(v.astype(jnp.bfloat16)).astype(jnp.float32)

@jax.custom_vjp
def low_back(v):
    return v

def low_keep(v):
    return (low(v), None)

def low_pass(kept, grad):
    return (grad,)

def back_keep(v):
    return (v, None)

def back_low(kept, grad):
    return (low(grad),)
low.defvjp(low_keep, low_pass)
low_back.defvjp(back_keep, back_low)

def layer_norm(values, gain_vec, bias_vec):
    center = values - lax.optimization_barrier(jnp.mean(values, -1, keepdims=True))
    return center * lax.rsqrt(lax.optimization_barrier(jnp.mean(center * center, -1, keepdims=True)) + NORM_EPSILON) * gain_vec + bias_vec

def product(left, right):
    return jnp.dot(left, right, precision=TOP_PRECISION)

def relative(table):
    offsets = jnp.arange(WIN)[:, None] - jnp.arange(WIN)[None, :] + (WIN - 1)
    return table[offsets]

def window_attention(window_tokens, qkv_weight, query_bias, value_bias, rel_rows, rel_cols, proj_weight, proj_bias):
    packed = product(window_tokens, qkv_weight)
    queries = low_back(low(packed[:, :D] + query_bias)).reshape(WIN * WIN, HEADS, HEAD)
    keys_w = low_back(low(packed[:, D:2 * D])).reshape(WIN * WIN, HEADS, HEAD)
    values = low_back(low(packed[:, 2 * D:] + value_bias)).reshape(WIN * WIN, HEADS, HEAD)
    grid_q = queries.reshape(WIN, WIN, HEADS, HEAD)
    rows_term = jnp.einsum('yxhc,ykc->hyxk', grid_q, relative(rel_rows), precision=TOP_PRECISION)
    cols_term = jnp.einsum('yxhc,xlc->hyxl', grid_q, relative(rel_cols), precision=TOP_PRECISION)
    base = jnp.einsum('ihc,jhc->hij', queries, keys_w, precision=TOP_PRECISION) * HEAD ** (-0.5)
    scores = base.reshape(HEADS, WIN, WIN, WIN, WIN) + rows_term[:, :, :, :, None] + cols_term[:, :, :, None, :]
    scores = low_back(scores.reshape(HEADS, WIN * WIN, WIN * WIN))
    softmax_out = low(jax.nn.softmax(scores, axis=-1))
    mixed_out = jnp.einsum('hij,jhc->ihc', softmax_out, values, precision=TOP_PRECISION).reshape(WIN * WIN, D)
    mixed_out = low_back(low(mixed_out))
    return low_back(low(product(mixed_out, proj_weight) + proj_bias))

def block(image, ln1_gain, ln1_bias, qkv_weight, query_bias, value_bias, rel_rows, rel_cols, proj_weight, proj_bias, ln2_gain, ln2_bias, fc1_weight, fc1_bias, fc2_weight, fc2_bias):
    normed = low_back(low(layer_norm(image, ln1_gain, ln1_bias)))
    edge_size = NWIN * WIN - GRID
    padded = jnp.pad(normed, ((0, edge_size), (0, edge_size), (0, 0)))
    windows = padded.reshape(NWIN, WIN, NWIN, WIN, D).transpose(0, 2, 1, 3, 4).reshape(NWIN * NWIN, WIN * WIN, D)
    attend_one = jax.checkpoint(lambda window_tokens: window_attention(window_tokens, qkv_weight, query_bias, value_bias, rel_rows, rel_cols, proj_weight, proj_bias))
    attended = lax.map(attend_one, windows)
    attended = attended.reshape(NWIN, NWIN, WIN, WIN, D).transpose(0, 2, 1, 3, 4).reshape(NWIN * WIN, NWIN * WIN, D)[:GRID, :GRID]
    middle = image + attended
    normed2 = low(layer_norm(middle, ln2_gain, ln2_bias)).reshape(GRID * GRID, D)
    upper = low_back(product(normed2, fc1_weight) + fc1_bias)
    activated = low(jax.nn.gelu(upper, approximate=False))
    branch = low_back(product(activated, fc2_weight) + fc2_bias).reshape(GRID, GRID, D)
    return (middle + branch, (attended, middle, branch))

def root_mean(values):
    return jnp.sqrt(jnp.mean(values * values))

def reference(tokens, ln1_gain, ln1_bias, qkv_weight, query_bias, value_bias, rel_rows, rel_cols, proj_weight, proj_bias, ln2_gain, ln2_bias, fc1_weight, fc1_bias, fc2_weight, fc2_bias, cotangent):
    params = tuple((p.astype(jnp.float32) for p in (ln1_gain, ln1_bias, qkv_weight, query_bias, value_bias, rel_rows, rel_cols, proj_weight, proj_bias, ln2_gain, ln2_bias, fc1_weight, fc1_bias, fc2_weight, fc2_bias)))

    def one_image(carried, inputs):
        image, grad_out = inputs
        image_f = image.astype(jnp.float32)
        result, pull_back, extras = jax.vjp(block, image_f, *params, has_aux=True)
        grads = pull_back(grad_out.astype(jnp.float32))
        attended, middle, branch = extras
        statistics = jnp.stack([root_mean(image_f), root_mean(middle), root_mean(result), root_mean(attended), root_mean(branch)])
        carried = tuple((c + g for c, g in zip(carried, grads[1:])))
        return (carried, (result.astype(jnp.bfloat16), grads[0].astype(jnp.bfloat16), statistics))
    zero_grads = tuple((jnp.zeros(p.shape, jnp.float32) for p in params))
    totals, (output, input_grad, statistics) = lax.scan(one_image, zero_grads, (tokens, cotangent))
    return (output, input_grad, totals[0], totals[1], totals[2], totals[3], totals[4], totals[5], totals[6], totals[7], totals[8], totals[9], totals[10], totals[11], totals[12], totals[13], totals[14], statistics)
```

```python
import functools

import jax
import jax.numpy as jnp
import numpy as np
from jax import lax
from jax.experimental import pallas as pl
from jax.experimental.pallas import tpu as pltpu
from jax.sharding import PartitionSpec as P

HEADS = 12
HEAD = 64
WIN = 14
EPS = 1e-06
MESH = pl.DeviceIdType.MESH
F32 = jnp.float32
BF = jnp.bfloat16

D = HEADS * HEAD
TILE = 16
TOK = TILE * TILE
HI, LO = 12, 6
SLOT = 256
QROWS = WIN * 16
PAIRS = HEADS // 2
FIELD = 1184
SENDS = 640
MIB = 2**20

LINKS = {
    (-1, 0): (True, 0, 192, 352),
    (1, 0): (True, 160, 96, 256),
    (0, -1): (False, 0, 192, 640),
    (0, 1): (False, 192, 96, 544),
    (-1, -1): (False, 288, 144, 1040),
    (-1, 1): (False, 432, 80, 960),
    (1, -1): (False, 512, 80, 880),
    (1, 1): (False, 592, 48, 832),
}


def nt(a, b):
    return lax.dot_general(a, b, (((1,), (1,)), ((), ())), preferred_element_type=F32)


def nn(a, b):
    return lax.dot_general(a, b, (((1,), (0,)), ((), ())), preferred_element_type=F32)


def tn(a, b):
    return lax.dot_general(a, b, (((0,), (0,)), ((), ())), preferred_element_type=F32)


def pick_rows():
    table = np.zeros((SENDS, TOK), np.float32)
    spans = {
        0: (range(16), range(12)),
        192: (range(16), range(10, 16)),
        288: (range(12), range(12)),
        432: (range(12), range(10, 16)),
        512: (range(10, 16), range(12)),
        592: (range(10, 16), range(10, 16)),
    }
    for base, (ys, xs) in spans.items():
        for i, (y, x) in enumerate((y, x) for y in ys for x in xs):
            table[base + i, y * TILE + x] = 1.0
    return table


def table_places(back):
    place = np.zeros((256, 64), np.float32)
    for head in range(2):
        for r in range(2 * WIN - 1):
            for copy in range(2):
                row_lane = (64 + 28 * copy + r + 64 * head) % 128
                col_lane = (28 * copy + r + 64 * head) % 128
                place[128 * head + row_lane, 26 - r] = 1.0
                place[128 * head + col_lane, 32 + (r if back else 26 - r)] = 1.0
    return place


def key_marks(back):
    marks = np.zeros((2, SLOT, 128), np.float32)
    for head in range(2):
        for j in range(SLOT):
            k, l = divmod(j, 16)
            if k < WIN and l < WIN:
                for copy in range(2):
                    marks[head, j, (64 + 28 * copy + k + 64 * head) % 128] = 1.0
                    marks[head, j, (78 + 28 * copy + (13 - l if back else l) + 64 * head) % 128] = 1.0
            else:
                marks[head, j, (120 + 64 * head) % 128] = -1e30
    return marks


def lane_kinds(rows):
    lane = lax.broadcasted_iota(jnp.int32, (rows, 128), 1)
    kinds = []
    for head in range(2):
        at = (lane + 64 * head) % 128 if head else lane
        own = at < 64
        first = (at >= 64) & (at < 92)
        second = (at >= 92) & (at < 120)
        is_row = ((at >= 64) & (at < 78)) | ((at >= 92) & (at < 106))
        kinds.append((own, first, second, is_row, at == 120))
    return kinds


def slot_axis(first, count, tile_at, tiles):
    rel = first + count - TILE * tile_at
    valid = (count < WIN) & (first + count < TILE * tiles)
    return rel, valid


def window_index(a, b, row, col, n_row, n_col):
    place = lax.broadcasted_iota(jnp.int32, (SLOT, 1), 0)
    y = place // 16
    x = place - 16 * y
    ry, ok_y = slot_axis(((TILE * row) // WIN + a) * WIN, y, row, n_row)
    rx, ok_x = slot_axis(((TILE * col) // WIN + b) * WIN, x, col, n_col)
    up, down = ry < 0, ry >= TILE
    left, right = rx < 0, rx >= TILE
    base_mid = jnp.where(up, 256, jnp.where(down, 352, 0))
    base_left = jnp.where(up, 832, jnp.where(down, 960, 544))
    base_right = jnp.where(up, 880, jnp.where(down, 1040, 640))
    base = jnp.where(left, base_left, jnp.where(right, base_right, base_mid))
    width = jnp.where(left, LO, jnp.where(right, HI, TILE))
    py = jnp.where(up, ry + LO, jnp.where(down, ry - TILE, ry))
    px = jnp.where(left, rx + LO, jnp.where(right, rx - TILE, rx))
    return jnp.where(ok_y & ok_x, base + py * width + px, -1)


def own_slot(row, col):
    place = lax.broadcasted_iota(jnp.int32, (TOK, 1), 0)
    ty = place // TILE
    tx = place - TILE * ty
    out = 0
    parts = []
    for t, at in ((ty, row), (tx, col)):
        y = TILE * at + t - ((TILE * at) // WIN) * WIN
        late = (y >= WIN).astype(jnp.int32)
        parts.append((late, y - WIN * late))
    (a, y), (b, x) = parts
    return (2 * a + b) * SLOT + 16 * y + x


def own_mask(row, col, n_row, n_col):
    place = lax.broadcasted_iota(jnp.int32, (1, 4 * SLOT), 1)
    slot = place // SLOT
    rest = place - slot * SLOT
    y = rest // 16
    x = rest - 16 * y
    a = slot // 2
    b = slot - 2 * a
    good = None
    for t, which, at, n in ((y, a, row, n_row), (x, b, col, n_col)):
        rel = ((TILE * at) // WIN + which) * WIN + t - TILE * at
        end = jnp.where(at == n - 1, 4096, TILE)
        ok = (t < WIN) & (rel >= 0) & (rel < end)
        good = ok if good is None else good & ok
    return good


def one_hot(index, size):
    lane = lax.broadcasted_iota(jnp.int32, (index.shape[0], size), 1)
    return jnp.where(lane == index, 1.0, 0.0).astype(BF)


def norm(v, gain, bias):
    mean = jnp.mean(v, -1, keepdims=True)
    center = v - mean
    inverse = lax.rsqrt(jnp.mean(center * center, -1, keepdims=True) + EPS)
    xhat = center * inverse
    return xhat * gain + bias, xhat, inverse


def norm_back(grad, xhat, inverse, gain):
    d = grad * gain
    return inverse * (
        d - jnp.mean(d, -1, keepdims=True) - xhat * jnp.mean(d * xhat, -1, keepdims=True)
    )


def grid_place():
    return lax.axis_index("dp"), lax.axis_index("row"), lax.axis_index("col")


def exists(step, row, col, n_row, n_col):
    r, c = row + step[0], col + step[1]
    return (r >= 0) & (r < n_row) & (c >= 0) & (c < n_col)


def greet(n_row, n_col, corners, lines):
    dp, row, col = grid_place()
    barrier = pltpu.get_barrier_semaphore()
    count = 0
    if lines:
        for d in (1, 2, 3):
            pl.semaphore_signal(
                barrier, inc=1, device_id=(dp, row, lax.rem(col + d, n_col)), device_id_type=MESH
            )
            pl.semaphore_signal(
                barrier, inc=1, device_id=(dp, lax.rem(row + d, n_row), col), device_id_type=MESH
            )
        pl.semaphore_signal(barrier, inc=1, device_id=(1 - dp, row, col), device_id_type=MESH)
        count += 7
    if corners:
        for step in LINKS:
            if lines and 0 in step:
                continue
            there = exists(step, row, col, n_row, n_col)

            @pl.when(there)
            def _():
                pl.semaphore_signal(
                    barrier,
                    inc=1,
                    device_id=(dp, row + step[0], col + step[1]),
                    device_id_type=MESH,
                )

            count = count + jnp.where(there, 1, 0)
    pl.semaphore_wait(barrier, count)


def halo_copies(field, picked, send, recv, n_row, n_col):
    dp, row, col = grid_place()
    out = []
    for i, (step, (own, first, rows, there)) in enumerate(LINKS.items()):
        src = (field if own else picked).at[pl.ds(first, rows)]
        out.append(
            (
                exists(step, row, col, n_row, n_col),
                pltpu.make_async_remote_copy(
                    src,
                    field.at[pl.ds(there, rows)],
                    send.at[i],
                    recv.at[i],
                    device_id=(dp, row + step[0], col + step[1]),
                    device_id_type=MESH,
                ),
                exists((-step[0], -step[1]), row, col, n_row, n_col),
            )
        )
    return out


def halo_start(field, picked, pick_ref, send, recv, n_row, n_col):
    picked[...] = nn(pick_ref[...], field[pl.ds(0, TOK), :]).astype(BF)
    for there, copy, _ in halo_copies(field, picked, send, recv, n_row, n_col):
        pl.when(there)(copy.start)


def halo_wait(field, picked, send, recv, n_row, n_col):
    for there, copy, comes in halo_copies(field, picked, send, recv, n_row, n_col):
        pl.when(there)(copy.wait_send)
        pl.when(comes)(copy.wait_recv)


def halo_xla(own, n_row, n_col):
    grid = own.reshape(TILE, TILE, -1)
    cut = {
        (-1, 0): grid[:12],
        (1, 0): grid[10:],
        (0, -1): grid[:, :12],
        (0, 1): grid[:, 10:],
        (-1, -1): grid[:12, :12],
        (-1, 1): grid[:12, 10:],
        (1, -1): grid[10:, :12],
        (1, 1): grid[10:, 10:],
    }
    pieces = {0: own}
    for step, block in cut.items():
        pairs = [
            (r * n_col + c, (r + step[0]) * n_col + c + step[1])
            for r in range(n_row)
            for c in range(n_col)
            if 0 <= r + step[0] < n_row and 0 <= c + step[1] < n_col
        ]
        flat = block.reshape(-1, own.shape[1])
        got = lax.ppermute(flat, ("row", "col"), pairs)
        rows, there = LINKS[step][2:]
        pieces[there] = jnp.pad(got, ((0, rows - got.shape[0]), (0, 0)))
    return jnp.concatenate([pieces[k] for k in sorted(pieces)], 0)


def blocks_of(shapes):
    return [(n // 16, k // 2) for n, k in shapes]


class Gather:
    def __init__(self, full, block, half, send, recv):
        dp, row, col = grid_place()
        self.full, self.b, self.h = full, block, half
        self.send, self.recv = send, recv
        self.dp, self.row, self.col = dp, row, col
        self.lanes = pl.ds(pl.multiple_of(dp * half, 128), half)
        self.other = pl.ds(pl.multiple_of((1 - dp) * half, 128), half)

    def region(self, first, rows, lanes):
        return self.full.at[pl.ds(pl.multiple_of(first, 16), rows), lanes]

    def group(self, flip, part=None):
        first = jnp.bitwise_xor(self.row, flip) * 4 * self.b
        if part is None:
            return first, 4 * self.b
        return first + part * 2 * self.b, 2 * self.b

    def copy(self, i, at, land, target):
        core = target == "core"
        if core:
            device = (1 - self.dp, self.row, self.col)
        elif isinstance(target, tuple):
            device = (self.dp, self.row, lax.rem(self.col + target[0], 4))
        else:
            device = (self.dp, jnp.bitwise_xor(self.row, target), self.col)

        def make(where):
            return pltpu.make_async_remote_copy(
                where, where, self.send.at[i], self.recv.at[i], device_id=device, device_id_type=MESH
            )

        return (
            lambda: make(self.region(*at, self.lanes)),
            lambda: make(self.region(*land, self.other if core else self.lanes)),
        )

    def stage(self, k):
        own = (self.row * 4 + self.col) * self.b
        out = []
        if k == 0:
            for d in (1, 2, 3):
                frm = (self.row * 4 + lax.rem(self.col + 4 - d, 4)) * self.b
                out.append(self.copy(d - 1, (own, self.b), (frm, self.b), (d,)))
        elif k == 1:
            for i, flip in ((3, 1), (4, 2)):
                out.append(self.copy(i, self.group(0), self.group(flip), flip))
            out.append(self.copy(7, self.group(0), self.group(0), "core"))
        elif k == 2:
            out.append(self.copy(5, self.group(2, 0), self.group(3, 0), 1))
            out.append(self.copy(6, self.group(1, 1), self.group(3, 1), 2))
            out.append(self.copy(8, self.group(1), self.group(1), "core"))
            out.append(self.copy(9, self.group(2), self.group(2), "core"))
        else:
            out.append(self.copy(10, self.group(3), self.group(3), "core"))
        return out

    def start(self, k):
        for out, _ in self.stage(k):
            out().start()

    def arrive(self, k):
        for (_, come), link in zip(self.stage(k), self.links(k)):
            if link:
                come().wait_recv()

    def links(self, k):
        return {0: (1, 1, 1), 1: (1, 1, 0), 2: (1, 1, 0, 0), 3: (0,)}[k]

    def finish(self):
        for k in range(4):
            for (out, come), link in zip(self.stage(k), self.links(k)):
                if not link:
                    come().wait_recv()
                out().wait_send()


GATHER_SEMS = 11


def gather_kernel(
    n_row, n_col, shapes,
    tokens, vecs, pick, w0, w1, w2, w3,
    field, f0, f1, f2, f3,
    picked, s0, s1, s2, s3, halo_send, halo_recv, local_sem, *sems,
):
    dp, row, col = grid_place()
    field[pl.ds(TOK, FIELD - TOK), :] = jnp.zeros((FIELD - TOK, D), BF)
    greet(n_row, n_col, True, True)
    ways = []
    for i, (shard, stage, full, (b, h)) in enumerate(
        zip((w0, w1, w2, w3), (s0, s1, s2, s3), (f0, f1, f2, f3), blocks_of(shapes))
    ):
        stage[...] = shard[...].T
        way = Gather(full, b, h, sems[2 * i], sems[2 * i + 1])
        mine = pltpu.make_async_copy(
            stage, way.region((row * 4 + col) * b, b, way.lanes), local_sem.at[i]
        )
        mine.start()
        ways.append((way, mine))
    normed, _, _ = norm(tokens[...].astype(F32), vecs[0:1, :], vecs[1:2, :])
    field[pl.ds(0, TOK), :] = normed.astype(BF)
    halo_start(field, picked, pick, halo_send, halo_recv, n_row, n_col)
    for way, mine in ways:
        mine.wait()
        way.start(0)
    for k in range(3):
        for way, _ in ways:
            way.arrive(k)
            way.start(k + 1)
    halo_wait(field, picked, halo_send, halo_recv, n_row, n_col)
    for way, _ in ways:
        way.finish()


def vmem():
    return pl.BlockSpec(memory_space=pltpu.VMEM)


def hbm():
    return pl.BlockSpec(memory_space=pl.ANY)


def gather_call(n_row, n_col, shapes, tokens, vecs, pick, shards):
    blocks = blocks_of(shapes)
    sems = []
    for _ in range(4):
        sems += [pltpu.SemaphoreType.DMA((GATHER_SEMS,)), pltpu.SemaphoreType.DMA((GATHER_SEMS,))]
    return pl.pallas_call(
        functools.partial(gather_kernel, n_row, n_col, shapes),
        name="gather",
        out_shape=[jax.ShapeDtypeStruct((FIELD, D), BF)]
        + [jax.ShapeDtypeStruct(s, BF) for s in shapes],
        in_specs=[vmem()] * 7,
        out_specs=[vmem()] + [hbm()] * 4,
        scratch_shapes=[pltpu.VMEM((SENDS, D), BF)]
        + [pltpu.VMEM(b, BF) for b in blocks]
        + [
            pltpu.SemaphoreType.DMA((8,)),
            pltpu.SemaphoreType.DMA((8,)),
            pltpu.SemaphoreType.DMA((4,)),
        ]
        + sems,
        compiler_params=pltpu.CompilerParams(
            collective_id=0, has_side_effects=True, vmem_limit_bytes=40 * MIB
        ),
    )(tokens, vecs, pick, *shards)


def halo_kernel(n_row, n_col, own, pick, field, picked, send, recv):
    field[pl.ds(TOK, FIELD - TOK), :] = jnp.zeros((FIELD - TOK, D), BF)
    field[pl.ds(0, TOK), :] = own[...]
    greet(n_row, n_col, True, False)
    halo_start(field, picked, pick, send, recv, n_row, n_col)
    halo_wait(field, picked, send, recv, n_row, n_col)


def halo_call(n_row, n_col, own, pick):
    return pl.pallas_call(
        functools.partial(halo_kernel, n_row, n_col),
        name="halo",
        out_shape=jax.ShapeDtypeStruct((FIELD, D), BF),
        in_specs=[vmem()] * 2,
        out_specs=vmem(),
        scratch_shapes=[
            pltpu.VMEM((SENDS, D), BF),
            pltpu.SemaphoreType.DMA((8,)),
            pltpu.SemaphoreType.DMA((8,)),
        ],
        compiler_params=pltpu.CompilerParams(
            collective_id=1, has_side_effects=True, vmem_limit_bytes=40 * MIB
        ),
    )(own, pick)


class Reduce:
    def __init__(self, grad, total, come, block, half, send, recv):
        self.dp, self.row, self.col = grid_place()
        self.grad, self.total, self.come = grad, total, come
        self.b, self.h, self.send, self.recv = block, half, send, recv
        self.lanes = pl.ds(pl.multiple_of(self.dp * half, 128), half)
        self.other = pl.ds(pl.multiple_of((1 - self.dp) * half, 128), half)

    def at(self, flip):
        return pl.multiple_of(jnp.bitwise_xor(self.row, flip) * 4 * self.b, 16)

    def copies(self, k):
        b, come = self.b, self.come
        if k == 0:
            plan = [
                (self.grad.at[:, self.other], come.at[pl.ds(0, 16 * b)], (1 - self.dp, self.row, self.col))
            ]
        elif k == 1:
            x = (self.dp, jnp.bitwise_xor(self.row, 1), self.col)
            y = (self.dp, jnp.bitwise_xor(self.row, 2), self.col)
            far = self.at(3)
            plan = [
                (self.total.at[pl.ds(far, 2 * b)], come.at[pl.ds(16 * b, 2 * b)], x),
                (
                    self.total.at[pl.ds(pl.multiple_of(far + 2 * b, 16), 2 * b)],
                    come.at[pl.ds(18 * b, 2 * b)],
                    y,
                ),
            ]
        elif k == 2:
            plan = [
                (
                    self.total.at[pl.ds(self.at(flip), 4 * b)],
                    come.at[pl.ds(20 * b + 4 * b * (flip - 1), 4 * b)],
                    (self.dp, jnp.bitwise_xor(self.row, flip), self.col),
                )
                for flip in (1, 2)
            ]
        else:
            plan = []
            for d in (1, 2, 3):
                to = lax.rem(self.col + d, 4)
                plan.append(
                    (
                        self.total.at[pl.ds(pl.multiple_of(self.at(0) + to * b, 16), b)],
                        come.at[pl.ds((27 + d) * b, b)],
                        (self.dp, self.row, to),
                    )
                )
        base = {0: 0, 1: 1, 2: 3, 3: 5}[k]
        return [
            pltpu.make_async_remote_copy(
                src, dst, self.send.at[base + i], self.recv.at[base + i], device_id=dev, device_id_type=MESH
            )
            for i, (src, dst, dev) in enumerate(plan)
        ]

    def start(self, k):
        for copy in self.copies(k):
            copy.start()

    def arrive(self, k):
        for copy in self.copies(k):
            copy.wait_recv()

    def sent(self, k):
        for copy in self.copies(k):
            copy.wait_send()

    def add(self, k):
        b, h = self.b, self.h
        total, come = self.total, self.come
        step = 48 if h <= 384 else 16

        def loop(rows, into, froms):
            def body(i, _):
                at = pl.ds(pl.multiple_of(into + i * step, 16), step)
                value = total[at, :].astype(F32)
                for f in froms:
                    value = value + come[pl.ds(pl.multiple_of(f + i * step, 16), step), :].astype(F32)
                total[at, :] = value.astype(BF)
                return 0

            lax.fori_loop(0, rows // step, body, 0)

        if k == 0:

            def body(i, _):
                at = pl.ds(pl.multiple_of(i * step, 16), step)
                value = self.grad[at, self.lanes].astype(F32) + come[at, :].astype(F32)
                total[at, :] = value.astype(BF)
                return 0

            lax.fori_loop(0, 16 * b // step, body, 0)
        elif k == 1:
            loop(2 * b, self.at(2), (16 * b,))
            loop(2 * b, self.at(1) + 2 * b, (18 * b,))
        elif k == 2:
            loop(4 * b, self.at(0), (20 * b, 24 * b))

    def result(self):
        b = self.b
        mine = pl.ds(pl.multiple_of(self.at(0) + self.col * b, 16), b)
        value = self.total[mine, :].astype(F32)
        for d in (1, 2, 3):
            value = value + self.come[pl.ds((27 + d) * b, b), :].astype(F32)
        return value.T


REDUCE_SEMS = 8


def reduce_kernel(
    n_row, n_col, shapes,
    small, g0, g1, g2, g3,
    o0, o1, o2, o3, small_out,
    t0, c0, t1, c1, t2, c2, t3, c3, small_in, small_sem, *sems,
):
    dp, row, col = grid_place()
    greet(n_row, n_col, False, True)
    ways = []
    for i, (g, t, c, (b, h)) in enumerate(
        zip((g0, g1, g2, g3), (t0, t1, t2, t3), (c0, c1, c2, c3), blocks_of(shapes))
    ):
        ways.append(Reduce(g, t, c, b, h, sems[2 * i], sems[2 * i + 1]))
    for way in ways:
        way.start(0)
    small_out[...] = small[...]
    partners = [
        (dp, jnp.bitwise_xor(row, 1), col),
        (dp, jnp.bitwise_xor(row, 2), col),
        (dp, row, jnp.bitwise_xor(col, 1)),
        (dp, row, jnp.bitwise_xor(col, 2)),
        (1 - dp, row, col),
    ]

    def small_copy(s):
        return pltpu.make_async_remote_copy(
            small_out, small_in.at[s], small_sem.at[0, s], small_sem.at[1, s], device_id=partners[s], device_id_type=MESH
        )

    def small_step(s):
        small_copy(s).wait()
        value = small_in[s]
        if s == 4:
            line = lax.broadcasted_iota(jnp.int32, value.shape, 0)
            value = jnp.where(line == 12, 0.0, value)
        small_out[...] = small_out[...] + value
        if s < 4:
            small_copy(s + 1).start()

    small_copy(0).start()
    for way in ways:
        way.arrive(0)
        way.add(0)
        way.start(1)
    small_step(0)
    for way in ways:
        way.arrive(1)
        way.add(1)
        way.start(2)
    small_step(1)
    for n, way in enumerate(ways):
        way.arrive(2)
        way.add(2)
        way.start(3)
        if n == 0:
            small_step(2)
        if n == 1:
            small_step(3)
    small_step(4)
    for way, out in zip(ways, (o0, o1, o2, o3)):
        way.arrive(3)
        out[...] = way.result()
        for k in range(4):
            way.sent(k)


def reduce_call(n_row, n_col, shapes, small, grads):
    blocks = blocks_of(shapes)
    scratch, sems = [], []
    for (n, k), (b, h) in zip(shapes, blocks):
        scratch += [pltpu.VMEM((n, h), BF), pltpu.VMEM((31 * b, h), BF)]
        sems += [pltpu.SemaphoreType.DMA((REDUCE_SEMS,)), pltpu.SemaphoreType.DMA((REDUCE_SEMS,))]
    return pl.pallas_call(
        functools.partial(reduce_kernel, n_row, n_col, shapes),
        name="reduce",
        out_shape=[jax.ShapeDtypeStruct((h, b), F32) for b, h in blocks]
        + [jax.ShapeDtypeStruct(small.shape, F32)],
        in_specs=[vmem()] * 5,
        out_specs=[vmem()] * 5,
        scratch_shapes=scratch
        + [pltpu.VMEM((5,) + small.shape, F32), pltpu.SemaphoreType.DMA((2, 5))]
        + sems,
        compiler_params=pltpu.CompilerParams(
            collective_id=2, has_side_effects=True, vmem_limit_bytes=60 * MIB
        ),
    )(small, *grads)


def table_kernel_value(places, table):
    value = nn(places, table)
    line = lax.broadcasted_iota(jnp.int32, value.shape, 0)
    lane = lax.broadcasted_iota(jnp.int32, value.shape, 1)
    return jnp.where((line < 128) == (lane < 64), value, 0.0).astype(BF)


def spread(a, back):
    rows, cols = [], []
    for y in range(WIN):
        part = a[16 * y : 16 * y + 16, :]
        if back:
            rows.append(pltpu.roll(part, 13 - y, 1))
        else:
            rows.append(pltpu.roll(part, (115 + y) % 128, 1))
            cols.append(pltpu.roll(part, 65, 1, stride=1, stride_axis=0))
    return rows, cols


def attend_pair(i, qkv, table, marks, masks, probs, mixed):
    r0 = pl.multiple_of((i // PAIRS) * SLOT, SLOT)
    pair = lax.rem(i, PAIRS)
    l0 = pl.multiple_of(pair * 128, 128)
    q2 = qkv[pl.ds(r0, QROWS), pl.ds(l0, 128)]
    k2 = qkv[pl.ds(r0, SLOT), pl.ds(D + l0, 128)]
    v2 = qkv[pl.ds(r0, SLOT), pl.ds(2 * D + l0, 128)]
    a2 = nt(q2, table[...])
    qf = q2.astype(F32) * HEAD**-0.5
    kinds = lane_kinds(QROWS)
    outs = []
    for head in range(2):
        own, first, second, is_row, one = kinds[head]
        rows, cols = spread(a2[:, 128 * head : 128 * head + 128], False)
        bias = jnp.where(is_row, jnp.concatenate(rows, 0), jnp.concatenate(cols, 0))
        high = bias.astype(BF).astype(F32)
        aug = jnp.where(
            own,
            qf,
            jnp.where(
                first, high, jnp.where(second, bias - high, jnp.where(one, 1.0, 0.0))
            ),
        ).astype(BF)
        keys = k2 * masks[head : head + 1, :] + marks[head]
        scores = nt(aug, keys)
        top = jnp.max(scores, -1, keepdims=True)
        e = jnp.exp(scores - top)
        p = (e * (1.0 / jnp.sum(e, -1, keepdims=True))).astype(BF)
        probs[(i // PAIRS) * HEADS + 2 * pair + head] = p
        outs.append(nn(p, v2))
    out = jnp.where(kinds[0][0], outs[0], outs[1]).astype(BF)
    mixed[pl.ds(r0, QROWS), pl.ds(l0, 128)] = out


def attend_kernel(
    n_row, n_col,
    field, wqkv, wproj, vecs, places, table_in, marks, masks,
    qkv, probs, mixed_own, attended,
    xw, mixed, table,
):
    _, row, col = grid_place()
    table[...] = table_kernel_value(places[...], table_in[...])
    for w in range(4):
        hot = one_hot(window_index(w // 2, w % 2, row, col, n_row, n_col), FIELD)
        xw[pl.ds(w * SLOT, SLOT), :] = nn(hot, field[...]).astype(BF)
    for part, line in ((0, 2), (1, None), (2, 3)):

        def body(n, _):
            at = pl.multiple_of(n * 256, 256)
            value = nt(xw[...], wqkv[pl.ds(part * D + at, 256), :])
            if line is not None:
                value = value + vecs[line : line + 1, pl.ds(at, 256)]
            qkv[:, pl.ds(part * D + at, 256)] = value.astype(BF)
            return 0

        lax.fori_loop(0, 3, body, 0)
    mixed[...] = jnp.zeros_like(mixed)

    def pair(i, _):
        attend_pair(i, qkv, table, marks, masks, probs, mixed)
        return 0

    lax.fori_loop(0, 4 * PAIRS, pair, 0)
    hot = one_hot(own_slot(row, col), 4 * SLOT)
    own = nn(hot, mixed[...]).astype(BF)
    mixed_own[...] = own
    attended[...] = (nt(own, wproj[...]) + vecs[4:5, :]).astype(BF)


def attend_call(n_row, n_col, field, wqkv, wproj, vecs, places, table, marks, masks):
    return pl.pallas_call(
        functools.partial(attend_kernel, n_row, n_col),
        name="attend",
        out_shape=[
            jax.ShapeDtypeStruct((4 * SLOT, 3 * D), BF),
            jax.ShapeDtypeStruct((4 * HEADS, QROWS, SLOT), BF),
            jax.ShapeDtypeStruct((TOK, D), BF),
            jax.ShapeDtypeStruct((TOK, D), BF),
        ],
        in_specs=[vmem()] * 8,
        out_specs=[vmem()] * 4,
        scratch_shapes=[
            pltpu.VMEM((4 * SLOT, D), BF),
            pltpu.VMEM((4 * SLOT, D), BF),
            pltpu.VMEM((256, 128), BF),
        ],
        compiler_params=pltpu.CompilerParams(vmem_limit_bytes=56 * MIB),
    )(field, wqkv, wproj, vecs, places, table, marks, masks)


def mlp_kernel(
    tokens, attended, cot, w1, w2, vecs,
    output, grad_middle, grad_attended, g1, g2, small,
    n2, cot_t, branch, gn2,
):
    gain = vecs[5:6, :]
    tok = tokens[...].astype(F32)
    middle = tok + attended[...].astype(F32)
    normed, xhat, inverse = norm(middle, gain, vecs[6:7, :])
    n2[...] = normed.astype(BF)
    cot_t[...] = cot[...].T
    branch[...] = jnp.zeros_like(branch)
    gn2[...] = jnp.zeros_like(gn2)
    small[...] = jnp.zeros_like(small)

    def body(j, _):
        at = pl.multiple_of(j * 256, 256)
        line = j // 3
        lane = pl.multiple_of(lax.rem(j, 3) * 256, 256)
        w1c = w1[pl.ds(at, 256), :]
        w2c = w2[:, pl.ds(at, 256)]
        u = nt(n2[...], w1c) + vecs[pl.ds(8 + line, 1), pl.ds(lane, 256)]
        cdf = 0.5 * (1.0 + lax.erf(u * 0.7071067811865476))
        act = (u * cdf).astype(BF)
        pdf = jnp.exp(-0.5 * u * u) * 0.3989422804014327
        branch[...] += nt(act, w2c)
        gact = nn(cot[...], w2c)
        gu = (gact * (cdf + u * pdf)).astype(BF)
        gn2[...] += nn(gu, w1c)
        g1[pl.ds(at, 256), :] = tn(gu, n2[...]).astype(BF)
        g2[:, pl.ds(at, 256)] = nn(cot_t[...], act).astype(BF)
        small[pl.ds(8 + line, 1), pl.ds(lane, 256)] = jnp.sum(gu.astype(F32), 0, keepdims=True)
        return 0

    lax.fori_loop(0, w1.shape[0] // 256, body, 0)
    att = attended[...].astype(F32)
    middle = tokens[...].astype(F32) + att
    normed, xhat, inverse = norm(middle, gain, vecs[6:7, :])
    br = branch[...] + vecs[7:8, :]
    result = middle + br
    output[...] = result.astype(BF)
    grad = gn2[...]
    cf = cot[...].astype(F32)
    gm = cf + norm_back(grad, xhat, inverse, gain)
    grad_middle[...] = gm
    grad_attended[...] = gm.astype(BF)
    small[5:6, :] = jnp.sum(grad * xhat, 0, keepdims=True)
    small[6:7, :] = jnp.sum(grad, 0, keepdims=True)
    small[7:8, :] = jnp.sum(cf, 0, keepdims=True)
    lane = lax.broadcasted_iota(jnp.int32, (1, D), 1)
    stats = jnp.zeros((1, D), F32)
    for n, v in enumerate((tokens[...].astype(F32), middle, result, att, br)):
        total = jnp.sum(jnp.sum(v * v, 0, keepdims=True), 1, keepdims=True)
        stats = jnp.where(lane == n, total, stats)
    small[12:13, :] = stats


def mlp_call(tokens, attended, cot, w1, w2, vecs):
    hidden = w1.shape[0]
    return pl.pallas_call(
        mlp_kernel,
        name="mlp",
        out_shape=[
            jax.ShapeDtypeStruct((TOK, D), BF),
            jax.ShapeDtypeStruct((TOK, D), F32),
            jax.ShapeDtypeStruct((TOK, D), BF),
            jax.ShapeDtypeStruct((hidden, D), BF),
            jax.ShapeDtypeStruct((D, hidden), BF),
            jax.ShapeDtypeStruct((16, D), F32),
        ],
        in_specs=[vmem()] * 6,
        out_specs=[vmem()] * 6,
        scratch_shapes=[
            pltpu.VMEM((TOK, D), BF),
            pltpu.VMEM((D, TOK), BF),
            pltpu.VMEM((TOK, D), F32),
            pltpu.VMEM((TOK, D), F32),
        ],
        compiler_params=pltpu.CompilerParams(vmem_limit_bytes=56 * MIB),
    )(tokens, attended, cot, w1, w2, vecs)


def attend_back_pair(i, qkv, gmix, probs, table, marks, masks, own_rows, dqkv, gtab):
    r0 = pl.multiple_of((i // PAIRS) * SLOT, SLOT)
    pair = lax.rem(i, PAIRS)
    l0 = pl.multiple_of(pair * 128, 128)
    scale = HEAD**-0.5
    q2 = qkv[pl.ds(r0, QROWS), pl.ds(l0, 128)]
    k2 = qkv[pl.ds(r0, SLOT), pl.ds(D + l0, 128)]
    v2 = qkv[pl.ds(r0, SLOT), pl.ds(2 * D + l0, 128)]
    g2 = gmix[pl.ds(r0, QROWS), pl.ds(l0, 128)]
    q_own = q2 * own_rows[pl.ds(r0, QROWS), :]
    kinds = lane_kinds(QROWS)
    dq, dk, dv = [], [], []
    for head in range(2):
        own, first, second, is_row, one = kinds[head]
        mask = masks[head : head + 1, :]
        p = probs[(i // PAIRS) * HEADS + 2 * pair + head]
        pf = p.astype(F32)
        dp = nt(g2, v2 * mask)
        ds = (pf * (dp - jnp.sum(pf * dp, -1, keepdims=True))).astype(BF)
        keys = k2 * (mask * jnp.asarray(scale, BF)) + marks[head]
        dqa = nn(ds, keys)
        rows, _ = spread(jnp.where(is_row, dqa, 0.0), True)
        line = jnp.where((first | second) & ~is_row, dqa, 0.0)
        back = jnp.concatenate(rows, 0) + unspread_cols(line)
        at = (lax.broadcasted_iota(jnp.int32, (QROWS, 128), 1) + 64 * head) % 128
        is_high = (at < 28) | ((at >= 64) & (at < 92))
        high = back.astype(BF).astype(F32)
        split = jnp.where(is_high, high, back - high).astype(BF)
        extra = nn(split, table[128 * head : 128 * head + 128, :])
        dq.append(dqa + extra)
        gtab[head] += tn(split, q_own)
        dk.append(tn(ds, q2))
        dv.append(tn(p, g2))
    wide = lane_kinds(SLOT)[0][0]
    dqkv[pl.ds(r0, QROWS), pl.ds(l0, 128)] = jnp.where(kinds[0][0], dq[0], dq[1]).astype(BF)
    dqkv[pl.ds(r0, SLOT), pl.ds(D + l0, 128)] = (jnp.where(wide, dk[0], dk[1]) * scale).astype(BF)
    dqkv[pl.ds(r0, SLOT), pl.ds(2 * D + l0, 128)] = jnp.where(wide, dv[0], dv[1]).astype(BF)


def unspread_cols(line):
    parts = []
    for y in range(WIN):
        parts.append(pltpu.roll(line[16 * y : 16 * y + 16, :], 50, 1, stride=1, stride_axis=0))
    return jnp.concatenate(parts, 0)


def attend_back_kernel(
    n_row, n_col,
    gfield, nfield, tokens, grad_middle, mixed_own, qkv, probs, wqkv, wproj, vecs, places, table_in, marks, masks, small_in,
    input_grad, gqkv, gproj, small,
    gw, gmix, dqkv, dqkv_own, table, own_rows, gtab,
):
    _, row, col = grid_place()
    table[...] = table_kernel_value(places[...], table_in[...])
    small[...] = jnp.zeros_like(small)
    small[0:16, :] = small_in[...]
    gtab[...] = jnp.zeros_like(gtab)
    dqkv[...] = jnp.zeros_like(dqkv)
    for w in range(4):
        index = window_index(w // 2, w % 2, row, col, n_row, n_col)
        hot = one_hot(index, FIELD)
        gw[pl.ds(w * SLOT, SLOT), :] = nn(hot, gfield[...]).astype(BF)
        own_rows[pl.ds(w * SLOT, SLOT), :] = jnp.broadcast_to(
            jnp.where((index >= 0) & (index < TOK), 1.0, 0.0), (SLOT, 128)
        ).astype(BF)
    gown = gfield[pl.ds(0, TOK), :]

    def mix(n, _):
        at = pl.multiple_of(n * 256, 256)
        gmix[:, pl.ds(at, 256)] = nn(gw[...], wproj[:, pl.ds(at, 256)]).astype(BF)
        gproj[pl.ds(at, 256), :] = tn(gfield[pl.ds(0, TOK), pl.ds(at, 256)], mixed_own[...]).astype(BF)
        return 0

    lax.fori_loop(0, 3, mix, 0)
    small[4:5, :] = jnp.sum(gown.astype(F32), 0, keepdims=True)

    def pair(i, _):
        attend_back_pair(i, qkv, gmix, probs, table, marks, masks, own_rows, dqkv, gtab)
        return 0

    lax.fori_loop(0, 4 * PAIRS, pair, 0)
    hot = one_hot(own_slot(row, col), 4 * SLOT)
    own = jnp.broadcast_to(jnp.where(own_mask(row, col, n_row, n_col), 1.0, 0.0), (16, 4 * SLOT)).astype(BF)
    small[2:3, :] = nn(own, dqkv[:, 0:D])[0:1, :]
    small[3:4, :] = nn(own, dqkv[:, 2 * D : 3 * D])[0:1, :]

    def weight(n, _):
        at = pl.multiple_of(n * 256, 256)
        part = nn(hot, dqkv[:, pl.ds(at, 256)]).astype(BF)
        dqkv_own[:, pl.ds(at, 256)] = part
        gqkv[pl.ds(at, 256), :] = tn(part, nfield[pl.ds(0, TOK), :]).astype(BF)
        return 0

    lax.fori_loop(0, 9, weight, 0)
    grad = nn(dqkv_own[...], wqkv[...]).astype(BF).astype(F32)
    gain = vecs[0:1, :]
    _, xhat, inverse = norm(tokens[...].astype(F32), gain, vecs[1:2, :])
    input_grad[...] = (grad_middle[...] + norm_back(grad, xhat, inverse, gain)).astype(BF)
    small[0:1, :] = jnp.sum(grad * xhat, 0, keepdims=True)
    small[1:2, :] = jnp.sum(grad, 0, keepdims=True)
    lane = lax.broadcasted_iota(jnp.int32, (128, 128), 1)
    left = jnp.where(lane < 64, gtab[0], 0.0)
    right = jnp.where(lane >= 64, gtab[1], 0.0)
    spots = places[...].astype(F32)
    tab = lax.dot_general(
        spots,
        jnp.concatenate([left, right], 0),
        (((0,), (0,)), ((), ())),
        precision=lax.Precision.HIGHEST,
        preferred_element_type=F32,
    )
    for t in range(4):
        small[16:32, 128 * t : 128 * t + 128] = tab[16 * t : 16 * t + 16, :]


def attend_back_call(n_row, n_col, *args):
    return pl.pallas_call(
        functools.partial(attend_back_kernel, n_row, n_col),
        name="attend_back",
        out_shape=[
            jax.ShapeDtypeStruct((TOK, D), BF),
            jax.ShapeDtypeStruct((3 * D, D), BF),
            jax.ShapeDtypeStruct((D, D), BF),
            jax.ShapeDtypeStruct((32, D), F32),
        ],
        in_specs=[vmem()] * 15,
        out_specs=[vmem()] * 4,
        scratch_shapes=[
            pltpu.VMEM((4 * SLOT, D), BF),
            pltpu.VMEM((4 * SLOT, D), BF),
            pltpu.VMEM((4 * SLOT, 3 * D), BF),
            pltpu.VMEM((TOK, 3 * D), BF),
            pltpu.VMEM((256, 128), BF),
            pltpu.VMEM((4 * SLOT, 128), BF),
            pltpu.VMEM((2, 128, 128), F32),
        ],
        compiler_params=pltpu.CompilerParams(vmem_limit_bytes=60 * MIB),
    )(*args)


def on_device(
    n_dp, n_row, n_col,
    tokens, ln1_gain, ln1_bias, qkv_weight, query_bias, value_bias, rel_rows, rel_cols,
    proj_weight, proj_bias, ln2_gain, ln2_bias, fc1_weight, fc1_bias, fc2_weight, fc2_bias, cotangent,
):
    direct = (n_dp, n_row, n_col) == (2, 4, 4)
    tok = tokens.reshape(TOK, D)
    cot = cotangent.reshape(TOK, D)
    vecs = jnp.concatenate(
        [
            jnp.stack(
                [ln1_gain, ln1_bias, query_bias, value_bias, proj_bias, ln2_gain, ln2_bias, fc2_bias]
            ),
            fc1_bias.reshape(-1, D),
        ],
        0,
    ).astype(F32)
    vecs = jnp.pad(vecs, ((0, 16 - vecs.shape[0]), (0, 0)))
    table = jnp.concatenate([jnp.pad(rel_rows, ((0, 5), (0, 0))), jnp.pad(rel_cols, ((0, 5), (0, 0)))], 0)
    table = jnp.concatenate([table, table], 1)
    pick = jnp.asarray(pick_rows(), BF)
    places, places_back = (jnp.asarray(table_places(back), BF) for back in (False, True))
    marks, marks_back = (jnp.asarray(key_marks(back), BF) for back in (False, True))
    mask_values = np.zeros((16, 128), np.float32)
    mask_values[0, :64] = 1.0
    mask_values[1, 64:] = 1.0
    masks = jnp.asarray(mask_values, BF)
    shards = (qkv_weight, proj_weight, fc1_weight, fc2_weight)
    shapes = [(s.shape[1] * n_row * n_col, s.shape[0] * n_dp) for s in shards]
    if direct:
        field, wqkv, wproj, w1, w2 = gather_call(n_row, n_col, shapes, tok, vecs, pick, shards)
    else:
        full = []
        for s in shards:
            s = lax.all_gather(s, ("row", "col"), axis=1, tiled=True)
            full.append(lax.all_gather(s, "dp", axis=0, tiled=True).T)
        wqkv, wproj, w1, w2 = full
        normed = norm(tok.astype(F32), vecs[0], vecs[1])[0].astype(BF)
        field = halo_xla(normed, n_row, n_col)
    qkv, probs, mixed_own, attended = attend_call(
        n_row, n_col, field, wqkv, wproj, vecs, places, table, marks, masks
    )
    output, grad_middle, grad_attended, g1, g2, small = mlp_call(tok, attended, cot, w1, w2, vecs)
    if direct:
        gfield = halo_call(n_row, n_col, grad_attended, pick)
    else:
        gfield = halo_xla(grad_attended, n_row, n_col)
    input_grad, gqkv, gproj, small = attend_back_call(
        n_row, n_col,
        gfield, field, tok, grad_middle, mixed_own, qkv, probs, wqkv, wproj, vecs, places_back, table, marks_back, masks, small,
    )
    grads = (gqkv, gproj, g1, g2)
    if direct:
        *sums, small = reduce_call(n_row, n_col, shapes, small, grads)
    else:
        sums = []
        for g in grads:
            g = lax.psum_scatter(g, ("row", "col"), scatter_dimension=0, tiled=True)
            g = lax.psum_scatter(g, "dp", scatter_dimension=1, tiled=True)
            sums.append(g.T.astype(F32))
        local = lax.psum(small, ("row", "col"))
        line = jnp.arange(32)[:, None] == 12
        small = jnp.where(line, local, lax.psum(jnp.where(line, 0.0, local), "dp"))
    count = TOK * n_row * n_col * D
    stats = jnp.sqrt(small[12:13, :5] / count)
    tables = jnp.concatenate([small[16:32, 128 * t : 128 * t + 128] for t in range(4)], 0)
    tables = tables[:, :64] + tables[:, 64:]
    return (
        output.reshape(tokens.shape),
        input_grad.reshape(tokens.shape),
        small[0],
        small[1],
        sums[0],
        small[2],
        small[3],
        tables[0:27],
        tables[32:59],
        sums[1],
        small[4],
        small[5],
        small[6],
        sums[2],
        small[8:12].reshape(-1),
        sums[3],
        small[7],
        stats,
    )


def solution(mesh):
    tile = P("dp", "row", "col", None)
    weight = P("dp", ("row", "col"))
    sizes = [mesh.shape[a] for a in ("dp", "row", "col")]
    ins = [tile] + [P()] * 16
    for i in (3, 8, 12, 14):
        ins[i] = weight
    ins[16] = tile
    outs = [tile, tile] + [P()] * 16
    for i in (4, 9, 13, 15):
        outs[i] = weight
    outs[17] = P("dp", None)
    return jax.shard_map(
        functools.partial(on_device, *sizes),
        mesh=mesh,
        in_specs=tuple(ins),
        out_specs=tuple(outs),
        check_vma=False,
    )
```

```python
import functools
import types

import jax
import jax.numpy as jnp
import numpy as np
from jax import lax
from jax.experimental import pallas as pl
from jax.experimental.pallas import tpu as pltpu
from jax.sharding import PartitionSpec as P

HEADS = 12
HEAD = 64
WIN = 14
EPS = 1e-06
MESH = pl.DeviceIdType.MESH
AXES = ("row", "col")
F32 = jnp.float32
BF = jnp.bfloat16

D = HEADS * HEAD
TILE = 16
TOK = TILE * TILE
LO = 6
SLOT = 256
PAIRS = HEADS // 2
FIELD = 496
PICKED = 144
MIB = 2**20

LINKS = {
    (1, 0): (True, 160, 96, 256),
    (0, 1): (False, 0, 96, 352),
    (1, 1): (False, 96, 48, 448),
}


def nt(a, b):
    return lax.dot_general(a, b, (((1,), (1,)), ((), ())), preferred_element_type=F32)


def nn(a, b):
    return lax.dot_general(a, b, (((1,), (0,)), ((), ())), preferred_element_type=F32)


def tn(a, b):
    return lax.dot_general(a, b, (((0,), (0,)), ((), ())), preferred_element_type=F32)


def pick_rows():
    table = np.zeros((PICKED, TOK), np.float32)
    for base, first in ((0, 0), (96, TILE - LO)):
        for i in range((TILE - first) * LO):
            y, x = divmod(i, LO)
            table[base + i, (first + y) * TILE + TILE - LO + x] = 1.0
    return table


def table_places(back):
    place = np.zeros((256, 64), np.float32)
    for head in range(2):
        for r in range(2 * WIN - 1):
            for copy in range(2):
                row_lane = (64 + 28 * copy + r + 64 * head) % 128
                col_lane = (28 * copy + r + 64 * head) % 128
                place[128 * head + row_lane, 26 - r] = 1.0
                place[128 * head + col_lane, 32 + (r if back else 26 - r)] = 1.0
    return place


def key_marks(back):
    marks = np.zeros((2, SLOT, 128), np.float32)
    for head in range(2):
        for j in range(SLOT):
            k, l = divmod(j, 16)
            if k < WIN and l < WIN:
                for copy in range(2):
                    marks[head, j, (64 + 28 * copy + k + 64 * head) % 128] = 1.0
                    marks[head, j, (78 + 28 * copy + (13 - l if back else l) + 64 * head) % 128] = 1.0
            else:
                marks[head, j, (120 + 64 * head) % 128] = -1e30
    return marks


def lane_kinds(rows):
    lane = lax.broadcasted_iota(jnp.int32, (rows, 128), 1)
    kinds = []
    for head in range(2):
        at = (lane + 64 * head) % 128 if head else lane
        own = at < 64
        first = (at >= 64) & (at < 92)
        second = (at >= 92) & (at < 120)
        is_row = ((at >= 64) & (at < 78)) | ((at >= 92) & (at < 106))
        kinds.append((own, first, second, is_row, at == 120))
    return kinds


def window_index(w, row, col, n_row, n_col):
    place = lax.broadcasted_iota(jnp.int32, (SLOT, 1), 0)
    y = place // 16
    x = place - 16 * y
    a, b = w // 2, w % 2
    ry = WIN * (row + a) + y - TILE * row
    rx = WIN * (col + b) + x - TILE * col
    good = (y < WIN) & (x < WIN) & (ry < TILE) & (rx < TILE)
    if a:
        good = good & (row == n_row - 1)
    if b:
        good = good & (col == n_col - 1)
    up, left = ry < 0, rx < 0
    base = jnp.where(up, jnp.where(left, 448, 256), jnp.where(left, 352, 0))
    width = jnp.where(left, LO, TILE)
    index = base + jnp.where(up, ry + LO, ry) * width + jnp.where(left, rx + LO, rx)
    return jnp.where(good, index, -1)


def field_slots(row, col, n_row, n_col):
    at = lax.broadcasted_iota(jnp.int32, (FIELD, 1), 0)
    above = (at >= 256) & (at < 352)
    left = (at >= 352) & (at < 448)
    corner = at >= 448
    narrow = left | corner
    rest = jnp.where(corner, at - 448, jnp.where(left, at - 352, jnp.where(above, at - 256, at)))
    sixth = sum((rest >= LO * k).astype(jnp.int32) for k in range(1, TILE))
    ty = jnp.where(narrow, sixth, rest // TILE)
    tx = rest - ty * jnp.where(narrow, LO, TILE)
    ty = jnp.where(above | corner, ty - LO, ty)
    tx = jnp.where(narrow, tx - LO, tx)
    good = at < 484
    where = 0
    for t, place, n, stride, unit in ((ty, row, n_row, 2, 16), (tx, col, n_col, 1, 1)):
        y = TILE * place + t - WIN * place
        late = y >= WIN
        good = good & (y >= 0) & (jnp.logical_not(late) | (place == n - 1))
        where = where + jnp.where(late, stride * SLOT + unit * (y - WIN), unit * y)
    return jnp.where(good, where, -1)


def home_index(row, col, n_row, n_col):
    place = lax.broadcasted_iota(jnp.int32, (TOK, 1), 0)
    ty = place // TILE
    tx = place - TILE * ty
    down = (TILE * row + ty - WIN * row >= WIN) & (row < n_row - 1)
    right = (TILE * col + tx - WIN * col >= WIN) & (col < n_col - 1)
    near = TILE - LO
    return jnp.where(
        down,
        jnp.where(right, 448 + (ty - near) * LO + tx - near, 256 + (ty - near) * TILE + tx),
        jnp.where(right, 352 + ty * LO + tx - near, place),
    )


def one_hot(index, size):
    lane = lax.broadcasted_iota(jnp.int32, (index.shape[0], size), 1)
    return jnp.where(lane == index, 1.0, 0.0).astype(BF)


def norm(v, gain, bias):
    mean = jnp.mean(v, -1, keepdims=True)
    center = v - mean
    inverse = lax.rsqrt(jnp.mean(center * center, -1, keepdims=True) + EPS)
    xhat = center * inverse
    return xhat * gain + bias, xhat, inverse


def norm_back(grad, xhat, inverse, gain):
    d = grad * gain
    return inverse * (
        d - jnp.mean(d, -1, keepdims=True) - xhat * jnp.mean(d * xhat, -1, keepdims=True)
    )


def grid_place():
    return lax.axis_index("dp"), lax.axis_index("row"), lax.axis_index("col")


def exists(step, row, col, n_row, n_col):
    r, c = row + step[0], col + step[1]
    return (r >= 0) & (r < n_row) & (c >= 0) & (c < n_col)


CORNERS = ((1, 1), (-1, -1))


def greet(n_row, n_col):
    dp, row, col = grid_place()
    barrier = pltpu.get_barrier_semaphore()
    others = [(dp, row, lax.rem(col + d, n_col)) for d in (1, 2, 3)]
    others += [(dp, lax.rem(row + d, n_row), col) for d in (1, 2, 3)]
    others.append((1 - dp, row, col))
    for other in others:
        pl.semaphore_signal(barrier, inc=1, device_id=other, device_id_type=MESH)
    count = len(others)
    for step in CORNERS:
        there = exists(step, row, col, n_row, n_col)

        @pl.when(there)
        def _():
            pl.semaphore_signal(
                barrier, inc=1, device_id=(dp, row + step[0], col + step[1]), device_id_type=MESH
            )

        count = count + jnp.where(there, 1, 0)
    pl.semaphore_wait(barrier, count)


class Halo:
    def __init__(self, source, picked, land, back, send, recv, n_row, n_col):
        self.source, self.picked, self.land, self.back = source, picked, land, back
        self.send, self.recv, self.size = send, recv, (n_row, n_col)

    def copies(self):
        dp, row, col = grid_place()
        sign = -1 if self.back else 1
        for i, ((dr, dc), (own, first, rows, there)) in enumerate(LINKS.items()):
            if self.back:
                src = self.source.at[pl.ds(there, rows)]
            else:
                src = (self.source if own else self.picked).at[pl.ds(first, rows)]
            copy = pltpu.make_async_remote_copy(
                src,
                self.land.at[pl.ds(there, rows)],
                self.send.at[i],
                self.recv.at[i],
                device_id=(dp, row + sign * dr, col + sign * dc),
                device_id_type=MESH,
            )
            goes = exists((sign * dr, sign * dc), row, col, *self.size)
            comes = exists((-sign * dr, -sign * dc), row, col, *self.size)
            yield copy, goes, comes

    def start(self):
        for copy, goes, _ in self.copies():
            pl.when(goes)(copy.start)

    def wait(self):
        for copy, goes, comes in self.copies():
            pl.when(goes)(copy.wait_send)
            pl.when(comes)(copy.wait_recv)


def pick_start(halo, pick):
    halo.picked[...] = nn(pick[...], halo.source[pl.ds(0, TOK), :]).astype(BF)
    halo.start()


def halo_xla(blocks, back, n_row, n_col):
    sign = -1 if back else 1
    pieces = [blocks[0]]
    for (dr, dc), block in zip(LINKS, blocks[1:]):
        dr, dc = sign * dr, sign * dc
        pairs = [
            (r * n_col + c, (r + dr) * n_col + c + dc)
            for r in range(n_row)
            for c in range(n_col)
            if 0 <= r + dr < n_row and 0 <= c + dc < n_col
        ]
        pieces.append(lax.ppermute(block, AXES, pairs))
    return jnp.concatenate(pieces, 0)


def lend_xla(own, n_row, n_col):
    grid = own.reshape(TILE, TILE, -1)
    corner = grid[TILE - LO :, TILE - LO :].reshape(LO * LO, -1)
    blocks = [
        own,
        own[TILE * (TILE - LO) :],
        grid[:, TILE - LO :].reshape(TILE * LO, -1),
        jnp.pad(corner, ((0, 48 - LO * LO), (0, 0))),
    ]
    return halo_xla(blocks, False, n_row, n_col)


def return_xla(field, n_row, n_col):
    return halo_xla([field[:256], field[256:352], field[352:448], field[448:]], True, n_row, n_col)


def blocks_of(shapes):
    return [(n // 16, k // 2) for n, k in shapes]


def rows_at(first, count):
    return pl.ds(pl.multiple_of(first, 16), count)


LINE, OWN, OWN_CORE, LINE_CORE, FAR, NEAR_CORE, FAR_CORE, CORE = range(10, 18)


class Gather:
    SEMS = 20

    def __init__(self, full, shard, block, half, send, recv):
        self.dp, self.row, self.col = grid_place()
        self.full, self.shard, self.b = full, shard, block
        self.send, self.recv = send, recv
        self.lanes = pl.ds(pl.multiple_of(self.dp * half, 128), half)
        self.other = pl.ds(pl.multiple_of((1 - self.dp) * half, 128), half)

    def block(self, flip, place):
        return (jnp.bitwise_xor(self.row, flip) * 4 + place) * self.b

    def came(self, d):
        return lax.rem(self.col + 4 - d, 4)

    def copy(self, i, first, count, land, target, shard=False):
        core = target == CORE
        if core:
            device = (1 - self.dp, self.row, self.col)
        elif isinstance(target, tuple):
            device = (self.dp, self.row, lax.rem(self.col + target[0], 4))
        else:
            device = (self.dp, jnp.bitwise_xor(self.row, target), self.col)

        def make(src, dst):
            return pltpu.make_async_remote_copy(
                src, dst, self.send.at[i], self.recv.at[i], device_id=device, device_id_type=MESH
            )

        def out():
            there = self.full.at[rows_at(first, count), self.lanes]
            return make(self.shard if shard else there, there)

        def come():
            here = self.full.at[rows_at(land, count), self.other if core else self.lanes]
            return make(here, here)

        return out, come

    def copies(self, k):
        b = self.b
        own = self.block(0, self.col)
        if k == LINE:
            return [
                self.copy(d - 1, own, b, self.block(0, self.came(d)), (d,), True) for d in (1, 2, 3)
            ]
        if k == OWN:
            return [self.copy(2 + f, own, b, self.block(f, self.col), f, True) for f in (1, 2)]
        if k == OWN_CORE:
            return [self.copy(5, own, b, own, CORE, True)]
        if k < LINE:
            at = self.came(k)
            return [
                self.copy(4 + 2 * k, self.block(0, at), b, self.block(1, at), 1),
                self.copy(5 + 2 * k, self.block(0, at), b, self.block(2, at), 2),
            ]
        if k == LINE_CORE:
            return [
                self.copy(11 + d, self.block(0, self.came(d)), b, self.block(0, self.came(d)), CORE)
                for d in (1, 2, 3)
            ]
        if k == FAR:
            return [
                self.copy(15, self.block(2, 0), 2 * b, self.block(3, 0), 1),
                self.copy(16, self.block(1, 2), 2 * b, self.block(3, 2), 2),
            ]
        if k == NEAR_CORE:
            return [self.copy(16 + f, self.block(f, 0), 4 * b, self.block(f, 0), CORE) for f in (1, 2)]
        return [self.copy(19, self.block(3, 0), 4 * b, self.block(3, 0), CORE)]

    def start(self, *kinds):
        for k in kinds:
            for out, _ in self.copies(k):
                out().start()

    def arrive(self, *kinds):
        for k in kinds:
            for _, come in self.copies(k):
                come().wait_recv()

    def step(self, n):
        if n == 0:
            for d in (1, 2, 3):
                self.copies(LINE)[d - 1][1]().wait_recv()
                self.start(d)
            self.start(LINE_CORE)
        elif n == 1:
            self.arrive(OWN, 1, 2, 3)
            self.start(FAR, NEAR_CORE)
        else:
            self.arrive(FAR)
            self.start(FAR_CORE)

    def whole(self):
        self.arrive(OWN_CORE, LINE_CORE, NEAR_CORE, FAR_CORE)

    def finish(self):
        for k in (LINE, OWN, OWN_CORE, 1, 2, 3, LINE_CORE, FAR, NEAR_CORE, FAR_CORE):
            for out, _ in self.copies(k):
                out().wait_send()


class Reduce:
    SEMS = 30

    def __init__(self, grad, total, base, come, block, half, pieces, parts, send, recv):
        self.dp, self.row, self.col = grid_place()
        self.grad, self.total, self.base, self.come = grad, total, base, come
        self.b, self.h, self.send, self.recv = block, half, send, recv
        self.pieces, self.parts, self.width = pieces, parts, half // parts
        self.other = pl.ds(pl.multiple_of((1 - self.dp) * half, 128), half)

    def at(self, flip, place=0):
        return (jnp.bitwise_xor(self.row, flip) * 4 + place) * self.b

    def lanes(self, part):
        return pl.ds(pl.multiple_of(self.base + part * self.width, 128), self.width)

    def came(self, first, count, part):
        return self.come.at[rows_at(first, count), pl.ds(part * self.width, self.width)]

    def tot(self, first, count, part):
        return self.total.at[rows_at(first, count), self.lanes(part)]

    def sem(self, k, part):
        if k == 0:
            return part
        return self.pieces + 7 * part + {1: 0, 2: 2, 3: 4}[k]

    def copies(self, k, part):
        b = self.b
        if k == 0:
            n = 16 * b // self.pieces
            rows = rows_at(part * n, n)
            plan = [(self.grad.at[rows, self.other], self.come.at[rows], (1 - self.dp, self.row, self.col))]
        elif k == 1:
            plan = [
                (
                    self.tot(self.at(3, 2 * half), 2 * b, part),
                    self.came((16 + 2 * half) * b, 2 * b, part),
                    (self.dp, jnp.bitwise_xor(self.row, 1 + half), self.col),
                )
                for half in (0, 1)
            ]
        elif k == 2:
            plan = [
                (
                    self.tot(self.at(flip), 4 * b, part),
                    self.came((16 + 4 * flip) * b, 4 * b, part),
                    (self.dp, jnp.bitwise_xor(self.row, flip), self.col),
                )
                for flip in (1, 2)
            ]
        else:
            plan = []
            for d in (1, 2, 3):
                to = lax.rem(self.col + d, 4)
                plan.append(
                    (
                        self.tot(self.at(0, to), b, part),
                        self.came((27 + d) * b, b, part),
                        (self.dp, self.row, to),
                    )
                )
        base = self.sem(k, part)
        return [
            pltpu.make_async_remote_copy(
                src, dst, self.send.at[base + i], self.recv.at[base + i], device_id=dev, device_id_type=MESH
            )
            for i, (src, dst, dev) in enumerate(plan)
        ]

    def start(self, k, part=0):
        for copy in self.copies(k, part):
            copy.start()

    def arrive(self, k, part=0):
        for copy in self.copies(k, part):
            copy.wait_recv()

    def sum_rows(self, first, count, froms, part):
        steps = (96, 64, 48, 32, 16) if self.width <= 384 else (32, 16)
        step = next(s for s in steps if count % s == 0)
        lanes = self.lanes(part)
        side = pl.ds(part * self.width, self.width)

        def body(i, _):
            at = rows_at(first + i * step, step)
            value = self.total[at, lanes]
            if len(froms) == 1:
                value = value + self.come[rows_at(froms[0] + i * step, step), side]
            else:
                value = value.astype(F32)
                for f in froms:
                    value = value + self.come[rows_at(f + i * step, step), side].astype(F32)
                value = value.astype(BF)
            self.total[at, lanes] = value
            return 0

        lax.fori_loop(0, count // step, body, 0)

    def add_piece(self, piece):
        n = 16 * self.b // self.pieces
        self.arrive(0, piece)
        for part in range(self.parts):
            self.sum_rows(piece * n, n, (piece * n,), part)

    def step(self, k, part=0):
        b = self.b
        if k == 0:
            for piece in range(self.pieces):
                self.add_piece(piece)
            for part in range(1, self.parts):
                self.start(1, part)
            part = 0
        else:
            self.arrive(k, part)
            if k == 1:
                self.sum_rows(self.at(2), 2 * b, (16 * b,), part)
                self.sum_rows(self.at(1, 2), 2 * b, (18 * b,), part)
            else:
                self.sum_rows(self.at(0), 4 * b, (20 * b, 24 * b), part)
        self.start(k + 1, part)

    def result(self, out, part=0):
        b = self.b
        self.arrive(3, part)
        value = self.total[rows_at(self.at(0, self.col), b), self.lanes(part)].astype(F32)
        side = pl.ds(part * self.width, self.width)
        for d in (1, 2, 3):
            value = value + self.come[pl.ds((27 + d) * b, b), side].astype(F32)
        out[:, side] = value

    def finish(self):
        for piece in range(self.pieces):
            self.copies(0, piece)[0].wait_send()
        for part in range(self.parts):
            for k in (1, 2, 3):
                for copy in self.copies(k, part):
                    copy.wait_send()


def vmem():
    return pl.BlockSpec(memory_space=pltpu.VMEM)


def hbm():
    return pl.BlockSpec(memory_space=pl.ANY)


def dma(*n):
    return pltpu.SemaphoreType.DMA(n)


def named_call(body, ins, outs, scratch, name, **params):
    names = [*ins, *outs, *scratch]

    def kernel(*refs):
        body(types.SimpleNamespace(**dict(zip(names, refs))))

    result = pl.pallas_call(
        kernel,
        name=name,
        out_shape=[shape for shape, _ in outs.values()],
        in_specs=[spec for _, spec in ins.values()],
        out_specs=[spec for _, spec in outs.values()],
        scratch_shapes=list(scratch.values()),
        compiler_params=pltpu.CompilerParams(**params),
    )(*[array for array, _ in ins.values()])
    return types.SimpleNamespace(**dict(zip(outs, result)))


def vector(ref):
    return ref[...].astype(F32).reshape(1, -1)


def joint_table(rel_rows, rel_cols):
    parts = [rel_rows[...], jnp.zeros((5, HEAD), BF), rel_cols[...], jnp.zeros((5, HEAD), BF)]
    table = jnp.concatenate([p.astype(F32) for p in parts], 0)
    return jnp.concatenate([table, table], 1).astype(BF)


def table_kernel_value(places, table):
    value = nn(places, table)
    line = lax.broadcasted_iota(jnp.int32, value.shape, 0)
    lane = lax.broadcasted_iota(jnp.int32, value.shape, 1)
    return jnp.where((line < 128) == (lane < 64), value, 0.0).astype(BF)


def spread(a, back):
    rows, cols = [], []
    for y in range(a.shape[0] // 16):
        part = a[16 * y : 16 * y + 16, :]
        rows.append(pltpu.roll(part, 13 - y if back else (115 + y) % 128, 1))
        cols.append(pltpu.roll(part, 50 if back else 65, 1, stride=1, stride_axis=0))
    return jnp.concatenate(rows, 0), jnp.concatenate(cols, 0)


def pair_place(w, pair):
    return pl.multiple_of(w * SLOT, SLOT), pl.multiple_of(pair * 128, 128)


def attend_pair(w, pair, n, qkv, table, marks, masks, probs, mixed):
    r0, l0 = pair_place(w, pair)
    q2 = qkv[pl.ds(r0, n), pl.ds(l0, 128)]
    k2 = qkv[pl.ds(r0, SLOT), pl.ds(D + l0, 128)]
    v2 = qkv[pl.ds(r0, SLOT), pl.ds(2 * D + l0, 128)]
    a2 = nt(q2, table[...])
    qf = q2.astype(F32) * HEAD**-0.5
    kinds = lane_kinds(n)
    outs = []
    for head in range(2):
        own, first, second, is_row, one = kinds[head]
        rows, cols = spread(a2[:, 128 * head : 128 * head + 128], False)
        bias = jnp.where(is_row, rows, cols)
        high = bias.astype(BF).astype(F32)
        low = jnp.where(second, bias - high, jnp.where(one, 1.0, 0.0))
        aug = jnp.where(own, qf, jnp.where(first, high, low)).astype(BF)
        keys = k2 * masks[head : head + 1, :] + marks[head]
        scores = nt(aug, keys)
        top = jnp.max(scores, -1, keepdims=True)
        e = jnp.exp(scores - top)
        p = (e * (1.0 / jnp.sum(e, -1, keepdims=True))).astype(BF)
        probs[w * HEADS + 2 * pair + head, 0:n, :] = p
        outs.append(nn(p, v2))
    mixed[pl.ds(r0, n), pl.ds(l0, 128)] = jnp.where(kinds[0][0], outs[0], outs[1]).astype(BF)


def attend_back_pair(w, pair, n, qkv, gmix, probs, table, marks, masks, dqkv, gtab):
    r0, l0 = pair_place(w, pair)
    scale = HEAD**-0.5
    q2 = qkv[pl.ds(r0, n), pl.ds(l0, 128)]
    k2 = qkv[pl.ds(r0, SLOT), pl.ds(D + l0, 128)]
    v2 = qkv[pl.ds(r0, SLOT), pl.ds(2 * D + l0, 128)]
    g2 = gmix[pl.ds(r0, n), pl.ds(l0, 128)]
    kinds = lane_kinds(n)
    dq, dk, dv = [], [], []
    for head in range(2):
        own, first, second, is_row, one = kinds[head]
        mask = masks[head : head + 1, :]
        p = probs[w * HEADS + 2 * pair + head, 0:n, :]
        pf = p.astype(F32)
        dp = nt(g2, v2 * mask)
        ds = (pf * (dp - jnp.sum(pf * dp, -1, keepdims=True))).astype(BF)
        keys = k2 * (mask * jnp.asarray(scale, BF)) + marks[head]
        dqa = nn(ds, keys)
        marked = jnp.where(first | second, dqa, 0.0)
        rows, _ = spread(jnp.where(is_row, marked, 0.0), True)
        _, cols = spread(jnp.where(is_row, 0.0, marked), True)
        back = rows + cols
        at = lax.broadcasted_iota(jnp.int32, (n, 128), 1)
        if head:
            at = (at + 64) % 128
        high = back.astype(BF).astype(F32)
        split = jnp.where((at < 28) | ((at >= 64) & (at < 92)), high, back - high).astype(BF)
        extra = nn(split, table[128 * head : 128 * head + 128, :])
        dq.append(dqa + extra)
        gtab[head] += tn(split, q2)
        dk.append(tn(ds, q2))
        dv.append(tn(p, g2))
    wide = lane_kinds(SLOT)[0][0]
    dqkv[pl.ds(r0, n), pl.ds(l0, 128)] = jnp.where(kinds[0][0], dq[0], dq[1]).astype(BF)
    dqkv[pl.ds(r0, SLOT), pl.ds(D + l0, 128)] = (jnp.where(wide, dk[0], dk[1]) * scale).astype(BF)
    dqkv[pl.ds(r0, SLOT), pl.ds(2 * D + l0, 128)] = jnp.where(wide, dv[0], dv[1]).astype(BF)


def over_windows(body, hooks, n_row, n_col):
    _, row, col = grid_place()
    for a, n in ((0, 16 * WIN), (1, 16 * (TILE * n_row - WIN * n_row))):

        def step(i, _):
            b = i // PAIRS
            good = (b == 0) | (col == n_col - 1)
            if a:
                good = good & (row == n_row - 1)

            @pl.when(good)
            def _():
                body(2 * a + b, lax.rem(i, PAIRS), n)

            for when, hook in hooks:
                if when // (2 * PAIRS) == a:
                    pl.when(i == when % (2 * PAIRS))(hook)
            return 0

        lax.fori_loop(0, 2 * PAIRS, step, 0)


def attend_part(r, n_row, n_col, hooks, between):
    _, row, col = grid_place()
    biases = (vector(r.query_bias), None, vector(r.value_bias))
    for part, bias in enumerate(biases):
        for n in range(3):
            at = part * D + 256 * n
            value = nt(r.xw[...], r.wqkv[pl.ds(at, 256), :])
            if bias is not None:
                value = value + bias[:, 256 * n : 256 * n + 256]
            r.qkv[:, pl.ds(at, 256)] = value.astype(BF)
        between(part)

    def body(w, pair, n):
        attend_pair(w, pair, n, r.qkv, r.table, r.marks, r.masks, r.probs, r.mixed)

    over_windows(body, hooks, n_row, n_col)
    hot = one_hot(field_slots(row, col, n_row, n_col), 4 * SLOT)
    r.ret[...] = nn(hot, r.mixed[...]).astype(BF)


def cut_windows(source, land, n_row, n_col, w):
    _, row, col = grid_place()
    hot = one_hot(window_index(w, row, col, n_row, n_col), FIELD)
    land[pl.ds(w * SLOT, SLOT), :] = nn(hot, source[...]).astype(BF)


def mlp_first(r, n_row, n_col, hidden):
    _, row, col = grid_place()
    hot = one_hot(home_index(row, col, n_row, n_col), FIELD)
    r.mixed_own[...] = nn(hot, r.home[...]).astype(BF)
    r.attended[...] = (nt(r.mixed_own[...], r.wproj[...]) + vector(r.proj_bias)).astype(BF)
    middle = r.tokens[...].astype(F32) + r.attended[...].astype(F32)
    r.n2[...] = norm(middle, vector(r.ln2_gain), vector(r.ln2_bias))[0].astype(BF)
    up_bias = vector(r.fc1_bias)
    for line in range(hidden // D):
        r.up_bias[line : line + 1, :] = up_bias[:, line * D : line * D + D]

    def chunk(j, _):
        at = pl.multiple_of(j * 256, 256)
        lane = pl.multiple_of(lax.rem(j, 3) * 256, 256)
        u = nt(r.n2[...], r.w1[pl.ds(at, 256), :]) + r.up_bias[pl.ds(j // 3, 1), pl.ds(lane, 256)]
        cdf = 0.5 * (1.0 + lax.erf(u * 0.7071067811865476))
        r.act[:, pl.ds(at, 256)] = (u * cdf).astype(BF)
        r.slope[:, pl.ds(at, 256)] = cdf + u * (jnp.exp(-0.5 * u * u) * 0.3989422804014327)
        return 0

    lax.fori_loop(0, hidden // 256, chunk, 0)


def mlp_second(r, hidden):
    r.gn2[...] = jnp.zeros_like(r.gn2)
    r.small[...] = jnp.zeros_like(r.small)

    def chunk(j, _):
        at = pl.multiple_of(j * 256, 256)
        lane = pl.multiple_of(lax.rem(j, 3) * 256, 256)
        gu = (nn(r.cot[...], r.w2[:, pl.ds(at, 256)]) * r.slope[:, pl.ds(at, 256)]).astype(BF)
        r.gu[:, pl.ds(at, 256)] = gu
        r.gn2[...] += nn(gu, r.w1[pl.ds(at, 256), :])
        r.small[pl.ds(8 + j // 3, 1), pl.ds(lane, 256)] = jnp.sum(gu.astype(F32), 0, keepdims=True)
        return 0

    lax.fori_loop(0, hidden // 256, chunk, 0)
    gain = vector(r.ln2_gain)
    middle = r.tokens[...].astype(F32) + r.attended[...].astype(F32)
    _, xhat, inverse = norm(middle, gain, vector(r.ln2_bias))
    grad = r.gn2[...]
    cf = r.cot[...].astype(F32)
    gm = cf + norm_back(grad, xhat, inverse, gain)
    r.grad_middle[...] = gm
    low = gm.astype(BF)
    r.gfield[pl.ds(0, TOK), :] = low
    r.small[4:5, :] = jnp.sum(low.astype(F32), 0, keepdims=True)
    r.small[5:6, :] = jnp.sum(grad * xhat, 0, keepdims=True)
    r.small[6:7, :] = jnp.sum(grad, 0, keepdims=True)
    r.small[7:8, :] = jnp.sum(cf, 0, keepdims=True)


def mlp_last(r, hidden):
    r.branch[...] = jnp.zeros_like(r.branch)

    def chunk(j, _):
        at = pl.multiple_of(j * 256, 256)
        r.branch[...] += nt(r.act[:, pl.ds(at, 256)], r.w2[:, pl.ds(at, 256)])
        return 0

    lax.fori_loop(0, hidden // 256, chunk, 0)
    att = r.attended[...].astype(F32)
    tok = r.tokens[...].astype(F32)
    middle = tok + att
    br = r.branch[...] + vector(r.fc2_bias)
    result = middle + br
    r.output[...] = result.astype(BF)
    lane = lax.broadcasted_iota(jnp.int32, (1, D), 1)
    stats = jnp.zeros((1, D), F32)
    for n, v in enumerate((tok, middle, result, att, br)):
        total = jnp.sum(jnp.sum(v * v, 0, keepdims=True), 1, keepdims=True)
        stats = jnp.where(lane == n, total, stats)
    r.small[12:13, :] = stats


UP_PIECES, DOWN_PIECES = 12, 6


def mlp_weights(r, hidden, up_sent, down_sent):
    r.cot_t[...] = r.cot[...].T

    def up(j, _):
        n = hidden // UP_PIECES
        at = pl.multiple_of(j * n, n)
        r.g1[pl.ds(at, n), :] = tn(r.gu[:, pl.ds(at, n)], r.n2[...]).astype(BF)
        up_sent(j)
        return 0

    def down(j, _):
        n = D // DOWN_PIECES
        at = pl.multiple_of(j * n, n)
        r.g2[pl.ds(at, n), :] = nn(r.cot_t[pl.ds(at, n), :], r.act[...]).astype(BF)
        down_sent(j)
        return 0

    lax.fori_loop(0, UP_PIECES, up, 0)
    lax.fori_loop(0, DOWN_PIECES, down, 0)


def proj_weight_grad(r):
    def chunk(n, _):
        at = pl.multiple_of(n * 256, 256)
        r.gproj[pl.ds(at, 256), :] = tn(r.gfield[pl.ds(0, TOK), pl.ds(at, 256)], r.mixed_own[...]).astype(BF)
        return 0

    lax.fori_loop(0, D // 256, chunk, 0)


def prepare(r):
    r.table[...] = table_kernel_value(r.places[...], joint_table(r.rel_rows, r.rel_cols))
    r.mixed[...] = jnp.zeros_like(r.mixed)


def front_body(n_row, n_col, shapes, hidden, r):
    rest = FIELD - TOK
    for ref in (r.field, r.gfield, r.home):
        ref[pl.ds(TOK, rest), :] = jnp.zeros((rest, D), BF)
    greet(n_row, n_col)
    ways = [
        Gather(full, shard, b, h, send, recv)
        for full, shard, (b, h), send, recv in zip(
            (r.wqkv, r.wproj, r.w1, r.w2),
            (r.s0, r.s1, r.s2, r.s3),
            blocks_of(shapes),
            (r.p0, r.p1, r.p2, r.p3),
            (r.r0, r.r1, r.r2, r.r3),
        )
    ]
    qkv_way, proj_way, up_way, down_way = ways
    qkv_way.start(LINE, OWN, OWN_CORE)
    normed, _, _ = norm(r.tokens[...].astype(F32), vector(r.ln1_gain), vector(r.ln1_bias))
    r.field[pl.ds(0, TOK), :] = normed.astype(BF)
    lend = Halo(r.field, r.picked, r.field, False, r.lend_sem.at[0], r.lend_sem.at[1], n_row, n_col)
    give = Halo(r.ret, None, r.home, True, r.give_sem.at[0], r.give_sem.at[1], n_row, n_col)
    glend = Halo(r.gfield, r.gpicked, r.gfield, False, r.glend_sem.at[0], r.glend_sem.at[1], n_row, n_col)
    pick_start(lend, r.pick)
    local = []
    for i, way in enumerate(ways):
        if i:
            way.start(OWN, OWN_CORE)
        own = way.full.at[rows_at(way.block(0, way.col), way.b), way.lanes]
        mine = pltpu.make_async_copy(way.shard, own, r.local_sem.at[i])
        mine.start()
        local.append(mine)
    prepare(r)
    for mine in local:
        mine.wait()
    lend.wait()
    for w in range(4):
        cut_windows(r.field, r.xw, n_row, n_col, w)
    qkv_way.step(0)
    proj_way.start(LINE)
    up_way.start(LINE)
    qkv_way.step(1)
    proj_way.step(0)
    qkv_way.step(2)
    down_way.start(LINE)
    up_way.step(0)
    qkv_way.whole()
    out_copies = [
        pltpu.make_async_copy(src, dst, r.out_sem.at[i])
        for i, (src, dst) in enumerate(
            [
                (r.qkv, r.qkv_out),
                (r.wqkv, r.wqkv_out),
                (r.probs, r.probs_out),
                (r.wproj, r.wproj_out),
                (r.xw, r.xw_out),
                (r.act, r.act_out),
                (r.gu, r.gu_out),
            ]
        )
    ]

    def between(part):
        if part == 0:
            proj_way.step(1)
        elif part == 2:
            out_copies[0].start()
            out_copies[1].start()
            out_copies[4].start()

    hooks = (
        (0, lambda: proj_way.step(2)),
        (1, lambda: down_way.step(0)),
        (3, lambda: up_way.step(1)),
        (11, lambda: up_way.step(2)),
        (14, lambda: down_way.step(1)),
    )
    attend_part(r, n_row, n_col, hooks, between)
    give.start()
    out_copies[2].start()
    r.home[pl.ds(0, TOK), :] = r.ret[pl.ds(0, TOK), :]
    proj_way.whole()
    out_copies[3].start()
    down_way.step(2)
    up_way.whole()
    give.wait()
    mlp_first(r, n_row, n_col, hidden)
    out_copies[5].start()
    down_way.whole()
    mlp_second(r, hidden)
    pick_start(glend, r.pick)
    out_copies[6].start()
    mlp_last(r, hidden)
    glend.wait()
    for way in ways:
        way.finish()
    for copy in out_copies:
        copy.wait()


def split_ins(tensors, *names):
    return {k: (tensors[k], vmem()) for k in names}


def forward_buffers(shapes, hidden):
    v = pltpu.VMEM
    first = dict(
        xw=v((4 * SLOT, D), BF),
        qkv=v((4 * SLOT, 3 * D), BF),
        probs=v((4 * HEADS, 16 * WIN, SLOT), BF),
        mixed=v((4 * SLOT, D), BF),
        table=v((256, 128), BF),
        ret=v((FIELD, D), BF),
    )
    second = dict(
        attended=v((TOK, D), BF),
        act=v((TOK, hidden), BF),
        slope=v((TOK, hidden), F32),
        gu=v((TOK, hidden), BF),
        branch=v((TOK, D), F32),
        gn2=v((TOK, D), F32),
        up_bias=v((hidden // D, D), F32),
    )
    sd = jax.ShapeDtypeStruct
    results = dict(
        n2=(sd((TOK, D), BF), vmem()),
        mixed_own=(sd((TOK, D), BF), vmem()),
        gfield=(sd((FIELD, D), BF), vmem()),
        grad_middle=(sd((TOK, D), F32), vmem()),
        output=(sd((TOK, D), BF), vmem()),
        small=(sd((16, D), F32), vmem()),
    )
    return first, second, results


def as_out(buffer):
    return (jax.ShapeDtypeStruct(buffer.shape, buffer.dtype), vmem())


def front_call(n_row, n_col, shapes, tensors, shards):
    hidden = shapes[2][0]
    sd, v = jax.ShapeDtypeStruct, pltpu.VMEM
    ins = {k: (t, vmem()) for k, t in tensors.items()}
    ins |= {"s" + str(i): (w, vmem()) for i, w in enumerate(shards)}
    first, second, results = forward_buffers(shapes, hidden)
    outs = dict(
        qkv_out=(sd((4 * SLOT, 3 * D), BF), hbm()),
        probs_out=(sd((4 * HEADS, 16 * WIN, SLOT), BF), hbm()),
        wqkv_out=(sd(shapes[0], BF), hbm()),
        wproj_out=(sd(shapes[1], BF), hbm()),
        xw_out=(sd((4 * SLOT, D), BF), hbm()),
        act_out=(sd((TOK, hidden), BF), hbm()),
        gu_out=(sd((TOK, hidden), BF), hbm()),
        **results,
    )
    wqkv, wproj, w1, w2 = [v(s, BF) for s in shapes]
    scratch = dict(
        **first,
        **second,
        wqkv=wqkv,
        wproj=wproj,
        w1=w1,
        w2=w2,
        field=v((FIELD, D), BF),
        home=v((FIELD, D), BF),
        picked=v((PICKED, D), BF),
        gpicked=v((PICKED, D), BF),
        out_sem=dma(7),
        local_sem=dma(4),
        lend_sem=dma(2, 3),
        give_sem=dma(2, 3),
        glend_sem=dma(2, 3),
    )
    for i in range(4):
        scratch |= {"p" + str(i): dma(Gather.SEMS), "r" + str(i): dma(Gather.SEMS)}
    return named_call(
        functools.partial(front_body, n_row, n_col, shapes, hidden), ins, outs, scratch, "front",
        vmem_limit_bytes=63 * MIB, collective_id=0, has_side_effects=True,
    )


def front_plain(n_row, n_col, shapes, tensors, weights, field):
    hidden = shapes[2][0]
    first, second, results = forward_buffers(shapes, hidden)
    wqkv, wproj, w1, w2 = [(w, vmem()) for w in weights]
    ins = split_ins(tensors, "query_bias", "value_bias", "rel_rows", "rel_cols", "masks") | split_ins(tensors, "places", "marks")
    outs = {k: as_out(first.pop(k)) for k in ("qkv", "probs", "ret")}

    def attend_body(r):
        prepare(r)
        for w in range(4):
            cut_windows(r.field, r.xw, n_row, n_col, w)
        attend_part(r, n_row, n_col, (), lambda part: None)

    one = named_call(
        attend_body, ins | dict(field=(field, vmem()), wqkv=wqkv), outs, first, "attend", vmem_limit_bytes=60 * MIB
    )
    home = return_xla(one.ret, n_row, n_col)
    ins = split_ins(tensors, "tokens", "cot", "proj_bias", "ln2_gain", "ln2_bias", "fc1_bias", "fc2_bias")
    outs = results | dict(act=as_out(second.pop("act")), gu=as_out(second.pop("gu")))

    def mlp_body(r):
        r.gfield[...] = jnp.zeros_like(r.gfield)
        mlp_first(r, n_row, n_col, hidden)
        mlp_second(r, hidden)
        mlp_last(r, hidden)

    two = named_call(
        mlp_body, ins | dict(home=(home, vmem()), wproj=wproj, w1=w1, w2=w2), outs, second, "mlp",
        vmem_limit_bytes=60 * MIB,
    )
    two.gfield = lend_xla(two.gfield[:TOK], n_row, n_col)
    two.qkv_out, two.probs_out, two.wqkv_out, two.wproj_out = one.qkv, one.probs, *weights[:2]
    two.act_out, two.gu_out = two.act, two.gu
    return two


def back_prepare(r, n_row, n_col):
    r.table[...] = table_kernel_value(r.places[...], joint_table(r.rel_rows, r.rel_cols))
    r.small[...] = jnp.zeros_like(r.small)
    r.small[0:16, :] = r.small_in[...]
    r.gtab[...] = jnp.zeros_like(r.gtab)
    r.dqkv[...] = jnp.zeros_like(r.dqkv)
    for w in range(4):
        cut_windows(r.gfield, r.gw, n_row, n_col, w)


def back_mix(r):
    def mix(n, _):
        at = pl.multiple_of(n * 256, 256)
        r.gmix[:, pl.ds(at, 256)] = nn(r.gw[...], r.wproj[:, pl.ds(at, 256)]).astype(BF)
        return 0

    lax.fori_loop(0, 3, mix, 0)


def back_windows(r, n_row, n_col, hooks):
    def body(w, pair, n):
        attend_back_pair(w, pair, n, r.qkv, r.gmix, r.probs, r.table, r.marks, r.masks, r.dqkv, r.gtab)

    over_windows(body, hooks, n_row, n_col)


def back_weights(r, n_row, n_col, sent):
    for n in range(9):
        r.gqkv[pl.ds(256 * n, 256), :] = tn(r.dqkv[:, pl.ds(256 * n, 256)], r.xw[...]).astype(BF)
        sent(n)
    ones = jnp.ones((16, 4 * SLOT), BF)
    r.small[2:3, :] = nn(ones, r.dqkv[:, 0:D])[0:1, :]
    r.small[3:4, :] = nn(ones, r.dqkv[:, 2 * D : 3 * D])[0:1, :]
    lane = lax.broadcasted_iota(jnp.int32, (128, 128), 1)
    left = jnp.where(lane < 64, r.gtab[0], 0.0)
    right = jnp.where(lane >= 64, r.gtab[1], 0.0)
    tab = lax.dot_general(
        r.places[...].astype(F32),
        jnp.concatenate([left, right], 0),
        (((0,), (0,)), ((), ())),
        precision=lax.Precision.HIGHEST,
        preferred_element_type=F32,
    )
    for t in range(4):
        r.small[16:32, 128 * t : 128 * t + 128] = tab[16 * t : 16 * t + 16, :]


def back_return(r, n_row, n_col):
    _, row, col = grid_place()

    def chunk(w, _):
        rows = pl.ds(pl.multiple_of(w * SLOT, SLOT), SLOT)
        r.gw[rows, :] = nn(r.dqkv[rows, :], r.wqkv[...]).astype(BF)
        return 0

    lax.fori_loop(0, 4, chunk, 0)
    hot = one_hot(field_slots(row, col, n_row, n_col), 4 * SLOT)
    r.ret[...] = nn(hot, r.gw[...]).astype(BF)


def back_last(r, n_row, n_col):
    _, row, col = grid_place()
    hot = one_hot(home_index(row, col, n_row, n_col), FIELD)
    grad = nn(hot, r.home[...])
    gain = vector(r.ln1_gain)
    _, xhat, inverse = norm(r.tokens[...].astype(F32), gain, vector(r.ln1_bias))
    r.input_grad[...] = (r.grad_middle[...] + norm_back(grad, xhat, inverse, gain)).astype(BF)
    r.late[0] = jnp.zeros((8, D), F32)
    r.late[0, 0:1, :] = jnp.sum(grad * xhat, 0, keepdims=True)
    r.late[0, 1:2, :] = jnp.sum(grad, 0, keepdims=True)


class Small:
    def __init__(self, value, come, send, recv, keep):
        dp, row, col = grid_place()
        self.value, self.come, self.send, self.recv, self.keep = value, come, send, recv, keep
        self.partners = [
            (dp, jnp.bitwise_xor(row, 1), col),
            (dp, jnp.bitwise_xor(row, 2), col),
            (dp, row, jnp.bitwise_xor(col, 1)),
            (dp, row, jnp.bitwise_xor(col, 2)),
            (1 - dp, row, col),
        ]

    def copy(self, s):
        return pltpu.make_async_remote_copy(
            self.value, self.come.at[s], self.send.at[s], self.recv.at[s],
            device_id=self.partners[s], device_id_type=MESH,
        )

    def start(self):
        self.copy(0).start()

    def step(self, s):
        self.copy(s).wait()
        value = self.come[s]
        if s == 4 and self.keep is not None:
            line = lax.broadcasted_iota(jnp.int32, value.shape, 0)
            value = jnp.where(line == self.keep, 0.0, value)
        self.value[...] = self.value[...] + value
        if s < 4:
            self.copy(s + 1).start()


class Late:
    def __init__(self, value, come, send, recv):
        self.dp, self.row, self.col = grid_place()
        self.value, self.come, self.send, self.recv = value, come, send, recv

    def copies(self, s):
        dp, row, col = self.dp, self.row, self.col
        plan = (
            [(dp, row, lax.rem(col + d, 4)) for d in (1, 2, 3)],
            [(dp, lax.rem(row + d, 4), col) for d in (1, 2, 3)],
            [(1 - dp, row, col)],
        )[s]
        return [
            pltpu.make_async_remote_copy(
                self.value.at[s], self.come.at[3 * s + i], self.send.at[3 * s + i], self.recv.at[3 * s + i],
                device_id=other, device_id_type=MESH,
            )
            for i, other in enumerate(plan)
        ]

    def start(self, s):
        for copy in self.copies(s):
            copy.start()

    def step(self, s):
        total = self.value[s]
        for i, copy in enumerate(self.copies(s)):
            copy.wait_recv()
            total = total + self.come[3 * s + i]
        self.value[s + 1] = total
        if s < 2:
            self.start(s + 1)

    def finish(self):
        for s in range(3):
            for copy in self.copies(s):
                copy.wait_send()


def back_body(n_row, n_col, shapes, r):
    dp, row, col = grid_place()
    blocks = blocks_of(shapes)
    rest = FIELD - TOK
    r.home[pl.ds(TOK, rest), :] = jnp.zeros((rest, D), BF)
    hidden = shapes[2][0]
    loads = [
        (r.gu_in, r.gu),
        (r.act_in, r.act),
        (r.wproj_in, r.wproj),
        (r.qkv_in, r.qkv),
        (r.probs_in, r.probs),
        (r.wqkv_in, r.wqkv),
        (r.xw_in, r.xw),
    ]
    loads = [pltpu.make_async_copy(src, dst, r.load_sem.at[i]) for i, (src, dst) in enumerate(loads)]
    for load in loads:
        load.start()
    greet(n_row, n_col)
    ways = [
        Reduce(g, g, dp * blocks[i][1], c, *blocks[i], pieces, parts, p, q)
        for i, (g, c, pieces, parts, p, q) in enumerate(
            [
                (r.gqkv, r.c0, 9, 3, r.p0, r.r0),
                (r.gproj, r.c1, 1, 1, r.p1, r.r1),
                (r.g1, r.c2, UP_PIECES, 1, r.p2, r.r2),
                (r.g2, r.c3, DOWN_PIECES, 1, r.p3, r.r3),
            ]
        )
    ]
    qkv_way, proj_way, up_way, down_way = ways
    loads[0].wait()
    loads[1].wait()
    mlp_weights(r, hidden, lambda j: up_way.start(0, j), lambda j: down_way.start(0, j))
    up_way.step(0)
    down_way.step(0)
    proj_weight_grad(r)
    proj_way.start(0)
    back_prepare(r, n_row, n_col)
    loads[2].wait()
    back_mix(r)
    loads[3].wait()
    loads[4].wait()
    hooks = (
        (0, lambda: proj_way.step(0)),
        (2, lambda: up_way.step(1)),
        (5, lambda: down_way.step(1)),
        (6, lambda: proj_way.step(1)),
        (19, lambda: up_way.step(2)),
    )
    back_windows(r, n_row, n_col, hooks)
    loads[6].wait()
    back_weights(r, n_row, n_col, lambda n: qkv_way.start(0, n))
    small = Small(r.small, r.small_come, r.small_sem.at[0], r.small_sem.at[1], 12)
    late = Late(r.late, r.late_come, r.late_sem.at[0], r.late_sem.at[1])
    small.start()
    qkv_way.step(0)
    down_way.step(2)
    loads[5].wait()
    back_return(r, n_row, n_col)
    give = Halo(r.ret, None, r.home, True, r.give_sem.at[0], r.give_sem.at[1], n_row, n_col)
    give.start()
    small.step(0)
    r.home[pl.ds(0, TOK), :] = r.ret[pl.ds(0, TOK), :]
    proj_way.step(2)
    qkv_way.step(1, 0)
    give.wait()
    back_last(r, n_row, n_col)
    late.start(0)
    small.step(1)
    qkv_way.step(1, 1)
    qkv_way.step(1, 2)
    up_way.result(r.o2)
    small.step(2)
    late.step(0)
    qkv_way.step(2, 0)
    down_way.result(r.o3)
    small.step(3)
    late.step(1)
    proj_way.result(r.o1)
    qkv_way.step(2, 1)
    small.step(4)
    late.step(2)
    qkv_way.step(2, 2)
    r.small[0:2, :] = r.late[3, 0:2, :]
    for part in range(3):
        qkv_way.result(r.o0, part)
    for way in ways:
        way.finish()
    late.finish()


def backward_buffers(shapes):
    v = pltpu.VMEM
    return dict(
        gw=v((4 * SLOT, D), BF),
        gmix=v((4 * SLOT, D), BF),
        dqkv=v((4 * SLOT, 3 * D), BF),
        table=v((256, 128), BF),
        gtab=v((2, 128, 128), F32),
    )


def back_call(n_row, n_col, shapes, tensors, first):
    sd, v = jax.ShapeDtypeStruct, pltpu.VMEM
    blocks = blocks_of(shapes)
    ins = {k: (t, vmem()) for k, t in tensors.items()}
    ins |= dict(
        gfield=(first.gfield, vmem()),
        grad_middle=(first.grad_middle, vmem()),
        small_in=(first.small, vmem()),
        n2=(first.n2, vmem()),
        mixed_own=(first.mixed_own, vmem()),
        qkv_in=(first.qkv_out, hbm()),
        probs_in=(first.probs_out, hbm()),
        wqkv_in=(first.wqkv_out, hbm()),
        wproj_in=(first.wproj_out, hbm()),
        xw_in=(first.xw_out, hbm()),
        act_in=(first.act_out, hbm()),
        gu_in=(first.gu_out, hbm()),
    )
    outs = dict(input_grad=(sd((TOK, D), BF), vmem()), small=(sd((32, D), F32), vmem()))
    outs |= {"o" + str(i): (sd(b, F32), vmem()) for i, b in enumerate(blocks)}
    come = [v((31 * b, h), BF) for b, h in blocks]
    scratch = backward_buffers(shapes) | dict(
        qkv=v((4 * SLOT, 3 * D), BF),
        probs=v((4 * HEADS, 16 * WIN, SLOT), BF),
        xw=v((4 * SLOT, D), BF),
        wqkv=v(shapes[0], BF),
        wproj=v(shapes[1], BF),
        gqkv=v(shapes[0], BF),
        gproj=v(shapes[1], BF),
        g1=v(shapes[2], BF),
        g2=v(shapes[3], BF),
        act=v((TOK, shapes[2][0]), BF),
        gu=v((TOK, shapes[2][0]), BF),
        cot_t=v((D, TOK), BF),
        c0=come[0],
        c1=come[1],
        c2=come[2],
        c3=come[3],
        ret=v((FIELD, D), BF),
        home=v((FIELD, D), BF),
        late=v((4, 8, D), F32),
        small_come=v((5, 32, D), F32),
        late_come=v((7, 8, D), F32),
        load_sem=dma(7),
        give_sem=dma(2, 3),
        small_sem=dma(2, 5),
        late_sem=dma(2, 7),
    )
    for i in range(4):
        scratch |= {"p" + str(i): dma(Reduce.SEMS), "r" + str(i): dma(Reduce.SEMS)}
    return named_call(
        functools.partial(back_body, n_row, n_col, shapes), ins, outs, scratch, "back",
        vmem_limit_bytes=63 * MIB, collective_id=1, has_side_effects=True,
    )


def back_plain(n_row, n_col, shapes, tensors, first, field):
    sd, v = jax.ShapeDtypeStruct, pltpu.VMEM
    hidden = shapes[2][0]
    ins = dict(
        act=(first.act_out, vmem()),
        gu=(first.gu_out, vmem()),
        n2=(first.n2, vmem()),
        gfield=(first.gfield, vmem()),
        mixed_own=(first.mixed_own, vmem()),
    ) | split_ins(tensors, "cot")

    def weights_body(r):
        mlp_weights(r, hidden, lambda j: None, lambda j: None)
        proj_weight_grad(r)

    outs = {k: (sd(s, BF), vmem()) for k, s in zip(("gproj", "g1", "g2"), shapes[1:])}
    three = named_call(
        weights_body, ins, outs, dict(cot_t=v((D, TOK), BF)), "weights", vmem_limit_bytes=60 * MIB
    )
    ins = split_ins(tensors, "rel_rows", "rel_cols", "masks", "places", "marks") | dict(
        gfield=(first.gfield, vmem()),
        small_in=(first.small, vmem()),
        qkv=(first.qkv_out, vmem()),
        probs=(first.probs_out, vmem()),
        wqkv=(first.wqkv_out, vmem()),
        wproj=(first.wproj_out, vmem()),
        field=(field, vmem()),
    )
    outs = dict(
        gqkv=(sd(shapes[0], BF), vmem()),
        ret=(sd((FIELD, D), BF), vmem()),
        small=(sd((32, D), F32), vmem()),
    )

    def windows_body(r):
        back_prepare(r, n_row, n_col)
        for w in range(4):
            cut_windows(r.field, r.xw, n_row, n_col, w)
        back_mix(r)
        back_windows(r, n_row, n_col, ())
        back_weights(r, n_row, n_col, lambda n: None)
        back_return(r, n_row, n_col)

    scratch = backward_buffers(shapes) | dict(xw=v((4 * SLOT, D), BF))
    one = named_call(windows_body, ins, outs, scratch, "windows", vmem_limit_bytes=60 * MIB)
    home = return_xla(one.ret, n_row, n_col)
    ins = split_ins(tensors, "tokens", "ln1_gain", "ln1_bias") | dict(
        home=(home, vmem()), grad_middle=(first.grad_middle, vmem())
    )
    outs = dict(input_grad=(sd((TOK, D), BF), vmem()), late=(sd((4, 8, D), F32), vmem()))
    two = named_call(lambda r: back_last(r, n_row, n_col), ins, outs, {}, "ends", vmem_limit_bytes=60 * MIB)
    one.input_grad = two.input_grad
    one.gproj, one.g1, one.g2 = three.gproj, three.g1, three.g2
    one.small = jnp.concatenate([two.late[0, :2], one.small[2:]], 0)
    return one


def last_body(count, r):
    for i in range(4):
        r.__dict__["t" + str(i)][...] = r.__dict__["s" + str(i)][...].astype(F32)
    r.output_out[...] = r.output[...]
    r.input_grad_out[...] = r.input_grad[...]
    for i in range(8):
        r.__dict__["v" + str(i)][...] = r.small[i : i + 1, :].reshape(D)
    r.up[...] = jnp.concatenate([r.small[8 + i : 9 + i, :] for i in range(r.up.shape[0] // D)], 1).reshape(-1)
    tables = jnp.concatenate([r.small[16:32, 128 * t : 128 * t + 128] for t in range(4)], 0)
    tables = tables[:, :HEAD] + pltpu.roll(tables, HEAD, 1)[:, :HEAD]
    r.rows[...] = tables[0 : 2 * WIN - 1, :]
    r.cols[...] = tables[32 : 32 + 2 * WIN - 1, :]
    r.stats[...] = jnp.sqrt(r.small[12:13, :5] / count)


def last_call(count, hidden, sums, output, input_grad, small):
    sd = jax.ShapeDtypeStruct
    ins = {"s" + str(i): (s, vmem()) for i, s in enumerate(sums)}
    ins |= dict(output=(output, vmem()), input_grad=(input_grad, vmem()), small=(small, vmem()))
    outs = {"t" + str(i): (sd(s.shape, F32), vmem()) for i, s in enumerate(sums)}
    outs |= dict(output_out=(sd((TOK, D), BF), vmem()), input_grad_out=(sd((TOK, D), BF), vmem()))
    outs |= {"v" + str(i): (sd((D,), F32), vmem()) for i in range(8)}
    outs |= dict(
        up=(sd((hidden,), F32), vmem()),
        rows=(sd((2 * WIN - 1, HEAD), F32), vmem()),
        cols=(sd((2 * WIN - 1, HEAD), F32), vmem()),
        stats=(sd((1, 5), F32), vmem()),
    )
    return named_call(functools.partial(last_body, count), ins, outs, {}, "last", vmem_limit_bytes=20 * MIB)


def on_device(
    n_dp, n_row, n_col,
    tokens, ln1_gain, ln1_bias, qkv_weight, query_bias, value_bias, rel_rows, rel_cols,
    proj_weight, proj_bias, ln2_gain, ln2_bias, fc1_weight, fc1_bias, fc2_weight, fc2_bias, cotangent,
):
    direct = (n_dp, n_row, n_col) == (2, 4, 4)
    tok = tokens.reshape(TOK, D)
    mask_values = np.zeros((16, 128), np.float32)
    mask_values[0, :64] = 1.0
    mask_values[1, 64:] = 1.0
    shared = dict(
        tokens=tok,
        cot=cotangent.reshape(TOK, D),
        ln1_gain=ln1_gain,
        ln1_bias=ln1_bias,
        rel_rows=rel_rows,
        rel_cols=rel_cols,
        masks=jnp.asarray(mask_values, BF),
    )
    forward = shared | dict(
        query_bias=query_bias,
        value_bias=value_bias,
        proj_bias=proj_bias,
        ln2_gain=ln2_gain,
        ln2_bias=ln2_bias,
        fc1_bias=fc1_bias,
        fc2_bias=fc2_bias,
        places=jnp.asarray(table_places(False), BF),
        marks=jnp.asarray(key_marks(False), BF),
    )
    backward = shared | dict(
        places=jnp.asarray(table_places(True), BF),
        marks=jnp.asarray(key_marks(True), BF),
    )
    shards = (qkv_weight, proj_weight, fc1_weight, fc2_weight)
    shapes = [(s.shape[1] * n_row * n_col, s.shape[0] * n_dp) for s in shards]
    if direct:
        forward |= dict(pick=jnp.asarray(pick_rows(), BF))
        weights, field = [s.T for s in shards], None
    else:
        weights = []
        for s in shards:
            s = lax.all_gather(s, AXES, axis=1, tiled=True)
            weights.append(lax.all_gather(s, "dp", axis=0, tiled=True).T)
        normed = norm(tok.astype(F32), ln1_gain.astype(F32), ln1_bias.astype(F32))[0].astype(BF)
        field = lend_xla(normed, n_row, n_col)
    if direct:
        first = front_call(n_row, n_col, shapes, forward, weights)
        second = back_call(n_row, n_col, shapes, backward, first)
        small = second.small
        sums = (second.o0, second.o1, second.o2, second.o3)
    else:
        first = front_plain(n_row, n_col, shapes, forward, weights, field)
        second = back_plain(n_row, n_col, shapes, backward, first, field)
        sums = []
        for g in (second.gqkv, second.gproj, second.g1, second.g2):
            g = lax.psum_scatter(g, AXES, scatter_dimension=0, tiled=True)
            sums.append(lax.psum_scatter(g, "dp", scatter_dimension=1, tiled=True))
        local = lax.psum(second.small, AXES)
        line = jnp.arange(32)[:, None] == 12
        small = jnp.where(line, local, lax.psum(jnp.where(line, 0.0, local), "dp"))
    out = last_call(TOK * n_row * n_col * D, shapes[2][0], sums, first.output, second.input_grad, small)
    return (
        out.output_out.reshape(tokens.shape),
        out.input_grad_out.reshape(tokens.shape),
        out.v0,
        out.v1,
        out.t0.T,
        out.v2,
        out.v3,
        out.rows,
        out.cols,
        out.t1.T,
        out.v4,
        out.v5,
        out.v6,
        out.t2.T,
        out.up,
        out.t3.T,
        out.v7,
        out.stats,
    )


def solution(mesh):
    tile = P("dp", "row", "col", None)
    weight = P("dp", AXES)
    sizes = [mesh.shape[a] for a in ("dp", "row", "col")]
    ins = [tile] + [P()] * 16
    for i in (3, 8, 12, 14):
        ins[i] = weight
    ins[16] = tile
    outs = [tile, tile] + [P()] * 16
    for i in (4, 9, 13, 15):
        outs[i] = weight
    outs[17] = P("dp", None)
    return jax.shard_map(
        functools.partial(on_device, *sizes),
        mesh=mesh,
        in_specs=tuple(ins),
        out_specs=tuple(outs),
        check_vma=False,
    )
```

```python
import functools
import types

import jax
import jax.numpy as jnp
import numpy as np
from jax import lax
from jax.experimental import pallas as pl
from jax.experimental.pallas import tpu as pltpu
from jax.sharding import PartitionSpec as P

HEADS = 12
HEAD = 64
WIN = 14
EPS = 1e-06
MESH = pl.DeviceIdType.MESH
AXES = ("row", "col")
F32 = jnp.float32
BF = jnp.bfloat16

D = HEADS * HEAD
TILE = 16
TOK = TILE * TILE
LO = 6
SLOT = 256
PAIRS = HEADS // 2
FIELD = 496
PICKED = 144
MIB = 2**20

LINKS = {
    (1, 0): (True, 160, 96, 256),
    (0, 1): (False, 0, 96, 352),
    (1, 1): (False, 96, 48, 448),
}


def nt(a, b):
    return lax.dot_general(a, b, (((1,), (1,)), ((), ())), preferred_element_type=F32)


def nn(a, b):
    return lax.dot_general(a, b, (((1,), (0,)), ((), ())), preferred_element_type=F32)


def tn(a, b):
    return lax.dot_general(a, b, (((0,), (0,)), ((), ())), preferred_element_type=F32)


def pick_rows():
    table = np.zeros((PICKED, TOK), np.float32)
    for base, first in ((0, 0), (96, TILE - LO)):
        for i in range((TILE - first) * LO):
            y, x = divmod(i, LO)
            table[base + i, (first + y) * TILE + TILE - LO + x] = 1.0
    return table


def table_places(back):
    place = np.zeros((256, 64), np.float32)
    for head in range(2):
        for r in range(2 * WIN - 1):
            for copy in range(2):
                row_lane = (64 + 28 * copy + r + 64 * head) % 128
                col_lane = (28 * copy + r + 64 * head) % 128
                place[128 * head + row_lane, 26 - r] = 1.0
                place[128 * head + col_lane, 32 + (r if back else 26 - r)] = 1.0
    return place


def key_marks(back):
    marks = np.zeros((2, SLOT, 128), np.float32)
    for head in range(2):
        for j in range(SLOT):
            k, l = divmod(j, 16)
            if k < WIN and l < WIN:
                for copy in range(2):
                    marks[head, j, (64 + 28 * copy + k + 64 * head) % 128] = 1.0
                    marks[head, j, (78 + 28 * copy + (13 - l if back else l) + 64 * head) % 128] = 1.0
            else:
                marks[head, j, (120 + 64 * head) % 128] = -1e30
    return marks


def lane_kinds(rows):
    lane = lax.broadcasted_iota(jnp.int32, (rows, 128), 1)
    kinds = []
    for head in range(2):
        at = (lane + 64 * head) % 128 if head else lane
        own = at < 64
        first = (at >= 64) & (at < 92)
        second = (at >= 92) & (at < 120)
        is_row = ((at >= 64) & (at < 78)) | ((at >= 92) & (at < 106))
        kinds.append((own, first, second, is_row, at == 120))
    return kinds


def window_index(w, row, col, n_row, n_col):
    place = lax.broadcasted_iota(jnp.int32, (SLOT, 1), 0)
    y = place // 16
    x = place - 16 * y
    a, b = w // 2, w % 2
    ry = WIN * (row + a) + y - TILE * row
    rx = WIN * (col + b) + x - TILE * col
    good = (y < WIN) & (x < WIN) & (ry < TILE) & (rx < TILE)
    if a:
        good = good & (row == n_row - 1)
    if b:
        good = good & (col == n_col - 1)
    up, left = ry < 0, rx < 0
    base = jnp.where(up, jnp.where(left, 448, 256), jnp.where(left, 352, 0))
    width = jnp.where(left, LO, TILE)
    index = base + jnp.where(up, ry + LO, ry) * width + jnp.where(left, rx + LO, rx)
    return jnp.where(good, index, -1)


def field_slots(row, col, n_row, n_col):
    at = lax.broadcasted_iota(jnp.int32, (FIELD, 1), 0)
    above = (at >= 256) & (at < 352)
    left = (at >= 352) & (at < 448)
    corner = at >= 448
    narrow = left | corner
    rest = jnp.where(corner, at - 448, jnp.where(left, at - 352, jnp.where(above, at - 256, at)))
    sixth = sum((rest >= LO * k).astype(jnp.int32) for k in range(1, TILE))
    ty = jnp.where(narrow, sixth, rest // TILE)
    tx = rest - ty * jnp.where(narrow, LO, TILE)
    ty = jnp.where(above | corner, ty - LO, ty)
    tx = jnp.where(narrow, tx - LO, tx)
    good = at < 484
    where = 0
    for t, place, n, stride, unit in ((ty, row, n_row, 2, 16), (tx, col, n_col, 1, 1)):
        y = TILE * place + t - WIN * place
        late = y >= WIN
        good = good & (y >= 0) & (jnp.logical_not(late) | (place == n - 1))
        where = where + jnp.where(late, stride * SLOT + unit * (y - WIN), unit * y)
    return jnp.where(good, where, -1)


def home_index(row, col, n_row, n_col):
    place = lax.broadcasted_iota(jnp.int32, (TOK, 1), 0)
    ty = place // TILE
    tx = place - TILE * ty
    down = (TILE * row + ty - WIN * row >= WIN) & (row < n_row - 1)
    right = (TILE * col + tx - WIN * col >= WIN) & (col < n_col - 1)
    near = TILE - LO
    return jnp.where(
        down,
        jnp.where(right, 448 + (ty - near) * LO + tx - near, 256 + (ty - near) * TILE + tx),
        jnp.where(right, 352 + ty * LO + tx - near, place),
    )


def one_hot(index, size):
    lane = lax.broadcasted_iota(jnp.int32, (index.shape[0], size), 1)
    return jnp.where(lane == index, 1.0, 0.0).astype(BF)


STEP = 64


def by_rows(body, sums):
    def step(i, kept):
        parts = body(pl.ds(pl.multiple_of(i * STEP, STEP), STEP))
        return tuple(k + sum(p[8 * q : 8 * q + 8] for q in range(STEP // 8)) for k, p in zip(kept, parts))

    return lax.fori_loop(0, TOK // STEP, step, (jnp.zeros((8, D), F32),) * sums)


def column_sum(v):
    return jnp.sum(v, 0, keepdims=True)


def norm(v, gain, bias):
    mean = jnp.mean(v, -1, keepdims=True)
    center = v - mean
    inverse = lax.rsqrt(jnp.mean(center * center, -1, keepdims=True) + EPS)
    xhat = center * inverse
    return xhat * gain + bias, xhat, inverse


def norm_back(grad, xhat, inverse, gain):
    d = grad * gain
    return inverse * (
        d - jnp.mean(d, -1, keepdims=True) - xhat * jnp.mean(d * xhat, -1, keepdims=True)
    )


def grid_place():
    return lax.axis_index("dp"), lax.axis_index("row"), lax.axis_index("col")


def exists(step, row, col, n_row, n_col):
    r, c = row + step[0], col + step[1]
    return (r >= 0) & (r < n_row) & (c >= 0) & (c < n_col)


CORNERS = ((1, 1), (-1, -1))


def greet(n_row, n_col):
    dp, row, col = grid_place()
    barrier = pltpu.get_barrier_semaphore()
    others = [(dp, row, lax.rem(col + d, n_col)) for d in (1, 2, 3)]
    others += [(dp, lax.rem(row + d, n_row), col) for d in (1, 2, 3)]
    others.append((1 - dp, row, col))
    for other in others:
        pl.semaphore_signal(barrier, inc=1, device_id=other, device_id_type=MESH)
    count = len(others)
    for step in CORNERS:
        there = exists(step, row, col, n_row, n_col)

        @pl.when(there)
        def _():
            pl.semaphore_signal(
                barrier, inc=1, device_id=(dp, row + step[0], col + step[1]), device_id_type=MESH
            )

        count = count + jnp.where(there, 1, 0)
    pl.semaphore_wait(barrier, count)


class Halo:
    def __init__(self, source, picked, land, back, send, recv, n_row, n_col):
        self.source, self.picked, self.land, self.back = source, picked, land, back
        self.send, self.recv, self.size = send, recv, (n_row, n_col)

    def copies(self):
        dp, row, col = grid_place()
        sign = -1 if self.back else 1
        for i, ((dr, dc), (own, first, rows, there)) in enumerate(LINKS.items()):
            if self.back:
                src = self.source.at[pl.ds(there, rows)]
            else:
                src = (self.source if own else self.picked).at[pl.ds(first, rows)]
            copy = pltpu.make_async_remote_copy(
                src,
                self.land.at[pl.ds(there, rows)],
                self.send.at[i],
                self.recv.at[i],
                device_id=(dp, row + sign * dr, col + sign * dc),
                device_id_type=MESH,
            )
            goes = exists((sign * dr, sign * dc), row, col, *self.size)
            comes = exists((-sign * dr, -sign * dc), row, col, *self.size)
            yield copy, goes, comes

    def start(self):
        for copy, goes, _ in self.copies():
            pl.when(goes)(copy.start)

    def wait(self):
        for copy, goes, comes in self.copies():
            pl.when(goes)(copy.wait_send)
            pl.when(comes)(copy.wait_recv)


def pick_start(halo, pick):
    halo.picked[...] = nn(pick[...], halo.source[pl.ds(0, TOK), :]).astype(BF)
    halo.start()


def halo_xla(blocks, back, n_row, n_col):
    sign = -1 if back else 1
    pieces = [blocks[0]]
    for (dr, dc), block in zip(LINKS, blocks[1:]):
        dr, dc = sign * dr, sign * dc
        pairs = [
            (r * n_col + c, (r + dr) * n_col + c + dc)
            for r in range(n_row)
            for c in range(n_col)
            if 0 <= r + dr < n_row and 0 <= c + dc < n_col
        ]
        pieces.append(lax.ppermute(block, AXES, pairs))
    return jnp.concatenate(pieces, 0)


def lend_xla(own, n_row, n_col):
    grid = own.reshape(TILE, TILE, -1)
    corner = grid[TILE - LO :, TILE - LO :].reshape(LO * LO, -1)
    blocks = [
        own,
        own[TILE * (TILE - LO) :],
        grid[:, TILE - LO :].reshape(TILE * LO, -1),
        jnp.pad(corner, ((0, 48 - LO * LO), (0, 0))),
    ]
    return halo_xla(blocks, False, n_row, n_col)


def return_xla(field, n_row, n_col):
    return halo_xla([field[:256], field[256:352], field[352:448], field[448:]], True, n_row, n_col)


def blocks_of(shapes):
    return [(n // 16, k // 2) for n, k in shapes]


def rows_at(first, count):
    return pl.ds(pl.multiple_of(first, 16), count)


LINE, OWN, OWN_CORE, LINE_CORE, FAR, NEAR_CORE, FAR_CORE, CORE = range(10, 18)


class Gather:
    SEMS = 20

    def __init__(self, full, shard, block, half, send, recv, part=0, parts=1):
        self.dp, self.row, self.col = grid_place()
        width = half // parts
        self.full, self.shard, self.b = full, shard.at[:, pl.ds(part * width, width)], block
        self.send, self.recv = send, recv
        self.lanes = pl.ds(pl.multiple_of(self.dp * half + part * width, 128), width)
        self.other = pl.ds(pl.multiple_of((1 - self.dp) * half + part * width, 128), width)

    def block(self, flip, place):
        return (jnp.bitwise_xor(self.row, flip) * 4 + place) * self.b

    def came(self, d):
        return lax.rem(self.col + 4 - d, 4)

    def copy(self, i, first, count, land, target, shard=False):
        core = target == CORE
        if core:
            device = (1 - self.dp, self.row, self.col)
        elif isinstance(target, tuple):
            device = (self.dp, self.row, lax.rem(self.col + target[0], 4))
        else:
            device = (self.dp, jnp.bitwise_xor(self.row, target), self.col)

        def make(src, dst):
            return pltpu.make_async_remote_copy(
                src, dst, self.send.at[i], self.recv.at[i], device_id=device, device_id_type=MESH
            )

        def out():
            there = self.full.at[rows_at(first, count), self.lanes]
            return make(self.shard if shard else there, there)

        def come():
            here = self.full.at[rows_at(land, count), self.other if core else self.lanes]
            return make(here, here)

        return out, come

    def copies(self, k):
        b = self.b
        own = self.block(0, self.col)
        if k == LINE:
            return [
                self.copy(d - 1, own, b, self.block(0, self.came(d)), (d,), True) for d in (1, 2, 3)
            ]
        if k == OWN:
            return [self.copy(2 + f, own, b, self.block(f, self.col), f, True) for f in (1, 2)]
        if k == OWN_CORE:
            return [self.copy(5, own, b, own, CORE, True)]
        if k < LINE:
            at = self.came(k)
            return [
                self.copy(4 + 2 * k, self.block(0, at), b, self.block(1, at), 1),
                self.copy(5 + 2 * k, self.block(0, at), b, self.block(2, at), 2),
            ]
        if k == LINE_CORE:
            return [
                self.copy(11 + d, self.block(0, self.came(d)), b, self.block(0, self.came(d)), CORE)
                for d in (1, 2, 3)
            ]
        if k == FAR:
            return [
                self.copy(15, self.block(2, 0), 2 * b, self.block(3, 0), 1),
                self.copy(16, self.block(1, 2), 2 * b, self.block(3, 2), 2),
            ]
        if k == NEAR_CORE:
            return [self.copy(16 + f, self.block(f, 0), 4 * b, self.block(f, 0), CORE) for f in (1, 2)]
        return [self.copy(19, self.block(3, 0), 4 * b, self.block(3, 0), CORE)]

    def start(self, *kinds):
        for k in kinds:
            for out, _ in self.copies(k):
                out().start()

    def arrive(self, *kinds):
        for k in kinds:
            for _, come in self.copies(k):
                come().wait_recv()

    def step(self, n):
        if n == 0:
            for d in (1, 2, 3):
                self.copies(LINE)[d - 1][1]().wait_recv()
                self.start(d)
            self.start(LINE_CORE)
        elif n == 1:
            self.arrive(OWN, 1, 2, 3)
            self.start(FAR, NEAR_CORE)
        else:
            self.arrive(FAR)
            self.start(FAR_CORE)

    def whole(self):
        self.arrive(OWN_CORE, LINE_CORE, NEAR_CORE, FAR_CORE)

    def finish(self):
        for k in (LINE, OWN, OWN_CORE, 1, 2, 3, LINE_CORE, FAR, NEAR_CORE, FAR_CORE):
            for out, _ in self.copies(k):
                out().wait_send()


class Reduce:
    SEMS = 34

    def __init__(self, grad, total, base, land, come, block, half, pieces, parts, send, recv):
        self.dp, self.row, self.col = grid_place()
        self.grad, self.total, self.base, self.come = grad, total, base, come
        self.land, self.land_row, mirrored = land
        self.land_there = self.dp * half if mirrored else 0
        self.land_here = (1 - self.dp) * half if mirrored else 0
        self.b, self.h, self.send, self.recv = block, half, send, recv
        self.pieces, self.parts, self.width = pieces, parts, half // parts
        self.other = pl.ds(pl.multiple_of((1 - self.dp) * half, 128), half)

    def side(self, base, part, width):
        return pl.ds(pl.multiple_of(base + part * width, 128), width)

    def at(self, flip, place=0):
        return (jnp.bitwise_xor(self.row, flip) * 4 + place) * self.b

    def lanes(self, part):
        return pl.ds(pl.multiple_of(self.base + part * self.width, 128), self.width)

    def came(self, first, count, part):
        return self.come.at[rows_at(first, count), pl.ds(part * self.width, self.width)]

    def tot(self, first, count, part):
        return self.total.at[rows_at(first, count), self.lanes(part)]

    def sem(self, k, part):
        if k == 0:
            return part
        return self.pieces + 7 * part + {1: 0, 2: 2, 3: 4}[k]

    def copies(self, k, part):
        b = self.b
        if k == 0:
            n = 16 * b // self.pieces
            there = self.land.at[rows_at(self.land_row + part * n, n), self.side(self.land_there, 0, self.h)]
            plan = [(self.grad.at[rows_at(part * n, n), self.other], there, (1 - self.dp, self.row, self.col))]
        elif k == 1:
            plan = [
                (
                    self.tot(self.at(3, 2 * half), 2 * b, part),
                    self.came(2 * half * b, 2 * b, part),
                    (self.dp, jnp.bitwise_xor(self.row, 1 + half), self.col),
                )
                for half in (0, 1)
            ]
        elif k == 2:
            plan = [
                (
                    self.tot(self.at(flip), 4 * b, part),
                    self.came(4 * flip * b, 4 * b, part),
                    (self.dp, jnp.bitwise_xor(self.row, flip), self.col),
                )
                for flip in (1, 2)
            ]
        else:
            plan = []
            for d in (1, 2, 3):
                to = lax.rem(self.col + d, 4)
                plan.append(
                    (
                        self.tot(self.at(0, to), b, part),
                        self.came((11 + d) * b, b, part),
                        (self.dp, self.row, to),
                    )
                )
        base = self.sem(k, part)
        return [
            pltpu.make_async_remote_copy(
                src, dst, self.send.at[base + i], self.recv.at[base + i], device_id=dev, device_id_type=MESH
            )
            for i, (src, dst, dev) in enumerate(plan)
        ]

    def start(self, k, part=0):
        for copy in self.copies(k, part):
            copy.start()

    def arrive(self, k, part=0):
        for copy in self.copies(k, part):
            copy.wait_recv()

    def sum_rows(self, first, count, froms, part, source=None, base=0):
        most = (256 if len(froms) == 1 else 96) * 384
        step = next(n for n in range(count, 0, -16) if count % n == 0 and n * self.width <= most)
        lanes = self.lanes(part)
        side = self.side(base, part, self.width)
        source = self.come if source is None else source

        def body(i, _):
            at = rows_at(first + i * step, step)
            value = self.total[at, lanes]
            if len(froms) == 1:
                value = value + source[rows_at(froms[0] + i * step, step), side]
            else:
                value = value.astype(F32)
                for f in froms:
                    value = value + source[rows_at(f + i * step, step), side].astype(F32)
                value = value.astype(BF)
            self.total[at, lanes] = value
            return 0

        lax.fori_loop(0, count // step, body, 0)

    def add_piece(self, piece):
        n = 16 * self.b // self.pieces
        self.arrive(0, piece)
        for part in range(self.parts):
            self.sum_rows(piece * n, n, (self.land_row + piece * n,), part, self.land, self.land_here)

    def step(self, k, part=0):
        b = self.b
        if k == 0:
            for piece in range(self.pieces):
                self.add_piece(piece)
            for part in range(1, self.parts):
                self.start(1, part)
            part = 0
        else:
            self.arrive(k, part)
            if k == 1:
                self.sum_rows(self.at(2), 2 * b, (0,), part)
                self.sum_rows(self.at(1, 2), 2 * b, (2 * b,), part)
            else:
                self.sum_rows(self.at(0), 4 * b, (4 * b, 8 * b), part)
        self.start(k + 1, part)

    def result(self, out, part=0):
        b = self.b
        self.arrive(3, part)
        value = self.total[rows_at(self.at(0, self.col), b), self.lanes(part)].astype(F32)
        side = pl.ds(part * self.width, self.width)
        for d in (1, 2, 3):
            value = value + self.come[pl.ds((11 + d) * b, b), side].astype(F32)
        out[:, side] = value

    def gone(self):
        for piece in range(self.pieces):
            self.copies(0, piece)[0].wait_send()

    def finish(self):
        for part in range(self.parts):
            for k in (1, 2, 3):
                for copy in self.copies(k, part):
                    copy.wait_send()


def vmem():
    return pl.BlockSpec(memory_space=pltpu.VMEM)


def hbm():
    return pl.BlockSpec(memory_space=pl.ANY)


def dma(*n):
    return pltpu.SemaphoreType.DMA(n)


def named_call(body, ins, outs, scratch, name, **params):
    names = [*ins, *outs, *scratch]

    def kernel(*refs):
        body(types.SimpleNamespace(**dict(zip(names, refs))))

    result = pl.pallas_call(
        kernel,
        name=name,
        out_shape=[shape for shape, _ in outs.values()],
        in_specs=[spec for _, spec in ins.values()],
        out_specs=[spec for _, spec in outs.values()],
        scratch_shapes=list(scratch.values()),
        compiler_params=pltpu.CompilerParams(**params),
    )(*[array for array, _ in ins.values()])
    return types.SimpleNamespace(**dict(zip(outs, result)))


def vector(ref):
    return ref[...].astype(F32).reshape(1, -1)


def joint_table(rel_rows, rel_cols):
    parts = [rel_rows[...], jnp.zeros((5, HEAD), BF), rel_cols[...], jnp.zeros((5, HEAD), BF)]
    table = jnp.concatenate([p.astype(F32) for p in parts], 0)
    return jnp.concatenate([table, table], 1).astype(BF)


def table_kernel_value(places, table):
    value = nn(places, table)
    line = lax.broadcasted_iota(jnp.int32, value.shape, 0)
    lane = lax.broadcasted_iota(jnp.int32, value.shape, 1)
    return jnp.where((line < 128) == (lane < 64), value, 0.0).astype(BF)


def spread(a, back):
    rows, cols = [], []
    for y in range(a.shape[0] // 16):
        part = a[16 * y : 16 * y + 16, :]
        rows.append(pltpu.roll(part, 13 - y if back else (115 + y) % 128, 1))
        cols.append(pltpu.roll(part, 50 if back else 65, 1, stride=1, stride_axis=0))
    return jnp.concatenate(rows, 0), jnp.concatenate(cols, 0)


def pair_place(w, pair):
    return pl.multiple_of(w * SLOT, SLOT), pl.multiple_of(pair * 128, 128)


def attend_pair(w, place, pair, n, qkv, table, marks, masks, probs, mixed):
    r0, l0 = pair_place(w, pair)
    q2 = qkv[pl.ds(r0, n), pl.ds(l0, 128)]
    k2 = qkv[pl.ds(r0, SLOT), pl.ds(D + l0, 128)]
    v2 = qkv[pl.ds(r0, SLOT), pl.ds(2 * D + l0, 128)]
    a2 = nt(q2, table[...])
    qf = q2.astype(F32) * HEAD**-0.5
    kinds = lane_kinds(n)
    outs = []
    for head in range(2):
        own, first, second, is_row, one = kinds[head]
        rows, cols = spread(a2[:, 128 * head : 128 * head + 128], False)
        bias = jnp.where(is_row, rows, cols)
        high = bias.astype(BF).astype(F32)
        low = jnp.where(second, bias - high, jnp.where(one, 1.0, 0.0))
        aug = jnp.where(own, qf, jnp.where(first, high, low)).astype(BF)
        keys = k2 * masks[head : head + 1, :] + marks[head]
        scores = nt(aug, keys)
        top = jnp.max(scores, -1, keepdims=True)
        e = jnp.exp(scores - top)
        p = (e * (1.0 / jnp.sum(e, -1, keepdims=True))).astype(BF)
        probs[2 * place + head] = p
        outs.append(nn(p, v2))
    mixed[pl.ds(r0, n), pl.ds(l0, 128)] = jnp.where(kinds[0][0], outs[0], outs[1]).astype(BF)


def attend_back_pair(w, place, pair, n, qkv, gmix, probs, table, marks, masks, dqkv, gtab):
    r0, l0 = pair_place(w, pair)
    scale = HEAD**-0.5
    q2 = qkv[pl.ds(r0, n), pl.ds(l0, 128)]
    k2 = qkv[pl.ds(r0, SLOT), pl.ds(D + l0, 128)]
    v2 = qkv[pl.ds(r0, SLOT), pl.ds(2 * D + l0, 128)]
    g2 = gmix[pl.ds(r0, n), pl.ds(l0, 128)]
    kinds = lane_kinds(n)
    dq, dk, dv = [], [], []
    for head in range(2):
        own, first, second, is_row, one = kinds[head]
        mask = masks[head : head + 1, :]
        p = probs[2 * place + head]
        pf = p.astype(F32)
        dp = nt(g2, v2 * mask)
        ds = (pf * (dp - jnp.sum(pf * dp, -1, keepdims=True))).astype(BF)
        keys = k2 * (mask * jnp.asarray(scale, BF)) + marks[head]
        dqa = nn(ds, keys)
        marked = jnp.where(first | second, dqa, 0.0)
        rows, _ = spread(jnp.where(is_row, marked, 0.0), True)
        _, cols = spread(jnp.where(is_row, 0.0, marked), True)
        back = rows + cols
        at = lax.broadcasted_iota(jnp.int32, (n, 128), 1)
        if head:
            at = (at + 64) % 128
        high = back.astype(BF).astype(F32)
        split = jnp.where((at < 28) | ((at >= 64) & (at < 92)), high, back - high).astype(BF)
        extra = nn(split, table[128 * head : 128 * head + 128, :])
        dq.append(dqa + extra)
        gtab[head] += tn(split, q2)
        dk.append(tn(ds, q2))
        dv.append(tn(p, g2))
    wide = lane_kinds(SLOT)[0][0]
    dqkv[pl.ds(r0, n), pl.ds(l0, 128)] = jnp.where(kinds[0][0], dq[0], dq[1]).astype(BF)
    dqkv[pl.ds(4 * SLOT + r0, SLOT), pl.ds(l0, 128)] = (jnp.where(wide, dk[0], dk[1]) * scale).astype(BF)
    dqkv[pl.ds(8 * SLOT + r0, SLOT), pl.ds(l0, 128)] = jnp.where(wide, dv[0], dv[1]).astype(BF)


def over_windows(body, hooks, n_row, n_col):
    _, row, col = grid_place()
    for a, n in ((0, 16 * WIN), (1, 16 * (TILE * n_row - WIN * n_row))):

        def step(i, _):
            b = i // PAIRS
            good = (b == 0) | (col == n_col - 1)
            if a:
                good = good & (row == n_row - 1)

            @pl.when(good)
            def _():
                body(a, 2 * a + b, i, lax.rem(i, PAIRS), n)

            for when, hook in hooks:
                if when // (2 * PAIRS) == a:
                    pl.when(i == when % (2 * PAIRS))(hook)
            return 0

        lax.fori_loop(0, 2 * PAIRS, step, 0)


def attend_part(r, n_row, n_col, hooks, between):
    _, row, col = grid_place()
    biases = (vector(r.query_bias), None, vector(r.value_bias))
    for part, bias in enumerate(biases):
        for n in range(3):
            at = part * D + 256 * n
            value = nt(r.xw[...], r.wqkv[pl.ds(at, 256), :])
            if bias is not None:
                value = value + bias[:, 256 * n : 256 * n + 256]
            r.qkv[:, pl.ds(at, 256)] = value.astype(BF)
        between(part)

    def body(a, w, i, pair, n):
        attend_pair(w, i, pair, n, r.qkv, r.table, r.marks, r.masks, (r.probs0, r.probs1)[a], r.mixed)

    over_windows(body, hooks, n_row, n_col)
    hot = one_hot(field_slots(row, col, n_row, n_col), 4 * SLOT)
    r.ret[...] = nn(hot, r.mixed[...]).astype(BF)


def cut_windows(source, land, n_row, n_col, w):
    _, row, col = grid_place()
    hot = one_hot(window_index(w, row, col, n_row, n_col), FIELD)
    land[pl.ds(w * SLOT, SLOT), :] = nn(hot, source[...]).astype(BF)


def mlp_first(r, n_row, n_col, hidden, between, hooks):
    _, row, col = grid_place()
    hot = one_hot(home_index(row, col, n_row, n_col), FIELD)
    r.mixed_own[...] = nn(hot, r.home[...]).astype(BF)
    r.acc[...] = nt(r.mixed_own[...], r.wproj[...])
    shift, gain, bias = vector(r.proj_bias), vector(r.ln2_gain), vector(r.ln2_bias)

    def rows_body(rows):
        attended = (r.acc[rows, :] + shift).astype(BF)
        r.attended[rows, :] = attended
        middle = r.tokens[rows, :].astype(F32) + attended.astype(F32)
        r.n2[rows, :] = norm(middle, gain, bias)[0].astype(BF)
        return ()

    by_rows(rows_body, 0)
    between()
    up_bias = vector(r.fc1_bias)
    for line in range(hidden // D):
        r.up_bias[line : line + 1, :] = up_bias[:, line * D : line * D + D]

    def chunk(j, _):
        at = pl.multiple_of(j * 256, 256)
        lane = pl.multiple_of(lax.rem(j, 3) * 256, 256)
        u = nt(r.n2[...], r.w1[pl.ds(at, 256), :]) + r.up_bias[pl.ds(j // 3, 1), pl.ds(lane, 256)]
        cdf = 0.5 * (1.0 + lax.erf(u * 0.7071067811865476))
        r.act[:, pl.ds(at, 256)] = (u * cdf).astype(BF)
        r.slope[:, pl.ds(at, 256)] = (cdf + u * (jnp.exp(-0.5 * u * u) * 0.3989422804014327)).astype(BF)
        for when, hook in hooks:
            pl.when(j == when)(hook)
        return 0

    lax.fori_loop(0, hidden // 256, chunk, 0)


PARTS = 3


def mlp_second(r, hidden, ready):
    r.acc[...] = jnp.zeros_like(r.acc)
    r.small[...] = jnp.zeros_like(r.small)
    n = hidden // (2 * PARTS)
    for part in range(PARTS):
        ready(part)

        def chunk(i, _):
            at = pl.multiple_of((i * PARTS + part) * n, n)
            wide = pl.ds(at, n)
            gu = (nn(r.cot[...], r.w2[:, wide]) * r.slope[:, wide].astype(F32)).astype(BF)
            r.gu[:, wide] = gu
            r.acc[...] += nn(gu, r.w1[wide, :])
            r.up_sum[:, wide] = jnp.sum(gu.astype(F32), 0, keepdims=True)
            return 0

        lax.fori_loop(0, 2, chunk, 0)
    for line in range(hidden // D):
        r.small[8 + line : 9 + line, :] = r.up_sum[:, line * D : line * D + D]
    gain, bias = vector(r.ln2_gain), vector(r.ln2_bias)

    def rows_body(rows):
        middle = r.tokens[rows, :].astype(F32) + r.attended[rows, :].astype(F32)
        _, xhat, inverse = norm(middle, gain, bias)
        grad = r.acc[rows, :]
        cf = r.cot[rows, :].astype(F32)
        gm = cf + norm_back(grad, xhat, inverse, gain)
        r.grad_middle[rows, :] = gm
        low = gm.astype(BF)
        r.gfield[rows, :] = low
        return low.astype(F32), grad * xhat, grad, cf

    for line, value in enumerate(by_rows(rows_body, 4)):
        r.small[4 + line : 5 + line, :] = column_sum(value)


def mlp_branch(r, hidden):
    r.acc[...] = jnp.zeros_like(r.acc)

    def chunk(j, _):
        wide = pl.ds(pl.multiple_of(j * 512, 512), 512)
        r.acc[...] += nt(r.act[:, wide], r.w2[:, wide])
        return 0

    lax.fori_loop(0, hidden // 512, chunk, 0)


def mlp_out(r):
    bias = vector(r.fc2_bias)

    def rows_body(rows):
        att = r.attended[rows, :].astype(F32)
        tok = r.tokens[rows, :].astype(F32)
        middle = tok + att
        br = r.acc[rows, :] + bias
        result = middle + br
        r.output[rows, :] = result.astype(BF)
        return tuple(v * v for v in (tok, middle, result, att, br))

    lane = lax.broadcasted_iota(jnp.int32, (1, D), 1)
    stats = jnp.zeros((1, D), F32)
    for n, v in enumerate(by_rows(rows_body, 5)):
        stats = jnp.where(lane == n, jnp.sum(column_sum(v), 1, keepdims=True), stats)
    r.small[12:13, :] = stats


UP_PIECES, DOWN_PIECES = 12, 6


def up_weights(r, hidden, sent):
    def up(j, _):
        n = hidden // UP_PIECES
        at = pl.multiple_of(j * n, n)
        r.g1[pl.ds(at, n), :] = tn(r.gu[:, pl.ds(at, n)], r.n2[...]).astype(BF)
        sent(j)
        return 0

    lax.fori_loop(0, UP_PIECES, up, 0)


def down_weights(r, sent):
    r.cot_t[...] = r.cot[...].T

    def down(j, _):
        n = D // DOWN_PIECES
        at = pl.multiple_of(j * n, n)
        r.g2[pl.ds(at, n), :] = nn(r.cot_t[pl.ds(at, n), :], r.act[...]).astype(BF)
        sent(j)
        return 0

    lax.fori_loop(0, DOWN_PIECES, down, 0)


def proj_weight_grad(r):
    def chunk(n, _):
        at = pl.multiple_of(n * 256, 256)
        r.gproj[pl.ds(at, 256), :] = tn(r.gfield[pl.ds(0, TOK), pl.ds(at, 256)], r.mixed_own[...]).astype(BF)
        return 0

    lax.fori_loop(0, D // 256, chunk, 0)


def prepare(r):
    r.table[...] = table_kernel_value(r.places[...], joint_table(r.rel_rows, r.rel_cols))
    r.mixed[...] = jnp.zeros_like(r.mixed)


def back_prepare(r, n_row, n_col):
    r.table[...] = table_kernel_value(r.places_back[...], joint_table(r.rel_rows, r.rel_cols))
    r.gtab[...] = jnp.zeros_like(r.gtab)
    r.dqkv[...] = jnp.zeros_like(r.dqkv)
    for w in range(4):
        cut_windows(r.gfield, r.gw, n_row, n_col, w)


def back_mix(r):
    def mix(n, _):
        at = pl.multiple_of(n * 256, 256)
        r.gmix[:, pl.ds(at, 256)] = nn(r.gw[...], r.wproj[:, pl.ds(at, 256)]).astype(BF)
        return 0

    lax.fori_loop(0, 3, mix, 0)


def back_windows(r, n_row, n_col, hooks):
    def body(a, w, i, pair, n):
        attend_back_pair(w, i, pair, n, r.qkv, r.gmix, (r.probs0, r.probs1)[a], r.table, r.marks_back, r.masks, r.dqkv, r.gtab)

    over_windows(body, hooks, n_row, n_col)


def back_weights(r, n_row, n_col, sent):
    for n in range(9):
        rows, lanes = pl.ds(n // 3 * 4 * SLOT, 4 * SLOT), pl.ds(n % 3 * 256, 256)
        r.gqkv[pl.ds(256 * n, 256), :] = tn(r.dqkv[rows, lanes], r.xw[...]).astype(BF)
        sent(n)
    ones = jnp.ones((16, 4 * SLOT), BF)
    r.mid[...] = jnp.zeros_like(r.mid)
    r.mid[16:17, :] = nn(ones, r.dqkv[pl.ds(0, 4 * SLOT), :])[0:1, :]
    r.mid[17:18, :] = nn(ones, r.dqkv[pl.ds(8 * SLOT, 4 * SLOT), :])[0:1, :]
    lane = lax.broadcasted_iota(jnp.int32, (128, 128), 1)
    left = jnp.where(lane < 64, r.gtab[0], 0.0)
    right = jnp.where(lane >= 64, r.gtab[1], 0.0)
    tab = lax.dot_general(
        r.places_back[...].astype(F32),
        jnp.concatenate([left, right], 0),
        (((0,), (0,)), ((), ())),
        precision=lax.Precision.HIGHEST,
        preferred_element_type=F32,
    )
    for t in range(4):
        r.mid[0:16, 128 * t : 128 * t + 128] = tab[16 * t : 16 * t + 16, :]


def back_return(r, n_row, n_col, between):
    _, row, col = grid_place()
    for n in range(3):
        value = 0
        for part in range(3):
            rows = pl.ds(4 * part * SLOT, 4 * SLOT)
            value = value + nn(r.dqkv[rows, :], r.wqkv[pl.ds(part * D, D), pl.ds(256 * n, 256)])
        r.gw[:, pl.ds(256 * n, 256)] = value.astype(BF)
        between(n)
    hot = one_hot(field_slots(row, col, n_row, n_col), 4 * SLOT)
    r.ret[...] = nn(hot, r.gw[...]).astype(BF)


def back_last(r, n_row, n_col):
    _, row, col = grid_place()
    hot = one_hot(home_index(row, col, n_row, n_col), FIELD)
    r.acc[...] = nn(hot, r.home2[...])
    gain, bias = vector(r.ln1_gain), vector(r.ln1_bias)

    def rows_body(rows):
        grad = r.acc[rows, :]
        _, xhat, inverse = norm(r.tokens[rows, :].astype(F32), gain, bias)
        r.input_grad[rows, :] = (r.grad_middle[rows, :] + norm_back(grad, xhat, inverse, gain)).astype(BF)
        return grad * xhat, grad

    r.late[...] = jnp.zeros_like(r.late)
    for line, value in enumerate(by_rows(rows_body, 2)):
        r.late[line : line + 1, :] = column_sum(value)


class Small:
    def __init__(self, value, come, send, recv, keep=None):
        self.dp, self.row, self.col = grid_place()
        self.value, self.come, self.send, self.recv, self.keep = value, come, send, recv, keep

    def copies(self, s):
        dp, row, col = self.dp, self.row, self.col
        plan = (
            [(dp, row, lax.rem(col + d, 4)) for d in (1, 2, 3)],
            [(dp, lax.rem(row + d, 4), col) for d in (1, 2, 3)],
            [(1 - dp, row, col)],
        )[s]
        return [
            pltpu.make_async_remote_copy(
                self.value, self.come.at[3 * s + i], self.send.at[3 * s + i], self.recv.at[3 * s + i],
                device_id=other, device_id_type=MESH,
            )
            for i, other in enumerate(plan)
        ]

    def start(self, s=0):
        for copy in self.copies(s):
            copy.start()

    def step(self, s):
        total = self.value[...]
        for i, copy in enumerate(self.copies(s)):
            copy.wait()
            value = self.come[3 * s + i]
            if s == 2 and self.keep is not None:
                line = lax.broadcasted_iota(jnp.int32, value.shape, 0)
                value = jnp.where(line == self.keep, 0.0, value)
            total = total + value
        self.value[...] = total
        if s < 2:
            self.start(s + 1)


GATHERS = ((0, 0, 1), (1, 0, 1), (2, 0, 1), *((3, part, PARTS) for part in range(PARTS)))


def block_body(n_row, n_col, shapes, hidden, r):
    dp, row, col = grid_place()
    rest = FIELD - TOK
    r.gfield, r.home2 = r.field, r.home
    for ref in (r.field, r.home):
        ref[pl.ds(TOK, rest), :] = jnp.zeros((rest, D), BF)
    greet(n_row, n_col)
    blocks = blocks_of(shapes)
    fulls, shards = (r.wqkv, r.wproj, r.w1, r.w2), (r.s0, r.s1, r.s2, r.s3)
    gathers = [
        Gather(fulls[i], shards[i], *blocks[i], r.gather_sem.at[0, n], r.gather_sem.at[1, n], part, parts)
        for n, (i, part, parts) in enumerate(GATHERS)
    ]
    qkv_way, proj_way, up_way, *down_ways = gathers
    qkv_way.start(LINE, OWN, OWN_CORE)
    gain, bias = vector(r.ln1_gain), vector(r.ln1_bias)

    def rows_body(rows):
        r.field[rows, :] = norm(r.tokens[rows, :].astype(F32), gain, bias)[0].astype(BF)
        return ()

    by_rows(rows_body, 0)
    size = (n_row, n_col)
    lend = Halo(r.field, r.picked, r.field, False, r.lend_sem.at[0], r.lend_sem.at[1], *size)
    give = Halo(r.ret, None, r.home, True, r.give_sem.at[0], r.give_sem.at[1], *size)
    lend2 = Halo(r.gfield, r.picked, r.gfield, False, r.lend_sem.at[2], r.lend_sem.at[3], *size)
    give2 = Halo(r.ret, None, r.home2, True, r.give_sem.at[2], r.give_sem.at[3], *size)
    pick_start(lend, r.pick)
    local = []
    for way in gathers[1:]:
        way.start(OWN, OWN_CORE)
    for i, way in enumerate(gathers):
        own = way.full.at[rows_at(way.block(0, way.col), way.b), way.lanes]
        mine = pltpu.make_async_copy(way.shard, own, r.local_sem.at[i])
        mine.start()
        local.append(mine)
    prepare(r)
    for mine in local:
        mine.wait()
    qkv_way.step(0)
    proj_way.start(LINE)
    up_way.start(LINE)
    lend.wait()
    for w in range(4):
        cut_windows(r.field, r.xw, n_row, n_col, w)
    qkv_way.step(1)
    for way in down_ways:
        way.start(LINE)
    qkv_way.step(2)
    qkv_way.whole()

    def between(part):
        if part == 0:
            proj_way.step(0)

    hooks = (
        (3, lambda: up_way.step(0)),
        (4, lambda: proj_way.step(1)),
        (8, lambda: down_ways[0].step(0)),
        (11, lambda: down_ways[1].step(0)),
        (14, lambda: up_way.step(1)),
        (16, lambda: proj_way.step(2)),
        (18, lambda: down_ways[2].step(0)),
        (20, lambda: down_ways[0].step(1)),
    )
    attend_part(r, n_row, n_col, hooks, between)
    give.start()
    r.home[pl.ds(0, TOK), :] = r.ret[pl.ds(0, TOK), :]
    proj_way.whole()
    up_way.step(2)
    down_ways[1].step(1)
    give.wait()

    qkv_sum, proj_sum, up_sum, down_sum = sums = [
        Reduce(g, g, dp * blocks[i][1], land, c, *blocks[i], pieces, parts, p, q)
        for i, (g, land, c, pieces, parts, p, q) in enumerate(
            [
                (r.gqkv, (r.g1, 0, True), r.c0, 9, PARTS, r.t0, r.u0),
                (r.gproj, (r.g1, shapes[0][0], True), r.c1, 1, 1, r.t1, r.u1),
                (r.g1, (r.w1, 0, False), r.c2, UP_PIECES, PARTS, r.t2, r.u2),
                (r.g2, (r.w2, 0, False), r.c3, DOWN_PIECES, PARTS, r.t3, r.u3),
            ]
        )
    ]

    def free(k):
        pl.semaphore_signal(r.free_sem.at[k], inc=1, device_id=(1 - dp, row, col), device_id_type=MESH)

    early = Small(r.small, r.small_come, r.small_sem.at[0], r.small_sem.at[1], 12)
    mid = Small(r.mid, r.mid_come, r.mid_sem.at[0], r.mid_sem.at[1])
    late = Small(r.late, r.late_come, r.late_sem.at[0], r.late_sem.at[1])

    def middle(act, slope, gu, cot_t):
        m = types.SimpleNamespace(**r.__dict__, act=act, slope=slope, gu=gu, cot_t=cot_t)

        def arrived():
            down_ways[2].step(1)
            up_way.whole()

        hooks = (
            (2, lambda: down_ways[0].step(2)),
            (6, lambda: down_ways[1].step(2)),
            (11, lambda: down_ways[2].step(2)),
        )
        mlp_first(m, n_row, n_col, hidden, arrived, hooks)
        mlp_second(m, hidden, lambda part: down_ways[part].whole())
        for way in gathers:
            way.finish()
        free(0)
        pick_start(lend2, r.pick)
        pl.semaphore_wait(r.free_sem.at[0], 1)
        up_weights(m, hidden, lambda j: up_sum.start(0, j))
        up_sum.step(0)
        up_sum.gone()
        mlp_branch(m, hidden)
        free(1)
        pl.semaphore_wait(r.free_sem.at[1], 1)
        down_weights(m, lambda j: down_sum.start(0, j))
        mlp_out(m)
        early.start()
        down_sum.step(0)

    v = pltpu.VMEM
    wide = (TOK, hidden)
    pl.run_scoped(middle, v(wide, BF), v(wide, BF), v(wide, BF), v((D, TOK), BF))
    proj_weight_grad(r)
    proj_sum.start(0)
    lend2.wait()

    def all_parts(way, k):
        for part in range(way.parts):
            way.step(k, part)

    def ends(gw):
        e = types.SimpleNamespace(**r.__dict__, gw=gw, gmix=r.mixed, dqkv=r.w1)
        all_parts(up_sum, 1)
        back_prepare(e, n_row, n_col)
        proj_sum.step(0)
        back_mix(e)
        early.step(0)
        hooks = (
            (2, lambda: all_parts(down_sum, 1)),
            (9, lambda: all_parts(up_sum, 2)),
            (10, lambda: proj_sum.step(1)),
            (20, lambda: all_parts(down_sum, 2)),
        )
        back_windows(e, n_row, n_col, hooks)
        back_return(e, n_row, n_col, lambda n: None)
        give2.start()
        r.home2[pl.ds(0, TOK), :] = r.ret[pl.ds(0, TOK), :]
        early.step(1)
        back_weights(e, n_row, n_col, lambda n: qkv_sum.start(0, n))
        mid.start()
        proj_sum.step(2)
        give2.wait()
        back_last(e, n_row, n_col)
        late.start()
        qkv_sum.step(0)
        early.step(2)
        mid.step(0)
        late.step(0)
        for part in range(PARTS):
            up_sum.result(r.o2, part)
        qkv_sum.step(1, 0)
        qkv_sum.step(1, 1)
        mid.step(1)
        late.step(1)
        qkv_sum.step(1, 2)
        for part in range(PARTS):
            down_sum.result(r.o3, part)
        proj_sum.result(r.o1)
        qkv_sum.step(2, 0)
        mid.step(2)
        late.step(2)
        qkv_sum.step(2, 1)
        qkv_sum.step(2, 2)
        for part in range(PARTS):
            qkv_sum.result(r.o0, part)
        for way in (qkv_sum, proj_sum, down_sum):
            way.gone()
        for way in sums:
            way.finish()

    pl.run_scoped(ends, v((4 * SLOT, D), BF))


def split_ins(tensors, *names):
    return {k: (tensors[k], vmem()) for k in names}


def as_out(buffer):
    return (jax.ShapeDtypeStruct(buffer.shape, buffer.dtype), vmem())


def window_buffers(n_row):
    v = pltpu.VMEM
    late = 16 * (TILE * n_row - WIN * n_row)
    return dict(
        xw=v((4 * SLOT, D), BF),
        qkv=v((4 * SLOT, 3 * D), BF),
        probs0=v((2 * HEADS, 16 * WIN, SLOT), BF),
        probs1=v((2 * HEADS, late, SLOT), BF),
        mixed=v((4 * SLOT, D), BF),
        table=v((256, 128), BF),
        ret=v((FIELD, D), BF),
    )


def mlp_buffers(hidden):
    v = pltpu.VMEM
    return dict(
        mixed_own=v((TOK, D), BF),
        attended=v((TOK, D), BF),
        n2=v((TOK, D), BF),
        acc=v((TOK, D), F32),
        up_bias=v((hidden // D, D), F32),
        up_sum=v((1, hidden), F32),
        grad_middle=v((TOK, D), F32),
    )


def block_call(n_row, n_col, shapes, tensors, shards):
    hidden = shapes[2][0]
    sd, v = jax.ShapeDtypeStruct, pltpu.VMEM
    blocks = blocks_of(shapes)
    ins = {k: (t, vmem()) for k, t in tensors.items()}
    ins |= {"s" + str(i): (w, vmem()) for i, w in enumerate(shards)}
    outs = dict(
        output=(sd((TOK, D), BF), vmem()),
        input_grad=(sd((TOK, D), BF), vmem()),
        small=(sd((16, D), F32), vmem()),
        mid=(sd((24, D), F32), vmem()),
        late=(sd((8, D), F32), vmem()),
    )
    outs |= {"o" + str(i): (sd(b, F32), vmem()) for i, b in enumerate(blocks)}
    wqkv, wproj, w1, w2 = [v(s, BF) for s in shapes]
    come = [v((15 * b, h), BF) for b, h in blocks]
    field = v((FIELD, D), BF)
    scratch = dict(
        **window_buffers(n_row),
        **mlp_buffers(hidden),
        wqkv=wqkv,
        wproj=wproj,
        w1=w1,
        w2=w2,
        gqkv=wqkv,
        gproj=wproj,
        g1=w1,
        g2=w2,
        c0=come[0],
        c1=come[1],
        c2=come[2],
        c3=come[3],
        field=field,
        home=field,
        picked=v((PICKED, D), BF),
        gtab=v((2, 128, 128), F32),
        small_come=v((7, 16, D), F32),
        mid_come=v((7, 24, D), F32),
        late_come=v((7, 8, D), F32),
        local_sem=dma(len(GATHERS)),
        gather_sem=dma(2, len(GATHERS), Gather.SEMS),
        lend_sem=dma(4, 3),
        give_sem=dma(4, 3),
        small_sem=dma(2, 7),
        mid_sem=dma(2, 7),
        late_sem=dma(2, 7),
        free_sem=pltpu.SemaphoreType.REGULAR((2,)),
    )
    for i in range(4):
        scratch |= {"t" + str(i): dma(Reduce.SEMS), "u" + str(i): dma(Reduce.SEMS)}
    return named_call(
        functools.partial(block_body, n_row, n_col, shapes, hidden), ins, outs, scratch, "block",
        vmem_limit_bytes=63 * MIB, collective_id=0, has_side_effects=True,
    )


def plain_block(n_row, n_col, shapes, tensors, weights, field):
    hidden = shapes[2][0]
    sd, v = jax.ShapeDtypeStruct, pltpu.VMEM
    wqkv, wproj, w1, w2 = [(w, vmem()) for w in weights]
    limit = dict(vmem_limit_bytes=60 * MIB)

    def given(value, *names):
        return {k: (getattr(value, k), vmem()) for k in names}

    names = ("query_bias", "value_bias", "rel_rows", "rel_cols", "masks", "places", "marks")
    windows = window_buffers(n_row)
    outs = {k: as_out(windows.pop(k)) for k in ("qkv", "xw", "probs0", "probs1", "ret")}

    def attend_body(r):
        prepare(r)
        for w in range(4):
            cut_windows(r.field, r.xw, n_row, n_col, w)
        attend_part(r, n_row, n_col, (), lambda part: None)

    ins = split_ins(tensors, *names) | dict(field=(field, vmem()), wqkv=wqkv)
    one = named_call(attend_body, ins, outs, windows, "attend", **limit)
    home = (return_xla(one.ret, n_row, n_col), vmem())
    names = ("tokens", "cot", "proj_bias", "ln2_gain", "ln2_bias", "fc1_bias", "fc2_bias")
    buffers = mlp_buffers(hidden)
    outs = dict(grad_middle=as_out(buffers.pop("grad_middle")), gfield=(sd((FIELD, D), BF), vmem()))
    outs |= {k: (sd(s, BF), vmem()) for k, s in zip(("gproj", "g1", "g2"), shapes[1:])}
    outs |= dict(output=(sd((TOK, D), BF), vmem()), small=(sd((16, D), F32), vmem()))
    wide = (TOK, hidden)
    buffers |= dict(act=v(wide, BF), slope=v(wide, BF), gu=v(wide, BF), cot_t=v((D, TOK), BF))

    def mlp_body(r):
        r.gfield[...] = jnp.zeros_like(r.gfield)
        mlp_first(r, n_row, n_col, hidden, lambda: None, ())
        mlp_second(r, hidden, lambda part: None)
        up_weights(r, hidden, lambda j: None)
        mlp_branch(r, hidden)
        down_weights(r, lambda j: None)
        mlp_out(r)
        proj_weight_grad(r)

    ins = split_ins(tensors, *names) | dict(home=home, wproj=wproj, w1=w1, w2=w2)
    two = named_call(mlp_body, ins, outs, buffers, "mlp", **limit)
    gfield = (lend_xla(two.gfield[:TOK], n_row, n_col), vmem())
    ins = split_ins(tensors, "rel_rows", "rel_cols", "masks", "places_back", "marks_back")
    ins |= given(one, "qkv", "xw", "probs0", "probs1") | dict(wqkv=wqkv, wproj=wproj, gfield=gfield)
    outs = dict(
        gqkv=(sd(shapes[0], BF), vmem()),
        ret=(sd((FIELD, D), BF), vmem()),
        mid=(sd((24, D), F32), vmem()),
    )
    rows = v((4 * SLOT, D), BF)
    scratch = dict(gw=rows, gmix=rows, dqkv=v((12 * SLOT, D), BF))
    scratch |= dict(table=v((256, 128), BF), gtab=v((2, 128, 128), F32))

    def windows_body(r):
        back_prepare(r, n_row, n_col)
        back_mix(r)
        back_windows(r, n_row, n_col, ())
        back_weights(r, n_row, n_col, lambda n: None)
        back_return(r, n_row, n_col, lambda w: None)

    three = named_call(windows_body, ins, outs, scratch, "windows", **limit)
    home = (return_xla(three.ret, n_row, n_col), vmem())
    ins = split_ins(tensors, "tokens", "ln1_gain", "ln1_bias") | dict(home2=home) | given(two, "grad_middle")
    outs = dict(input_grad=(sd((TOK, D), BF), vmem()), late=(sd((8, D), F32), vmem()))
    four = named_call(lambda r: back_last(r, n_row, n_col), ins, outs, dict(acc=v((TOK, D), F32)), "ends", **limit)
    grads = []
    for g in (three.gqkv, two.gproj, two.g1, two.g2):
        g = lax.psum_scatter(g, AXES, scatter_dimension=0, tiled=True)
        grads.append(lax.psum_scatter(g, "dp", scatter_dimension=1, tiled=True))
    line = jnp.arange(16)[:, None] == 12
    local = lax.psum(two.small, AXES)
    small = jnp.where(line, local, lax.psum(jnp.where(line, 0.0, local), "dp"))
    mid, late = (lax.psum(v, ("dp", *AXES)) for v in (three.mid, four.late))
    return grads, two.output, four.input_grad, small, mid, late


def last_body(count, r):
    for i in range(4):
        r.__dict__["t" + str(i)][...] = r.__dict__["s" + str(i)][...].astype(F32)
    r.output_out[...] = r.output[...]
    r.input_grad_out[...] = r.input_grad[...]
    lines = ((r.late, 0), (r.late, 1), (r.mid, 16), (r.mid, 17), (r.small, 4), (r.small, 5), (r.small, 6), (r.small, 7))
    for i, (ref, line) in enumerate(lines):
        r.__dict__["v" + str(i)][...] = ref[line : line + 1, :].reshape(D)
    r.up[...] = jnp.concatenate([r.small[8 + i : 9 + i, :] for i in range(r.up.shape[0] // D)], 1).reshape(-1)
    tables = jnp.concatenate([r.mid[0:16, 128 * t : 128 * t + 128] for t in range(4)], 0)
    tables = tables[:, :HEAD] + pltpu.roll(tables, HEAD, 1)[:, :HEAD]
    r.rows[...] = tables[0 : 2 * WIN - 1, :]
    r.cols[...] = tables[32 : 32 + 2 * WIN - 1, :]
    r.stats[...] = jnp.sqrt(r.small[12:13, :5] / count)


def last_call(count, hidden, sums, output, input_grad, small, mid, late):
    sd = jax.ShapeDtypeStruct
    ins = {"s" + str(i): (s, vmem()) for i, s in enumerate(sums)}
    ins |= dict(output=(output, vmem()), input_grad=(input_grad, vmem()), small=(small, vmem()))
    ins |= dict(mid=(mid, vmem()), late=(late, vmem()))
    outs = {"t" + str(i): (sd(s.shape, F32), vmem()) for i, s in enumerate(sums)}
    outs |= dict(output_out=(sd((TOK, D), BF), vmem()), input_grad_out=(sd((TOK, D), BF), vmem()))
    outs |= {"v" + str(i): (sd((D,), F32), vmem()) for i in range(8)}
    outs |= dict(
        up=(sd((hidden,), F32), vmem()),
        rows=(sd((2 * WIN - 1, HEAD), F32), vmem()),
        cols=(sd((2 * WIN - 1, HEAD), F32), vmem()),
        stats=(sd((1, 5), F32), vmem()),
    )
    return named_call(functools.partial(last_body, count), ins, outs, {}, "last", vmem_limit_bytes=63 * MIB)


def on_device(
    n_dp, n_row, n_col,
    tokens, ln1_gain, ln1_bias, qkv_weight, query_bias, value_bias, rel_rows, rel_cols,
    proj_weight, proj_bias, ln2_gain, ln2_bias, fc1_weight, fc1_bias, fc2_weight, fc2_bias, cotangent,
):
    direct = (n_dp, n_row, n_col) == (2, 4, 4)
    tok = tokens.reshape(TOK, D)
    mask_values = np.zeros((16, 128), np.float32)
    mask_values[0, :64] = 1.0
    mask_values[1, 64:] = 1.0
    shared = dict(
        tokens=tok,
        cot=cotangent.reshape(TOK, D),
        ln1_gain=ln1_gain,
        ln1_bias=ln1_bias,
        rel_rows=rel_rows,
        rel_cols=rel_cols,
        masks=jnp.asarray(mask_values, BF),
    )
    tensors = shared | dict(
        query_bias=query_bias,
        value_bias=value_bias,
        proj_bias=proj_bias,
        ln2_gain=ln2_gain,
        ln2_bias=ln2_bias,
        fc1_bias=fc1_bias,
        fc2_bias=fc2_bias,
        places=jnp.asarray(table_places(False), BF),
        marks=jnp.asarray(key_marks(False), BF),
        places_back=jnp.asarray(table_places(True), BF),
        marks_back=jnp.asarray(key_marks(True), BF),
    )
    shards = (qkv_weight, proj_weight, fc1_weight, fc2_weight)
    shapes = [(s.shape[1] * n_row * n_col, s.shape[0] * n_dp) for s in shards]
    if direct:
        tensors |= dict(pick=jnp.asarray(pick_rows(), BF))
        done = block_call(n_row, n_col, shapes, tensors, [s.T for s in shards])
        sums = (done.o0, done.o1, done.o2, done.o3)
        rest = (done.output, done.input_grad, done.small, done.mid, done.late)
    else:
        weights = []
        for s in shards:
            s = lax.all_gather(s, AXES, axis=1, tiled=True)
            weights.append(lax.all_gather(s, "dp", axis=0, tiled=True).T)
        normed = norm(tok.astype(F32), ln1_gain.astype(F32), ln1_bias.astype(F32))[0].astype(BF)
        field = lend_xla(normed, n_row, n_col)
        sums, *rest = plain_block(n_row, n_col, shapes, tensors, weights, field)
    out = last_call(TOK * n_row * n_col * D, shapes[2][0], sums, *rest)
    return (
        out.output_out.reshape(tokens.shape),
        out.input_grad_out.reshape(tokens.shape),
        out.v0,
        out.v1,
        out.t0.T,
        out.v2,
        out.v3,
        out.rows,
        out.cols,
        out.t1.T,
        out.v4,
        out.v5,
        out.v6,
        out.t2.T,
        out.up,
        out.t3.T,
        out.v7,
        out.stats,
    )


def solution(mesh):
    tile = P("dp", "row", "col", None)
    weight = P("dp", AXES)
    sizes = [mesh.shape[a] for a in ("dp", "row", "col")]
    ins = [tile] + [P()] * 16
    for i in (3, 8, 12, 14):
        ins[i] = weight
    ins[16] = tile
    outs = [tile, tile] + [P()] * 16
    for i in (4, 9, 13, 15):
        outs[i] = weight
    outs[17] = P("dp", None)
    return jax.shard_map(
        functools.partial(on_device, *sizes),
        mesh=mesh,
        in_specs=tuple(ins),
        out_specs=tuple(outs),
        check_vma=False,
    )
```

```python
import functools
import types

import jax
import jax.numpy as jnp
import numpy as np
from jax import lax
from jax.experimental import pallas as pl
from jax.experimental.pallas import tpu as pltpu
from jax.sharding import PartitionSpec as P

HEADS = 12
HEAD = 64
WIN = 14
EPS = 1e-06
MESH = pl.DeviceIdType.MESH
AXES = ("row", "col")
F32 = jnp.float32
BF = jnp.bfloat16

D = HEADS * HEAD
TILE = 16
TOK = TILE * TILE
LO = 6
SLOT = 256
PAIRS = HEADS // 2
FIELD = 496
PICKED = 144
MIB = 2**20

LINKS = {
    (1, 0): (True, 160, 96, 256),
    (0, 1): (False, 0, 96, 352),
    (1, 1): (False, 96, 48, 448),
}


def nt(a, b):
    return lax.dot_general(a, b, (((1,), (1,)), ((), ())), preferred_element_type=F32)


def nn(a, b):
    return lax.dot_general(a, b, (((1,), (0,)), ((), ())), preferred_element_type=F32)


def tn(a, b):
    return lax.dot_general(a, b, (((0,), (0,)), ((), ())), preferred_element_type=F32)


def pick_rows():
    table = np.zeros((PICKED, TOK), np.float32)
    for base, first in ((0, 0), (96, TILE - LO)):
        for i in range((TILE - first) * LO):
            y, x = divmod(i, LO)
            table[base + i, (first + y) * TILE + TILE - LO + x] = 1.0
    return table


def table_places(back):
    place = np.zeros((256, 64), np.float32)
    for head in range(2):
        for r in range(2 * WIN - 1):
            for copy in range(2):
                row_lane = (64 + 28 * copy + r + 64 * head) % 128
                col_lane = (28 * copy + r + 64 * head) % 128
                place[128 * head + row_lane, 26 - r] = 1.0
                place[128 * head + col_lane, 32 + (r if back else 26 - r)] = 1.0
    return place


def key_marks(back):
    marks = np.zeros((2, SLOT, 128), np.float32)
    for head in range(2):
        for j in range(SLOT):
            k, l = divmod(j, 16)
            if k < WIN and l < WIN:
                for copy in range(2):
                    marks[head, j, (64 + 28 * copy + k + 64 * head) % 128] = 1.0
                    marks[head, j, (78 + 28 * copy + (13 - l if back else l) + 64 * head) % 128] = 1.0
            else:
                marks[head, j, (120 + 64 * head) % 128] = -1e30
    return marks


def lane_kinds(rows):
    lane = lax.broadcasted_iota(jnp.int32, (rows, 128), 1)
    kinds = []
    for head in range(2):
        at = (lane + 64 * head) % 128 if head else lane
        own = at < 64
        first = (at >= 64) & (at < 92)
        second = (at >= 92) & (at < 120)
        is_row = ((at >= 64) & (at < 78)) | ((at >= 92) & (at < 106))
        kinds.append((own, first, second, is_row, at == 120))
    return kinds


def window_index(w, row, col, n_row, n_col):
    place = lax.broadcasted_iota(jnp.int32, (SLOT, 1), 0)
    y = place // 16
    x = place - 16 * y
    a, b = w // 2, w % 2
    ry = WIN * (row + a) + y - TILE * row
    rx = WIN * (col + b) + x - TILE * col
    good = (y < WIN) & (x < WIN) & (ry < TILE) & (rx < TILE)
    if a:
        good = good & (row == n_row - 1)
    if b:
        good = good & (col == n_col - 1)
    up, left = ry < 0, rx < 0
    base = jnp.where(up, jnp.where(left, 448, 256), jnp.where(left, 352, 0))
    width = jnp.where(left, LO, TILE)
    index = base + jnp.where(up, ry + LO, ry) * width + jnp.where(left, rx + LO, rx)
    return jnp.where(good, index, -1)


def field_slots(row, col, n_row, n_col):
    at = lax.broadcasted_iota(jnp.int32, (FIELD, 1), 0)
    above = (at >= 256) & (at < 352)
    left = (at >= 352) & (at < 448)
    corner = at >= 448
    narrow = left | corner
    rest = jnp.where(corner, at - 448, jnp.where(left, at - 352, jnp.where(above, at - 256, at)))
    sixth = sum((rest >= LO * k).astype(jnp.int32) for k in range(1, TILE))
    ty = jnp.where(narrow, sixth, rest // TILE)
    tx = rest - ty * jnp.where(narrow, LO, TILE)
    ty = jnp.where(above | corner, ty - LO, ty)
    tx = jnp.where(narrow, tx - LO, tx)
    good = at < 484
    where = 0
    for t, place, n, stride, unit in ((ty, row, n_row, 2, 16), (tx, col, n_col, 1, 1)):
        y = TILE * place + t - WIN * place
        late = y >= WIN
        good = good & (y >= 0) & (jnp.logical_not(late) | (place == n - 1))
        where = where + jnp.where(late, stride * SLOT + unit * (y - WIN), unit * y)
    return jnp.where(good, where, -1)


def home_index(row, col, n_row, n_col):
    place = lax.broadcasted_iota(jnp.int32, (TOK, 1), 0)
    ty = place // TILE
    tx = place - TILE * ty
    down = (TILE * row + ty - WIN * row >= WIN) & (row < n_row - 1)
    right = (TILE * col + tx - WIN * col >= WIN) & (col < n_col - 1)
    near = TILE - LO
    return jnp.where(
        down,
        jnp.where(right, 448 + (ty - near) * LO + tx - near, 256 + (ty - near) * TILE + tx),
        jnp.where(right, 352 + ty * LO + tx - near, place),
    )


def one_hot(index, size):
    lane = lax.broadcasted_iota(jnp.int32, (index.shape[0], size), 1)
    return jnp.where(lane == index, 1.0, 0.0).astype(BF)


STEP = 64


def by_rows(body, sums):
    def step(i, kept):
        parts = body(pl.ds(pl.multiple_of(i * STEP, STEP), STEP))
        return tuple(k + sum(p[8 * q : 8 * q + 8] for q in range(STEP // 8)) for k, p in zip(kept, parts))

    return lax.fori_loop(0, TOK // STEP, step, (jnp.zeros((8, D), F32),) * sums)


def column_sum(v):
    return jnp.sum(v, 0, keepdims=True)


def norm(v, gain, bias):
    mean = jnp.mean(v, -1, keepdims=True)
    center = v - mean
    inverse = lax.rsqrt(jnp.mean(center * center, -1, keepdims=True) + EPS)
    xhat = center * inverse
    return xhat * gain + bias, xhat, inverse


def norm_back(grad, xhat, inverse, gain):
    d = grad * gain
    return inverse * (
        d - jnp.mean(d, -1, keepdims=True) - xhat * jnp.mean(d * xhat, -1, keepdims=True)
    )


def grid_place():
    return lax.axis_index("dp"), lax.axis_index("row"), lax.axis_index("col")


def exists(step, row, col, n_row, n_col):
    r, c = row + step[0], col + step[1]
    return (r >= 0) & (r < n_row) & (c >= 0) & (c < n_col)


CORNERS = ((1, 1), (-1, -1))


def greet(n_row, n_col):
    dp, row, col = grid_place()
    barrier = pltpu.get_barrier_semaphore()
    others = [(dp, row, lax.rem(col + d, n_col)) for d in (1, 2, 3)]
    others += [(dp, lax.rem(row + d, n_row), col) for d in (1, 2, 3)]
    others.append((1 - dp, row, col))
    for other in others:
        pl.semaphore_signal(barrier, inc=1, device_id=other, device_id_type=MESH)
    count = len(others)
    for step in CORNERS:
        there = exists(step, row, col, n_row, n_col)

        @pl.when(there)
        def _():
            pl.semaphore_signal(
                barrier, inc=1, device_id=(dp, row + step[0], col + step[1]), device_id_type=MESH
            )

        count = count + jnp.where(there, 1, 0)
    pl.semaphore_wait(barrier, count)


class Halo:
    def __init__(self, source, picked, land, back, send, recv, n_row, n_col):
        self.source, self.picked, self.land, self.back = source, picked, land, back
        self.send, self.recv, self.size = send, recv, (n_row, n_col)

    def copies(self):
        dp, row, col = grid_place()
        sign = -1 if self.back else 1
        for i, ((dr, dc), (own, first, rows, there)) in enumerate(LINKS.items()):
            if self.back:
                src = self.source.at[pl.ds(there, rows)]
            else:
                src = (self.source if own else self.picked).at[pl.ds(first, rows)]
            copy = pltpu.make_async_remote_copy(
                src,
                self.land.at[pl.ds(there, rows)],
                self.send.at[i],
                self.recv.at[i],
                device_id=(dp, row + sign * dr, col + sign * dc),
                device_id_type=MESH,
            )
            goes = exists((sign * dr, sign * dc), row, col, *self.size)
            comes = exists((-sign * dr, -sign * dc), row, col, *self.size)
            yield copy, goes, comes

    def start(self):
        for copy, goes, _ in self.copies():
            pl.when(goes)(copy.start)

    def arrive(self):
        for copy, _, comes in self.copies():
            pl.when(comes)(copy.wait_recv)

    def gone(self):
        for copy, goes, _ in self.copies():
            pl.when(goes)(copy.wait_send)

    def wait(self):
        self.arrive()
        self.gone()


def pick_start(halo, pick):
    halo.picked[...] = nn(pick[...], halo.source[pl.ds(0, TOK), :]).astype(BF)
    halo.start()


def halo_xla(blocks, back, n_row, n_col):
    sign = -1 if back else 1
    pieces = [blocks[0]]
    for (dr, dc), block in zip(LINKS, blocks[1:]):
        dr, dc = sign * dr, sign * dc
        pairs = [
            (r * n_col + c, (r + dr) * n_col + c + dc)
            for r in range(n_row)
            for c in range(n_col)
            if 0 <= r + dr < n_row and 0 <= c + dc < n_col
        ]
        pieces.append(lax.ppermute(block, AXES, pairs))
    return jnp.concatenate(pieces, 0)


def lend_xla(own, n_row, n_col):
    grid = own.reshape(TILE, TILE, -1)
    corner = grid[TILE - LO :, TILE - LO :].reshape(LO * LO, -1)
    blocks = [
        own,
        own[TILE * (TILE - LO) :],
        grid[:, TILE - LO :].reshape(TILE * LO, -1),
        jnp.pad(corner, ((0, 48 - LO * LO), (0, 0))),
    ]
    return halo_xla(blocks, False, n_row, n_col)


def return_xla(field, n_row, n_col):
    return halo_xla([field[:256], field[256:352], field[352:448], field[448:]], True, n_row, n_col)


def blocks_of(shapes):
    return [(n // 16, k // 2) for n, k in shapes]


def rows_at(first, count):
    return pl.ds(pl.multiple_of(first, 16), count)


LINE, OWN, OWN_CORE, LINE_CORE, FAR, NEAR_CORE, FAR_CORE, CORE = range(10, 18)


class Gather:
    SEMS = 20

    def __init__(self, full, shard, block, half, send, recv, part=0, parts=1):
        self.dp, self.row, self.col = grid_place()
        width = half // parts
        self.full, self.shard, self.b = full, shard.at[:, pl.ds(part * width, width)], block
        self.send, self.recv = send, recv
        self.lanes = pl.ds(pl.multiple_of(self.dp * half + part * width, 128), width)
        self.other = pl.ds(pl.multiple_of((1 - self.dp) * half + part * width, 128), width)

    def block(self, flip, place):
        return (jnp.bitwise_xor(self.row, flip) * 4 + place) * self.b

    def came(self, d):
        return lax.rem(self.col + 4 - d, 4)

    def copy(self, i, first, count, land, target, shard=False):
        core = target == CORE
        if core:
            device = (1 - self.dp, self.row, self.col)
        elif isinstance(target, tuple):
            device = (self.dp, self.row, lax.rem(self.col + target[0], 4))
        else:
            device = (self.dp, jnp.bitwise_xor(self.row, target), self.col)

        def make(src, dst):
            return pltpu.make_async_remote_copy(
                src, dst, self.send.at[i], self.recv.at[i], device_id=device, device_id_type=MESH
            )

        def out():
            there = self.full.at[rows_at(first, count), self.lanes]
            return make(self.shard if shard else there, there)

        def come():
            here = self.full.at[rows_at(land, count), self.other if core else self.lanes]
            return make(here, here)

        return out, come

    def copies(self, k):
        b = self.b
        own = self.block(0, self.col)
        if k == LINE:
            return [
                self.copy(d - 1, own, b, self.block(0, self.came(d)), (d,), True) for d in (1, 2, 3)
            ]
        if k == OWN:
            return [self.copy(2 + f, own, b, self.block(f, self.col), f, True) for f in (1, 2)]
        if k == OWN_CORE:
            return [self.copy(5, own, b, own, CORE, True)]
        if k < LINE:
            at = self.came(k)
            return [
                self.copy(4 + 2 * k, self.block(0, at), b, self.block(1, at), 1),
                self.copy(5 + 2 * k, self.block(0, at), b, self.block(2, at), 2),
            ]
        if k == LINE_CORE:
            return [
                self.copy(11 + d, self.block(0, self.came(d)), b, self.block(0, self.came(d)), CORE)
                for d in (1, 2, 3)
            ]
        if k == FAR:
            return [
                self.copy(15, self.block(2, 0), 2 * b, self.block(3, 0), 1),
                self.copy(16, self.block(1, 2), 2 * b, self.block(3, 2), 2),
            ]
        if k == NEAR_CORE:
            return [self.copy(16 + f, self.block(f, 0), 4 * b, self.block(f, 0), CORE) for f in (1, 2)]
        return [self.copy(19, self.block(3, 0), 4 * b, self.block(3, 0), CORE)]

    def start(self, *kinds):
        for k in kinds:
            for out, _ in self.copies(k):
                out().start()

    def arrive(self, *kinds):
        for k in kinds:
            for _, come in self.copies(k):
                come().wait_recv()

    def step(self, n):
        if n == 0:
            for d in (1, 2, 3):
                self.copies(LINE)[d - 1][1]().wait_recv()
                self.start(d)
            self.start(LINE_CORE)
        elif n == 1:
            self.arrive(OWN, 1, 2, 3)
            self.start(FAR, NEAR_CORE)
        else:
            self.arrive(FAR)
            self.start(FAR_CORE)

    def whole(self):
        self.arrive(OWN_CORE, LINE_CORE, NEAR_CORE, FAR_CORE)

    def finish(self):
        for k in (LINE, OWN, OWN_CORE, 1, 2, 3, LINE_CORE, FAR, NEAR_CORE, FAR_CORE):
            for out, _ in self.copies(k):
                out().wait_send()


class Reduce:
    SEMS = 34

    def __init__(self, grad, total, base, land, come, block, half, pieces, parts, send, recv):
        self.dp, self.row, self.col = grid_place()
        self.grad, self.total, self.base, self.come = grad, total, base, come
        self.land, self.land_row, mirrored = land
        self.land_there = self.dp * half if mirrored else 0
        self.land_here = (1 - self.dp) * half if mirrored else 0
        self.b, self.h, self.send, self.recv = block, half, send, recv
        self.pieces, self.parts, self.width = pieces, parts, half // parts
        self.other = pl.ds(pl.multiple_of((1 - self.dp) * half, 128), half)

    def side(self, base, part, width):
        return pl.ds(pl.multiple_of(base + part * width, 128), width)

    def at(self, flip, place=0):
        return (jnp.bitwise_xor(self.row, flip) * 4 + place) * self.b

    def lanes(self, part):
        return pl.ds(pl.multiple_of(self.base + part * self.width, 128), self.width)

    def came(self, first, count, part):
        return self.come.at[rows_at(first, count), pl.ds(part * self.width, self.width)]

    def tot(self, first, count, part):
        return self.total.at[rows_at(first, count), self.lanes(part)]

    def sem(self, k, part):
        if k == 0:
            return part
        return self.pieces + 7 * part + {1: 0, 2: 2, 3: 4}[k]

    def copies(self, k, part):
        b = self.b
        if k == 0:
            n = 16 * b // self.pieces
            there = self.land.at[rows_at(self.land_row + part * n, n), self.side(self.land_there, 0, self.h)]
            plan = [(self.grad.at[rows_at(part * n, n), self.other], there, (1 - self.dp, self.row, self.col))]
        elif k == 1:
            plan = [
                (
                    self.tot(self.at(3, 2 * half), 2 * b, part),
                    self.came(2 * half * b, 2 * b, part),
                    (self.dp, jnp.bitwise_xor(self.row, 1 + half), self.col),
                )
                for half in (0, 1)
            ]
        elif k == 2:
            plan = [
                (
                    self.tot(self.at(flip), 4 * b, part),
                    self.came(4 * flip * b, 4 * b, part),
                    (self.dp, jnp.bitwise_xor(self.row, flip), self.col),
                )
                for flip in (1, 2)
            ]
        else:
            plan = []
            for d in (1, 2, 3):
                to = lax.rem(self.col + d, 4)
                plan.append(
                    (
                        self.tot(self.at(0, to), b, part),
                        self.came((11 + d) * b, b, part),
                        (self.dp, self.row, to),
                    )
                )
        base = self.sem(k, part)
        return [
            pltpu.make_async_remote_copy(
                src, dst, self.send.at[base + i], self.recv.at[base + i], device_id=dev, device_id_type=MESH
            )
            for i, (src, dst, dev) in enumerate(plan)
        ]

    def start(self, k, part=0):
        for copy in self.copies(k, part):
            copy.start()

    def arrive(self, k, part=0):
        for copy in self.copies(k, part):
            copy.wait_recv()

    def sum_rows(self, first, count, froms, part, source=None, base=0):
        most = (256 if len(froms) == 1 else 96) * 384
        step = next(n for n in range(count, 0, -16) if count % n == 0 and n * self.width <= most)
        lanes = self.lanes(part)
        side = self.side(base, part, self.width)
        source = self.come if source is None else source

        def body(i, _):
            at = rows_at(first + i * step, step)
            value = self.total[at, lanes]
            if len(froms) == 1:
                value = value + source[rows_at(froms[0] + i * step, step), side]
            else:
                value = value.astype(F32)
                for f in froms:
                    value = value + source[rows_at(f + i * step, step), side].astype(F32)
                value = value.astype(BF)
            self.total[at, lanes] = value
            return 0

        lax.fori_loop(0, count // step, body, 0)

    def add_piece(self, piece):
        n = 16 * self.b // self.pieces
        self.arrive(0, piece)
        for part in range(self.parts):
            self.sum_rows(piece * n, n, (self.land_row + piece * n,), part, self.land, self.land_here)

    def step(self, k, part=0):
        b = self.b
        if k == 0:
            for piece in range(self.pieces):
                self.add_piece(piece)
            for part in range(1, self.parts):
                self.start(1, part)
            part = 0
        else:
            self.arrive(k, part)
            if k == 1:
                self.sum_rows(self.at(2), 2 * b, (0,), part)
                self.sum_rows(self.at(1, 2), 2 * b, (2 * b,), part)
            else:
                self.sum_rows(self.at(0), 4 * b, (4 * b, 8 * b), part)
        self.start(k + 1, part)

    def result(self, out, part=0):
        b = self.b
        self.arrive(3, part)
        value = self.total[rows_at(self.at(0, self.col), b), self.lanes(part)].astype(F32)
        side = pl.ds(part * self.width, self.width)
        for d in (1, 2, 3):
            value = value + self.come[pl.ds((11 + d) * b, b), side].astype(F32)
        out[:, side] = value

    def gone(self):
        for piece in range(self.pieces):
            self.copies(0, piece)[0].wait_send()

    def finish(self):
        for part in range(self.parts):
            for k in (1, 2, 3):
                for copy in self.copies(k, part):
                    copy.wait_send()


def vmem():
    return pl.BlockSpec(memory_space=pltpu.VMEM)


def hbm():
    return pl.BlockSpec(memory_space=pl.ANY)


def dma(*n):
    return pltpu.SemaphoreType.DMA(n)


def named_call(body, ins, outs, scratch, name, **params):
    names = [*ins, *outs, *scratch]

    def kernel(*refs):
        body(types.SimpleNamespace(**dict(zip(names, refs))))

    result = pl.pallas_call(
        kernel,
        name=name,
        out_shape=[shape for shape, _ in outs.values()],
        in_specs=[spec for _, spec in ins.values()],
        out_specs=[spec for _, spec in outs.values()],
        scratch_shapes=list(scratch.values()),
        compiler_params=pltpu.CompilerParams(**params),
    )(*[array for array, _ in ins.values()])
    return types.SimpleNamespace(**dict(zip(outs, result)))


def vector(ref):
    return ref[...].astype(F32).reshape(1, -1)


def joint_table(rel_rows, rel_cols):
    parts = [rel_rows[...], jnp.zeros((5, HEAD), BF), rel_cols[...], jnp.zeros((5, HEAD), BF)]
    table = jnp.concatenate([p.astype(F32) for p in parts], 0)
    return jnp.concatenate([table, table], 1).astype(BF)


def table_kernel_value(places, table):
    value = nn(places, table)
    line = lax.broadcasted_iota(jnp.int32, value.shape, 0)
    lane = lax.broadcasted_iota(jnp.int32, value.shape, 1)
    return jnp.where((line < 128) == (lane < 64), value, 0.0).astype(BF)


def spread(a, back):
    rows, cols = [], []
    for y in range(a.shape[0] // 16):
        part = a[16 * y : 16 * y + 16, :]
        rows.append(pltpu.roll(part, 13 - y if back else (115 + y) % 128, 1))
        cols.append(pltpu.roll(part, 50 if back else 65, 1, stride=1, stride_axis=0))
    return jnp.concatenate(rows, 0), jnp.concatenate(cols, 0)


def pair_place(w, pair):
    return pl.multiple_of(w * SLOT, SLOT), pl.multiple_of(pair * 128, 128)


def attend_pair(w, place, pair, n, qkv, table, marks, masks, probs, mixed):
    r0, l0 = pair_place(w, pair)
    q2 = qkv[pl.ds(r0, n), pl.ds(l0, 128)]
    k2 = qkv[pl.ds(r0, SLOT), pl.ds(D + l0, 128)]
    v2 = qkv[pl.ds(r0, SLOT), pl.ds(2 * D + l0, 128)]
    a2 = nt(q2, table[...])
    qf = q2.astype(F32) * HEAD**-0.5
    kinds = lane_kinds(n)
    outs = []
    for head in range(2):
        own, first, second, is_row, one = kinds[head]
        rows, cols = spread(a2[:, 128 * head : 128 * head + 128], False)
        bias = jnp.where(is_row, rows, cols)
        high = bias.astype(BF).astype(F32)
        low = jnp.where(second, bias - high, jnp.where(one, 1.0, 0.0))
        aug = jnp.where(own, qf, jnp.where(first, high, low)).astype(BF)
        keys = k2 * masks[head : head + 1, :] + marks[head]
        scores = nt(aug, keys)
        top = jnp.max(scores, -1, keepdims=True)
        e = jnp.exp(scores - top)
        p = (e * (1.0 / jnp.sum(e, -1, keepdims=True))).astype(BF)
        probs[2 * place + head] = p
        outs.append(nn(p, v2))
    mixed[pl.ds(r0, n), pl.ds(l0, 128)] = jnp.where(kinds[0][0], outs[0], outs[1]).astype(BF)


def attend_back_pair(w, place, pair, n, qkv, gmix, probs, table, marks, masks, dqkv, gtab):
    r0, l0 = pair_place(w, pair)
    scale = HEAD**-0.5
    q2 = qkv[pl.ds(r0, n), pl.ds(l0, 128)]
    k2 = qkv[pl.ds(r0, SLOT), pl.ds(D + l0, 128)]
    v2 = qkv[pl.ds(r0, SLOT), pl.ds(2 * D + l0, 128)]
    g2 = gmix[pl.ds(r0, n), pl.ds(l0, 128)]
    kinds = lane_kinds(n)
    dq, dk, dv = [], [], []
    for head in range(2):
        own, first, second, is_row, one = kinds[head]
        mask = masks[head : head + 1, :]
        p = probs[2 * place + head]
        pf = p.astype(F32)
        dp = nt(g2, v2 * mask)
        ds = (pf * (dp - jnp.sum(pf * dp, -1, keepdims=True))).astype(BF)
        keys = k2 * (mask * jnp.asarray(scale, BF)) + marks[head]
        dqa = nn(ds, keys)
        marked = jnp.where(first | second, dqa, 0.0)
        rows, _ = spread(jnp.where(is_row, marked, 0.0), True)
        _, cols = spread(jnp.where(is_row, 0.0, marked), True)
        back = rows + cols
        at = lax.broadcasted_iota(jnp.int32, (n, 128), 1)
        if head:
            at = (at + 64) % 128
        high = back.astype(BF).astype(F32)
        split = jnp.where((at < 28) | ((at >= 64) & (at < 92)), high, back - high).astype(BF)
        extra = nn(split, table[128 * head : 128 * head + 128, :])
        dq.append(dqa + extra)
        gtab[head] += tn(split, q2)
        dk.append(tn(ds, q2))
        dv.append(tn(p, g2))
    wide = lane_kinds(SLOT)[0][0]
    dqkv[pl.ds(r0, n), pl.ds(l0, 128)] = jnp.where(kinds[0][0], dq[0], dq[1]).astype(BF)
    dqkv[pl.ds(4 * SLOT + r0, SLOT), pl.ds(l0, 128)] = (jnp.where(wide, dk[0], dk[1]) * scale).astype(BF)
    dqkv[pl.ds(8 * SLOT + r0, SLOT), pl.ds(l0, 128)] = jnp.where(wide, dv[0], dv[1]).astype(BF)


def over_windows(body, hooks, n_row, n_col):
    _, row, col = grid_place()
    for a, n in ((0, 16 * WIN), (1, 16 * (TILE * n_row - WIN * n_row))):

        def step(i, _):
            b = i // PAIRS
            good = (b == 0) | (col == n_col - 1)
            if a:
                good = good & (row == n_row - 1)

            @pl.when(good)
            def _():
                body(a, 2 * a + b, i, lax.rem(i, PAIRS), n)

            for when, hook in hooks:
                if when // (2 * PAIRS) == a:
                    pl.when(i == when % (2 * PAIRS))(hook)
            return 0

        lax.fori_loop(0, 2 * PAIRS, step, 0)


def attend_part(r, n_row, n_col, hooks, between):
    _, row, col = grid_place()
    biases = (vector(r.query_bias), None, vector(r.value_bias))
    for part, bias in enumerate(biases):
        for n in range(3):
            at = part * D + 256 * n
            value = nt(r.xw[...], r.wqkv[pl.ds(at, 256), :])
            if bias is not None:
                value = value + bias[:, 256 * n : 256 * n + 256]
            r.qkv[:, pl.ds(at, 256)] = value.astype(BF)
        between(part)

    def body(a, w, i, pair, n):
        attend_pair(w, i, pair, n, r.qkv, r.table, r.marks, r.masks, (r.probs0, r.probs1)[a], r.mixed)

    over_windows(body, hooks, n_row, n_col)
    hot = one_hot(field_slots(row, col, n_row, n_col), 4 * SLOT)
    r.ret[...] = nn(hot, r.mixed[...]).astype(BF)


def cut_windows(source, land, n_row, n_col, w):
    _, row, col = grid_place()
    hot = one_hot(window_index(w, row, col, n_row, n_col), FIELD)
    land[pl.ds(w * SLOT, SLOT), :] = nn(hot, source[...]).astype(BF)


def mlp_first(r, n_row, n_col, hidden, between, hooks):
    _, row, col = grid_place()
    hot = one_hot(home_index(row, col, n_row, n_col), FIELD)
    r.mixed_own[...] = nn(hot, r.home[...]).astype(BF)
    r.acc[...] = nt(r.mixed_own[...], r.wproj[...])
    shift, gain, bias = vector(r.proj_bias), vector(r.ln2_gain), vector(r.ln2_bias)

    def rows_body(rows):
        attended = (r.acc[rows, :] + shift).astype(BF)
        r.attended[rows, :] = attended
        middle = r.tokens[rows, :].astype(F32) + attended.astype(F32)
        r.n2[rows, :] = norm(middle, gain, bias)[0].astype(BF)
        return ()

    by_rows(rows_body, 0)
    between()
    up_bias = vector(r.fc1_bias)
    for line in range(hidden // D):
        r.up_bias[line : line + 1, :] = up_bias[:, line * D : line * D + D]

    def chunk(j, _):
        at = pl.multiple_of(j * 256, 256)
        lane = pl.multiple_of(lax.rem(j, 3) * 256, 256)
        u = nt(r.n2[...], r.w1[pl.ds(at, 256), :]) + r.up_bias[pl.ds(j // 3, 1), pl.ds(lane, 256)]
        cdf = 0.5 * (1.0 + lax.erf(u * 0.7071067811865476))
        r.act[:, pl.ds(at, 256)] = (u * cdf).astype(BF)
        r.slope[:, pl.ds(at, 256)] = (cdf + u * (jnp.exp(-0.5 * u * u) * 0.3989422804014327)).astype(BF)
        for when, hook in hooks:
            pl.when(j == when)(hook)
        return 0

    lax.fori_loop(0, hidden // 256, chunk, 0)


PARTS = 3


def mlp_second(r, hidden, ready):
    r.acc[...] = jnp.zeros_like(r.acc)
    r.small[...] = jnp.zeros_like(r.small)
    n = hidden // (2 * PARTS)
    for part in range(PARTS):
        ready(part)

        def chunk(i, _):
            at = pl.multiple_of((i * PARTS + part) * n, n)
            wide = pl.ds(at, n)
            gu = (nn(r.cot[...], r.w2[:, wide]) * r.slope[:, wide].astype(F32)).astype(BF)
            r.gu[:, wide] = gu
            r.acc[...] += nn(gu, r.w1[wide, :])
            r.up_sum[:, wide] = jnp.sum(gu.astype(F32), 0, keepdims=True)
            return 0

        lax.fori_loop(0, 2, chunk, 0)
    for line in range(hidden // D):
        r.small[8 + line : 9 + line, :] = r.up_sum[:, line * D : line * D + D]
    gain, bias = vector(r.ln2_gain), vector(r.ln2_bias)

    def rows_body(rows):
        middle = r.tokens[rows, :].astype(F32) + r.attended[rows, :].astype(F32)
        _, xhat, inverse = norm(middle, gain, bias)
        grad = r.acc[rows, :]
        cf = r.cot[rows, :].astype(F32)
        gm = cf + norm_back(grad, xhat, inverse, gain)
        r.grad_middle[rows, :] = gm
        low = gm.astype(BF)
        r.gfield[rows, :] = low
        return low.astype(F32), grad * xhat, grad, cf

    for line, value in enumerate(by_rows(rows_body, 4)):
        r.small[4 + line : 5 + line, :] = column_sum(value)


def mlp_branch(r, hidden):
    r.acc[...] = jnp.zeros_like(r.acc)

    def chunk(j, _):
        wide = pl.ds(pl.multiple_of(j * 512, 512), 512)
        r.acc[...] += nt(r.act[:, wide], r.w2[:, wide])
        return 0

    lax.fori_loop(0, hidden // 512, chunk, 0)


def mlp_out(r):
    bias = vector(r.fc2_bias)

    def rows_body(rows):
        att = r.attended[rows, :].astype(F32)
        tok = r.tokens[rows, :].astype(F32)
        middle = tok + att
        br = r.acc[rows, :] + bias
        result = middle + br
        r.output[rows, :] = result.astype(BF)
        return tuple(v * v for v in (tok, middle, result, att, br))

    lane = lax.broadcasted_iota(jnp.int32, (1, D), 1)
    stats = jnp.zeros((1, D), F32)
    for n, v in enumerate(by_rows(rows_body, 5)):
        stats = jnp.where(lane == n, jnp.sum(column_sum(v), 1, keepdims=True), stats)
    r.small[12:13, :] = stats


UP_PIECES, DOWN_PIECES = 12, 6


def up_weights(r, hidden, sent):
    def up(j, _):
        n = hidden // UP_PIECES
        at = pl.multiple_of(j * n, n)
        r.g1[pl.ds(at, n), :] = tn(r.gu[:, pl.ds(at, n)], r.n2[...]).astype(BF)
        sent(j)
        return 0

    lax.fori_loop(0, UP_PIECES, up, 0)


def down_weights(r, sent):
    r.cot_t[...] = r.cot[...].T

    def down(j, _):
        n = D // DOWN_PIECES
        at = pl.multiple_of(j * n, n)
        r.g2[pl.ds(at, n), :] = nn(r.cot_t[pl.ds(at, n), :], r.act[...]).astype(BF)
        sent(j)
        return 0

    lax.fori_loop(0, DOWN_PIECES, down, 0)


def proj_weight_grad(r):
    def chunk(n, _):
        at = pl.multiple_of(n * 256, 256)
        r.gproj[pl.ds(at, 256), :] = tn(r.gfield[pl.ds(0, TOK), pl.ds(at, 256)], r.mixed_own[...]).astype(BF)
        return 0

    lax.fori_loop(0, D // 256, chunk, 0)


def prepare(r):
    r.table[...] = table_kernel_value(r.places[...], joint_table(r.rel_rows, r.rel_cols))
    r.mixed[...] = jnp.zeros_like(r.mixed)


def back_prepare(r, n_row, n_col):
    r.table[...] = table_kernel_value(r.places_back[...], joint_table(r.rel_rows, r.rel_cols))
    r.gtab[...] = jnp.zeros_like(r.gtab)
    r.dqkv[...] = jnp.zeros_like(r.dqkv)
    for w in range(4):
        cut_windows(r.gfield, r.gw, n_row, n_col, w)


def back_mix(r):
    def mix(n, _):
        at = pl.multiple_of(n * 256, 256)
        r.gmix[:, pl.ds(at, 256)] = nn(r.gw[...], r.wproj[:, pl.ds(at, 256)]).astype(BF)
        return 0

    lax.fori_loop(0, 3, mix, 0)


def back_windows(r, n_row, n_col, hooks):
    def body(a, w, i, pair, n):
        attend_back_pair(w, i, pair, n, r.qkv, r.gmix, (r.probs0, r.probs1)[a], r.table, r.marks_back, r.masks, r.dqkv, r.gtab)

    over_windows(body, hooks, n_row, n_col)


def back_weights(r, n_row, n_col, sent):
    for n in range(9):
        rows, lanes = pl.ds(n // 3 * 4 * SLOT, 4 * SLOT), pl.ds(n % 3 * 256, 256)
        r.gqkv[pl.ds(256 * n, 256), :] = tn(r.dqkv[rows, lanes], r.xw[...]).astype(BF)
        sent(n)
    ones = jnp.ones((16, 4 * SLOT), BF)
    r.mid[...] = jnp.zeros_like(r.mid)
    r.mid[8:9, :] = nn(ones, r.dqkv[pl.ds(0, 4 * SLOT), :])[0:1, :]
    r.mid[9:10, :] = nn(ones, r.dqkv[pl.ds(8 * SLOT, 4 * SLOT), :])[0:1, :]
    lane = lax.broadcasted_iota(jnp.int32, (128, 128), 1)
    left = jnp.where(lane < 64, r.gtab[0], 0.0)
    right = jnp.where(lane >= 64, r.gtab[1], 0.0)
    tab = lax.dot_general(
        r.places_back[...].astype(F32),
        jnp.concatenate([left, right], 0),
        (((0,), (0,)), ((), ())),
        precision=lax.Precision.HIGHEST,
        preferred_element_type=F32,
    )
    tab = tab + pltpu.roll(tab, HEAD, 1)
    low = lax.broadcasted_iota(jnp.int32, (32, 128), 1) < HEAD
    tab = jnp.where(low, tab[:32], tab[32:])
    for t in range(4):
        r.mid[0:8, 128 * t : 128 * t + 128] = tab[8 * t : 8 * t + 8, :]


def back_return(r, n_row, n_col, between):
    _, row, col = grid_place()
    for n in range(3):
        value = 0
        for part in range(3):
            rows = pl.ds(4 * part * SLOT, 4 * SLOT)
            value = value + nn(r.dqkv[rows, :], r.wqkv[pl.ds(part * D, D), pl.ds(256 * n, 256)])
        r.gw[:, pl.ds(256 * n, 256)] = value.astype(BF)
        between(n)
    hot = one_hot(field_slots(row, col, n_row, n_col), 4 * SLOT)
    r.ret[...] = nn(hot, r.gw[...]).astype(BF)


def back_last(r, n_row, n_col):
    _, row, col = grid_place()
    hot = one_hot(home_index(row, col, n_row, n_col), FIELD)
    r.acc[...] = nn(hot, r.home2[...])
    gain, bias = vector(r.ln1_gain), vector(r.ln1_bias)

    def rows_body(rows):
        grad = r.acc[rows, :]
        _, xhat, inverse = norm(r.tokens[rows, :].astype(F32), gain, bias)
        r.input_grad[rows, :] = (r.grad_middle[rows, :] + norm_back(grad, xhat, inverse, gain)).astype(BF)
        return grad * xhat, grad

    r.late[...] = jnp.zeros_like(r.late)
    for line, value in enumerate(by_rows(rows_body, 2)):
        r.late[line : line + 1, :] = column_sum(value)


class Small:
    def __init__(self, value, come, send, recv, keep=None):
        self.dp, self.row, self.col = grid_place()
        self.value, self.come, self.send, self.recv, self.keep = value, come, send, recv, keep

    def copies(self, s):
        dp, row, col = self.dp, self.row, self.col
        plan = (
            [(dp, row, lax.rem(col + d, 4)) for d in (1, 2, 3)],
            [(dp, lax.rem(row + d, 4), col) for d in (1, 2, 3)],
            [(1 - dp, row, col)],
        )[s]
        return [
            pltpu.make_async_remote_copy(
                self.value, self.come.at[3 * s + i], self.send.at[3 * s + i], self.recv.at[3 * s + i],
                device_id=other, device_id_type=MESH,
            )
            for i, other in enumerate(plan)
        ]

    def start(self, s=0):
        for copy in self.copies(s):
            copy.start()

    def step(self, s):
        total = self.value[...]
        for i, copy in enumerate(self.copies(s)):
            copy.wait()
            value = self.come[3 * s + i]
            if s == 2 and self.keep is not None:
                line = lax.broadcasted_iota(jnp.int32, value.shape, 0)
                value = jnp.where(line == self.keep, 0.0, value)
            total = total + value
        self.value[...] = total
        if s < 2:
            self.start(s + 1)


GATHERS = ((0, 0, 1), (1, 0, 1), *((i, part, PARTS) for i in (2, 3) for part in range(PARTS)))


def block_body(n_row, n_col, shapes, hidden, r):
    dp, row, col = grid_place()
    rest = FIELD - TOK
    r.gfield, r.home2 = r.field, r.home
    for ref in (r.field, r.home):
        ref[pl.ds(TOK, rest), :] = jnp.zeros((rest, D), BF)
    greet(n_row, n_col)
    blocks = blocks_of(shapes)
    fulls, shards = (r.wqkv, r.wproj, r.w1, r.w2), (r.s0, r.s1, r.s2, r.s3)
    gathers = [
        Gather(fulls[i], shards[i], *blocks[i], r.gather_sem.at[0, n], r.gather_sem.at[1, n], part, parts)
        for n, (i, part, parts) in enumerate(GATHERS)
    ]
    qkv_way, proj_way = gathers[:2]
    up_ways, down_ways = gathers[2 : 2 + PARTS], gathers[2 + PARTS :]
    qkv_way.start(LINE, OWN, OWN_CORE)
    gain, bias = vector(r.ln1_gain), vector(r.ln1_bias)

    def rows_body(rows):
        r.field[rows, :] = norm(r.tokens[rows, :].astype(F32), gain, bias)[0].astype(BF)
        return ()

    by_rows(rows_body, 0)
    size = (n_row, n_col)
    lend = Halo(r.field, r.picked, r.field, False, r.lend_sem.at[0], r.lend_sem.at[1], *size)
    give = Halo(r.ret, None, r.home, True, r.give_sem.at[0], r.give_sem.at[1], *size)
    lend2 = Halo(r.gfield, r.picked, r.gfield, False, r.lend_sem.at[2], r.lend_sem.at[3], *size)
    give2 = Halo(r.ret, None, r.home2, True, r.give_sem.at[2], r.give_sem.at[3], *size)
    pick_start(lend, r.pick)
    local = []
    for way in gathers[1:]:
        way.start(OWN, OWN_CORE)
    for i, way in enumerate(gathers):
        own = way.full.at[rows_at(way.block(0, way.col), way.b), way.lanes]
        mine = pltpu.make_async_copy(way.shard, own, r.local_sem.at[i])
        mine.start()
        local.append(mine)
    prepare(r)
    for mine in local:
        mine.wait()
    qkv_way.step(0)
    proj_way.start(LINE)
    for way in up_ways:
        way.start(LINE)
    lend.wait()
    for w in range(4):
        cut_windows(r.field, r.xw, n_row, n_col, w)
    qkv_way.step(1)
    for way in down_ways:
        way.start(LINE)
    qkv_way.step(2)
    qkv_way.whole()

    def between(part):
        if part == 0:
            up_ways[0].step(0)
        elif part == 1:
            proj_way.step(0)
        else:
            up_ways[1].step(0)

    hooks = (
        (2, lambda: up_ways[2].step(0)),
        (4, lambda: up_ways[0].step(1)),
        (5, lambda: proj_way.step(1)),
        (8, lambda: down_ways[0].step(0)),
        (10, lambda: up_ways[1].step(1)),
        (12, lambda: down_ways[1].step(0)),
        (14, lambda: up_ways[2].step(1)),
        (16, lambda: proj_way.step(2)),
        (17, lambda: up_ways[0].step(2)),
        (18, lambda: down_ways[2].step(0)),
        (20, lambda: down_ways[0].step(1)),
        (22, lambda: up_ways[1].step(2)),
    )
    attend_part(r, n_row, n_col, hooks, between)
    give.start()
    r.home[pl.ds(0, TOK), :] = r.ret[pl.ds(0, TOK), :]
    proj_way.whole()
    down_ways[1].step(1)
    up_ways[2].step(2)
    give.arrive()

    qkv_sum, proj_sum, up_sum, down_sum = sums = [
        Reduce(g, g, dp * blocks[i][1], land, c, *blocks[i], pieces, parts, p, q)
        for i, (g, land, c, pieces, parts, p, q) in enumerate(
            [
                (r.gqkv, (r.g1, 0, True), r.c0, 9, PARTS, r.t0, r.u0),
                (r.gproj, (r.g1, shapes[0][0], True), r.c1, 1, 1, r.t1, r.u1),
                (r.g1, (r.w1, 0, False), r.c2, UP_PIECES, PARTS, r.t2, r.u2),
                (r.g2, (r.w2, 0, False), r.c3, DOWN_PIECES, PARTS, r.t3, r.u3),
            ]
        )
    ]

    def free(k):
        pl.semaphore_signal(r.free_sem.at[k], inc=1, device_id=(1 - dp, row, col), device_id_type=MESH)

    early = Small(r.small, r.small_come, r.small_sem.at[0], r.small_sem.at[1], 12)
    mid = Small(r.mid, r.mid_come, r.mid_sem.at[0], r.mid_sem.at[1])
    late = Small(r.late, r.late_come, r.late_sem.at[0], r.late_sem.at[1])

    def middle(act, slope, gu, cot_t):
        m = types.SimpleNamespace(**r.__dict__, act=act, slope=slope, gu=gu, cot_t=cot_t)

        def arrived():
            for way in up_ways:
                way.whole()
            give.gone()

        hooks = (
            (1, lambda: down_ways[2].step(1)),
            (2, lambda: down_ways[0].step(2)),
            (6, lambda: down_ways[1].step(2)),
            (11, lambda: down_ways[2].step(2)),
        )
        mlp_first(m, n_row, n_col, hidden, arrived, hooks)
        mlp_second(m, hidden, lambda part: down_ways[part].whole())
        for way in gathers:
            way.finish()
        free(0)
        pick_start(lend2, r.pick)
        pl.semaphore_wait(r.free_sem.at[0], 1)
        up_weights(m, hidden, lambda j: up_sum.start(0, j))
        up_sum.step(0)
        up_sum.gone()
        mlp_branch(m, hidden)
        free(1)
        pl.semaphore_wait(r.free_sem.at[1], 1)
        down_weights(m, lambda j: down_sum.start(0, j))
        mlp_out(m)
        early.start()
        down_sum.step(0)

    v = pltpu.VMEM
    wide = (TOK, hidden)
    pl.run_scoped(middle, v(wide, BF), v(wide, BF), v(wide, BF), v((D, TOK), BF))
    proj_weight_grad(r)
    proj_sum.start(0)
    lend2.wait()

    def all_parts(way, k):
        for part in range(way.parts):
            way.step(k, part)

    def ends(gw):
        e = types.SimpleNamespace(**r.__dict__, gw=gw, gmix=r.mixed, dqkv=r.w1)
        all_parts(up_sum, 1)
        back_prepare(e, n_row, n_col)
        proj_sum.step(0)
        back_mix(e)
        early.step(0)
        hooks = (
            (2, lambda: all_parts(down_sum, 1)),
            (12, lambda: all_parts(up_sum, 2)),
            (13, lambda: proj_sum.step(1)),
        )
        back_windows(e, n_row, n_col, hooks)
        back_return(e, n_row, n_col, lambda n: None)
        give2.start()
        r.home2[pl.ds(0, TOK), :] = r.ret[pl.ds(0, TOK), :]
        all_parts(down_sum, 2)
        early.step(1)
        back_weights(e, n_row, n_col, lambda n: qkv_sum.start(0, n))
        mid.start()
        proj_sum.step(2)
        give2.wait()
        back_last(e, n_row, n_col)
        late.start()
        qkv_sum.step(0)
        early.step(2)
        for part in range(PARTS):
            up_sum.result(r.o2, part)
        all_parts(qkv_sum, 1)
        mid.step(0)
        late.step(0)
        for part in range(PARTS):
            down_sum.result(r.o3, part)
        proj_sum.result(r.o1)
        all_parts(qkv_sum, 2)
        mid.step(1)
        late.step(1)
        mid.step(2)
        late.step(2)
        for part in range(PARTS):
            qkv_sum.result(r.o0, part)
        for way in (qkv_sum, proj_sum, down_sum):
            way.gone()
        for way in sums:
            way.finish()

    pl.run_scoped(ends, v((4 * SLOT, D), BF))


def split_ins(tensors, *names):
    return {k: (tensors[k], vmem()) for k in names}


def as_out(buffer):
    return (jax.ShapeDtypeStruct(buffer.shape, buffer.dtype), vmem())


def window_buffers(n_row):
    v = pltpu.VMEM
    late = 16 * (TILE * n_row - WIN * n_row)
    return dict(
        xw=v((4 * SLOT, D), BF),
        qkv=v((4 * SLOT, 3 * D), BF),
        probs0=v((2 * HEADS, 16 * WIN, SLOT), BF),
        probs1=v((2 * HEADS, late, SLOT), BF),
        mixed=v((4 * SLOT, D), BF),
        table=v((256, 128), BF),
        ret=v((FIELD, D), BF),
    )


def mlp_buffers(hidden):
    v = pltpu.VMEM
    return dict(
        mixed_own=v((TOK, D), BF),
        attended=v((TOK, D), BF),
        n2=v((TOK, D), BF),
        acc=v((TOK, D), F32),
        up_bias=v((hidden // D, D), F32),
        up_sum=v((1, hidden), F32),
        grad_middle=v((TOK, D), F32),
    )


def block_call(n_row, n_col, shapes, tensors, shards):
    hidden = shapes[2][0]
    sd, v = jax.ShapeDtypeStruct, pltpu.VMEM
    blocks = blocks_of(shapes)
    ins = {k: (t, vmem()) for k, t in tensors.items()}
    ins |= {"s" + str(i): (w, vmem()) for i, w in enumerate(shards)}
    outs = dict(
        output=(sd((TOK, D), BF), vmem()),
        input_grad=(sd((TOK, D), BF), vmem()),
        small=(sd((16, D), F32), vmem()),
        mid=(sd((16, D), F32), vmem()),
        late=(sd((8, D), F32), vmem()),
    )
    outs |= {"o" + str(i): (sd(b, F32), vmem()) for i, b in enumerate(blocks)}
    wqkv, wproj, w1, w2 = [v(s, BF) for s in shapes]
    come = [v((15 * b, h), BF) for b, h in blocks]
    field = v((FIELD, D), BF)
    scratch = dict(
        **window_buffers(n_row),
        **mlp_buffers(hidden),
        wqkv=wqkv,
        wproj=wproj,
        w1=w1,
        w2=w2,
        gqkv=wqkv,
        gproj=wproj,
        g1=w1,
        g2=w2,
        c0=come[0],
        c1=come[1],
        c2=come[2],
        c3=come[3],
        field=field,
        home=field,
        picked=v((PICKED, D), BF),
        gtab=v((2, 128, 128), F32),
        small_come=v((7, 16, D), F32),
        mid_come=v((7, 16, D), F32),
        late_come=v((7, 8, D), F32),
        local_sem=dma(len(GATHERS)),
        gather_sem=dma(2, len(GATHERS), Gather.SEMS),
        lend_sem=dma(4, 3),
        give_sem=dma(4, 3),
        small_sem=dma(2, 7),
        mid_sem=dma(2, 7),
        late_sem=dma(2, 7),
        free_sem=pltpu.SemaphoreType.REGULAR((2,)),
    )
    for i in range(4):
        scratch |= {"t" + str(i): dma(Reduce.SEMS), "u" + str(i): dma(Reduce.SEMS)}
    return named_call(
        functools.partial(block_body, n_row, n_col, shapes, hidden), ins, outs, scratch, "block",
        vmem_limit_bytes=63 * MIB, collective_id=0, has_side_effects=True,
    )


def plain_block(n_row, n_col, shapes, tensors, weights, field):
    hidden = shapes[2][0]
    sd, v = jax.ShapeDtypeStruct, pltpu.VMEM
    wqkv, wproj, w1, w2 = [(w, vmem()) for w in weights]
    limit = dict(vmem_limit_bytes=60 * MIB)

    def given(value, *names):
        return {k: (getattr(value, k), vmem()) for k in names}

    names = ("query_bias", "value_bias", "rel_rows", "rel_cols", "masks", "places", "marks")
    windows = window_buffers(n_row)
    outs = {k: as_out(windows.pop(k)) for k in ("qkv", "xw", "probs0", "probs1", "ret")}

    def attend_body(r):
        prepare(r)
        for w in range(4):
            cut_windows(r.field, r.xw, n_row, n_col, w)
        attend_part(r, n_row, n_col, (), lambda part: None)

    ins = split_ins(tensors, *names) | dict(field=(field, vmem()), wqkv=wqkv)
    one = named_call(attend_body, ins, outs, windows, "attend", **limit)
    home = (return_xla(one.ret, n_row, n_col), vmem())
    names = ("tokens", "cot", "proj_bias", "ln2_gain", "ln2_bias", "fc1_bias", "fc2_bias")
    buffers = mlp_buffers(hidden)
    outs = dict(grad_middle=as_out(buffers.pop("grad_middle")), gfield=(sd((FIELD, D), BF), vmem()))
    outs |= {k: (sd(s, BF), vmem()) for k, s in zip(("gproj", "g1", "g2"), shapes[1:])}
    outs |= dict(output=(sd((TOK, D), BF), vmem()), small=(sd((16, D), F32), vmem()))
    wide = (TOK, hidden)
    buffers |= dict(act=v(wide, BF), slope=v(wide, BF), gu=v(wide, BF), cot_t=v((D, TOK), BF))

    def mlp_body(r):
        r.gfield[...] = jnp.zeros_like(r.gfield)
        mlp_first(r, n_row, n_col, hidden, lambda: None, ())
        mlp_second(r, hidden, lambda part: None)
        up_weights(r, hidden, lambda j: None)
        mlp_branch(r, hidden)
        down_weights(r, lambda j: None)
        mlp_out(r)
        proj_weight_grad(r)

    ins = split_ins(tensors, *names) | dict(home=home, wproj=wproj, w1=w1, w2=w2)
    two = named_call(mlp_body, ins, outs, buffers, "mlp", **limit)
    gfield = (lend_xla(two.gfield[:TOK], n_row, n_col), vmem())
    ins = split_ins(tensors, "rel_rows", "rel_cols", "masks", "places_back", "marks_back")
    ins |= given(one, "qkv", "xw", "probs0", "probs1") | dict(wqkv=wqkv, wproj=wproj, gfield=gfield)
    outs = dict(
        gqkv=(sd(shapes[0], BF), vmem()),
        ret=(sd((FIELD, D), BF), vmem()),
        mid=(sd((16, D), F32), vmem()),
    )
    rows = v((4 * SLOT, D), BF)
    scratch = dict(gw=rows, gmix=rows, dqkv=v((12 * SLOT, D), BF))
    scratch |= dict(table=v((256, 128), BF), gtab=v((2, 128, 128), F32))

    def windows_body(r):
        back_prepare(r, n_row, n_col)
        back_mix(r)
        back_windows(r, n_row, n_col, ())
        back_weights(r, n_row, n_col, lambda n: None)
        back_return(r, n_row, n_col, lambda w: None)

    three = named_call(windows_body, ins, outs, scratch, "windows", **limit)
    home = (return_xla(three.ret, n_row, n_col), vmem())
    ins = split_ins(tensors, "tokens", "ln1_gain", "ln1_bias") | dict(home2=home) | given(two, "grad_middle")
    outs = dict(input_grad=(sd((TOK, D), BF), vmem()), late=(sd((8, D), F32), vmem()))
    four = named_call(lambda r: back_last(r, n_row, n_col), ins, outs, dict(acc=v((TOK, D), F32)), "ends", **limit)
    grads = []
    for g in (three.gqkv, two.gproj, two.g1, two.g2):
        g = lax.psum_scatter(g, AXES, scatter_dimension=0, tiled=True)
        grads.append(lax.psum_scatter(g, "dp", scatter_dimension=1, tiled=True))
    line = jnp.arange(16)[:, None] == 12
    local = lax.psum(two.small, AXES)
    small = jnp.where(line, local, lax.psum(jnp.where(line, 0.0, local), "dp"))
    mid, late = (lax.psum(v, ("dp", *AXES)) for v in (three.mid, four.late))
    return grads, two.output, four.input_grad, small, mid, late


def last_body(count, r):
    for i in range(4):
        r.__dict__["t" + str(i)][...] = r.__dict__["s" + str(i)][...].astype(F32)
    r.output_out[...] = r.output[...]
    r.input_grad_out[...] = r.input_grad[...]
    lines = ((r.late, 0), (r.late, 1), (r.mid, 8), (r.mid, 9), (r.small, 4), (r.small, 5), (r.small, 6), (r.small, 7))
    for i, (ref, line) in enumerate(lines):
        r.__dict__["v" + str(i)][...] = ref[line : line + 1, :].reshape(D)
    r.up[...] = jnp.concatenate([r.small[8 + i : 9 + i, :] for i in range(r.up.shape[0] // D)], 1).reshape(-1)
    tables = jnp.concatenate([r.mid[0:8, 128 * t : 128 * t + 128] for t in range(4)], 0)
    r.rows[...] = tables[0 : 2 * WIN - 1, :HEAD]
    r.cols[...] = pltpu.roll(tables, HEAD, 1)[0 : 2 * WIN - 1, :HEAD]
    r.stats[...] = jnp.sqrt(r.small[12:13, :5] / count)


def last_call(count, hidden, sums, output, input_grad, small, mid, late):
    sd = jax.ShapeDtypeStruct
    ins = {"s" + str(i): (s, vmem()) for i, s in enumerate(sums)}
    ins |= dict(output=(output, vmem()), input_grad=(input_grad, vmem()), small=(small, vmem()))
    ins |= dict(mid=(mid, vmem()), late=(late, vmem()))
    outs = {"t" + str(i): (sd(s.shape, F32), vmem()) for i, s in enumerate(sums)}
    outs |= dict(output_out=(sd((TOK, D), BF), vmem()), input_grad_out=(sd((TOK, D), BF), vmem()))
    outs |= {"v" + str(i): (sd((D,), F32), vmem()) for i in range(8)}
    outs |= dict(
        up=(sd((hidden,), F32), vmem()),
        rows=(sd((2 * WIN - 1, HEAD), F32), vmem()),
        cols=(sd((2 * WIN - 1, HEAD), F32), vmem()),
        stats=(sd((1, 5), F32), vmem()),
    )
    return named_call(functools.partial(last_body, count), ins, outs, {}, "last", vmem_limit_bytes=63 * MIB)


def on_device(
    n_dp, n_row, n_col,
    tokens, ln1_gain, ln1_bias, qkv_weight, query_bias, value_bias, rel_rows, rel_cols,
    proj_weight, proj_bias, ln2_gain, ln2_bias, fc1_weight, fc1_bias, fc2_weight, fc2_bias, cotangent,
):
    direct = (n_dp, n_row, n_col) == (2, 4, 4)
    tok = tokens.reshape(TOK, D)
    mask_values = np.zeros((16, 128), np.float32)
    mask_values[0, :64] = 1.0
    mask_values[1, 64:] = 1.0
    shared = dict(
        tokens=tok,
        cot=cotangent.reshape(TOK, D),
        ln1_gain=ln1_gain,
        ln1_bias=ln1_bias,
        rel_rows=rel_rows,
        rel_cols=rel_cols,
        masks=jnp.asarray(mask_values, BF),
    )
    tensors = shared | dict(
        query_bias=query_bias,
        value_bias=value_bias,
        proj_bias=proj_bias,
        ln2_gain=ln2_gain,
        ln2_bias=ln2_bias,
        fc1_bias=fc1_bias,
        fc2_bias=fc2_bias,
        places=jnp.asarray(table_places(False), BF),
        marks=jnp.asarray(key_marks(False), BF),
        places_back=jnp.asarray(table_places(True), BF),
        marks_back=jnp.asarray(key_marks(True), BF),
    )
    shards = (qkv_weight, proj_weight, fc1_weight, fc2_weight)
    shapes = [(s.shape[1] * n_row * n_col, s.shape[0] * n_dp) for s in shards]
    if direct:
        tensors |= dict(pick=jnp.asarray(pick_rows(), BF))
        done = block_call(n_row, n_col, shapes, tensors, [s.T for s in shards])
        sums = (done.o0, done.o1, done.o2, done.o3)
        rest = (done.output, done.input_grad, done.small, done.mid, done.late)
    else:
        weights = []
        for s in shards:
            s = lax.all_gather(s, AXES, axis=1, tiled=True)
            weights.append(lax.all_gather(s, "dp", axis=0, tiled=True).T)
        normed = norm(tok.astype(F32), ln1_gain.astype(F32), ln1_bias.astype(F32))[0].astype(BF)
        field = lend_xla(normed, n_row, n_col)
        sums, *rest = plain_block(n_row, n_col, shapes, tensors, weights, field)
    out = last_call(TOK * n_row * n_col * D, shapes[2][0], sums, *rest)
    return (
        out.output_out.reshape(tokens.shape),
        out.input_grad_out.reshape(tokens.shape),
        out.v0,
        out.v1,
        out.t0.T,
        out.v2,
        out.v3,
        out.rows,
        out.cols,
        out.t1.T,
        out.v4,
        out.v5,
        out.v6,
        out.t2.T,
        out.up,
        out.t3.T,
        out.v7,
        out.stats,
    )


def solution(mesh):
    tile = P("dp", "row", "col", None)
    weight = P("dp", AXES)
    sizes = [mesh.shape[a] for a in ("dp", "row", "col")]
    ins = [tile] + [P()] * 16
    for i in (3, 8, 12, 14):
        ins[i] = weight
    ins[16] = tile
    outs = [tile, tile] + [P()] * 16
    for i in (4, 9, 13, 15):
        outs[i] = weight
    outs[17] = P("dp", None)
    return jax.shard_map(
        functools.partial(on_device, *sizes),
        mesh=mesh,
        in_specs=tuple(ins),
        out_specs=tuple(outs),
        check_vma=False,
    )
```

```python
import functools
import types

import jax
import jax.numpy as jnp
import numpy as np
from jax import lax
from jax.experimental import pallas as pl
from jax.experimental.pallas import tpu as pltpu
from jax.sharding import PartitionSpec as P

HEADS = 12
HEAD = 64
WIN = 14
EPS = 1e-06
MESH = pl.DeviceIdType.MESH
AXES = ("row", "col")
F32 = jnp.float32
BF = jnp.bfloat16

D = HEADS * HEAD
TILE = 16
TOK = TILE * TILE
LO = 6
SLOT = 256
PAIRS = HEADS // 2
FIELD = 496
PICKED = 144
MIB = 2**20

LINKS = {
    (1, 0): (True, 160, 96, 256),
    (0, 1): (False, 0, 96, 352),
    (1, 1): (False, 96, 48, 448),
}


def nt(a, b):
    return lax.dot_general(a, b, (((1,), (1,)), ((), ())), preferred_element_type=F32)


def nn(a, b):
    return lax.dot_general(a, b, (((1,), (0,)), ((), ())), preferred_element_type=F32)


def tn(a, b):
    return lax.dot_general(a, b, (((0,), (0,)), ((), ())), preferred_element_type=F32)


def pick_rows():
    table = np.zeros((PICKED, TOK), np.float32)
    for base, first in ((0, 0), (96, TILE - LO)):
        for i in range((TILE - first) * LO):
            y, x = divmod(i, LO)
            table[base + i, (first + y) * TILE + TILE - LO + x] = 1.0
    return table


def table_places(back):
    place = np.zeros((256, 64), np.float32)
    for head in range(2):
        for r in range(2 * WIN - 1):
            for copy in range(2):
                row_lane = (64 + 28 * copy + r + 64 * head) % 128
                col_lane = (28 * copy + r + 64 * head) % 128
                place[128 * head + row_lane, 26 - r] = 1.0
                place[128 * head + col_lane, 32 + (r if back else 26 - r)] = 1.0
    return place


def key_marks(back):
    marks = np.zeros((2, SLOT, 128), np.float32)
    for head in range(2):
        for j in range(SLOT):
            k, l = divmod(j, 16)
            if k < WIN and l < WIN:
                for copy in range(2):
                    marks[head, j, (64 + 28 * copy + k + 64 * head) % 128] = 1.0
                    marks[head, j, (78 + 28 * copy + (13 - l if back else l) + 64 * head) % 128] = 1.0
            else:
                marks[head, j, (120 + 64 * head) % 128] = -1e30
    return marks


def lane_kinds(rows):
    lane = lax.broadcasted_iota(jnp.int32, (rows, 128), 1)
    kinds = []
    for head in range(2):
        at = (lane + 64 * head) % 128 if head else lane
        own = at < 64
        first = (at >= 64) & (at < 92)
        second = (at >= 92) & (at < 120)
        is_row = ((at >= 64) & (at < 78)) | ((at >= 92) & (at < 106))
        kinds.append((own, first, second, is_row, at == 120))
    return kinds


def window_index(w, row, col, n_row, n_col):
    place = lax.broadcasted_iota(jnp.int32, (SLOT, 1), 0)
    y = place // 16
    x = place - 16 * y
    a, b = w // 2, w % 2
    ry = WIN * (row + a) + y - TILE * row
    rx = WIN * (col + b) + x - TILE * col
    good = (y < WIN) & (x < WIN) & (ry < TILE) & (rx < TILE)
    if a:
        good = good & (row == n_row - 1)
    if b:
        good = good & (col == n_col - 1)
    up, left = ry < 0, rx < 0
    base = jnp.where(up, jnp.where(left, 448, 256), jnp.where(left, 352, 0))
    width = jnp.where(left, LO, TILE)
    index = base + jnp.where(up, ry + LO, ry) * width + jnp.where(left, rx + LO, rx)
    return jnp.where(good, index, -1)


def field_slots(row, col, n_row, n_col):
    at = lax.broadcasted_iota(jnp.int32, (FIELD, 1), 0)
    above = (at >= 256) & (at < 352)
    left = (at >= 352) & (at < 448)
    corner = at >= 448
    narrow = left | corner
    rest = jnp.where(corner, at - 448, jnp.where(left, at - 352, jnp.where(above, at - 256, at)))
    sixth = sum((rest >= LO * k).astype(jnp.int32) for k in range(1, TILE))
    ty = jnp.where(narrow, sixth, rest // TILE)
    tx = rest - ty * jnp.where(narrow, LO, TILE)
    ty = jnp.where(above | corner, ty - LO, ty)
    tx = jnp.where(narrow, tx - LO, tx)
    good = at < 484
    where = 0
    for t, place, n, stride, unit in ((ty, row, n_row, 2, 16), (tx, col, n_col, 1, 1)):
        y = TILE * place + t - WIN * place
        late = y >= WIN
        good = good & (y >= 0) & (jnp.logical_not(late) | (place == n - 1))
        where = where + jnp.where(late, stride * SLOT + unit * (y - WIN), unit * y)
    return jnp.where(good, where, -1)


def home_index(row, col, n_row, n_col):
    place = lax.broadcasted_iota(jnp.int32, (TOK, 1), 0)
    ty = place // TILE
    tx = place - TILE * ty
    down = (TILE * row + ty - WIN * row >= WIN) & (row < n_row - 1)
    right = (TILE * col + tx - WIN * col >= WIN) & (col < n_col - 1)
    near = TILE - LO
    return jnp.where(
        down,
        jnp.where(right, 448 + (ty - near) * LO + tx - near, 256 + (ty - near) * TILE + tx),
        jnp.where(right, 352 + ty * LO + tx - near, place),
    )


def one_hot(index, size):
    lane = lax.broadcasted_iota(jnp.int32, (index.shape[0], size), 1)
    return jnp.where(lane == index, 1.0, 0.0).astype(BF)


STEP = 64


def by_rows(body, sums):
    def step(i, kept):
        parts = body(pl.ds(pl.multiple_of(i * STEP, STEP), STEP))
        return tuple(k + sum(p[8 * q : 8 * q + 8] for q in range(STEP // 8)) for k, p in zip(kept, parts))

    return lax.fori_loop(0, TOK // STEP, step, (jnp.zeros((8, D), F32),) * sums)


def column_sum(v):
    return jnp.sum(v, 0, keepdims=True)


def norm(v, gain, bias):
    mean = jnp.mean(v, -1, keepdims=True)
    center = v - mean
    inverse = lax.rsqrt(jnp.mean(center * center, -1, keepdims=True) + EPS)
    xhat = center * inverse
    return xhat * gain + bias, xhat, inverse


def norm_back(grad, xhat, inverse, gain):
    d = grad * gain
    return inverse * (
        d - jnp.mean(d, -1, keepdims=True) - xhat * jnp.mean(d * xhat, -1, keepdims=True)
    )


def grid_place():
    return lax.axis_index("dp"), lax.axis_index("row"), lax.axis_index("col")


def exists(step, row, col, n_row, n_col):
    r, c = row + step[0], col + step[1]
    return (r >= 0) & (r < n_row) & (c >= 0) & (c < n_col)


CORNERS = ((1, 1), (-1, -1))


def greet(n_row, n_col):
    dp, row, col = grid_place()
    barrier = pltpu.get_barrier_semaphore()
    others = [(dp, row, lax.rem(col + d, n_col)) for d in (1, 2, 3)]
    others += [(dp, lax.rem(row + d, n_row), col) for d in (1, 2, 3)]
    others.append((1 - dp, row, col))
    for other in others:
        pl.semaphore_signal(barrier, inc=1, device_id=other, device_id_type=MESH)
    count = len(others)
    for step in CORNERS:
        there = exists(step, row, col, n_row, n_col)

        @pl.when(there)
        def _():
            pl.semaphore_signal(
                barrier, inc=1, device_id=(dp, row + step[0], col + step[1]), device_id_type=MESH
            )

        count = count + jnp.where(there, 1, 0)
    pl.semaphore_wait(barrier, count)


class Halo:
    def __init__(self, source, picked, land, back, send, recv, n_row, n_col):
        self.source, self.picked, self.land, self.back = source, picked, land, back
        self.send, self.recv, self.size = send, recv, (n_row, n_col)

    def copies(self):
        dp, row, col = grid_place()
        sign = -1 if self.back else 1
        for i, ((dr, dc), (own, first, rows, there)) in enumerate(LINKS.items()):
            if self.back:
                src = self.source.at[pl.ds(there, rows)]
            else:
                src = (self.source if own else self.picked).at[pl.ds(first, rows)]
            copy = pltpu.make_async_remote_copy(
                src,
                self.land.at[pl.ds(there, rows)],
                self.send.at[i],
                self.recv.at[i],
                device_id=(dp, row + sign * dr, col + sign * dc),
                device_id_type=MESH,
            )
            goes = exists((sign * dr, sign * dc), row, col, *self.size)
            comes = exists((-sign * dr, -sign * dc), row, col, *self.size)
            yield copy, goes, comes

    def start(self):
        for copy, goes, _ in self.copies():
            pl.when(goes)(copy.start)

    def arrive(self):
        for copy, _, comes in self.copies():
            pl.when(comes)(copy.wait_recv)

    def gone(self):
        for copy, goes, _ in self.copies():
            pl.when(goes)(copy.wait_send)

    def wait(self):
        self.arrive()
        self.gone()


def pick_start(halo, pick):
    halo.picked[...] = nn(pick[...], halo.source[pl.ds(0, TOK), :]).astype(BF)
    halo.start()


def halo_xla(blocks, back, n_row, n_col):
    sign = -1 if back else 1
    pieces = [blocks[0]]
    for (dr, dc), block in zip(LINKS, blocks[1:]):
        dr, dc = sign * dr, sign * dc
        pairs = [
            (r * n_col + c, (r + dr) * n_col + c + dc)
            for r in range(n_row)
            for c in range(n_col)
            if 0 <= r + dr < n_row and 0 <= c + dc < n_col
        ]
        pieces.append(lax.ppermute(block, AXES, pairs))
    return jnp.concatenate(pieces, 0)


def lend_xla(own, n_row, n_col):
    grid = own.reshape(TILE, TILE, -1)
    corner = grid[TILE - LO :, TILE - LO :].reshape(LO * LO, -1)
    blocks = [
        own,
        own[TILE * (TILE - LO) :],
        grid[:, TILE - LO :].reshape(TILE * LO, -1),
        jnp.pad(corner, ((0, 48 - LO * LO), (0, 0))),
    ]
    return halo_xla(blocks, False, n_row, n_col)


def return_xla(field, n_row, n_col):
    return halo_xla([field[:256], field[256:352], field[352:448], field[448:]], True, n_row, n_col)


def blocks_of(shapes):
    return [(n // 16, k // 2) for n, k in shapes]


def rows_at(first, count):
    return pl.ds(pl.multiple_of(first, 16), count)


LINE, OWN, OWN_CORE, LINE_CORE, FAR, NEAR_CORE, FAR_CORE, CORE = range(10, 18)


class Gather:
    SEMS = 20

    def __init__(self, full, shard, block, half, send, recv, part=0, parts=1):
        self.dp, self.row, self.col = grid_place()
        width = half // parts
        self.full, self.shard, self.b = full, shard.at[:, pl.ds(part * width, width)], block
        self.send, self.recv = send, recv
        self.lanes = pl.ds(pl.multiple_of(self.dp * half + part * width, 128), width)
        self.other = pl.ds(pl.multiple_of((1 - self.dp) * half + part * width, 128), width)

    def block(self, flip, place):
        return (jnp.bitwise_xor(self.row, flip) * 4 + place) * self.b

    def came(self, d):
        return lax.rem(self.col + 4 - d, 4)

    def copy(self, i, first, count, land, target, shard=False):
        core = target == CORE
        if core:
            device = (1 - self.dp, self.row, self.col)
        elif isinstance(target, tuple):
            device = (self.dp, self.row, lax.rem(self.col + target[0], 4))
        else:
            device = (self.dp, jnp.bitwise_xor(self.row, target), self.col)

        def make(src, dst):
            return pltpu.make_async_remote_copy(
                src, dst, self.send.at[i], self.recv.at[i], device_id=device, device_id_type=MESH
            )

        def out():
            there = self.full.at[rows_at(first, count), self.lanes]
            return make(self.shard if shard else there, there)

        def come():
            here = self.full.at[rows_at(land, count), self.other if core else self.lanes]
            return make(here, here)

        return out, come

    def copies(self, k):
        b = self.b
        own = self.block(0, self.col)
        if k == LINE:
            return [
                self.copy(d - 1, own, b, self.block(0, self.came(d)), (d,), True) for d in (1, 2, 3)
            ]
        if k == OWN:
            return [self.copy(2 + f, own, b, self.block(f, self.col), f, True) for f in (1, 2)]
        if k == OWN_CORE:
            return [self.copy(5, own, b, own, CORE, True)]
        if k < LINE:
            at = self.came(k)
            return [
                self.copy(4 + 2 * k, self.block(0, at), b, self.block(1, at), 1),
                self.copy(5 + 2 * k, self.block(0, at), b, self.block(2, at), 2),
            ]
        if k == LINE_CORE:
            return [
                self.copy(11 + d, self.block(0, self.came(d)), b, self.block(0, self.came(d)), CORE)
                for d in (1, 2, 3)
            ]
        if k == FAR:
            return [
                self.copy(15, self.block(2, 0), 2 * b, self.block(3, 0), 1),
                self.copy(16, self.block(1, 2), 2 * b, self.block(3, 2), 2),
            ]
        if k == NEAR_CORE:
            return [self.copy(16 + f, self.block(f, 0), 4 * b, self.block(f, 0), CORE) for f in (1, 2)]
        return [self.copy(19, self.block(3, 0), 4 * b, self.block(3, 0), CORE)]

    def start(self, *kinds):
        for k in kinds:
            for out, _ in self.copies(k):
                out().start()

    def arrive(self, *kinds):
        for k in kinds:
            for _, come in self.copies(k):
                come().wait_recv()

    def step(self, n):
        if n == 0:
            for d in (1, 2, 3):
                self.copies(LINE)[d - 1][1]().wait_recv()
                self.start(d)
            self.start(LINE_CORE)
        elif n == 1:
            self.arrive(OWN, 1, 2, 3)
            self.start(FAR, NEAR_CORE)
        else:
            self.arrive(FAR)
            self.start(FAR_CORE)

    def whole(self):
        self.arrive(OWN_CORE, LINE_CORE, NEAR_CORE, FAR_CORE)

    def finish(self):
        for k in (LINE, OWN, OWN_CORE, 1, 2, 3, LINE_CORE, FAR, NEAR_CORE, FAR_CORE):
            for out, _ in self.copies(k):
                out().wait_send()


class Reduce:
    SEMS = 34

    def __init__(self, grad, total, base, land, come, block, half, pieces, parts, send, recv):
        self.dp, self.row, self.col = grid_place()
        self.grad, self.total, self.base, self.come = grad, total, base, come
        self.land, self.land_row, mirrored = land
        self.land_there = self.dp * half if mirrored else 0
        self.land_here = (1 - self.dp) * half if mirrored else 0
        self.b, self.h, self.send, self.recv = block, half, send, recv
        self.pieces, self.parts, self.width = pieces, parts, half // parts
        self.other = pl.ds(pl.multiple_of((1 - self.dp) * half, 128), half)

    def side(self, base, part, width):
        return pl.ds(pl.multiple_of(base + part * width, 128), width)

    def at(self, flip, place=0):
        return (jnp.bitwise_xor(self.row, flip) * 4 + place) * self.b

    def lanes(self, part):
        return pl.ds(pl.multiple_of(self.base + part * self.width, 128), self.width)

    def came(self, first, count, part):
        return self.come.at[rows_at(first, count), pl.ds(part * self.width, self.width)]

    def tot(self, first, count, part):
        return self.total.at[rows_at(first, count), self.lanes(part)]

    def sem(self, k, part):
        if k == 0:
            return part
        return self.pieces + 7 * part + {1: 0, 2: 2, 3: 4}[k]

    def copies(self, k, part):
        b = self.b
        if k == 0:
            n = 16 * b // self.pieces
            there = self.land.at[rows_at(self.land_row + part * n, n), self.side(self.land_there, 0, self.h)]
            plan = [(self.grad.at[rows_at(part * n, n), self.other], there, (1 - self.dp, self.row, self.col))]
        elif k == 1:
            plan = [
                (
                    self.tot(self.at(3, 2 * half), 2 * b, part),
                    self.came(2 * half * b, 2 * b, part),
                    (self.dp, jnp.bitwise_xor(self.row, 1 + half), self.col),
                )
                for half in (0, 1)
            ]
        elif k == 2:
            plan = [
                (
                    self.tot(self.at(flip), 4 * b, part),
                    self.came(4 * flip * b, 4 * b, part),
                    (self.dp, jnp.bitwise_xor(self.row, flip), self.col),
                )
                for flip in (1, 2)
            ]
        else:
            plan = []
            for d in (1, 2, 3):
                to = lax.rem(self.col + d, 4)
                plan.append(
                    (
                        self.tot(self.at(0, to), b, part),
                        self.came((11 + d) * b, b, part),
                        (self.dp, self.row, to),
                    )
                )
        base = self.sem(k, part)
        return [
            pltpu.make_async_remote_copy(
                src, dst, self.send.at[base + i], self.recv.at[base + i], device_id=dev, device_id_type=MESH
            )
            for i, (src, dst, dev) in enumerate(plan)
        ]

    def start(self, k, part=0):
        for copy in self.copies(k, part):
            copy.start()

    def arrive(self, k, part=0):
        for copy in self.copies(k, part):
            copy.wait_recv()

    def sum_rows(self, first, count, froms, part, source=None, base=0):
        most = (256 if len(froms) == 1 else 96) * 384
        step = next(n for n in range(count, 0, -16) if count % n == 0 and n * self.width <= most)
        lanes = self.lanes(part)
        side = self.side(base, part, self.width)
        source = self.come if source is None else source

        def body(i, _):
            at = rows_at(first + i * step, step)
            value = self.total[at, lanes]
            if len(froms) == 1:
                value = value + source[rows_at(froms[0] + i * step, step), side]
            else:
                value = value.astype(F32)
                for f in froms:
                    value = value + source[rows_at(f + i * step, step), side].astype(F32)
                value = value.astype(BF)
            self.total[at, lanes] = value
            return 0

        lax.fori_loop(0, count // step, body, 0)

    def add_piece(self, piece):
        n = 16 * self.b // self.pieces
        self.arrive(0, piece)
        for part in range(self.parts):
            self.sum_rows(piece * n, n, (self.land_row + piece * n,), part, self.land, self.land_here)

    def step(self, k, part=0):
        b = self.b
        if k == 0:
            for piece in range(self.pieces):
                self.add_piece(piece)
            for part in range(1, self.parts):
                self.start(1, part)
            part = 0
        else:
            self.arrive(k, part)
            if k == 1:
                self.sum_rows(self.at(2), 2 * b, (0,), part)
                self.sum_rows(self.at(1, 2), 2 * b, (2 * b,), part)
            else:
                self.sum_rows(self.at(0), 4 * b, (4 * b, 8 * b), part)
        self.start(k + 1, part)

    def result(self, out, part=0):
        b = self.b
        self.arrive(3, part)
        value = self.total[rows_at(self.at(0, self.col), b), self.lanes(part)].astype(F32)
        side = pl.ds(part * self.width, self.width)
        for d in (1, 2, 3):
            value = value + self.come[pl.ds((11 + d) * b, b), side].astype(F32)
        out[:, side] = value

    def gone(self):
        for piece in range(self.pieces):
            self.copies(0, piece)[0].wait_send()

    def finish(self):
        for part in range(self.parts):
            for k in (1, 2, 3):
                for copy in self.copies(k, part):
                    copy.wait_send()


def vmem():
    return pl.BlockSpec(memory_space=pltpu.VMEM)


def hbm():
    return pl.BlockSpec(memory_space=pl.ANY)


def dma(*n):
    return pltpu.SemaphoreType.DMA(n)


def named_call(body, ins, outs, scratch, name, **params):
    names = [*ins, *outs, *scratch]

    def kernel(*refs):
        body(types.SimpleNamespace(**dict(zip(names, refs))))

    result = pl.pallas_call(
        kernel,
        name=name,
        out_shape=[shape for shape, _ in outs.values()],
        in_specs=[spec for _, spec in ins.values()],
        out_specs=[spec for _, spec in outs.values()],
        scratch_shapes=list(scratch.values()),
        compiler_params=pltpu.CompilerParams(**params),
    )(*[array for array, _ in ins.values()])
    return types.SimpleNamespace(**dict(zip(outs, result)))


def vector(ref):
    return ref[...].astype(F32).reshape(1, -1)


def joint_table(rel_rows, rel_cols):
    parts = [rel_rows[...], jnp.zeros((5, HEAD), BF), rel_cols[...], jnp.zeros((5, HEAD), BF)]
    table = jnp.concatenate([p.astype(F32) for p in parts], 0)
    return jnp.concatenate([table, table], 1).astype(BF)


def table_kernel_value(places, table):
    value = nn(places, table)
    line = lax.broadcasted_iota(jnp.int32, value.shape, 0)
    lane = lax.broadcasted_iota(jnp.int32, value.shape, 1)
    return jnp.where((line < 128) == (lane < 64), value, 0.0).astype(BF)


def narrow(v, wide):
    if wide:
        return v
    return v.astype(F32).reshape(-1, 16, 128)[:, :8].reshape(-1, 128).astype(v.dtype)


def widen(v, wide):
    if not wide:
        v = v.reshape(-1, 8, 128)
        v = jnp.concatenate([v, jnp.zeros_like(v)], 1).reshape(-1, 128)
    return v.astype(BF)


def spread(a, back, line):
    rows, cols = [], []
    for y in range(a.shape[0] // line):
        part = a[line * y : line * y + line, :]
        rows.append(pltpu.roll(part, 13 - y if back else (115 + y) % 128, 1))
        cols.append(pltpu.roll(part, 50 if back else 65, 1, stride=1, stride_axis=0))
    return jnp.concatenate(rows, 0), jnp.concatenate(cols, 0)


def pair_place(w, pair):
    return pl.multiple_of(w * SLOT, SLOT), pl.multiple_of(pair * 128, 128)


def attend_pair(w, place, pair, n, wide, qkv, table, marks, masks, probs, mixed):
    r0, l0 = pair_place(w, pair)
    q2 = narrow(qkv[pl.ds(r0, n), pl.ds(l0, 128)], wide)
    count = q2.shape[0]
    k2 = qkv[pl.ds(r0, SLOT), pl.ds(D + l0, 128)]
    v2 = qkv[pl.ds(r0, SLOT), pl.ds(2 * D + l0, 128)]
    a2 = nt(q2, table[...])
    qf = q2.astype(F32) * HEAD**-0.5
    kinds = lane_kinds(count)
    outs = []
    for head in range(2):
        own, first, second, is_row, one = kinds[head]
        rows, cols = spread(a2[:, 128 * head : 128 * head + 128], False, count // (n // 16))
        bias = jnp.where(is_row, rows, cols)
        high = bias.astype(BF).astype(F32)
        low = jnp.where(second, bias - high, jnp.where(one, 1.0, 0.0))
        aug = jnp.where(own, qf, jnp.where(first, high, low)).astype(BF)
        keys = k2 * masks[head : head + 1, :] + marks[head]
        scores = nt(aug, keys)
        top = jnp.max(scores, -1, keepdims=True)
        e = jnp.exp(scores - top)
        p = (e * (1.0 / jnp.sum(e, -1, keepdims=True))).astype(BF)
        probs[2 * place + head, 0:count, :] = p
        outs.append(nn(p, v2))
    mixed[pl.ds(r0, n), pl.ds(l0, 128)] = widen(jnp.where(kinds[0][0], outs[0], outs[1]), wide)


def attend_back_pair(w, place, pair, n, wide, qkv, gmix, probs, table, marks, masks, dqkv, gtab):
    r0, l0 = pair_place(w, pair)
    scale = HEAD**-0.5
    q2 = narrow(qkv[pl.ds(r0, n), pl.ds(l0, 128)], wide)
    count = q2.shape[0]
    k2 = qkv[pl.ds(r0, SLOT), pl.ds(D + l0, 128)]
    v2 = qkv[pl.ds(r0, SLOT), pl.ds(2 * D + l0, 128)]
    g2 = narrow(gmix[pl.ds(r0, n), pl.ds(l0, 128)], wide)
    kinds = lane_kinds(count)
    dq, dk, dv = [], [], []
    for head in range(2):
        own, first, second, is_row, one = kinds[head]
        mask = masks[head : head + 1, :]
        p = probs[2 * place + head, 0:count, :]
        pf = p.astype(F32)
        dp = nt(g2, v2 * mask)
        ds = (pf * (dp - jnp.sum(pf * dp, -1, keepdims=True))).astype(BF)
        keys = k2 * (mask * jnp.asarray(scale, BF)) + marks[head]
        dqa = nn(ds, keys)
        marked = jnp.where(first | second, dqa, 0.0)
        rows, _ = spread(jnp.where(is_row, marked, 0.0), True, count // (n // 16))
        _, cols = spread(jnp.where(is_row, 0.0, marked), True, count // (n // 16))
        back = rows + cols
        at = lax.broadcasted_iota(jnp.int32, (count, 128), 1)
        if head:
            at = (at + 64) % 128
        high = back.astype(BF).astype(F32)
        split = jnp.where((at < 28) | ((at >= 64) & (at < 92)), high, back - high).astype(BF)
        extra = nn(split, table[128 * head : 128 * head + 128, :])
        dq.append(dqa + extra)
        gtab[head] += tn(split, q2)
        dk.append(tn(ds, q2))
        dv.append(tn(p, g2))
    left = lane_kinds(SLOT)[0][0]
    dqkv[pl.ds(r0, n), pl.ds(l0, 128)] = widen(jnp.where(kinds[0][0], dq[0], dq[1]), wide)
    dqkv[pl.ds(4 * SLOT + r0, SLOT), pl.ds(l0, 128)] = (jnp.where(left, dk[0], dk[1]) * scale).astype(BF)
    dqkv[pl.ds(8 * SLOT + r0, SLOT), pl.ds(l0, 128)] = jnp.where(left, dv[0], dv[1]).astype(BF)


TOGETHER = 3


def over_windows(body, hooks, n_row, n_col):
    _, row, col = grid_place()
    for w in range(4):
        a, b = w // 2, w % 2
        n = 16 * (TILE * n_row - WIN * n_row if a else WIN)
        good = True
        if a:
            good = row == n_row - 1
        if b:
            good = good & (col == n_col - 1)

        def step(i, _):
            def work():
                for pair in range(TOGETHER):
                    pair = i * TOGETHER + pair
                    body(w, PAIRS * b + pair, pair, n, b == 0)

            if w:
                pl.when(good)(work)
            else:
                work()
            for when, hook in hooks:
                if when // PAIRS == w:
                    pl.when(i == when % PAIRS // TOGETHER)(hook)
            return 0

        lax.fori_loop(0, PAIRS // TOGETHER, step, 0)


def attend_part(r, n_row, n_col, hooks, between):
    _, row, col = grid_place()
    biases = (vector(r.query_bias), None, vector(r.value_bias))
    for part, bias in enumerate(biases):
        for n in range(3):
            at = part * D + 256 * n
            value = nt(r.xw[...], r.wqkv[pl.ds(at, 256), :])
            if bias is not None:
                value = value + bias[:, 256 * n : 256 * n + 256]
            r.qkv[:, pl.ds(at, 256)] = value.astype(BF)
        between(part)

    def body(w, place, pair, n, wide):
        probs = (r.probs0, r.probs1)[w // 2]
        attend_pair(w, place, pair, n, wide, r.qkv, r.table, r.marks, r.masks, probs, r.mixed)

    over_windows(body, hooks, n_row, n_col)
    hot = one_hot(field_slots(row, col, n_row, n_col), 4 * SLOT)
    r.ret[...] = nn(hot, r.mixed[...]).astype(BF)


def cut_windows(source, land, n_row, n_col, w):
    _, row, col = grid_place()
    hot = one_hot(window_index(w, row, col, n_row, n_col), FIELD)
    land[pl.ds(w * SLOT, SLOT), :] = nn(hot, source[...]).astype(BF)


def mlp_first(r, n_row, n_col, hidden, between, hooks):
    _, row, col = grid_place()
    hot = one_hot(home_index(row, col, n_row, n_col), FIELD)
    r.mixed_own[...] = nn(hot, r.home[...]).astype(BF)
    r.acc[...] = nt(r.mixed_own[...], r.wproj[...])
    shift, gain, bias = vector(r.proj_bias), vector(r.ln2_gain), vector(r.ln2_bias)

    def rows_body(rows):
        attended = (r.acc[rows, :] + shift).astype(BF)
        r.attended[rows, :] = attended
        middle = r.tokens[rows, :].astype(F32) + attended.astype(F32)
        r.n2[rows, :] = norm(middle, gain, bias)[0].astype(BF)
        return ()

    by_rows(rows_body, 0)
    between()
    up_bias = vector(r.fc1_bias)
    for line in range(hidden // D):
        r.up_bias[line : line + 1, :] = up_bias[:, line * D : line * D + D]

    def chunk(j, _):
        at = pl.multiple_of(j * 256, 256)
        lane = pl.multiple_of(lax.rem(j, 3) * 256, 256)
        u = nt(r.n2[...], r.w1[pl.ds(at, 256), :]) + r.up_bias[pl.ds(j // 3, 1), pl.ds(lane, 256)]
        cdf = 0.5 * (1.0 + lax.erf(u * 0.7071067811865476))
        r.act[:, pl.ds(at, 256)] = (u * cdf).astype(BF)
        r.slope[:, pl.ds(at, 256)] = (cdf + u * (jnp.exp(-0.5 * u * u) * 0.3989422804014327)).astype(BF)
        for when, hook in hooks:
            pl.when(j == when)(hook)
        return 0

    lax.fori_loop(0, hidden // 256, chunk, 0)


PARTS = 3


def mlp_second(r, hidden, ready):
    r.acc[...] = jnp.zeros_like(r.acc)
    r.small[...] = jnp.zeros_like(r.small)
    n = hidden // (2 * PARTS)
    for part in range(PARTS):
        ready(part)

        def chunk(i, _):
            at = pl.multiple_of((i * PARTS + part) * n, n)
            wide = pl.ds(at, n)
            gu = (nn(r.cot[...], r.w2[:, wide]) * r.slope[:, wide].astype(F32)).astype(BF)
            r.gu[:, wide] = gu
            r.acc[...] += nn(gu, r.w1[wide, :])
            r.up_sum[:, wide] = jnp.sum(gu.astype(F32), 0, keepdims=True)
            return 0

        lax.fori_loop(0, 2, chunk, 0)
    for line in range(hidden // D):
        r.small[8 + line : 9 + line, :] = r.up_sum[:, line * D : line * D + D]
    gain, bias = vector(r.ln2_gain), vector(r.ln2_bias)

    def rows_body(rows):
        middle = r.tokens[rows, :].astype(F32) + r.attended[rows, :].astype(F32)
        _, xhat, inverse = norm(middle, gain, bias)
        grad = r.acc[rows, :]
        cf = r.cot[rows, :].astype(F32)
        gm = cf + norm_back(grad, xhat, inverse, gain)
        r.grad_middle[rows, :] = gm
        low = gm.astype(BF)
        r.gfield[rows, :] = low
        return low.astype(F32), grad * xhat, grad, cf

    for line, value in enumerate(by_rows(rows_body, 4)):
        r.small[4 + line : 5 + line, :] = column_sum(value)


def mlp_branch(r, hidden):
    r.acc[...] = jnp.zeros_like(r.acc)

    def chunk(j, _):
        wide = pl.ds(pl.multiple_of(j * 512, 512), 512)
        r.acc[...] += nt(r.act[:, wide], r.w2[:, wide])
        return 0

    lax.fori_loop(0, hidden // 512, chunk, 0)


def mlp_out(r):
    bias = vector(r.fc2_bias)

    def rows_body(rows):
        att = r.attended[rows, :].astype(F32)
        tok = r.tokens[rows, :].astype(F32)
        middle = tok + att
        br = r.acc[rows, :] + bias
        result = middle + br
        r.output[rows, :] = result.astype(BF)
        return tuple(v * v for v in (tok, middle, result, att, br))

    lane = lax.broadcasted_iota(jnp.int32, (1, D), 1)
    stats = jnp.zeros((1, D), F32)
    for n, v in enumerate(by_rows(rows_body, 5)):
        stats = jnp.where(lane == n, jnp.sum(column_sum(v), 1, keepdims=True), stats)
    r.small[12:13, :] = stats


UP_PIECES, DOWN_PIECES = 12, 6


def up_weights(r, hidden, sent):
    def up(j, _):
        n = hidden // UP_PIECES
        at = pl.multiple_of(j * n, n)
        r.g1[pl.ds(at, n), :] = tn(r.gu[:, pl.ds(at, n)], r.n2[...]).astype(BF)
        sent(j)
        return 0

    lax.fori_loop(0, UP_PIECES, up, 0)


def down_weights(r, sent):
    r.cot_t[...] = r.cot[...].T

    def down(j, _):
        n = D // DOWN_PIECES
        at = pl.multiple_of(j * n, n)
        r.g2[pl.ds(at, n), :] = nn(r.cot_t[pl.ds(at, n), :], r.act[...]).astype(BF)
        sent(j)
        return 0

    lax.fori_loop(0, DOWN_PIECES, down, 0)


def proj_weight_grad(r):
    def chunk(n, _):
        at = pl.multiple_of(n * 256, 256)
        r.gproj[pl.ds(at, 256), :] = tn(r.gfield[pl.ds(0, TOK), pl.ds(at, 256)], r.mixed_own[...]).astype(BF)
        return 0

    lax.fori_loop(0, D // 256, chunk, 0)


def prepare(r):
    r.table[...] = table_kernel_value(r.places[...], joint_table(r.rel_rows, r.rel_cols))
    r.mixed[...] = jnp.zeros_like(r.mixed)


def back_prepare(r, n_row, n_col):
    r.table[...] = table_kernel_value(r.places_back[...], joint_table(r.rel_rows, r.rel_cols))
    r.gtab[...] = jnp.zeros_like(r.gtab)
    r.dqkv[...] = jnp.zeros_like(r.dqkv)
    for w in range(4):
        cut_windows(r.gfield, r.gw, n_row, n_col, w)


def back_mix(r):
    def mix(n, _):
        at = pl.multiple_of(n * 256, 256)
        r.gmix[:, pl.ds(at, 256)] = nn(r.gw[...], r.wproj[:, pl.ds(at, 256)]).astype(BF)
        return 0

    lax.fori_loop(0, 3, mix, 0)


def back_windows(r, n_row, n_col, hooks):
    def body(w, place, pair, n, wide):
        probs = (r.probs0, r.probs1)[w // 2]
        attend_back_pair(
            w, place, pair, n, wide, r.qkv, r.gmix, probs, r.table, r.marks_back, r.masks, r.dqkv, r.gtab
        )

    over_windows(body, hooks, n_row, n_col)


def back_weights(r, n_row, n_col, sent):
    for n in range(9):
        rows, lanes = pl.ds(n // 3 * 4 * SLOT, 4 * SLOT), pl.ds(n % 3 * 256, 256)
        r.gqkv[pl.ds(256 * n, 256), :] = tn(r.dqkv[rows, lanes], r.xw[...]).astype(BF)
        sent(n)
    ones = jnp.ones((16, 4 * SLOT), BF)
    r.mid[...] = jnp.zeros_like(r.mid)
    r.mid[8:9, :] = nn(ones, r.dqkv[pl.ds(0, 4 * SLOT), :])[0:1, :]
    r.mid[9:10, :] = nn(ones, r.dqkv[pl.ds(8 * SLOT, 4 * SLOT), :])[0:1, :]
    lane = lax.broadcasted_iota(jnp.int32, (128, 128), 1)
    left = jnp.where(lane < 64, r.gtab[0], 0.0)
    right = jnp.where(lane >= 64, r.gtab[1], 0.0)
    tab = lax.dot_general(
        r.places_back[...].astype(F32),
        jnp.concatenate([left, right], 0),
        (((0,), (0,)), ((), ())),
        precision=lax.Precision.HIGHEST,
        preferred_element_type=F32,
    )
    tab = tab + pltpu.roll(tab, HEAD, 1)
    low = lax.broadcasted_iota(jnp.int32, (32, 128), 1) < HEAD
    tab = jnp.where(low, tab[:32], tab[32:])
    for t in range(4):
        r.mid[0:8, 128 * t : 128 * t + 128] = tab[8 * t : 8 * t + 8, :]


def back_return(r, n_row, n_col):
    _, row, col = grid_place()
    for n in range(3):
        value = 0
        for part in range(3):
            rows = pl.ds(4 * part * SLOT, 4 * SLOT)
            value = value + nn(r.dqkv[rows, :], r.wqkv[pl.ds(part * D, D), pl.ds(256 * n, 256)])
        r.gw[:, pl.ds(256 * n, 256)] = value.astype(BF)
    hot = one_hot(field_slots(row, col, n_row, n_col), 4 * SLOT)
    r.ret[...] = nn(hot, r.gw[...]).astype(BF)


def norm_sums(r, n_row, n_col):
    _, row, col = grid_place()
    hot = one_hot(field_slots(row, col, n_row, n_col), 4 * SLOT)
    r.gmix[pl.ds(0, FIELD), :] = nn(hot, r.xw[...]).astype(BF)
    bias = vector(r.ln1_bias)

    def step(i, kept):
        rows = pl.ds(pl.multiple_of(i * 16, 16), 16)
        grad = r.ret[rows, :].astype(F32)
        parts = (grad * (r.gmix[rows, :].astype(F32) - bias), grad)
        return tuple(k + p[:8] + p[8:] for k, p in zip(kept, parts))

    scaled, total = lax.fori_loop(0, FIELD // 16, step, (jnp.zeros((8, D), F32),) * 2)
    r.mid[10:11, :] = column_sum(scaled) / vector(r.ln1_gain)
    r.mid[11:12, :] = column_sum(total)


def back_last(r, n_row, n_col):
    _, row, col = grid_place()
    hot = one_hot(home_index(row, col, n_row, n_col), FIELD)
    r.acc[...] = nn(hot, r.home2[...])
    gain, bias = vector(r.ln1_gain), vector(r.ln1_bias)

    def rows_body(rows):
        grad = r.acc[rows, :]
        _, xhat, inverse = norm(r.tokens[rows, :].astype(F32), gain, bias)
        r.input_grad[rows, :] = (r.grad_middle[rows, :] + norm_back(grad, xhat, inverse, gain)).astype(BF)
        return ()

    by_rows(rows_body, 0)


class Small:
    def __init__(self, value, come, send, recv, keep=None):
        self.dp, self.row, self.col = grid_place()
        self.value, self.come, self.send, self.recv, self.keep = value, come, send, recv, keep

    def copies(self, s):
        dp, row, col = self.dp, self.row, self.col
        plan = (
            [(dp, row, lax.rem(col + d, 4)) for d in (1, 2, 3)],
            [(dp, lax.rem(row + d, 4), col) for d in (1, 2, 3)],
            [(1 - dp, row, col)],
        )[s]
        return [
            pltpu.make_async_remote_copy(
                self.value, self.come.at[3 * s + i], self.send.at[3 * s + i], self.recv.at[3 * s + i],
                device_id=other, device_id_type=MESH,
            )
            for i, other in enumerate(plan)
        ]

    def start(self, s=0):
        for copy in self.copies(s):
            copy.start()

    def step(self, s):
        total = self.value[...]
        for i, copy in enumerate(self.copies(s)):
            copy.wait()
            value = self.come[3 * s + i]
            if s == 2 and self.keep is not None:
                line = lax.broadcasted_iota(jnp.int32, value.shape, 0)
                value = jnp.where(line == self.keep, 0.0, value)
            total = total + value
        self.value[...] = total
        if s < 2:
            self.start(s + 1)


GATHERS = ((0, 0, 1), (1, 0, 1), *((i, part, PARTS) for i in (2, 3) for part in range(PARTS)))


def block_body(n_row, n_col, shapes, hidden, r):
    dp, row, col = grid_place()
    rest = FIELD - TOK
    r.gfield, r.home2 = r.field, r.home
    for ref in (r.field, r.home):
        ref[pl.ds(TOK, rest), :] = jnp.zeros((rest, D), BF)
    greet(n_row, n_col)
    blocks = blocks_of(shapes)
    fulls, shards = (r.wqkv, r.wproj, r.w1, r.w2), (r.s0, r.s1, r.s2, r.s3)
    gathers = [
        Gather(fulls[i], shards[i], *blocks[i], r.gather_sem.at[0, n], r.gather_sem.at[1, n], part, parts)
        for n, (i, part, parts) in enumerate(GATHERS)
    ]
    qkv_way, proj_way = gathers[:2]
    up_ways, down_ways = gathers[2 : 2 + PARTS], gathers[2 + PARTS :]
    qkv_way.start(LINE, OWN, OWN_CORE)
    gain, bias = vector(r.ln1_gain), vector(r.ln1_bias)

    def rows_body(rows):
        r.field[rows, :] = norm(r.tokens[rows, :].astype(F32), gain, bias)[0].astype(BF)
        return ()

    by_rows(rows_body, 0)
    size = (n_row, n_col)
    lend = Halo(r.field, r.picked, r.field, False, r.lend_sem.at[0], r.lend_sem.at[1], *size)
    give = Halo(r.ret, None, r.home, True, r.give_sem.at[0], r.give_sem.at[1], *size)
    lend2 = Halo(r.gfield, r.picked, r.gfield, False, r.lend_sem.at[2], r.lend_sem.at[3], *size)
    give2 = Halo(r.ret, None, r.home2, True, r.give_sem.at[2], r.give_sem.at[3], *size)
    pick_start(lend, r.pick)
    local = []
    for way in gathers[1:]:
        way.start(OWN, OWN_CORE)
    for i, way in enumerate(gathers):
        own = way.full.at[rows_at(way.block(0, way.col), way.b), way.lanes]
        mine = pltpu.make_async_copy(way.shard, own, r.local_sem.at[i])
        mine.start()
        local.append(mine)
    prepare(r)
    for mine in local:
        mine.wait()
    qkv_way.step(0)
    proj_way.start(LINE)
    for way in up_ways:
        way.start(LINE)
    lend.wait()
    for w in range(4):
        cut_windows(r.field, r.xw, n_row, n_col, w)
    qkv_way.step(1)
    for way in down_ways:
        way.start(LINE)
    qkv_way.step(2)
    qkv_way.whole()

    def between(part):
        if part == 0:
            up_ways[0].step(0)
        elif part == 1:
            proj_way.step(0)
        else:
            up_ways[1].step(0)

    hooks = (
        (2, lambda: up_ways[2].step(0)),
        (4, lambda: up_ways[0].step(1)),
        (5, lambda: proj_way.step(1)),
        (8, lambda: down_ways[0].step(0)),
        (10, lambda: up_ways[1].step(1)),
        (12, lambda: down_ways[1].step(0)),
        (14, lambda: up_ways[2].step(1)),
        (16, lambda: proj_way.step(2)),
        (17, lambda: up_ways[0].step(2)),
        (18, lambda: down_ways[2].step(0)),
        (20, lambda: down_ways[0].step(1)),
        (22, lambda: up_ways[1].step(2)),
    )
    attend_part(r, n_row, n_col, hooks, between)
    give.start()
    r.home[pl.ds(0, TOK), :] = r.ret[pl.ds(0, TOK), :]
    proj_way.whole()
    down_ways[1].step(1)
    up_ways[2].step(2)
    give.arrive()

    qkv_sum, proj_sum, up_sum, down_sum = sums = [
        Reduce(g, g, dp * blocks[i][1], land, c, *blocks[i], pieces, parts, p, q)
        for i, (g, land, c, pieces, parts, p, q) in enumerate(
            [
                (r.gqkv, (r.g1, 0, True), r.c0, 9, PARTS, r.t0, r.u0),
                (r.gproj, (r.g1, shapes[0][0], True), r.c1, 1, 1, r.t1, r.u1),
                (r.g1, (r.w1, 0, False), r.c2, UP_PIECES, PARTS, r.t2, r.u2),
                (r.g2, (r.w2, 0, False), r.c3, DOWN_PIECES, PARTS, r.t3, r.u3),
            ]
        )
    ]

    def free(k):
        pl.semaphore_signal(r.free_sem.at[k], inc=1, device_id=(1 - dp, row, col), device_id_type=MESH)

    early = Small(r.small, r.small_come, r.small_sem.at[0], r.small_sem.at[1], 12)
    mid = Small(r.mid, r.mid_come, r.mid_sem.at[0], r.mid_sem.at[1])

    def middle(act, slope, gu, cot_t):
        m = types.SimpleNamespace(**r.__dict__, act=act, slope=slope, gu=gu, cot_t=cot_t)

        def arrived():
            for way in up_ways:
                way.whole()
            give.gone()

        hooks = (
            (1, lambda: down_ways[2].step(1)),
            (2, lambda: down_ways[0].step(2)),
            (6, lambda: down_ways[1].step(2)),
            (11, lambda: down_ways[2].step(2)),
        )
        mlp_first(m, n_row, n_col, hidden, arrived, hooks)
        mlp_second(m, hidden, lambda part: down_ways[part].whole())
        for way in gathers:
            way.finish()
        free(0)
        pick_start(lend2, r.pick)
        pl.semaphore_wait(r.free_sem.at[0], 1)
        up_weights(m, hidden, lambda j: up_sum.start(0, j))
        up_sum.step(0)
        up_sum.gone()
        mlp_branch(m, hidden)
        free(1)
        pl.semaphore_wait(r.free_sem.at[1], 1)
        down_weights(m, lambda j: down_sum.start(0, j))
        mlp_out(m)
        early.start()
        down_sum.step(0)

    v = pltpu.VMEM
    wide = (TOK, hidden)
    pl.run_scoped(middle, v(wide, BF), v(wide, BF), v(wide, BF), v((D, TOK), BF))
    proj_weight_grad(r)
    proj_sum.start(0)
    lend2.wait()

    def all_parts(way, k):
        for part in range(way.parts):
            way.step(k, part)

    def ends(gw):
        e = types.SimpleNamespace(**r.__dict__, gw=gw, gmix=r.mixed, dqkv=r.w1)
        all_parts(up_sum, 1)
        back_prepare(e, n_row, n_col)
        proj_sum.step(0)
        back_mix(e)
        early.step(0)
        hooks = (
            (2, lambda: all_parts(down_sum, 1)),
            (12, lambda: all_parts(up_sum, 2)),
            (13, lambda: proj_sum.step(1)),
        )
        back_windows(e, n_row, n_col, hooks)
        back_weights(e, n_row, n_col, lambda n: qkv_sum.start(0, n))
        all_parts(down_sum, 2)
        qkv_sum.step(0)
        proj_sum.step(2)
        early.step(1)
        back_return(e, n_row, n_col)
        give2.start()
        r.home2[pl.ds(0, TOK), :] = r.ret[pl.ds(0, TOK), :]
        all_parts(qkv_sum, 1)
        norm_sums(e, n_row, n_col)
        mid.start()
        early.step(2)
        for part in range(PARTS):
            up_sum.result(r.o2, part)
        all_parts(qkv_sum, 2)
        mid.step(0)
        give2.arrive()
        back_last(e, n_row, n_col)
        mid.step(1)
        for part in range(PARTS):
            down_sum.result(r.o3, part)
        proj_sum.result(r.o1)
        mid.step(2)
        give2.gone()
        for part in range(PARTS):
            qkv_sum.result(r.o0, part)
        for way in (qkv_sum, proj_sum, down_sum):
            way.gone()
        for way in sums:
            way.finish()

    pl.run_scoped(ends, v((4 * SLOT, D), BF))


def split_ins(tensors, *names):
    return {k: (tensors[k], vmem()) for k in names}


def as_out(buffer):
    return (jax.ShapeDtypeStruct(buffer.shape, buffer.dtype), vmem())


def window_buffers(n_row):
    v = pltpu.VMEM
    late = 16 * (TILE * n_row - WIN * n_row)
    return dict(
        xw=v((4 * SLOT, D), BF),
        qkv=v((4 * SLOT, 3 * D), BF),
        probs0=v((2 * HEADS, 16 * WIN, SLOT), BF),
        probs1=v((2 * HEADS, late, SLOT), BF),
        mixed=v((4 * SLOT, D), BF),
        table=v((256, 128), BF),
        ret=v((FIELD, D), BF),
    )


def mlp_buffers(hidden):
    v = pltpu.VMEM
    return dict(
        mixed_own=v((TOK, D), BF),
        attended=v((TOK, D), BF),
        n2=v((TOK, D), BF),
        acc=v((TOK, D), F32),
        up_bias=v((hidden // D, D), F32),
        up_sum=v((1, hidden), F32),
        grad_middle=v((TOK, D), F32),
    )


def block_call(n_row, n_col, shapes, tensors, shards):
    hidden = shapes[2][0]
    sd, v = jax.ShapeDtypeStruct, pltpu.VMEM
    blocks = blocks_of(shapes)
    ins = {k: (t, vmem()) for k, t in tensors.items()}
    ins |= {"s" + str(i): (w, vmem()) for i, w in enumerate(shards)}
    outs = dict(
        output=(sd((TOK, D), BF), vmem()),
        input_grad=(sd((TOK, D), BF), vmem()),
        small=(sd((16, D), F32), vmem()),
        mid=(sd((16, D), F32), vmem()),
    )
    outs |= {"o" + str(i): (sd(b, F32), vmem()) for i, b in enumerate(blocks)}
    wqkv, wproj, w1, w2 = [v(s, BF) for s in shapes]
    come = [v((15 * b, h), BF) for b, h in blocks]
    field = v((FIELD, D), BF)
    scratch = dict(
        **window_buffers(n_row),
        **mlp_buffers(hidden),
        wqkv=wqkv,
        wproj=wproj,
        w1=w1,
        w2=w2,
        gqkv=wqkv,
        gproj=wproj,
        g1=w1,
        g2=w2,
        c0=come[0],
        c1=come[1],
        c2=come[2],
        c3=come[3],
        field=field,
        home=field,
        picked=v((PICKED, D), BF),
        gtab=v((2, 128, 128), F32),
        small_come=v((7, 16, D), F32),
        mid_come=v((7, 16, D), F32),
        local_sem=dma(len(GATHERS)),
        gather_sem=dma(2, len(GATHERS), Gather.SEMS),
        lend_sem=dma(4, 3),
        give_sem=dma(4, 3),
        small_sem=dma(2, 7),
        mid_sem=dma(2, 7),
        free_sem=pltpu.SemaphoreType.REGULAR((2,)),
    )
    for i in range(4):
        scratch |= {"t" + str(i): dma(Reduce.SEMS), "u" + str(i): dma(Reduce.SEMS)}
    return named_call(
        functools.partial(block_body, n_row, n_col, shapes, hidden), ins, outs, scratch, "block",
        vmem_limit_bytes=63 * MIB, collective_id=0, has_side_effects=True,
    )


def plain_block(n_row, n_col, shapes, tensors, weights, field):
    hidden = shapes[2][0]
    sd, v = jax.ShapeDtypeStruct, pltpu.VMEM
    wqkv, wproj, w1, w2 = [(w, vmem()) for w in weights]
    limit = dict(vmem_limit_bytes=60 * MIB)

    def given(value, *names):
        return {k: (getattr(value, k), vmem()) for k in names}

    names = ("query_bias", "value_bias", "rel_rows", "rel_cols", "masks", "places", "marks")
    windows = window_buffers(n_row)
    outs = {k: as_out(windows.pop(k)) for k in ("qkv", "xw", "probs0", "probs1", "ret")}

    def attend_body(r):
        prepare(r)
        for w in range(4):
            cut_windows(r.field, r.xw, n_row, n_col, w)
        attend_part(r, n_row, n_col, (), lambda part: None)

    ins = split_ins(tensors, *names) | dict(field=(field, vmem()), wqkv=wqkv)
    one = named_call(attend_body, ins, outs, windows, "attend", **limit)
    home = (return_xla(one.ret, n_row, n_col), vmem())
    names = ("tokens", "cot", "proj_bias", "ln2_gain", "ln2_bias", "fc1_bias", "fc2_bias")
    buffers = mlp_buffers(hidden)
    outs = dict(grad_middle=as_out(buffers.pop("grad_middle")), gfield=(sd((FIELD, D), BF), vmem()))
    outs |= {k: (sd(s, BF), vmem()) for k, s in zip(("gproj", "g1", "g2"), shapes[1:])}
    outs |= dict(output=(sd((TOK, D), BF), vmem()), small=(sd((16, D), F32), vmem()))
    wide = (TOK, hidden)
    buffers |= dict(act=v(wide, BF), slope=v(wide, BF), gu=v(wide, BF), cot_t=v((D, TOK), BF))

    def mlp_body(r):
        r.gfield[...] = jnp.zeros_like(r.gfield)
        mlp_first(r, n_row, n_col, hidden, lambda: None, ())
        mlp_second(r, hidden, lambda part: None)
        up_weights(r, hidden, lambda j: None)
        mlp_branch(r, hidden)
        down_weights(r, lambda j: None)
        mlp_out(r)
        proj_weight_grad(r)

    ins = split_ins(tensors, *names) | dict(home=home, wproj=wproj, w1=w1, w2=w2)
    two = named_call(mlp_body, ins, outs, buffers, "mlp", **limit)
    gfield = (lend_xla(two.gfield[:TOK], n_row, n_col), vmem())
    ins = split_ins(tensors, "rel_rows", "rel_cols", "masks", "places_back", "marks_back", "ln1_gain", "ln1_bias")
    ins |= given(one, "qkv", "xw", "probs0", "probs1") | dict(wqkv=wqkv, wproj=wproj, gfield=gfield)
    outs = dict(
        gqkv=(sd(shapes[0], BF), vmem()),
        ret=(sd((FIELD, D), BF), vmem()),
        mid=(sd((16, D), F32), vmem()),
    )
    rows = v((4 * SLOT, D), BF)
    scratch = dict(gw=rows, gmix=rows, dqkv=v((12 * SLOT, D), BF))
    scratch |= dict(table=v((256, 128), BF), gtab=v((2, 128, 128), F32))

    def windows_body(r):
        back_prepare(r, n_row, n_col)
        back_mix(r)
        back_windows(r, n_row, n_col, ())
        back_weights(r, n_row, n_col, lambda n: None)
        back_return(r, n_row, n_col)
        norm_sums(r, n_row, n_col)

    three = named_call(windows_body, ins, outs, scratch, "windows", **limit)
    home = (return_xla(three.ret, n_row, n_col), vmem())
    ins = split_ins(tensors, "tokens", "ln1_gain", "ln1_bias") | dict(home2=home) | given(two, "grad_middle")
    outs = dict(input_grad=(sd((TOK, D), BF), vmem()))
    four = named_call(lambda r: back_last(r, n_row, n_col), ins, outs, dict(acc=v((TOK, D), F32)), "ends", **limit)
    grads = []
    for g in (three.gqkv, two.gproj, two.g1, two.g2):
        g = lax.psum_scatter(g, AXES, scatter_dimension=0, tiled=True)
        grads.append(lax.psum_scatter(g, "dp", scatter_dimension=1, tiled=True))
    line = jnp.arange(16)[:, None] == 12
    local = lax.psum(two.small, AXES)
    small = jnp.where(line, local, lax.psum(jnp.where(line, 0.0, local), "dp"))
    return grads, two.output, four.input_grad, small, lax.psum(three.mid, ("dp", *AXES))


def last_body(count, r):
    for i in range(4):
        r.__dict__["t" + str(i)][...] = r.__dict__["s" + str(i)][...].astype(F32)
    r.output_out[...] = r.output[...]
    r.input_grad_out[...] = r.input_grad[...]
    lines = ((r.mid, 10), (r.mid, 11), (r.mid, 8), (r.mid, 9), (r.small, 4), (r.small, 5), (r.small, 6), (r.small, 7))
    for i, (ref, line) in enumerate(lines):
        r.__dict__["v" + str(i)][...] = ref[line : line + 1, :].reshape(D)
    r.up[...] = jnp.concatenate([r.small[8 + i : 9 + i, :] for i in range(r.up.shape[0] // D)], 1).reshape(-1)
    tables = jnp.concatenate([r.mid[0:8, 128 * t : 128 * t + 128] for t in range(4)], 0)
    r.rows[...] = tables[0 : 2 * WIN - 1, :HEAD]
    r.cols[...] = pltpu.roll(tables, HEAD, 1)[0 : 2 * WIN - 1, :HEAD]
    r.stats[...] = jnp.sqrt(r.small[12:13, :5] / count)


def last_call(count, hidden, sums, output, input_grad, small, mid):
    sd = jax.ShapeDtypeStruct
    ins = {"s" + str(i): (s, vmem()) for i, s in enumerate(sums)}
    ins |= dict(output=(output, vmem()), input_grad=(input_grad, vmem()), small=(small, vmem()))
    ins |= dict(mid=(mid, vmem()))
    outs = {"t" + str(i): (sd(s.shape, F32), vmem()) for i, s in enumerate(sums)}
    outs |= dict(output_out=(sd((TOK, D), BF), vmem()), input_grad_out=(sd((TOK, D), BF), vmem()))
    outs |= {"v" + str(i): (sd((D,), F32), vmem()) for i in range(8)}
    outs |= dict(
        up=(sd((hidden,), F32), vmem()),
        rows=(sd((2 * WIN - 1, HEAD), F32), vmem()),
        cols=(sd((2 * WIN - 1, HEAD), F32), vmem()),
        stats=(sd((1, 5), F32), vmem()),
    )
    return named_call(functools.partial(last_body, count), ins, outs, {}, "last", vmem_limit_bytes=63 * MIB)


def on_device(
    n_dp, n_row, n_col,
    tokens, ln1_gain, ln1_bias, qkv_weight, query_bias, value_bias, rel_rows, rel_cols,
    proj_weight, proj_bias, ln2_gain, ln2_bias, fc1_weight, fc1_bias, fc2_weight, fc2_bias, cotangent,
):
    direct = (n_dp, n_row, n_col) == (2, 4, 4)
    tok = tokens.reshape(TOK, D)
    mask_values = np.zeros((16, 128), np.float32)
    mask_values[0, :64] = 1.0
    mask_values[1, 64:] = 1.0
    shared = dict(
        tokens=tok,
        cot=cotangent.reshape(TOK, D),
        ln1_gain=ln1_gain,
        ln1_bias=ln1_bias,
        rel_rows=rel_rows,
        rel_cols=rel_cols,
        masks=jnp.asarray(mask_values, BF),
    )
    tensors = shared | dict(
        query_bias=query_bias,
        value_bias=value_bias,
        proj_bias=proj_bias,
        ln2_gain=ln2_gain,
        ln2_bias=ln2_bias,
        fc1_bias=fc1_bias,
        fc2_bias=fc2_bias,
        places=jnp.asarray(table_places(False), BF),
        marks=jnp.asarray(key_marks(False), BF),
        places_back=jnp.asarray(table_places(True), BF),
        marks_back=jnp.asarray(key_marks(True), BF),
    )
    shards = (qkv_weight, proj_weight, fc1_weight, fc2_weight)
    shapes = [(s.shape[1] * n_row * n_col, s.shape[0] * n_dp) for s in shards]
    if direct:
        tensors |= dict(pick=jnp.asarray(pick_rows(), BF))
        done = block_call(n_row, n_col, shapes, tensors, [s.T for s in shards])
        sums = (done.o0, done.o1, done.o2, done.o3)
        rest = (done.output, done.input_grad, done.small, done.mid)
    else:
        weights = []
        for s in shards:
            s = lax.all_gather(s, AXES, axis=1, tiled=True)
            weights.append(lax.all_gather(s, "dp", axis=0, tiled=True).T)
        normed = norm(tok.astype(F32), ln1_gain.astype(F32), ln1_bias.astype(F32))[0].astype(BF)
        field = lend_xla(normed, n_row, n_col)
        sums, *rest = plain_block(n_row, n_col, shapes, tensors, weights, field)
    out = last_call(TOK * n_row * n_col * D, shapes[2][0], sums, *rest)
    return (
        out.output_out.reshape(tokens.shape),
        out.input_grad_out.reshape(tokens.shape),
        out.v0,
        out.v1,
        out.t0.T,
        out.v2,
        out.v3,
        out.rows,
        out.cols,
        out.t1.T,
        out.v4,
        out.v5,
        out.v6,
        out.t2.T,
        out.up,
        out.t3.T,
        out.v7,
        out.stats,
    )


def solution(mesh):
    tile = P("dp", "row", "col", None)
    weight = P("dp", AXES)
    sizes = [mesh.shape[a] for a in ("dp", "row", "col")]
    ins = [tile] + [P()] * 16
    for i in (3, 8, 12, 14):
        ins[i] = weight
    ins[16] = tile
    outs = [tile, tile] + [P()] * 16
    for i in (4, 9, 13, 15):
        outs[i] = weight
    outs[17] = P("dp", None)
    return jax.shard_map(
        functools.partial(on_device, *sizes),
        mesh=mesh,
        in_specs=tuple(ins),
        out_specs=tuple(outs),
        check_vma=False,
    )
```

```python
import functools
import types

import jax
import jax.numpy as jnp
import numpy as np
from jax import lax
from jax.experimental import pallas as pl
from jax.experimental.pallas import tpu as pltpu
from jax.sharding import PartitionSpec as P

HEADS = 12
HEAD = 64
WIN = 14
EPS = 1e-06
MESH = pl.DeviceIdType.MESH
AXES = ("row", "col")
F32 = jnp.float32
BF = jnp.bfloat16

D = HEADS * HEAD
TILE = 16
TOK = TILE * TILE
LO = 6
SLOT = 256
PAIRS = HEADS // 2
FIELD = 496
PICKED = 144
MIB = 2**20

LINKS = {
    (1, 0): (True, 160, 96, 256),
    (0, 1): (False, 0, 96, 352),
    (1, 1): (False, 96, 48, 448),
}


def nt(a, b):
    return lax.dot_general(a, b, (((1,), (1,)), ((), ())), preferred_element_type=F32)


def nn(a, b):
    return lax.dot_general(a, b, (((1,), (0,)), ((), ())), preferred_element_type=F32)


def tn(a, b):
    return lax.dot_general(a, b, (((0,), (0,)), ((), ())), preferred_element_type=F32)


def pick_rows():
    table = np.zeros((PICKED, TOK), np.float32)
    for base, first in ((0, 0), (96, TILE - LO)):
        for i in range((TILE - first) * LO):
            y, x = divmod(i, LO)
            table[base + i, (first + y) * TILE + TILE - LO + x] = 1.0
    return table


def table_places(back):
    place = np.zeros((256, 64), np.float32)
    for head in range(2):
        for r in range(2 * WIN - 1):
            for copy in range(2):
                row_lane = (64 + 28 * copy + r + 64 * head) % 128
                col_lane = (28 * copy + r + 64 * head) % 128
                place[128 * head + row_lane, 26 - r] = 1.0
                place[128 * head + col_lane, 32 + (r if back else 26 - r)] = 1.0
    return place


def key_marks(back):
    marks = np.zeros((2, SLOT, 128), np.float32)
    for head in range(2):
        for j in range(SLOT):
            k, l = divmod(j, 16)
            if k < WIN and l < WIN:
                for copy in range(2):
                    marks[head, j, (64 + 28 * copy + k + 64 * head) % 128] = 1.0
                    marks[head, j, (78 + 28 * copy + (13 - l if back else l) + 64 * head) % 128] = 1.0
            else:
                marks[head, j, (120 + 64 * head) % 128] = -1e30
    return marks


def lane_kinds(rows):
    lane = lax.broadcasted_iota(jnp.int32, (rows, 128), 1)
    kinds = []
    for head in range(2):
        at = (lane + 64 * head) % 128 if head else lane
        own = at < 64
        first = (at >= 64) & (at < 92)
        second = (at >= 92) & (at < 120)
        is_row = ((at >= 64) & (at < 78)) | ((at >= 92) & (at < 106))
        kinds.append((own, first, second, is_row, at == 120))
    return kinds


def window_index(w, row, col, n_row, n_col):
    place = lax.broadcasted_iota(jnp.int32, (SLOT, 1), 0)
    y = place // 16
    x = place - 16 * y
    a, b = w // 2, w % 2
    ry = WIN * (row + a) + y - TILE * row
    rx = WIN * (col + b) + x - TILE * col
    good = (y < WIN) & (x < WIN) & (ry < TILE) & (rx < TILE)
    if a:
        good = good & (row == n_row - 1)
    if b:
        good = good & (col == n_col - 1)
    up, left = ry < 0, rx < 0
    base = jnp.where(up, jnp.where(left, 448, 256), jnp.where(left, 352, 0))
    width = jnp.where(left, LO, TILE)
    index = base + jnp.where(up, ry + LO, ry) * width + jnp.where(left, rx + LO, rx)
    return jnp.where(good, index, -1)


def field_slots(row, col, n_row, n_col):
    at = lax.broadcasted_iota(jnp.int32, (FIELD, 1), 0)
    above = (at >= 256) & (at < 352)
    left = (at >= 352) & (at < 448)
    corner = at >= 448
    narrow = left | corner
    rest = jnp.where(corner, at - 448, jnp.where(left, at - 352, jnp.where(above, at - 256, at)))
    sixth = sum((rest >= LO * k).astype(jnp.int32) for k in range(1, TILE))
    ty = jnp.where(narrow, sixth, rest // TILE)
    tx = rest - ty * jnp.where(narrow, LO, TILE)
    ty = jnp.where(above | corner, ty - LO, ty)
    tx = jnp.where(narrow, tx - LO, tx)
    good = at < 484
    where = 0
    for t, place, n, stride, unit in ((ty, row, n_row, 2, 16), (tx, col, n_col, 1, 1)):
        y = TILE * place + t - WIN * place
        late = y >= WIN
        good = good & (y >= 0) & (jnp.logical_not(late) | (place == n - 1))
        where = where + jnp.where(late, stride * SLOT + unit * (y - WIN), unit * y)
    return jnp.where(good, where, -1)


def home_index(row, col, n_row, n_col):
    place = lax.broadcasted_iota(jnp.int32, (TOK, 1), 0)
    ty = place // TILE
    tx = place - TILE * ty
    down = (TILE * row + ty - WIN * row >= WIN) & (row < n_row - 1)
    right = (TILE * col + tx - WIN * col >= WIN) & (col < n_col - 1)
    near = TILE - LO
    return jnp.where(
        down,
        jnp.where(right, 448 + (ty - near) * LO + tx - near, 256 + (ty - near) * TILE + tx),
        jnp.where(right, 352 + ty * LO + tx - near, place),
    )


def one_hot(index, size):
    lane = lax.broadcasted_iota(jnp.int32, (index.shape[0], size), 1)
    return jnp.where(lane == index, 1.0, 0.0).astype(BF)


STEP = 64


def by_rows(body, sums):
    def step(i, kept):
        parts = body(pl.ds(pl.multiple_of(i * STEP, STEP), STEP))
        return tuple(k + sum(p[8 * q : 8 * q + 8] for q in range(STEP // 8)) for k, p in zip(kept, parts))

    return lax.fori_loop(0, TOK // STEP, step, (jnp.zeros((8, D), F32),) * sums)


def column_sum(v):
    return jnp.sum(v, 0, keepdims=True)


def norm(v, gain, bias):
    mean = jnp.mean(v, -1, keepdims=True)
    center = v - mean
    inverse = lax.rsqrt(jnp.mean(center * center, -1, keepdims=True) + EPS)
    xhat = center * inverse
    return xhat * gain + bias, xhat, inverse


def norm_back(grad, xhat, inverse, gain):
    d = grad * gain
    return inverse * (
        d - jnp.mean(d, -1, keepdims=True) - xhat * jnp.mean(d * xhat, -1, keepdims=True)
    )


def grid_place():
    return lax.axis_index("dp"), lax.axis_index("row"), lax.axis_index("col")


def exists(step, row, col, n_row, n_col):
    r, c = row + step[0], col + step[1]
    return (r >= 0) & (r < n_row) & (c >= 0) & (c < n_col)


CORNERS = ((1, 1), (-1, -1))


def greet(n_row, n_col):
    dp, row, col = grid_place()
    barrier = pltpu.get_barrier_semaphore()
    others = [(dp, row, lax.rem(col + d, n_col)) for d in (1, 2, 3)]
    others += [(dp, lax.rem(row + d, n_row), col) for d in (1, 2, 3)]
    others.append((1 - dp, row, col))
    for other in others:
        pl.semaphore_signal(barrier, inc=1, device_id=other, device_id_type=MESH)
    count = len(others)
    for step in CORNERS:
        there = exists(step, row, col, n_row, n_col)

        @pl.when(there)
        def _():
            pl.semaphore_signal(
                barrier, inc=1, device_id=(dp, row + step[0], col + step[1]), device_id_type=MESH
            )

        count = count + jnp.where(there, 1, 0)
    pl.semaphore_wait(barrier, count)


class Halo:
    def __init__(self, source, picked, land, back, send, recv, n_row, n_col):
        self.source, self.picked, self.land, self.back = source, picked, land, back
        self.send, self.recv, self.size = send, recv, (n_row, n_col)

    def copies(self):
        dp, row, col = grid_place()
        sign = -1 if self.back else 1
        for i, ((dr, dc), (own, first, rows, there)) in enumerate(LINKS.items()):
            if self.back:
                src = self.source.at[pl.ds(there, rows)]
            else:
                src = (self.source if own else self.picked).at[pl.ds(first, rows)]
            copy = pltpu.make_async_remote_copy(
                src,
                self.land.at[pl.ds(there, rows)],
                self.send.at[i],
                self.recv.at[i],
                device_id=(dp, row + sign * dr, col + sign * dc),
                device_id_type=MESH,
            )
            goes = exists((sign * dr, sign * dc), row, col, *self.size)
            comes = exists((-sign * dr, -sign * dc), row, col, *self.size)
            yield copy, goes, comes

    def start(self):
        for copy, goes, _ in self.copies():
            pl.when(goes)(copy.start)

    def arrive(self):
        for copy, _, comes in self.copies():
            pl.when(comes)(copy.wait_recv)

    def gone(self):
        for copy, goes, _ in self.copies():
            pl.when(goes)(copy.wait_send)

    def wait(self):
        self.arrive()
        self.gone()


def pick_start(halo, pick):
    halo.picked[...] = nn(pick[...], halo.source[pl.ds(0, TOK), :]).astype(BF)
    halo.start()


def halo_xla(blocks, back, n_row, n_col):
    sign = -1 if back else 1
    pieces = [blocks[0]]
    for (dr, dc), block in zip(LINKS, blocks[1:]):
        dr, dc = sign * dr, sign * dc
        pairs = [
            (r * n_col + c, (r + dr) * n_col + c + dc)
            for r in range(n_row)
            for c in range(n_col)
            if 0 <= r + dr < n_row and 0 <= c + dc < n_col
        ]
        pieces.append(lax.ppermute(block, AXES, pairs))
    return jnp.concatenate(pieces, 0)


def lend_xla(own, n_row, n_col):
    grid = own.reshape(TILE, TILE, -1)
    corner = grid[TILE - LO :, TILE - LO :].reshape(LO * LO, -1)
    blocks = [
        own,
        own[TILE * (TILE - LO) :],
        grid[:, TILE - LO :].reshape(TILE * LO, -1),
        jnp.pad(corner, ((0, 48 - LO * LO), (0, 0))),
    ]
    return halo_xla(blocks, False, n_row, n_col)


def return_xla(field, n_row, n_col):
    return halo_xla([field[:256], field[256:352], field[352:448], field[448:]], True, n_row, n_col)


def blocks_of(shapes):
    return [(n // 16, k // 2) for n, k in shapes]


def rows_at(first, count):
    return pl.ds(pl.multiple_of(first, 16), count)


LINE, OWN, LINE_CORE, FAR, NEAR_CORE, FAR_CORE, CORE = range(10, 17)


class Gather:
    SEMS = 17

    def __init__(self, full, shard, block, half, send, recv, part=0, parts=1):
        self.dp, self.row, self.col = grid_place()
        width = half // parts
        self.full, self.shard, self.b = full, shard.at[:, pl.ds(part * width, width)], block
        self.send, self.recv = send, recv
        self.lanes = pl.ds(pl.multiple_of(self.dp * half + part * width, 128), width)
        self.other = pl.ds(pl.multiple_of((1 - self.dp) * half + part * width, 128), width)

    def block(self, flip, place):
        return (jnp.bitwise_xor(self.row, flip) * 4 + place) * self.b

    def came(self, d):
        return lax.rem(self.col + 4 - d, 4)

    def copy(self, i, first, count, land, target, shard=False):
        core = target == CORE
        if core:
            device = (1 - self.dp, self.row, self.col)
        elif isinstance(target, tuple):
            device = (self.dp, self.row, lax.rem(self.col + target[0], 4))
        else:
            device = (self.dp, jnp.bitwise_xor(self.row, target), self.col)

        def make(src, dst):
            return pltpu.make_async_remote_copy(
                src, dst, self.send.at[i], self.recv.at[i], device_id=device, device_id_type=MESH
            )

        def out():
            there = self.full.at[rows_at(first, count), self.lanes]
            return make(self.shard if shard else there, there)

        def come():
            here = self.full.at[rows_at(land, count), self.other if core else self.lanes]
            return make(here, here)

        return out, come

    def copies(self, k):
        b = self.b
        own = self.block(0, self.col)
        if k == LINE:
            return [
                self.copy(d - 1, own, b, self.block(0, self.came(d)), (d,), True) for d in (1, 2, 3)
            ]
        if k == OWN:
            return [self.copy(2 + f, own, b, self.block(f, self.col), f, True) for f in (1, 2)]
        if k < LINE:
            at = self.came(k)
            return [
                self.copy(4 + 2 * k, self.block(0, at), b, self.block(1, at), 1),
                self.copy(5 + 2 * k, self.block(0, at), b, self.block(2, at), 2),
            ]
        if k == LINE_CORE:
            return [self.copy(5, self.block(0, 0), 4 * b, self.block(0, 0), CORE)]
        if k == FAR:
            return [
                self.copy(12, self.block(2, 0), 2 * b, self.block(3, 0), 1),
                self.copy(13, self.block(1, 2), 2 * b, self.block(3, 2), 2),
            ]
        if k == NEAR_CORE:
            return [self.copy(13 + f, self.block(f, 0), 4 * b, self.block(f, 0), CORE) for f in (1, 2)]
        return [self.copy(16, self.block(3, 0), 4 * b, self.block(3, 0), CORE)]

    def start(self, *kinds):
        for k in kinds:
            for out, _ in self.copies(k):
                out().start()

    def arrive(self, *kinds):
        for k in kinds:
            for _, come in self.copies(k):
                come().wait_recv()

    def step(self, n):
        if n == 0:
            for d in (1, 2, 3):
                self.copies(LINE)[d - 1][1]().wait_recv()
                self.start(d)
            self.start(LINE_CORE)
        elif n == 1:
            self.arrive(OWN, 1, 2, 3)
            self.start(FAR, NEAR_CORE)
        else:
            self.arrive(FAR)
            self.start(FAR_CORE)

    def whole(self):
        self.arrive(LINE_CORE, NEAR_CORE, FAR_CORE)

    def finish(self):
        for k in (LINE, OWN, 1, 2, 3, LINE_CORE, FAR, NEAR_CORE, FAR_CORE):
            for out, _ in self.copies(k):
                out().wait_send()


class Reduce:
    def __init__(self, grad, total, base, land, come, block, half, pieces, parts, send, recv):
        self.dp, self.row, self.col = grid_place()
        self.grad, self.total, self.base, self.come = grad, total, base, come
        self.land, self.land_row, mirrored = land
        self.land_there = self.dp * half if mirrored else 0
        self.land_here = (1 - self.dp) * half if mirrored else 0
        self.b, self.h, self.send, self.recv = block, half, send, recv
        self.pieces, self.parts, self.width = pieces, parts, half // parts
        self.other = pl.ds(pl.multiple_of((1 - self.dp) * half, 128), half)

    def side(self, base, part, width):
        return pl.ds(pl.multiple_of(base + part * width, 128), width)

    def at(self, flip, place=0):
        return (jnp.bitwise_xor(self.row, flip) * 4 + place) * self.b

    def lanes(self, part):
        return pl.ds(pl.multiple_of(self.base + part * self.width, 128), self.width)

    def came(self, first, count, part):
        return self.come.at[rows_at(first, count), pl.ds(part * self.width, self.width)]

    def tot(self, first, count, part):
        return self.total.at[rows_at(first, count), self.lanes(part)]

    def sem(self, k, part):
        if k == 0:
            return part
        return self.pieces + 7 * part + {1: 0, 2: 2, 3: 4}[k]

    def copies(self, k, part):
        b = self.b
        if k == 0:
            n = 16 * b // self.pieces
            there = self.land.at[rows_at(self.land_row + part * n, n), self.side(self.land_there, 0, self.h)]
            plan = [(self.grad.at[rows_at(part * n, n), self.other], there, (1 - self.dp, self.row, self.col))]
        elif k == 1:
            plan = [
                (
                    self.tot(self.at(3, 2 * half), 2 * b, part),
                    self.came(2 * half * b, 2 * b, part),
                    (self.dp, jnp.bitwise_xor(self.row, 1 + half), self.col),
                )
                for half in (0, 1)
            ]
        elif k == 2:
            plan = [
                (
                    self.tot(self.at(flip), 4 * b, part),
                    self.came(4 * flip * b, 4 * b, part),
                    (self.dp, jnp.bitwise_xor(self.row, flip), self.col),
                )
                for flip in (1, 2)
            ]
        else:
            plan = []
            for d in (1, 2, 3):
                to = lax.rem(self.col + d, 4)
                plan.append(
                    (
                        self.tot(self.at(0, to), b, part),
                        self.came((11 + d) * b, b, part),
                        (self.dp, self.row, to),
                    )
                )
        base = self.sem(k, part)
        return [
            pltpu.make_async_remote_copy(
                src, dst, self.send.at[base + i], self.recv.at[base + i], device_id=dev, device_id_type=MESH
            )
            for i, (src, dst, dev) in enumerate(plan)
        ]

    def start(self, k, part=0):
        for copy in self.copies(k, part):
            copy.start()

    def arrive(self, k, part=0):
        for copy in self.copies(k, part):
            copy.wait_recv()

    def sum_rows(self, first, count, froms, part, source=None, base=0):
        most = (256 if len(froms) == 1 else 96) * 384
        step = next(n for n in range(count, 0, -16) if count % n == 0 and n * self.width <= most)
        lanes = self.lanes(part)
        side = self.side(base, part, self.width)
        source = self.come if source is None else source

        def body(i, _):
            at = rows_at(first + i * step, step)
            value = self.total[at, lanes]
            if len(froms) == 1:
                value = value + source[rows_at(froms[0] + i * step, step), side]
            else:
                value = value.astype(F32)
                for f in froms:
                    value = value + source[rows_at(f + i * step, step), side].astype(F32)
                value = value.astype(BF)
            self.total[at, lanes] = value
            return 0

        lax.fori_loop(0, count // step, body, 0)

    def add_piece(self, piece):
        n = 16 * self.b // self.pieces
        self.arrive(0, piece)
        for part in range(self.parts):
            self.sum_rows(piece * n, n, (self.land_row + piece * n,), part, self.land, self.land_here)

    def step(self, k, part=0):
        b = self.b
        if k == 0:
            for piece in range(self.pieces):
                self.add_piece(piece)
            for part in range(1, self.parts):
                self.start(1, part)
            part = 0
        else:
            self.arrive(k, part)
            if k == 1:
                self.sum_rows(self.at(2), 2 * b, (0,), part)
                self.sum_rows(self.at(1, 2), 2 * b, (2 * b,), part)
            else:
                self.sum_rows(self.at(0), 4 * b, (4 * b, 8 * b), part)
        self.start(k + 1, part)

    def result(self, out, part=0):
        b = self.b
        self.arrive(3, part)
        value = self.total[rows_at(self.at(0, self.col), b), self.lanes(part)].astype(F32)
        side = pl.ds(part * self.width, self.width)
        for d in (1, 2, 3):
            value = value + self.come[pl.ds((11 + d) * b, b), side].astype(F32)
        out[:, side] = value

    def gone(self):
        for piece in range(self.pieces):
            self.copies(0, piece)[0].wait_send()

    def finish(self):
        for part in range(self.parts):
            for k in (1, 2, 3):
                for copy in self.copies(k, part):
                    copy.wait_send()


def vmem():
    return pl.BlockSpec(memory_space=pltpu.VMEM)


def hbm():
    return pl.BlockSpec(memory_space=pl.ANY)


def dma(*n):
    return pltpu.SemaphoreType.DMA(n)


def named_call(body, ins, outs, scratch, name, **params):
    names = [*ins, *outs, *scratch]

    def kernel(*refs):
        body(types.SimpleNamespace(**dict(zip(names, refs))))

    result = pl.pallas_call(
        kernel,
        name=name,
        out_shape=[shape for shape, _ in outs.values()],
        in_specs=[spec for _, spec in ins.values()],
        out_specs=[spec for _, spec in outs.values()],
        scratch_shapes=list(scratch.values()),
        compiler_params=pltpu.CompilerParams(**params),
    )(*[array for array, _ in ins.values()])
    return types.SimpleNamespace(**dict(zip(outs, result)))


def vector(ref):
    return ref[...].astype(F32).reshape(1, -1)


def joint_table(rel_rows, rel_cols):
    parts = [rel_rows[...], jnp.zeros((5, HEAD), BF), rel_cols[...], jnp.zeros((5, HEAD), BF)]
    table = jnp.concatenate([p.astype(F32) for p in parts], 0)
    return jnp.concatenate([table, table], 1).astype(BF)


def table_kernel_value(places, table):
    value = nn(places, table)
    line = lax.broadcasted_iota(jnp.int32, value.shape, 0)
    lane = lax.broadcasted_iota(jnp.int32, value.shape, 1)
    return jnp.where((line < 128) == (lane < 64), value, 0.0).astype(BF)


def narrow(v, wide):
    if wide:
        return v
    return v.astype(F32).reshape(-1, 16, 128)[:, :8].reshape(-1, 128).astype(v.dtype)


def widen(v, wide):
    if not wide:
        v = v.reshape(-1, 8, 128)
        v = jnp.concatenate([v, jnp.zeros_like(v)], 1).reshape(-1, 128)
    return v.astype(BF)


def spread(a, back, line):
    rows, cols = [], []
    for y in range(a.shape[0] // line):
        part = a[line * y : line * y + line, :]
        rows.append(pltpu.roll(part, 13 - y if back else (115 + y) % 128, 1))
        cols.append(pltpu.roll(part, 50 if back else 65, 1, stride=1, stride_axis=0))
    return jnp.concatenate(rows, 0), jnp.concatenate(cols, 0)


def pair_place(w, pair):
    return pl.multiple_of(w * SLOT, SLOT), pl.multiple_of(pair * 128, 128)


def attend_pair(w, place, pair, n, wide, qkv, table, marks, masks, probs, mixed):
    r0, l0 = pair_place(w, pair)
    q2 = narrow(qkv[pl.ds(r0, n), pl.ds(l0, 128)], wide)
    count = q2.shape[0]
    k2 = qkv[pl.ds(r0, SLOT), pl.ds(D + l0, 128)]
    v2 = qkv[pl.ds(r0, SLOT), pl.ds(2 * D + l0, 128)]
    a2 = nt(q2, table[...])
    qf = q2.astype(F32) * HEAD**-0.5
    kinds = lane_kinds(count)
    outs = []
    for head in range(2):
        own, first, second, is_row, one = kinds[head]
        rows, cols = spread(a2[:, 128 * head : 128 * head + 128], False, count // (n // 16))
        bias = jnp.where(is_row, rows, cols)
        high = bias.astype(BF).astype(F32)
        low = jnp.where(second, bias - high, jnp.where(one, 1.0, 0.0))
        aug = jnp.where(own, qf, jnp.where(first, high, low)).astype(BF)
        keys = k2 * masks[head : head + 1, :] + marks[head]
        scores = nt(aug, keys)
        top = jnp.max(scores, -1, keepdims=True)
        e = jnp.exp(scores - top)
        p = (e * (1.0 / jnp.sum(e, -1, keepdims=True))).astype(BF)
        probs[2 * place + head, 0:count, :] = p
        outs.append(nn(p, v2))
    mixed[pl.ds(r0, n), pl.ds(l0, 128)] = widen(jnp.where(kinds[0][0], outs[0], outs[1]), wide)


def attend_back_pair(w, place, pair, n, wide, qkv, gmix, probs, table, marks, masks, dqkv, gtab):
    r0, l0 = pair_place(w, pair)
    scale = HEAD**-0.5
    q2 = narrow(qkv[pl.ds(r0, n), pl.ds(l0, 128)], wide)
    count = q2.shape[0]
    k2 = qkv[pl.ds(r0, SLOT), pl.ds(D + l0, 128)]
    v2 = qkv[pl.ds(r0, SLOT), pl.ds(2 * D + l0, 128)]
    g2 = narrow(gmix[pl.ds(r0, n), pl.ds(l0, 128)], wide)
    kinds = lane_kinds(count)
    dq, dk, dv = [], [], []
    for head in range(2):
        own, first, second, is_row, one = kinds[head]
        mask = masks[head : head + 1, :]
        p = probs[2 * place + head, 0:count, :]
        pf = p.astype(F32)
        dp = nt(g2, v2 * mask)
        ds = (pf * (dp - jnp.sum(pf * dp, -1, keepdims=True))).astype(BF)
        keys = k2 * (mask * jnp.asarray(scale, BF)) + marks[head]
        dqa = nn(ds, keys)
        marked = jnp.where(first | second, dqa, 0.0)
        rows, _ = spread(jnp.where(is_row, marked, 0.0), True, count // (n // 16))
        _, cols = spread(jnp.where(is_row, 0.0, marked), True, count // (n // 16))
        back = rows + cols
        at = lax.broadcasted_iota(jnp.int32, (count, 128), 1)
        if head:
            at = (at + 64) % 128
        high = back.astype(BF).astype(F32)
        split = jnp.where((at < 28) | ((at >= 64) & (at < 92)), high, back - high).astype(BF)
        extra = nn(split, table[128 * head : 128 * head + 128, :])
        dq.append(dqa + extra)
        gtab[head] += tn(split, q2)
        dk.append(tn(ds, q2))
        dv.append(tn(p, g2))
    left = lane_kinds(SLOT)[0][0]
    dqkv[pl.ds(r0, n), pl.ds(l0, 128)] = widen(jnp.where(kinds[0][0], dq[0], dq[1]), wide)
    dqkv[pl.ds(4 * SLOT + r0, SLOT), pl.ds(l0, 128)] = (jnp.where(left, dk[0], dk[1]) * scale).astype(BF)
    dqkv[pl.ds(8 * SLOT + r0, SLOT), pl.ds(l0, 128)] = jnp.where(left, dv[0], dv[1]).astype(BF)


TOGETHER = 3


def over_windows(body, hooks, n_row, n_col):
    _, row, col = grid_place()
    for w in range(4):
        a, b = w // 2, w % 2
        n = 16 * (TILE * n_row - WIN * n_row if a else WIN)
        good = True
        if a:
            good = row == n_row - 1
        if b:
            good = good & (col == n_col - 1)

        def step(i, _):
            def work():
                for pair in range(TOGETHER):
                    pair = i * TOGETHER + pair
                    body(w, PAIRS * b + pair, pair, n, b == 0)

            if w:
                pl.when(good)(work)
            else:
                work()
            for when, hook in hooks:
                if when // PAIRS == w:
                    pl.when(i == when % PAIRS // TOGETHER)(hook)
            return 0

        lax.fori_loop(0, PAIRS // TOGETHER, step, 0)


def attend_part(r, n_row, n_col, hooks, between):
    _, row, col = grid_place()
    biases = (vector(r.query_bias), None, vector(r.value_bias))
    for part, bias in enumerate(biases):
        for n in range(3):
            at = part * D + 256 * n
            value = nt(r.xw[...], r.wqkv[pl.ds(at, 256), :])
            if bias is not None:
                value = value + bias[:, 256 * n : 256 * n + 256]
            r.qkv[:, pl.ds(at, 256)] = value.astype(BF)
        between(part)

    def body(w, place, pair, n, wide):
        probs = (r.probs0, r.probs1)[w // 2]
        attend_pair(w, place, pair, n, wide, r.qkv, r.table, r.marks, r.masks, probs, r.mixed)

    over_windows(body, hooks, n_row, n_col)
    hot = one_hot(field_slots(row, col, n_row, n_col), 4 * SLOT)
    r.ret[...] = nn(hot, r.mixed[...]).astype(BF)


def cut_windows(source, land, n_row, n_col, w):
    _, row, col = grid_place()
    hot = one_hot(window_index(w, row, col, n_row, n_col), FIELD)
    land[pl.ds(w * SLOT, SLOT), :] = nn(hot, source[...]).astype(BF)


def mlp_first(r, n_row, n_col, hidden, between, hooks):
    _, row, col = grid_place()
    hot = one_hot(home_index(row, col, n_row, n_col), FIELD)
    r.mixed_own[...] = nn(hot, r.home[...]).astype(BF)
    r.acc[...] = nt(r.mixed_own[...], r.wproj[...])
    shift, gain, bias = vector(r.proj_bias), vector(r.ln2_gain), vector(r.ln2_bias)

    def rows_body(rows):
        attended = (r.acc[rows, :] + shift).astype(BF)
        r.attended[rows, :] = attended
        middle = r.tokens[rows, :].astype(F32) + attended.astype(F32)
        r.n2[rows, :] = norm(middle, gain, bias)[0].astype(BF)
        return ()

    by_rows(rows_body, 0)
    between()
    up_bias = vector(r.fc1_bias)
    for line in range(hidden // D):
        r.up_bias[line : line + 1, :] = up_bias[:, line * D : line * D + D]

    def chunk(j, _):
        at = pl.multiple_of(j * 256, 256)
        lane = pl.multiple_of(lax.rem(j, 3) * 256, 256)
        u = nt(r.n2[...], r.w1[pl.ds(at, 256), :]) + r.up_bias[pl.ds(j // 3, 1), pl.ds(lane, 256)]
        cdf = 0.5 * (1.0 + lax.erf(u * 0.7071067811865476))
        r.act[:, pl.ds(at, 256)] = (u * cdf).astype(BF)
        r.slope[:, pl.ds(at, 256)] = (cdf + u * (jnp.exp(-0.5 * u * u) * 0.3989422804014327)).astype(BF)
        for when, hook in hooks:
            pl.when(j == when)(hook)
        return 0

    lax.fori_loop(0, hidden // 256, chunk, 0)


PARTS = 3


def mlp_second(r, hidden, ready):
    r.acc[...] = jnp.zeros_like(r.acc)
    r.small[...] = jnp.zeros_like(r.small)
    n = hidden // (2 * PARTS)
    for part in range(PARTS):
        ready(part)

        def chunk(i, _):
            at = pl.multiple_of((i * PARTS + part) * n, n)
            wide = pl.ds(at, n)
            gu = (nn(r.cot[...], r.w2[:, wide]) * r.slope[:, wide].astype(F32)).astype(BF)
            r.gu[:, wide] = gu
            r.acc[...] += nn(gu, r.w1[wide, :])
            r.up_sum[:, wide] = jnp.sum(gu.astype(F32), 0, keepdims=True)
            return 0

        lax.fori_loop(0, 2, chunk, 0)
    for line in range(hidden // D):
        r.small[8 + line : 9 + line, :] = r.up_sum[:, line * D : line * D + D]
    gain, bias = vector(r.ln2_gain), vector(r.ln2_bias)

    def rows_body(rows):
        middle = r.tokens[rows, :].astype(F32) + r.attended[rows, :].astype(F32)
        _, xhat, inverse = norm(middle, gain, bias)
        grad = r.acc[rows, :]
        cf = r.cot[rows, :].astype(F32)
        gm = cf + norm_back(grad, xhat, inverse, gain)
        r.grad_middle[rows, :] = gm
        low = gm.astype(BF)
        r.gfield[rows, :] = low
        return low.astype(F32), grad * xhat, grad, cf

    for line, value in enumerate(by_rows(rows_body, 4)):
        r.small[4 + line : 5 + line, :] = column_sum(value)


def mlp_branch(r, hidden):
    r.acc[...] = jnp.zeros_like(r.acc)

    def chunk(j, _):
        wide = pl.ds(pl.multiple_of(j * 512, 512), 512)
        r.acc[...] += nt(r.act[:, wide], r.w2[:, wide])
        return 0

    lax.fori_loop(0, hidden // 512, chunk, 0)


def mlp_out(r):
    bias = vector(r.fc2_bias)

    def rows_body(rows):
        att = r.attended[rows, :].astype(F32)
        tok = r.tokens[rows, :].astype(F32)
        middle = tok + att
        br = r.acc[rows, :] + bias
        result = middle + br
        r.output[rows, :] = result.astype(BF)
        return tuple(v * v for v in (tok, middle, result, att, br))

    lane = lax.broadcasted_iota(jnp.int32, (1, D), 1)
    stats = jnp.zeros((1, D), F32)
    for n, v in enumerate(by_rows(rows_body, 5)):
        stats = jnp.where(lane == n, jnp.sum(column_sum(v), 1, keepdims=True), stats)
    r.small[12:13, :] = stats


UP_PIECES, DOWN_PIECES = 12, 6
SENT = (3, 1, 4, 3)
LANES = (PARTS, 1, PARTS, PARTS)


def up_weights(r, hidden, sent):
    def up(j, _):
        n = hidden // UP_PIECES
        at = pl.multiple_of(j * n, n)
        r.g1[pl.ds(at, n), :] = tn(r.gu[:, pl.ds(at, n)], r.n2[...]).astype(BF)
        sent(j)
        return 0

    lax.fori_loop(0, UP_PIECES, up, 0)


def down_weights(r, sent):
    r.cot_t[...] = r.cot[...].T

    def down(j, _):
        n = D // DOWN_PIECES
        at = pl.multiple_of(j * n, n)
        r.g2[pl.ds(at, n), :] = nn(r.cot_t[pl.ds(at, n), :], r.act[...]).astype(BF)
        sent(j)
        return 0

    lax.fori_loop(0, DOWN_PIECES, down, 0)


def proj_weight_grad(r):
    def chunk(n, _):
        at = pl.multiple_of(n * 256, 256)
        r.gproj[pl.ds(at, 256), :] = tn(r.gfield[pl.ds(0, TOK), pl.ds(at, 256)], r.mixed_own[...]).astype(BF)
        return 0

    lax.fori_loop(0, D // 256, chunk, 0)


def prepare(r):
    r.table[...] = table_kernel_value(r.places[...], joint_table(r.rel_rows, r.rel_cols))
    r.mixed[...] = jnp.zeros_like(r.mixed)


def back_prepare(r, n_row, n_col):
    r.table[...] = table_kernel_value(r.places_back[...], joint_table(r.rel_rows, r.rel_cols))
    r.gtab[...] = jnp.zeros_like(r.gtab)
    r.dqkv[...] = jnp.zeros_like(r.dqkv)
    for w in range(4):
        cut_windows(r.gfield, r.gw, n_row, n_col, w)


def back_mix(r):
    def mix(n, _):
        at = pl.multiple_of(n * 256, 256)
        r.gmix[:, pl.ds(at, 256)] = nn(r.gw[...], r.wproj[:, pl.ds(at, 256)]).astype(BF)
        return 0

    lax.fori_loop(0, 3, mix, 0)


def back_windows(r, n_row, n_col, hooks):
    def body(w, place, pair, n, wide):
        probs = (r.probs0, r.probs1)[w // 2]
        attend_back_pair(
            w, place, pair, n, wide, r.qkv, r.gmix, probs, r.table, r.marks_back, r.masks, r.dqkv, r.gtab
        )

    over_windows(body, hooks, n_row, n_col)


def back_weights(r, n_row, n_col, sent):
    for n in range(9):
        rows, lanes = pl.ds(n // 3 * 4 * SLOT, 4 * SLOT), pl.ds(n % 3 * 256, 256)
        r.gqkv[pl.ds(256 * n, 256), :] = tn(r.dqkv[rows, lanes], r.xw[...]).astype(BF)
        sent(n)
    ones = jnp.ones((16, 4 * SLOT), BF)
    r.mid[...] = jnp.zeros_like(r.mid)
    r.mid[8:9, :] = nn(ones, r.dqkv[pl.ds(0, 4 * SLOT), :])[0:1, :]
    r.mid[9:10, :] = nn(ones, r.dqkv[pl.ds(8 * SLOT, 4 * SLOT), :])[0:1, :]
    lane = lax.broadcasted_iota(jnp.int32, (128, 128), 1)
    left = jnp.where(lane < 64, r.gtab[0], 0.0)
    right = jnp.where(lane >= 64, r.gtab[1], 0.0)
    tab = lax.dot_general(
        r.places_back[...].astype(F32),
        jnp.concatenate([left, right], 0),
        (((0,), (0,)), ((), ())),
        precision=lax.Precision.HIGHEST,
        preferred_element_type=F32,
    )
    tab = tab + pltpu.roll(tab, HEAD, 1)
    low = lax.broadcasted_iota(jnp.int32, (32, 128), 1) < HEAD
    tab = jnp.where(low, tab[:32], tab[32:])
    for t in range(4):
        r.mid[0:8, 128 * t : 128 * t + 128] = tab[8 * t : 8 * t + 8, :]


def back_return(r, n_row, n_col):
    _, row, col = grid_place()
    for n in range(3):
        value = 0
        for part in range(3):
            rows = pl.ds(4 * part * SLOT, 4 * SLOT)
            value = value + nn(r.dqkv[rows, :], r.wqkv[pl.ds(part * D, D), pl.ds(256 * n, 256)])
        r.gw[:, pl.ds(256 * n, 256)] = value.astype(BF)
    hot = one_hot(field_slots(row, col, n_row, n_col), 4 * SLOT)
    r.ret[...] = nn(hot, r.gw[...]).astype(BF)


def norm_sums(r, n_row, n_col):
    _, row, col = grid_place()
    hot = one_hot(field_slots(row, col, n_row, n_col), 4 * SLOT)
    r.gmix[pl.ds(0, FIELD), :] = nn(hot, r.xw[...]).astype(BF)
    bias = vector(r.ln1_bias)

    def step(i, kept):
        rows = pl.ds(pl.multiple_of(i * 16, 16), 16)
        grad = r.ret[rows, :].astype(F32)
        parts = (grad * (r.gmix[rows, :].astype(F32) - bias), grad)
        return tuple(k + p[:8] + p[8:] for k, p in zip(kept, parts))

    scaled, total = lax.fori_loop(0, FIELD // 16, step, (jnp.zeros((8, D), F32),) * 2)
    r.mid[10:11, :] = column_sum(scaled) / vector(r.ln1_gain)
    r.mid[11:12, :] = column_sum(total)


def back_last(r, n_row, n_col):
    _, row, col = grid_place()
    hot = one_hot(home_index(row, col, n_row, n_col), FIELD)
    r.acc[...] = nn(hot, r.home2[...])
    gain, bias = vector(r.ln1_gain), vector(r.ln1_bias)

    def rows_body(rows):
        grad = r.acc[rows, :]
        _, xhat, inverse = norm(r.tokens[rows, :].astype(F32), gain, bias)
        r.input_grad[rows, :] = (r.grad_middle[rows, :] + norm_back(grad, xhat, inverse, gain)).astype(BF)
        return ()

    by_rows(rows_body, 0)


class Small:
    def __init__(self, value, come, send, recv, keep=None):
        self.dp, self.row, self.col = grid_place()
        self.value, self.come, self.send, self.recv, self.keep = value, come, send, recv, keep

    def copies(self, s):
        dp, row, col = self.dp, self.row, self.col
        plan = (
            [(dp, row, lax.rem(col + d, 4)) for d in (1, 2, 3)],
            [(dp, lax.rem(row + d, 4), col) for d in (1, 2, 3)],
            [(1 - dp, row, col)],
        )[s]
        return [
            pltpu.make_async_remote_copy(
                self.value, self.come.at[3 * s + i], self.send.at[3 * s + i], self.recv.at[3 * s + i],
                device_id=other, device_id_type=MESH,
            )
            for i, other in enumerate(plan)
        ]

    def start(self, s=0):
        for copy in self.copies(s):
            copy.start()

    def step(self, s):
        total = self.value[...]
        for i, copy in enumerate(self.copies(s)):
            copy.wait()
            value = self.come[3 * s + i]
            if s == 2 and self.keep is not None:
                line = lax.broadcasted_iota(jnp.int32, value.shape, 0)
                value = jnp.where(line == self.keep, 0.0, value)
            total = total + value
        self.value[...] = total
        if s < 2:
            self.start(s + 1)


GATHERS = ((0, 0, 1), (1, 0, 1), *((i, part, PARTS) for i in (2, 3) for part in range(PARTS)))


def block_body(n_row, n_col, shapes, hidden, ins, outs, r):
    dp, row, col = grid_place()
    loads = []
    for n, (name, source) in enumerate(ins):
        loads.append(pltpu.make_async_copy(source, r.__dict__[name], r.load_sem.at[n]))
        loads[-1].start()
    rest = FIELD - TOK

    def leaving(n):
        name, there = outs[n]
        return pltpu.make_async_copy(r.__dict__[name], there, r.leave_sem.at[n])

    def leave(n):
        leaving(n).start()

    r.gfield, r.home2 = r.field, r.home
    for ref in (r.field, r.home):
        ref[pl.ds(TOK, rest), :] = jnp.zeros((rest, D), BF)
    greet(n_row, n_col)
    for load in loads:
        load.wait()
    blocks = blocks_of(shapes)
    fulls, shards = (r.wqkv, r.wproj, r.w1, r.w2), (r.s0, r.s1, r.s2, r.s3)
    gathers = [
        Gather(fulls[i], shards[i], *blocks[i], r.gather_sem.at[0, n], r.gather_sem.at[1, n], part, parts)
        for n, (i, part, parts) in enumerate(GATHERS)
    ]
    qkv_way, proj_way = gathers[:2]
    up_ways, down_ways = gathers[2 : 2 + PARTS], gathers[2 + PARTS :]
    qkv_way.start(LINE, OWN)
    gain, bias = vector(r.ln1_gain), vector(r.ln1_bias)

    def rows_body(rows):
        r.field[rows, :] = norm(r.tokens[rows, :].astype(F32), gain, bias)[0].astype(BF)
        return ()

    by_rows(rows_body, 0)
    size = (n_row, n_col)
    lend = Halo(r.field, r.picked, r.field, False, r.lend_sem.at[0], r.lend_sem.at[1], *size)
    give = Halo(r.ret, None, r.home, True, r.give_sem.at[0], r.give_sem.at[1], *size)
    lend2 = Halo(r.gfield, r.picked, r.gfield, False, r.lend_sem.at[2], r.lend_sem.at[3], *size)
    give2 = Halo(r.ret, None, r.home2, True, r.give_sem.at[2], r.give_sem.at[3], *size)
    pick_start(lend, r.pick)
    local = []
    for way in gathers[1:]:
        way.start(OWN)
    for i, way in enumerate(gathers):
        own = way.full.at[rows_at(way.block(0, way.col), way.b), way.lanes]
        mine = pltpu.make_async_copy(way.shard, own, r.local_sem.at[i])
        mine.start()
        local.append(mine)
    prepare(r)
    for mine in local:
        mine.wait()
    qkv_way.step(0)
    proj_way.start(LINE)
    for way in up_ways:
        way.start(LINE)
    lend.wait()
    for w in range(4):
        cut_windows(r.field, r.xw, n_row, n_col, w)
    qkv_way.step(1)
    for way in down_ways:
        way.start(LINE)
    qkv_way.step(2)
    qkv_way.whole()

    def between(part):
        if part == 0:
            up_ways[0].step(0)
        elif part == 1:
            proj_way.step(0)
        else:
            up_ways[1].step(0)

    hooks = (
        (2, lambda: up_ways[2].step(0)),
        (4, lambda: up_ways[0].step(1)),
        (5, lambda: proj_way.step(1)),
        (8, lambda: down_ways[0].step(0)),
        (10, lambda: up_ways[1].step(1)),
        (12, lambda: down_ways[1].step(0)),
        (14, lambda: up_ways[2].step(1)),
        (16, lambda: proj_way.step(2)),
        (17, lambda: up_ways[0].step(2)),
        (18, lambda: down_ways[2].step(0)),
        (20, lambda: down_ways[0].step(1)),
        (22, lambda: up_ways[1].step(2)),
    )
    attend_part(r, n_row, n_col, hooks, between)
    give.start()
    r.home[pl.ds(0, TOK), :] = r.ret[pl.ds(0, TOK), :]
    proj_way.whole()
    down_ways[1].step(1)
    up_ways[2].step(2)
    give.arrive()

    qkv_sum, proj_sum, up_sum, down_sum = sums = [
        Reduce(g, g, dp * blocks[i][1], land, c, *blocks[i], SENT[i], LANES[i], p, q)
        for i, (g, land, c, p, q) in enumerate(
            [
                (r.gqkv, (r.g1, 0, True), r.c0, r.t0, r.u0),
                (r.gproj, (r.g1, shapes[0][0], True), r.c1, r.t1, r.u1),
                (r.g1, (r.w1, 0, False), r.c2, r.t2, r.u2),
                (r.g2, (r.w2, 0, False), r.c3, r.t3, r.u3),
            ]
        )
    ]

    def free(k):
        pl.semaphore_signal(r.free_sem.at[k], inc=1, device_id=(1 - dp, row, col), device_id_type=MESH)

    early = Small(r.small, r.small_come, r.small_sem.at[0], r.small_sem.at[1], 12)
    mid = Small(r.mid, r.mid_come, r.mid_sem.at[0], r.mid_sem.at[1])

    def every(n, j, way):
        pl.when(lax.rem(j, n) == n - 1)(lambda: way.start(0, j // n))

    def middle(act, slope, gu, cot_t):
        m = types.SimpleNamespace(**r.__dict__, act=act, slope=slope, gu=gu, cot_t=cot_t)

        def arrived():
            for way in up_ways:
                way.whole()
            give.gone()

        hooks = (
            (1, lambda: down_ways[2].step(1)),
            (2, lambda: down_ways[0].step(2)),
            (6, lambda: down_ways[1].step(2)),
            (11, lambda: down_ways[2].step(2)),
        )
        mlp_first(m, n_row, n_col, hidden, arrived, hooks)
        mlp_second(m, hidden, lambda part: down_ways[part].whole())
        for way in gathers:
            way.finish()
        free(0)
        pick_start(lend2, r.pick)
        pl.semaphore_wait(r.free_sem.at[0], 1)
        up_weights(m, hidden, lambda j: every(UP_PIECES // SENT[2], j, up_sum))
        up_sum.step(0)
        up_sum.gone()
        mlp_branch(m, hidden)
        free(1)
        pl.semaphore_wait(r.free_sem.at[1], 1)
        down_weights(m, lambda j: every(DOWN_PIECES // SENT[3], j, down_sum))
        mlp_out(m)
        leave(4)
        early.start()
        down_sum.step(0)

    v = pltpu.VMEM
    wide = (TOK, hidden)
    pl.run_scoped(middle, v(wide, BF), v(wide, BF), v(wide, BF), v((D, TOK), BF))
    proj_weight_grad(r)
    proj_sum.start(0)
    lend2.wait()

    def all_parts(way, k):
        for part in range(way.parts):
            way.step(k, part)

    def ends(gw):
        e = types.SimpleNamespace(**r.__dict__, gw=gw, gmix=r.mixed, dqkv=r.w1)
        all_parts(up_sum, 1)
        back_prepare(e, n_row, n_col)
        proj_sum.step(0)
        back_mix(e)
        early.step(0)
        hooks = (
            (2, lambda: all_parts(down_sum, 1)),
            (12, lambda: all_parts(up_sum, 2)),
            (13, lambda: proj_sum.step(1)),
        )
        back_windows(e, n_row, n_col, hooks)
        back_weights(e, n_row, n_col, lambda n: qkv_sum.start(0, n // 3) if n % 3 == 2 else None)
        qkv_sum.step(0)
        all_parts(down_sum, 2)
        back_return(e, n_row, n_col)
        give2.start()
        proj_sum.step(2)
        r.home2[pl.ds(0, TOK), :] = r.ret[pl.ds(0, TOK), :]
        all_parts(qkv_sum, 1)
        norm_sums(e, n_row, n_col)
        mid.start()
        early.step(1)
        for part in range(PARTS):
            up_sum.result(r.o2, part)
        leave(2)
        all_parts(qkv_sum, 2)
        mid.step(0)
        give2.arrive()
        back_last(e, n_row, n_col)
        leave(5)
        early.step(2)
        leave(6)
        mid.step(1)
        for part in range(PARTS):
            down_sum.result(r.o3, part)
        leave(3)
        proj_sum.result(r.o1)
        leave(1)
        mid.step(2)
        leave(7)
        give2.gone()
        for part in range(PARTS):
            qkv_sum.result(r.o0, part)
        leave(0)
        for way in (qkv_sum, proj_sum, down_sum):
            way.gone()
        for way in sums:
            way.finish()

    pl.run_scoped(ends, v((4 * SLOT, D), BF))
    for n in range(len(outs)):
        leaving(n).wait()


def split_ins(tensors, *names):
    return {k: (tensors[k], vmem()) for k in names}


def as_out(buffer):
    return (jax.ShapeDtypeStruct(buffer.shape, buffer.dtype), vmem())


def window_buffers(n_row):
    v = pltpu.VMEM
    late = 16 * (TILE * n_row - WIN * n_row)
    return dict(
        xw=v((4 * SLOT, D), BF),
        qkv=v((4 * SLOT, 3 * D), BF),
        probs0=v((2 * HEADS, 16 * WIN, SLOT), BF),
        probs1=v((2 * HEADS, late, SLOT), BF),
        mixed=v((4 * SLOT, D), BF),
        table=v((256, 128), BF),
        ret=v((FIELD, D), BF),
    )


def mlp_buffers(hidden):
    v = pltpu.VMEM
    return dict(
        mixed_own=v((TOK, D), BF),
        attended=v((TOK, D), BF),
        n2=v((TOK, D), BF),
        acc=v((TOK, D), F32),
        up_bias=v((hidden // D, D), F32),
        up_sum=v((1, hidden), F32),
        grad_middle=v((TOK, D), F32),
    )


def block_call(n_row, n_col, shapes, tensors, shards):
    hidden = shapes[2][0]
    sd, v = jax.ShapeDtypeStruct, pltpu.VMEM
    blocks = blocks_of(shapes)
    arrays = tensors | {"s" + str(i): w for i, w in enumerate(shards)}
    results = {"o" + str(i): v(b, F32) for i, b in enumerate(blocks)}
    results |= dict(output=v((TOK, D), BF), input_grad=v((TOK, D), BF), small=v((16, D), F32), mid=v((16, D), F32))
    there = "_"
    ins = {k + there: (t, hbm()) for k, t in arrays.items()}
    outs = {k + there: (sd(t.shape, t.dtype), hbm()) for k, t in results.items()}
    wqkv, wproj, w1, w2 = [v(s, BF) for s in shapes]
    come = [v((15 * b, h), BF) for b, h in blocks]
    field = v((FIELD, D), BF)
    scratch = dict(
        **window_buffers(n_row),
        **mlp_buffers(hidden),
        wqkv=wqkv,
        wproj=wproj,
        w1=w1,
        w2=w2,
        gqkv=wqkv,
        gproj=wproj,
        g1=w1,
        g2=w2,
        c0=come[0],
        c1=come[1],
        c2=come[2],
        c3=come[3],
        field=field,
        home=field,
        picked=v((PICKED, D), BF),
        gtab=v((2, 128, 128), F32),
        small_come=v((7, 16, D), F32),
        mid_come=v((7, 16, D), F32),
        **{k: v(t.shape, t.dtype) for k, t in arrays.items()},
        **results,
        load_sem=dma(len(arrays)),
        leave_sem=dma(len(results)),
        local_sem=dma(len(GATHERS)),
        gather_sem=dma(2, len(GATHERS), Gather.SEMS),
        lend_sem=dma(4, 3),
        give_sem=dma(4, 3),
        small_sem=dma(2, 7),
        mid_sem=dma(2, 7),
        free_sem=pltpu.SemaphoreType.REGULAR((2,)),
    )
    for i in range(4):
        count = SENT[i] + 7 * LANES[i]
        scratch |= {"t" + str(i): dma(count), "u" + str(i): dma(count)}

    def body(r):
        given = [(k, r.__dict__[k + there]) for k in arrays]
        taken = [(k, r.__dict__[k + there]) for k in results]
        block_body(n_row, n_col, shapes, hidden, given, taken, r)

    done = named_call(
        body, ins, outs, scratch, "block", vmem_limit_bytes=63 * MIB, collective_id=0, has_side_effects=True
    )
    return types.SimpleNamespace(**{k: done.__dict__[k + there] for k in results})


def plain_block(n_row, n_col, shapes, tensors, weights, field):
    hidden = shapes[2][0]
    sd, v = jax.ShapeDtypeStruct, pltpu.VMEM
    wqkv, wproj, w1, w2 = [(w, vmem()) for w in weights]
    limit = dict(vmem_limit_bytes=60 * MIB)

    def given(value, *names):
        return {k: (getattr(value, k), vmem()) for k in names}

    names = ("query_bias", "value_bias", "rel_rows", "rel_cols", "masks", "places", "marks")
    windows = window_buffers(n_row)
    outs = {k: as_out(windows.pop(k)) for k in ("qkv", "xw", "probs0", "probs1", "ret")}

    def attend_body(r):
        prepare(r)
        for w in range(4):
            cut_windows(r.field, r.xw, n_row, n_col, w)
        attend_part(r, n_row, n_col, (), lambda part: None)

    ins = split_ins(tensors, *names) | dict(field=(field, vmem()), wqkv=wqkv)
    one = named_call(attend_body, ins, outs, windows, "attend", **limit)
    home = (return_xla(one.ret, n_row, n_col), vmem())
    names = ("tokens", "cot", "proj_bias", "ln2_gain", "ln2_bias", "fc1_bias", "fc2_bias")
    buffers = mlp_buffers(hidden)
    outs = dict(grad_middle=as_out(buffers.pop("grad_middle")), gfield=(sd((FIELD, D), BF), vmem()))
    outs |= {k: (sd(s, BF), vmem()) for k, s in zip(("gproj", "g1", "g2"), shapes[1:])}
    outs |= dict(output=(sd((TOK, D), BF), vmem()), small=(sd((16, D), F32), vmem()))
    wide = (TOK, hidden)
    buffers |= dict(act=v(wide, BF), slope=v(wide, BF), gu=v(wide, BF), cot_t=v((D, TOK), BF))

    def mlp_body(r):
        r.gfield[...] = jnp.zeros_like(r.gfield)
        mlp_first(r, n_row, n_col, hidden, lambda: None, ())
        mlp_second(r, hidden, lambda part: None)
        up_weights(r, hidden, lambda j: None)
        mlp_branch(r, hidden)
        down_weights(r, lambda j: None)
        mlp_out(r)
        proj_weight_grad(r)

    ins = split_ins(tensors, *names) | dict(home=home, wproj=wproj, w1=w1, w2=w2)
    two = named_call(mlp_body, ins, outs, buffers, "mlp", **limit)
    gfield = (lend_xla(two.gfield[:TOK], n_row, n_col), vmem())
    ins = split_ins(tensors, "rel_rows", "rel_cols", "masks", "places_back", "marks_back", "ln1_gain", "ln1_bias")
    ins |= given(one, "qkv", "xw", "probs0", "probs1") | dict(wqkv=wqkv, wproj=wproj, gfield=gfield)
    outs = dict(
        gqkv=(sd(shapes[0], BF), vmem()),
        ret=(sd((FIELD, D), BF), vmem()),
        mid=(sd((16, D), F32), vmem()),
    )
    rows = v((4 * SLOT, D), BF)
    scratch = dict(gw=rows, gmix=rows, dqkv=v((12 * SLOT, D), BF))
    scratch |= dict(table=v((256, 128), BF), gtab=v((2, 128, 128), F32))

    def windows_body(r):
        back_prepare(r, n_row, n_col)
        back_mix(r)
        back_windows(r, n_row, n_col, ())
        back_weights(r, n_row, n_col, lambda n: None)
        back_return(r, n_row, n_col)
        norm_sums(r, n_row, n_col)

    three = named_call(windows_body, ins, outs, scratch, "windows", **limit)
    home = (return_xla(three.ret, n_row, n_col), vmem())
    ins = split_ins(tensors, "tokens", "ln1_gain", "ln1_bias") | dict(home2=home) | given(two, "grad_middle")
    outs = dict(input_grad=(sd((TOK, D), BF), vmem()))
    four = named_call(lambda r: back_last(r, n_row, n_col), ins, outs, dict(acc=v((TOK, D), F32)), "ends", **limit)
    grads = []
    for g in (three.gqkv, two.gproj, two.g1, two.g2):
        g = lax.psum_scatter(g, AXES, scatter_dimension=0, tiled=True)
        grads.append(lax.psum_scatter(g, "dp", scatter_dimension=1, tiled=True))
    line = jnp.arange(16)[:, None] == 12
    local = lax.psum(two.small, AXES)
    small = jnp.where(line, local, lax.psum(jnp.where(line, 0.0, local), "dp"))
    return grads, two.output, four.input_grad, small, lax.psum(three.mid, ("dp", *AXES))


def last_body(count, r):
    for i in range(4):
        r.__dict__["t" + str(i)][...] = r.__dict__["s" + str(i)][...].astype(F32)
    r.output_out[...] = r.output[...]
    r.input_grad_out[...] = r.input_grad[...]
    lines = ((r.mid, 10), (r.mid, 11), (r.mid, 8), (r.mid, 9), (r.small, 4), (r.small, 5), (r.small, 6), (r.small, 7))
    for i, (ref, line) in enumerate(lines):
        r.__dict__["v" + str(i)][...] = ref[line : line + 1, :].reshape(D)
    r.up[...] = jnp.concatenate([r.small[8 + i : 9 + i, :] for i in range(r.up.shape[0] // D)], 1).reshape(-1)
    tables = jnp.concatenate([r.mid[0:8, 128 * t : 128 * t + 128] for t in range(4)], 0)
    r.rows[...] = tables[0 : 2 * WIN - 1, :HEAD]
    r.cols[...] = pltpu.roll(tables, HEAD, 1)[0 : 2 * WIN - 1, :HEAD]
    r.stats[...] = jnp.sqrt(r.small[12:13, :5] / count)


def last_call(count, hidden, sums, output, input_grad, small, mid):
    sd = jax.ShapeDtypeStruct
    ins = {"s" + str(i): (s, vmem()) for i, s in enumerate(sums)}
    ins |= dict(output=(output, vmem()), input_grad=(input_grad, vmem()), small=(small, vmem()))
    ins |= dict(mid=(mid, vmem()))
    outs = {"t" + str(i): (sd(s.shape, F32), vmem()) for i, s in enumerate(sums)}
    outs |= dict(output_out=(sd((TOK, D), BF), vmem()), input_grad_out=(sd((TOK, D), BF), vmem()))
    outs |= {"v" + str(i): (sd((D,), F32), vmem()) for i in range(8)}
    outs |= dict(
        up=(sd((hidden,), F32), vmem()),
        rows=(sd((2 * WIN - 1, HEAD), F32), vmem()),
        cols=(sd((2 * WIN - 1, HEAD), F32), vmem()),
        stats=(sd((1, 5), F32), vmem()),
    )
    return named_call(functools.partial(last_body, count), ins, outs, {}, "last", vmem_limit_bytes=63 * MIB)


def on_device(
    n_dp, n_row, n_col,
    tokens, ln1_gain, ln1_bias, qkv_weight, query_bias, value_bias, rel_rows, rel_cols,
    proj_weight, proj_bias, ln2_gain, ln2_bias, fc1_weight, fc1_bias, fc2_weight, fc2_bias, cotangent,
):
    direct = (n_dp, n_row, n_col) == (2, 4, 4)
    tok = tokens.reshape(TOK, D)
    mask_values = np.zeros((16, 128), np.float32)
    mask_values[0, :64] = 1.0
    mask_values[1, 64:] = 1.0
    shared = dict(
        tokens=tok,
        cot=cotangent.reshape(TOK, D),
        ln1_gain=ln1_gain,
        ln1_bias=ln1_bias,
        rel_rows=rel_rows,
        rel_cols=rel_cols,
        masks=jnp.asarray(mask_values, BF),
    )
    tensors = shared | dict(
        query_bias=query_bias,
        value_bias=value_bias,
        proj_bias=proj_bias,
        ln2_gain=ln2_gain,
        ln2_bias=ln2_bias,
        fc1_bias=fc1_bias,
        fc2_bias=fc2_bias,
        places=jnp.asarray(table_places(False), BF),
        marks=jnp.asarray(key_marks(False), BF),
        places_back=jnp.asarray(table_places(True), BF),
        marks_back=jnp.asarray(key_marks(True), BF),
    )
    shards = (qkv_weight, proj_weight, fc1_weight, fc2_weight)
    shapes = [(s.shape[1] * n_row * n_col, s.shape[0] * n_dp) for s in shards]
    if direct:
        tensors |= dict(pick=jnp.asarray(pick_rows(), BF))
        done = block_call(n_row, n_col, shapes, tensors, [s.T for s in shards])
        sums = (done.o0, done.o1, done.o2, done.o3)
        rest = (done.output, done.input_grad, done.small, done.mid)
    else:
        weights = []
        for s in shards:
            s = lax.all_gather(s, AXES, axis=1, tiled=True)
            weights.append(lax.all_gather(s, "dp", axis=0, tiled=True).T)
        normed = norm(tok.astype(F32), ln1_gain.astype(F32), ln1_bias.astype(F32))[0].astype(BF)
        field = lend_xla(normed, n_row, n_col)
        sums, *rest = plain_block(n_row, n_col, shapes, tensors, weights, field)
    out = last_call(TOK * n_row * n_col * D, shapes[2][0], sums, *rest)
    return (
        out.output_out.reshape(tokens.shape),
        out.input_grad_out.reshape(tokens.shape),
        out.v0,
        out.v1,
        out.t0.T,
        out.v2,
        out.v3,
        out.rows,
        out.cols,
        out.t1.T,
        out.v4,
        out.v5,
        out.v6,
        out.t2.T,
        out.up,
        out.t3.T,
        out.v7,
        out.stats,
    )


def solution(mesh):
    tile = P("dp", "row", "col", None)
    weight = P("dp", AXES)
    sizes = [mesh.shape[a] for a in ("dp", "row", "col")]
    ins = [tile] + [P()] * 16
    for i in (3, 8, 12, 14):
        ins[i] = weight
    ins[16] = tile
    outs = [tile, tile] + [P()] * 16
    for i in (4, 9, 13, 15):
        outs[i] = weight
    outs[17] = P("dp", None)
    return jax.shard_map(
        functools.partial(on_device, *sizes),
        mesh=mesh,
        in_specs=tuple(ins),
        out_specs=tuple(outs),
        check_vma=False,
    )
```

```python
import functools
import types

import jax
import jax.numpy as jnp
import numpy as np
from jax import lax
from jax.experimental import pallas as pl
from jax.experimental.pallas import tpu as pltpu
from jax.sharding import PartitionSpec as P

HEADS = 12
HEAD = 64
WIN = 14
EPS = 1e-06
MESH = pl.DeviceIdType.MESH
AXES = ("row", "col")
F32 = jnp.float32
BF = jnp.bfloat16

D = HEADS * HEAD
TILE = 16
TOK = TILE * TILE
LO = 6
SLOT = 256
PAIRS = HEADS // 2
FIELD = 496
PICKED = 144
MIB = 2**20

LINKS = {
    (1, 0): (True, 160, 96, 256),
    (0, 1): (False, 0, 96, 352),
    (1, 1): (False, 96, 48, 448),
}


def nt(a, b):
    return lax.dot_general(a, b, (((1,), (1,)), ((), ())), preferred_element_type=F32)


def nn(a, b):
    return lax.dot_general(a, b, (((1,), (0,)), ((), ())), preferred_element_type=F32)


def tn(a, b):
    return lax.dot_general(a, b, (((0,), (0,)), ((), ())), preferred_element_type=F32)


def pick_rows():
    table = np.zeros((PICKED, TOK), np.float32)
    for base, first in ((0, 0), (96, TILE - LO)):
        for i in range((TILE - first) * LO):
            y, x = divmod(i, LO)
            table[base + i, (first + y) * TILE + TILE - LO + x] = 1.0
    return table


def table_places(back):
    place = np.zeros((256, 64), np.float32)
    for head in range(2):
        for r in range(2 * WIN - 1):
            for copy in range(2):
                row_lane = (64 + 28 * copy + r + 64 * head) % 128
                col_lane = (28 * copy + r + 64 * head) % 128
                place[128 * head + row_lane, 26 - r] = 1.0
                place[128 * head + col_lane, 32 + (r if back else 26 - r)] = 1.0
    return place


def key_marks(back):
    marks = np.zeros((2, SLOT, 128), np.float32)
    for head in range(2):
        for j in range(SLOT):
            k, l = divmod(j, 16)
            if k < WIN and l < WIN:
                for copy in range(2):
                    marks[head, j, (64 + 28 * copy + k + 64 * head) % 128] = 1.0
                    marks[head, j, (78 + 28 * copy + (13 - l if back else l) + 64 * head) % 128] = 1.0
            else:
                marks[head, j, (120 + 64 * head) % 128] = -1e30
    return marks


def lane_kinds(rows):
    lane = lax.broadcasted_iota(jnp.int32, (rows, 128), 1)
    kinds = []
    for head in range(2):
        at = (lane + 64 * head) % 128 if head else lane
        own = at < 64
        first = (at >= 64) & (at < 92)
        second = (at >= 92) & (at < 120)
        is_row = ((at >= 64) & (at < 78)) | ((at >= 92) & (at < 106))
        kinds.append((own, first, second, is_row, at == 120))
    return kinds


def window_index(w, row, col, n_row, n_col):
    place = lax.broadcasted_iota(jnp.int32, (SLOT, 1), 0)
    y = place // 16
    x = place - 16 * y
    a, b = w // 2, w % 2
    ry = WIN * (row + a) + y - TILE * row
    rx = WIN * (col + b) + x - TILE * col
    good = (y < WIN) & (x < WIN) & (ry < TILE) & (rx < TILE)
    if a:
        good = good & (row == n_row - 1)
    if b:
        good = good & (col == n_col - 1)
    up, left = ry < 0, rx < 0
    base = jnp.where(up, jnp.where(left, 448, 256), jnp.where(left, 352, 0))
    width = jnp.where(left, LO, TILE)
    index = base + jnp.where(up, ry + LO, ry) * width + jnp.where(left, rx + LO, rx)
    return jnp.where(good, index, -1)


def field_slots(row, col, n_row, n_col):
    at = lax.broadcasted_iota(jnp.int32, (FIELD, 1), 0)
    above = (at >= 256) & (at < 352)
    left = (at >= 352) & (at < 448)
    corner = at >= 448
    narrow = left | corner
    rest = jnp.where(corner, at - 448, jnp.where(left, at - 352, jnp.where(above, at - 256, at)))
    sixth = sum((rest >= LO * k).astype(jnp.int32) for k in range(1, TILE))
    ty = jnp.where(narrow, sixth, rest // TILE)
    tx = rest - ty * jnp.where(narrow, LO, TILE)
    ty = jnp.where(above | corner, ty - LO, ty)
    tx = jnp.where(narrow, tx - LO, tx)
    good = at < 484
    where = 0
    for t, place, n, stride, unit in ((ty, row, n_row, 2, 16), (tx, col, n_col, 1, 1)):
        y = TILE * place + t - WIN * place
        late = y >= WIN
        good = good & (y >= 0) & (jnp.logical_not(late) | (place == n - 1))
        where = where + jnp.where(late, stride * SLOT + unit * (y - WIN), unit * y)
    return jnp.where(good, where, -1)


def home_index(row, col, n_row, n_col):
    place = lax.broadcasted_iota(jnp.int32, (TOK, 1), 0)
    ty = place // TILE
    tx = place - TILE * ty
    down = (TILE * row + ty - WIN * row >= WIN) & (row < n_row - 1)
    right = (TILE * col + tx - WIN * col >= WIN) & (col < n_col - 1)
    near = TILE - LO
    return jnp.where(
        down,
        jnp.where(right, 448 + (ty - near) * LO + tx - near, 256 + (ty - near) * TILE + tx),
        jnp.where(right, 352 + ty * LO + tx - near, place),
    )


def one_hot(index, size):
    lane = lax.broadcasted_iota(jnp.int32, (index.shape[0], size), 1)
    return jnp.where(lane == index, 1.0, 0.0).astype(BF)


STEP = 64


def by_rows(body, sums):
    def step(i, kept):
        parts = body(pl.ds(pl.multiple_of(i * STEP, STEP), STEP))
        return tuple(k + sum(p[8 * q : 8 * q + 8] for q in range(STEP // 8)) for k, p in zip(kept, parts))

    return lax.fori_loop(0, TOK // STEP, step, (jnp.zeros((8, D), F32),) * sums)


def column_sum(v):
    return jnp.sum(v, 0, keepdims=True)


def norm(v, gain, bias):
    mean = jnp.mean(v, -1, keepdims=True)
    center = v - mean
    inverse = lax.rsqrt(jnp.mean(center * center, -1, keepdims=True) + EPS)
    xhat = center * inverse
    return xhat * gain + bias, xhat, inverse


def norm_back(grad, xhat, inverse, gain):
    d = grad * gain
    return inverse * (
        d - jnp.mean(d, -1, keepdims=True) - xhat * jnp.mean(d * xhat, -1, keepdims=True)
    )


def grid_place():
    return lax.axis_index("dp"), lax.axis_index("row"), lax.axis_index("col")


def exists(step, row, col, n_row, n_col):
    r, c = row + step[0], col + step[1]
    return (r >= 0) & (r < n_row) & (c >= 0) & (c < n_col)


CORNERS = ((1, 1), (-1, -1))


def greet(n_row, n_col):
    dp, row, col = grid_place()
    barrier = pltpu.get_barrier_semaphore()
    others = [(dp, row, lax.rem(col + d, n_col)) for d in (1, 2, 3)]
    others += [(dp, lax.rem(row + d, n_row), col) for d in (1, 2, 3)]
    others.append((1 - dp, row, col))
    for other in others:
        pl.semaphore_signal(barrier, inc=1, device_id=other, device_id_type=MESH)
    count = len(others)
    for step in CORNERS:
        there = exists(step, row, col, n_row, n_col)

        @pl.when(there)
        def _():
            pl.semaphore_signal(
                barrier, inc=1, device_id=(dp, row + step[0], col + step[1]), device_id_type=MESH
            )

        count = count + jnp.where(there, 1, 0)
    pl.semaphore_wait(barrier, count)


class Halo:
    def __init__(self, source, picked, land, back, send, recv, n_row, n_col):
        self.source, self.picked, self.land, self.back = source, picked, land, back
        self.send, self.recv, self.size = send, recv, (n_row, n_col)

    def copies(self):
        dp, row, col = grid_place()
        sign = -1 if self.back else 1
        for i, ((dr, dc), (own, first, rows, there)) in enumerate(LINKS.items()):
            if self.back:
                src = self.source.at[pl.ds(there, rows)]
            else:
                src = (self.source if own else self.picked).at[pl.ds(first, rows)]
            copy = pltpu.make_async_remote_copy(
                src,
                self.land.at[pl.ds(there, rows)],
                self.send.at[i],
                self.recv.at[i],
                device_id=(dp, row + sign * dr, col + sign * dc),
                device_id_type=MESH,
            )
            goes = exists((sign * dr, sign * dc), row, col, *self.size)
            comes = exists((-sign * dr, -sign * dc), row, col, *self.size)
            yield copy, goes, comes

    def start(self):
        for copy, goes, _ in self.copies():
            pl.when(goes)(copy.start)

    def arrive(self):
        for copy, _, comes in self.copies():
            pl.when(comes)(copy.wait_recv)

    def gone(self):
        for copy, goes, _ in self.copies():
            pl.when(goes)(copy.wait_send)

    def wait(self):
        self.arrive()
        self.gone()


def pick_start(halo, pick):
    halo.picked[...] = nn(pick[...], halo.source[pl.ds(0, TOK), :]).astype(BF)
    halo.start()


def halo_xla(blocks, back, n_row, n_col):
    sign = -1 if back else 1
    pieces = [blocks[0]]
    for (dr, dc), block in zip(LINKS, blocks[1:]):
        dr, dc = sign * dr, sign * dc
        pairs = [
            (r * n_col + c, (r + dr) * n_col + c + dc)
            for r in range(n_row)
            for c in range(n_col)
            if 0 <= r + dr < n_row and 0 <= c + dc < n_col
        ]
        pieces.append(lax.ppermute(block, AXES, pairs))
    return jnp.concatenate(pieces, 0)


def lend_xla(own, n_row, n_col):
    grid = own.reshape(TILE, TILE, -1)
    corner = grid[TILE - LO :, TILE - LO :].reshape(LO * LO, -1)
    blocks = [
        own,
        own[TILE * (TILE - LO) :],
        grid[:, TILE - LO :].reshape(TILE * LO, -1),
        jnp.pad(corner, ((0, 48 - LO * LO), (0, 0))),
    ]
    return halo_xla(blocks, False, n_row, n_col)


def return_xla(field, n_row, n_col):
    return halo_xla([field[:256], field[256:352], field[352:448], field[448:]], True, n_row, n_col)


def blocks_of(shapes):
    return [(n // 16, k // 2) for n, k in shapes]


def rows_at(first, count):
    return pl.ds(pl.multiple_of(first, 16), count)


LINE, OWN, LINE_CORE, FAR, NEAR_CORE, FAR_CORE, CORE = range(10, 17)


class Gather:
    SEMS = 17

    def __init__(self, full, shard, block, half, send, recv, part=0, parts=1):
        self.dp, self.row, self.col = grid_place()
        width = half // parts
        self.full, self.shard, self.b = full, shard.at[:, pl.ds(part * width, width)], block
        self.send, self.recv = send, recv
        self.lanes = pl.ds(pl.multiple_of(self.dp * half + part * width, 128), width)
        self.other = pl.ds(pl.multiple_of((1 - self.dp) * half + part * width, 128), width)

    def block(self, flip, place):
        return (jnp.bitwise_xor(self.row, flip) * 4 + place) * self.b

    def came(self, d):
        return lax.rem(self.col + 4 - d, 4)

    def copy(self, i, first, count, land, target, shard=False):
        core = target == CORE
        if core:
            device = (1 - self.dp, self.row, self.col)
        elif isinstance(target, tuple):
            device = (self.dp, self.row, lax.rem(self.col + target[0], 4))
        else:
            device = (self.dp, jnp.bitwise_xor(self.row, target), self.col)

        def make(src, dst):
            return pltpu.make_async_remote_copy(
                src, dst, self.send.at[i], self.recv.at[i], device_id=device, device_id_type=MESH
            )

        def out():
            there = self.full.at[rows_at(first, count), self.lanes]
            return make(self.shard if shard else there, there)

        def come():
            here = self.full.at[rows_at(land, count), self.other if core else self.lanes]
            return make(here, here)

        return out, come

    def copies(self, k):
        b = self.b
        own = self.block(0, self.col)
        if k == LINE:
            return [
                self.copy(d - 1, own, b, self.block(0, self.came(d)), (d,), True) for d in (1, 2, 3)
            ]
        if k == OWN:
            return [self.copy(2 + f, own, b, self.block(f, self.col), f, True) for f in (1, 2)]
        if k < LINE:
            at = self.came(k)
            return [
                self.copy(4 + 2 * k, self.block(0, at), b, self.block(1, at), 1),
                self.copy(5 + 2 * k, self.block(0, at), b, self.block(2, at), 2),
            ]
        if k == LINE_CORE:
            return [self.copy(5, self.block(0, 0), 4 * b, self.block(0, 0), CORE)]
        if k == FAR:
            return [
                self.copy(12, self.block(2, 0), 2 * b, self.block(3, 0), 1),
                self.copy(13, self.block(1, 2), 2 * b, self.block(3, 2), 2),
            ]
        if k == NEAR_CORE:
            return [self.copy(13 + f, self.block(f, 0), 4 * b, self.block(f, 0), CORE) for f in (1, 2)]
        return [self.copy(16, self.block(3, 0), 4 * b, self.block(3, 0), CORE)]

    def start(self, *kinds):
        for k in kinds:
            for out, _ in self.copies(k):
                out().start()

    def arrive(self, *kinds):
        for k in kinds:
            for _, come in self.copies(k):
                come().wait_recv()

    def step(self, n):
        if n == 0:
            for d in (1, 2, 3):
                self.copies(LINE)[d - 1][1]().wait_recv()
                self.start(d)
            self.start(LINE_CORE)
        elif n == 1:
            self.arrive(OWN, 1, 2, 3)
            self.start(FAR, NEAR_CORE)
        else:
            self.arrive(FAR)
            self.start(FAR_CORE)

    def whole(self):
        self.arrive(LINE_CORE, NEAR_CORE, FAR_CORE)

    def finish(self):
        for k in (LINE, OWN, 1, 2, 3, LINE_CORE, FAR, NEAR_CORE, FAR_CORE):
            for out, _ in self.copies(k):
                out().wait_send()


class Reduce:
    def __init__(self, grad, total, base, land, come, block, half, pieces, parts, send, recv):
        self.dp, self.row, self.col = grid_place()
        self.grad, self.total, self.base, self.come = grad, total, base, come
        self.land, self.land_row, mirrored = land
        self.land_there = self.dp * half if mirrored else 0
        self.land_here = (1 - self.dp) * half if mirrored else 0
        self.b, self.h, self.send, self.recv = block, half, send, recv
        self.pieces, self.parts, self.width = pieces, parts, half // parts
        self.other = pl.ds(pl.multiple_of((1 - self.dp) * half, 128), half)

    def side(self, base, part, width):
        return pl.ds(pl.multiple_of(base + part * width, 128), width)

    def at(self, flip, place=0):
        return (jnp.bitwise_xor(self.row, flip) * 4 + place) * self.b

    def lanes(self, part):
        return pl.ds(pl.multiple_of(self.base + part * self.width, 128), self.width)

    def came(self, first, count, part):
        return self.come.at[rows_at(first, count), pl.ds(part * self.width, self.width)]

    def tot(self, first, count, part):
        return self.total.at[rows_at(first, count), self.lanes(part)]

    def sem(self, k, part):
        if k == 0:
            return part
        return self.pieces + 7 * part + {1: 0, 2: 2, 3: 4}[k]

    def copies(self, k, part):
        b = self.b
        if k == 0:
            n = 16 * b // self.pieces
            there = self.land.at[rows_at(self.land_row + part * n, n), self.side(self.land_there, 0, self.h)]
            plan = [(self.grad.at[rows_at(part * n, n), self.other], there, (1 - self.dp, self.row, self.col))]
        elif k == 1:
            plan = [
                (
                    self.tot(self.at(3, 2 * half), 2 * b, part),
                    self.came(2 * half * b, 2 * b, part),
                    (self.dp, jnp.bitwise_xor(self.row, 1 + half), self.col),
                )
                for half in (0, 1)
            ]
        elif k == 2:
            plan = [
                (
                    self.tot(self.at(flip), 4 * b, part),
                    self.came(4 * flip * b, 4 * b, part),
                    (self.dp, jnp.bitwise_xor(self.row, flip), self.col),
                )
                for flip in (1, 2)
            ]
        else:
            plan = []
            for d in (1, 2, 3):
                to = lax.rem(self.col + d, 4)
                plan.append(
                    (
                        self.tot(self.at(0, to), b, part),
                        self.came((11 + d) * b, b, part),
                        (self.dp, self.row, to),
                    )
                )
        base = self.sem(k, part)
        return [
            pltpu.make_async_remote_copy(
                src, dst, self.send.at[base + i], self.recv.at[base + i], device_id=dev, device_id_type=MESH
            )
            for i, (src, dst, dev) in enumerate(plan)
        ]

    def start(self, k, part=0):
        for copy in self.copies(k, part):
            copy.start()

    def arrive(self, k, part=0):
        for copy in self.copies(k, part):
            copy.wait_recv()

    def sum_rows(self, first, count, froms, part, source=None, base=0):
        most = (256 if len(froms) == 1 else 96) * 384
        step = next(n for n in range(count, 0, -16) if count % n == 0 and n * self.width <= most)
        lanes = self.lanes(part)
        side = self.side(base, part, self.width)
        source = self.come if source is None else source

        def body(i, _):
            at = rows_at(first + i * step, step)
            value = self.total[at, lanes]
            if len(froms) == 1:
                value = value + source[rows_at(froms[0] + i * step, step), side]
            else:
                value = value.astype(F32)
                for f in froms:
                    value = value + source[rows_at(f + i * step, step), side].astype(F32)
                value = value.astype(BF)
            self.total[at, lanes] = value
            return 0

        lax.fori_loop(0, count // step, body, 0)

    def add_piece(self, piece):
        n = 16 * self.b // self.pieces
        self.arrive(0, piece)
        for part in range(self.parts):
            self.sum_rows(piece * n, n, (self.land_row + piece * n,), part, self.land, self.land_here)

    def step(self, k, part=0):
        b = self.b
        if k == 0:
            for piece in range(self.pieces):
                self.add_piece(piece)
            for part in range(1, self.parts):
                self.start(1, part)
            part = 0
        else:
            self.arrive(k, part)
            if k == 1:
                self.sum_rows(self.at(2), 2 * b, (0,), part)
                self.sum_rows(self.at(1, 2), 2 * b, (2 * b,), part)
            else:
                self.sum_rows(self.at(0), 4 * b, (4 * b, 8 * b), part)
        self.start(k + 1, part)

    def result(self, out, part=0):
        b = self.b
        self.arrive(3, part)
        value = self.total[rows_at(self.at(0, self.col), b), self.lanes(part)].astype(F32)
        side = pl.ds(part * self.width, self.width)
        for d in (1, 2, 3):
            value = value + self.come[pl.ds((11 + d) * b, b), side].astype(F32)
        out[:, side] = value

    def gone(self):
        for piece in range(self.pieces):
            self.copies(0, piece)[0].wait_send()

    def finish(self):
        for part in range(self.parts):
            for k in (1, 2, 3):
                for copy in self.copies(k, part):
                    copy.wait_send()


def vmem():
    return pl.BlockSpec(memory_space=pltpu.VMEM)


def hbm():
    return pl.BlockSpec(memory_space=pl.ANY)


def dma(*n):
    return pltpu.SemaphoreType.DMA(n)


def named_call(body, ins, outs, scratch, name, **params):
    names = [*ins, *outs, *scratch]

    def kernel(*refs):
        body(types.SimpleNamespace(**dict(zip(names, refs))))

    result = pl.pallas_call(
        kernel,
        name=name,
        out_shape=[shape for shape, _ in outs.values()],
        in_specs=[spec for _, spec in ins.values()],
        out_specs=[spec for _, spec in outs.values()],
        scratch_shapes=list(scratch.values()),
        compiler_params=pltpu.CompilerParams(**params),
    )(*[array for array, _ in ins.values()])
    return types.SimpleNamespace(**dict(zip(outs, result)))


def vector(ref):
    return ref[...].astype(F32).reshape(1, -1)


def joint_table(rel_rows, rel_cols):
    parts = [rel_rows[...], jnp.zeros((5, HEAD), BF), rel_cols[...], jnp.zeros((5, HEAD), BF)]
    table = jnp.concatenate([p.astype(F32) for p in parts], 0)
    return jnp.concatenate([table, table], 1).astype(BF)


def table_kernel_value(places, table):
    value = nn(places, table)
    line = lax.broadcasted_iota(jnp.int32, value.shape, 0)
    lane = lax.broadcasted_iota(jnp.int32, value.shape, 1)
    return jnp.where((line < 128) == (lane < 64), value, 0.0).astype(BF)


def narrow(v, wide):
    if wide:
        return v
    return v.astype(F32).reshape(-1, 16, 128)[:, :8].reshape(-1, 128).astype(v.dtype)


def widen(v, wide):
    if not wide:
        v = v.reshape(-1, 8, 128)
        v = jnp.concatenate([v, jnp.zeros_like(v)], 1).reshape(-1, 128)
    return v.astype(BF)


def spread(a, back, line):
    rows, cols = [], []
    for y in range(a.shape[0] // line):
        part = a[line * y : line * y + line, :]
        rows.append(pltpu.roll(part, 13 - y if back else (115 + y) % 128, 1))
        cols.append(pltpu.roll(part, 50 if back else 65, 1, stride=1, stride_axis=0))
    return jnp.concatenate(rows, 0), jnp.concatenate(cols, 0)


def pair_place(w, pair):
    return pl.multiple_of(w * SLOT, SLOT), pl.multiple_of(pair * 128, 128)


def attend_pair(w, place, pair, n, wide, qkv, table, marks, masks, probs, mixed):
    r0, l0 = pair_place(w, pair)
    q2 = narrow(qkv[pl.ds(r0, n), pl.ds(l0, 128)], wide)
    count = q2.shape[0]
    k2 = qkv[pl.ds(r0, SLOT), pl.ds(D + l0, 128)]
    v2 = qkv[pl.ds(r0, SLOT), pl.ds(2 * D + l0, 128)]
    a2 = nt(q2, table[...])
    qf = q2.astype(F32) * HEAD**-0.5
    kinds = lane_kinds(count)
    outs = []
    for head in range(2):
        own, first, second, is_row, one = kinds[head]
        rows, cols = spread(a2[:, 128 * head : 128 * head + 128], False, count // (n // 16))
        bias = jnp.where(is_row, rows, cols)
        high = bias.astype(BF).astype(F32)
        low = jnp.where(second, bias - high, jnp.where(one, 1.0, 0.0))
        aug = jnp.where(own, qf, jnp.where(first, high, low)).astype(BF)
        keys = k2 * masks[head : head + 1, :] + marks[head]
        scores = nt(aug, keys)
        top = jnp.max(scores, -1, keepdims=True)
        e = jnp.exp(scores - top)
        p = (e * (1.0 / jnp.sum(e, -1, keepdims=True))).astype(BF)
        probs[2 * place + head, 0:count, :] = p
        outs.append(nn(p, v2))
    mixed[pl.ds(r0, n), pl.ds(l0, 128)] = widen(jnp.where(kinds[0][0], outs[0], outs[1]), wide)


def attend_back_pair(w, place, pair, n, wide, qkv, gmix, probs, table, marks, masks, dqkv, gtab):
    r0, l0 = pair_place(w, pair)
    scale = HEAD**-0.5
    q2 = narrow(qkv[pl.ds(r0, n), pl.ds(l0, 128)], wide)
    count = q2.shape[0]
    k2 = qkv[pl.ds(r0, SLOT), pl.ds(D + l0, 128)]
    v2 = qkv[pl.ds(r0, SLOT), pl.ds(2 * D + l0, 128)]
    g2 = narrow(gmix[pl.ds(r0, n), pl.ds(l0, 128)], wide)
    kinds = lane_kinds(count)
    dq, dk, dv = [], [], []
    for head in range(2):
        own, first, second, is_row, one = kinds[head]
        mask = masks[head : head + 1, :]
        p = probs[2 * place + head, 0:count, :]
        pf = p.astype(F32)
        dp = nt(g2, v2 * mask)
        ds = (pf * (dp - jnp.sum(pf * dp, -1, keepdims=True))).astype(BF)
        keys = k2 * (mask * jnp.asarray(scale, BF)) + marks[head]
        dqa = nn(ds, keys)
        marked = jnp.where(first | second, dqa, 0.0)
        rows, _ = spread(jnp.where(is_row, marked, 0.0), True, count // (n // 16))
        _, cols = spread(jnp.where(is_row, 0.0, marked), True, count // (n // 16))
        back = rows + cols
        at = lax.broadcasted_iota(jnp.int32, (count, 128), 1)
        if head:
            at = (at + 64) % 128
        high = back.astype(BF).astype(F32)
        split = jnp.where((at < 28) | ((at >= 64) & (at < 92)), high, back - high).astype(BF)
        extra = nn(split, table[128 * head : 128 * head + 128, :])
        dq.append(dqa + extra)
        gtab[head] += tn(split, q2)
        dk.append(tn(ds, q2))
        dv.append(tn(p, g2))
    left = lane_kinds(SLOT)[0][0]
    dqkv[pl.ds(r0, n), pl.ds(l0, 128)] = widen(jnp.where(kinds[0][0], dq[0], dq[1]), wide)
    dqkv[pl.ds(4 * SLOT + r0, SLOT), pl.ds(l0, 128)] = (jnp.where(left, dk[0], dk[1]) * scale).astype(BF)
    dqkv[pl.ds(8 * SLOT + r0, SLOT), pl.ds(l0, 128)] = jnp.where(left, dv[0], dv[1]).astype(BF)


TOGETHER = 2


def over_windows(body, hooks, n_row, n_col):
    _, row, col = grid_place()
    for w in range(4):
        a, b = w // 2, w % 2
        n = 16 * (TILE * n_row - WIN * n_row if a else WIN)
        good = True
        if a:
            good = row == n_row - 1
        if b:
            good = good & (col == n_col - 1)

        def step(i, _):
            def work():
                for pair in range(TOGETHER):
                    pair = i * TOGETHER + pair
                    body(w, PAIRS * b + pair, pair, n, b == 0)

            if w:
                pl.when(good)(work)
            else:
                work()
            for when, hook in hooks:
                if when // PAIRS == w:
                    pl.when(i == when % PAIRS // TOGETHER)(hook)
            return 0

        lax.fori_loop(0, PAIRS // TOGETHER, step, 0)


def attend_part(r, n_row, n_col, hooks, between):
    _, row, col = grid_place()
    biases = (vector(r.query_bias), None, vector(r.value_bias))
    for part, bias in enumerate(biases):
        r.shift[...] = jnp.zeros((1, D), F32) if bias is None else bias

        def columns(n, _):
            lane = pl.multiple_of(256 * n, 256)
            value = nt(r.xw[...], r.wqkv[pl.ds(part * D + lane, 256), :]) + r.shift[:, pl.ds(lane, 256)]
            r.qkv[:, pl.ds(part * D + lane, 256)] = value.astype(BF)
            return 0

        lax.fori_loop(0, 3, columns, 0)
        between(part)

    def body(w, place, pair, n, wide):
        probs = (r.probs0, r.probs1)[w // 2]
        attend_pair(w, place, pair, n, wide, r.qkv, r.table, r.marks, r.masks, probs, r.mixed)

    over_windows(body, hooks, n_row, n_col)
    hot = one_hot(field_slots(row, col, n_row, n_col), 4 * SLOT)
    r.ret[...] = nn(hot, r.mixed[...]).astype(BF)


def cut_windows(source, land, n_row, n_col, w):
    _, row, col = grid_place()
    hot = one_hot(window_index(w, row, col, n_row, n_col), FIELD)
    land[pl.ds(w * SLOT, SLOT), :] = nn(hot, source[...]).astype(BF)


def mlp_first(r, n_row, n_col, hidden, between, hooks):
    _, row, col = grid_place()
    hot = one_hot(home_index(row, col, n_row, n_col), FIELD)
    r.mixed_own[...] = nn(hot, r.home[...]).astype(BF)
    r.acc[...] = nt(r.mixed_own[...], r.wproj[...])
    shift, gain, bias = vector(r.proj_bias), vector(r.ln2_gain), vector(r.ln2_bias)

    def rows_body(rows):
        attended = (r.acc[rows, :] + shift).astype(BF)
        r.attended[rows, :] = attended
        middle = r.tokens[rows, :].astype(F32) + attended.astype(F32)
        r.n2[rows, :] = norm(middle, gain, bias)[0].astype(BF)
        return ()

    by_rows(rows_body, 0)
    between()
    up_bias = vector(r.fc1_bias)
    for line in range(hidden // D):
        r.up_bias[line : line + 1, :] = up_bias[:, line * D : line * D + D]

    def chunk(j, _):
        at = pl.multiple_of(j * 256, 256)
        lane = pl.multiple_of(lax.rem(j, 3) * 256, 256)
        u = nt(r.n2[...], r.w1[pl.ds(at, 256), :]) + r.up_bias[pl.ds(j // 3, 1), pl.ds(lane, 256)]
        cdf = 0.5 * (1.0 + lax.erf(u * 0.7071067811865476))
        r.act[:, pl.ds(at, 256)] = (u * cdf).astype(BF)
        r.slope[:, pl.ds(at, 256)] = (cdf + u * (jnp.exp(-0.5 * u * u) * 0.3989422804014327)).astype(BF)
        for when, hook in hooks:
            pl.when(j == when)(hook)
        return 0

    lax.fori_loop(0, hidden // 256, chunk, 0)


PARTS = 3


def mlp_second(r, hidden, ready):
    r.acc[...] = jnp.zeros_like(r.acc)
    r.small[...] = jnp.zeros_like(r.small)
    n = hidden // (2 * PARTS)
    for part in range(PARTS):
        ready(part)

        def chunk(i, _):
            at = pl.multiple_of((i * PARTS + part) * n, n)
            wide = pl.ds(at, n)
            gu = (nn(r.cot[...], r.w2[:, wide]) * r.slope[:, wide].astype(F32)).astype(BF)
            r.gu[:, wide] = gu
            r.acc[...] += nn(gu, r.w1[wide, :])
            r.up_sum[:, wide] = jnp.sum(gu.astype(F32), 0, keepdims=True)
            return 0

        lax.fori_loop(0, 2, chunk, 0)
    for line in range(hidden // D):
        r.small[8 + line : 9 + line, :] = r.up_sum[:, line * D : line * D + D]
    gain, bias = vector(r.ln2_gain), vector(r.ln2_bias)

    def rows_body(rows):
        middle = r.tokens[rows, :].astype(F32) + r.attended[rows, :].astype(F32)
        _, xhat, inverse = norm(middle, gain, bias)
        grad = r.acc[rows, :]
        cf = r.cot[rows, :].astype(F32)
        gm = cf + norm_back(grad, xhat, inverse, gain)
        r.grad_middle[rows, :] = gm
        low = gm.astype(BF)
        r.gfield[rows, :] = low
        return low.astype(F32), grad * xhat, grad, cf

    for line, value in enumerate(by_rows(rows_body, 4)):
        r.small[4 + line : 5 + line, :] = column_sum(value)


def mlp_branch(r, hidden):
    r.acc[...] = jnp.zeros_like(r.acc)

    def chunk(j, _):
        wide = pl.ds(pl.multiple_of(j * 512, 512), 512)
        r.acc[...] += nt(r.act[:, wide], r.w2[:, wide])
        return 0

    lax.fori_loop(0, hidden // 512, chunk, 0)


def mlp_out(r):
    bias = vector(r.fc2_bias)

    def rows_body(rows):
        att = r.attended[rows, :].astype(F32)
        tok = r.tokens[rows, :].astype(F32)
        middle = tok + att
        br = r.acc[rows, :] + bias
        result = middle + br
        r.output[rows, :] = result.astype(BF)
        return tuple(v * v for v in (tok, middle, result, att, br))

    lane = lax.broadcasted_iota(jnp.int32, (1, D), 1)
    stats = jnp.zeros((1, D), F32)
    for n, v in enumerate(by_rows(rows_body, 5)):
        stats = jnp.where(lane == n, jnp.sum(column_sum(v), 1, keepdims=True), stats)
    r.small[12:13, :] = stats


UP_PIECES, DOWN_PIECES = 12, 6
SENT = (3, 1, 4, 3)
LANES = (PARTS, 1, PARTS, PARTS)


def up_weights(r, hidden, sent):
    def up(j, _):
        n = hidden // UP_PIECES
        at = pl.multiple_of(j * n, n)
        r.g1[pl.ds(at, n), :] = tn(r.gu[:, pl.ds(at, n)], r.n2[...]).astype(BF)
        sent(j)
        return 0

    lax.fori_loop(0, UP_PIECES, up, 0)


def down_weights(r, sent):
    r.cot_t[...] = r.cot[...].T

    def down(j, _):
        n = D // DOWN_PIECES
        at = pl.multiple_of(j * n, n)
        r.g2[pl.ds(at, n), :] = nn(r.cot_t[pl.ds(at, n), :], r.act[...]).astype(BF)
        sent(j)
        return 0

    lax.fori_loop(0, DOWN_PIECES, down, 0)


def proj_weight_grad(r):
    def chunk(n, _):
        at = pl.multiple_of(n * 256, 256)
        r.gproj[pl.ds(at, 256), :] = tn(r.gfield[pl.ds(0, TOK), pl.ds(at, 256)], r.mixed_own[...]).astype(BF)
        return 0

    lax.fori_loop(0, D // 256, chunk, 0)


def prepare(r):
    r.table[...] = table_kernel_value(r.places[...], joint_table(r.rel_rows, r.rel_cols))
    r.mixed[...] = jnp.zeros_like(r.mixed)


def back_prepare(r, n_row, n_col):
    r.table[...] = table_kernel_value(r.places_back[...], joint_table(r.rel_rows, r.rel_cols))
    r.gtab[...] = jnp.zeros_like(r.gtab)
    r.dqkv[...] = jnp.zeros_like(r.dqkv)
    for w in range(4):
        cut_windows(r.gfield, r.gw, n_row, n_col, w)


def back_mix(r):
    def mix(n, _):
        at = pl.multiple_of(n * 256, 256)
        r.gmix[:, pl.ds(at, 256)] = nn(r.gw[...], r.wproj[:, pl.ds(at, 256)]).astype(BF)
        return 0

    lax.fori_loop(0, 3, mix, 0)


def back_windows(r, n_row, n_col, hooks):
    def body(w, place, pair, n, wide):
        probs = (r.probs0, r.probs1)[w // 2]
        attend_back_pair(
            w, place, pair, n, wide, r.qkv, r.gmix, probs, r.table, r.marks_back, r.masks, r.dqkv, r.gtab
        )

    over_windows(body, hooks, n_row, n_col)


def back_weights(r, n_row, n_col, sent):
    for part in range(3):

        def columns(n, _):
            lane = pl.multiple_of(256 * n, 256)
            piece = r.dqkv[pl.ds(4 * part * SLOT, 4 * SLOT), pl.ds(lane, 256)]
            r.gqkv[pl.ds(part * D + lane, 256), :] = tn(piece, r.xw[...]).astype(BF)
            return 0

        lax.fori_loop(0, 3, columns, 0)
        sent(part)
    ones = jnp.ones((16, 4 * SLOT), BF)
    r.mid[...] = jnp.zeros_like(r.mid)
    r.mid[8:9, :] = nn(ones, r.dqkv[pl.ds(0, 4 * SLOT), :])[0:1, :]
    r.mid[9:10, :] = nn(ones, r.dqkv[pl.ds(8 * SLOT, 4 * SLOT), :])[0:1, :]
    lane = lax.broadcasted_iota(jnp.int32, (128, 128), 1)
    left = jnp.where(lane < 64, r.gtab[0], 0.0)
    right = jnp.where(lane >= 64, r.gtab[1], 0.0)
    tab = lax.dot_general(
        r.places_back[...].astype(F32),
        jnp.concatenate([left, right], 0),
        (((0,), (0,)), ((), ())),
        precision=lax.Precision.HIGHEST,
        preferred_element_type=F32,
    )
    tab = tab + pltpu.roll(tab, HEAD, 1)
    low = lax.broadcasted_iota(jnp.int32, (32, 128), 1) < HEAD
    tab = jnp.where(low, tab[:32], tab[32:])
    for t in range(4):
        r.mid[0:8, 128 * t : 128 * t + 128] = tab[8 * t : 8 * t + 8, :]


def back_return(r, n_row, n_col):
    _, row, col = grid_place()

    def columns(n, _):
        lanes = pl.ds(pl.multiple_of(256 * n, 256), 256)
        value = 0
        for part in range(3):
            rows = pl.ds(4 * part * SLOT, 4 * SLOT)
            value = value + nn(r.dqkv[rows, :], r.wqkv[pl.ds(part * D, D), lanes])
        r.gw[:, lanes] = value.astype(BF)
        return 0

    lax.fori_loop(0, 3, columns, 0)
    hot = one_hot(field_slots(row, col, n_row, n_col), 4 * SLOT)
    r.ret[...] = nn(hot, r.gw[...]).astype(BF)


def norm_sums(r, n_row, n_col):
    _, row, col = grid_place()
    hot = one_hot(field_slots(row, col, n_row, n_col), 4 * SLOT)
    r.gmix[pl.ds(0, FIELD), :] = nn(hot, r.xw[...]).astype(BF)
    bias = vector(r.ln1_bias)

    def step(i, kept):
        rows = pl.ds(pl.multiple_of(i * 16, 16), 16)
        grad = r.ret[rows, :].astype(F32)
        parts = (grad * (r.gmix[rows, :].astype(F32) - bias), grad)
        return tuple(k + p[:8] + p[8:] for k, p in zip(kept, parts))

    scaled, total = lax.fori_loop(0, FIELD // 16, step, (jnp.zeros((8, D), F32),) * 2)
    r.mid[10:11, :] = column_sum(scaled) / vector(r.ln1_gain)
    r.mid[11:12, :] = column_sum(total)


def back_last(r, n_row, n_col):
    _, row, col = grid_place()
    hot = one_hot(home_index(row, col, n_row, n_col), FIELD)
    r.acc[...] = nn(hot, r.home2[...])
    gain, bias = vector(r.ln1_gain), vector(r.ln1_bias)

    def rows_body(rows):
        grad = r.acc[rows, :]
        _, xhat, inverse = norm(r.tokens[rows, :].astype(F32), gain, bias)
        r.input_grad[rows, :] = (r.grad_middle[rows, :] + norm_back(grad, xhat, inverse, gain)).astype(BF)
        return ()

    by_rows(rows_body, 0)


class Small:
    def __init__(self, value, come, send, recv, keep=None):
        self.dp, self.row, self.col = grid_place()
        self.value, self.come, self.send, self.recv, self.keep = value, come, send, recv, keep

    def copies(self, s):
        dp, row, col = self.dp, self.row, self.col
        plan = (
            [(dp, row, lax.rem(col + d, 4)) for d in (1, 2, 3)],
            [(dp, lax.rem(row + d, 4), col) for d in (1, 2, 3)],
            [(1 - dp, row, col)],
        )[s]
        return [
            pltpu.make_async_remote_copy(
                self.value, self.come.at[3 * s + i], self.send.at[3 * s + i], self.recv.at[3 * s + i],
                device_id=other, device_id_type=MESH,
            )
            for i, other in enumerate(plan)
        ]

    def start(self, s=0):
        for copy in self.copies(s):
            copy.start()

    def step(self, s):
        total = self.value[...]
        for i, copy in enumerate(self.copies(s)):
            copy.wait()
            value = self.come[3 * s + i]
            if s == 2 and self.keep is not None:
                line = lax.broadcasted_iota(jnp.int32, value.shape, 0)
                value = jnp.where(line == self.keep, 0.0, value)
            total = total + value
        self.value[...] = total
        if s < 2:
            self.start(s + 1)


GATHERS = ((0, 0, 1), (1, 0, 1), *((i, part, PARTS) for i in (2, 3) for part in range(PARTS)))


def block_body(n_row, n_col, shapes, hidden, ins, outs, r):
    dp, row, col = grid_place()
    loads = []
    for n, (name, source) in enumerate(ins):
        loads.append(pltpu.make_async_copy(source, r.__dict__[name], r.load_sem.at[n]))
        loads[-1].start()
    rest = FIELD - TOK

    def leaving(n):
        name, there = outs[n]
        return pltpu.make_async_copy(r.__dict__[name], there, r.leave_sem.at[n])

    def leave(n):
        leaving(n).start()

    r.gfield, r.home2 = r.field, r.home
    for ref in (r.field, r.home):
        ref[pl.ds(TOK, rest), :] = jnp.zeros((rest, D), BF)
    greet(n_row, n_col)
    for load in loads:
        load.wait()
    blocks = blocks_of(shapes)
    fulls, shards = (r.wqkv, r.wproj, r.w1, r.w2), (r.s0, r.s1, r.s2, r.s3)
    gathers = [
        Gather(fulls[i], shards[i], *blocks[i], r.gather_sem.at[0, n], r.gather_sem.at[1, n], part, parts)
        for n, (i, part, parts) in enumerate(GATHERS)
    ]
    qkv_way, proj_way = gathers[:2]
    up_ways, down_ways = gathers[2 : 2 + PARTS], gathers[2 + PARTS :]
    qkv_way.start(LINE, OWN)
    gain, bias = vector(r.ln1_gain), vector(r.ln1_bias)

    def rows_body(rows):
        r.field[rows, :] = norm(r.tokens[rows, :].astype(F32), gain, bias)[0].astype(BF)
        return ()

    by_rows(rows_body, 0)
    size = (n_row, n_col)
    lend = Halo(r.field, r.picked, r.field, False, r.lend_sem.at[0], r.lend_sem.at[1], *size)
    give = Halo(r.ret, None, r.home, True, r.give_sem.at[0], r.give_sem.at[1], *size)
    lend2 = Halo(r.gfield, r.picked, r.gfield, False, r.lend_sem.at[2], r.lend_sem.at[3], *size)
    give2 = Halo(r.ret, None, r.home2, True, r.give_sem.at[2], r.give_sem.at[3], *size)
    pick_start(lend, r.pick)
    local = []
    for way in gathers[1:]:
        way.start(OWN)
    for i, way in enumerate(gathers):
        own = way.full.at[rows_at(way.block(0, way.col), way.b), way.lanes]
        mine = pltpu.make_async_copy(way.shard, own, r.local_sem.at[i])
        mine.start()
        local.append(mine)
    prepare(r)
    for mine in local:
        mine.wait()
    qkv_way.step(0)
    proj_way.start(LINE)
    for way in up_ways:
        way.start(LINE)
    lend.wait()
    for w in range(4):
        cut_windows(r.field, r.xw, n_row, n_col, w)
    qkv_way.step(1)
    for way in down_ways:
        way.start(LINE)
    qkv_way.step(2)
    qkv_way.whole()

    def between(part):
        if part == 0:
            up_ways[0].step(0)
        elif part == 1:
            proj_way.step(0)
        else:
            up_ways[1].step(0)

    hooks = (
        (2, lambda: up_ways[2].step(0)),
        (4, lambda: up_ways[0].step(1)),
        (5, lambda: proj_way.step(1)),
        (8, lambda: down_ways[0].step(0)),
        (10, lambda: up_ways[1].step(1)),
        (12, lambda: down_ways[1].step(0)),
        (14, lambda: up_ways[2].step(1)),
        (16, lambda: proj_way.step(2)),
        (17, lambda: up_ways[0].step(2)),
        (18, lambda: down_ways[2].step(0)),
        (20, lambda: down_ways[0].step(1)),
        (22, lambda: up_ways[1].step(2)),
    )
    attend_part(r, n_row, n_col, hooks, between)
    give.start()
    r.home[pl.ds(0, TOK), :] = r.ret[pl.ds(0, TOK), :]
    proj_way.whole()
    down_ways[1].step(1)
    up_ways[2].step(2)
    give.arrive()

    qkv_sum, proj_sum, up_sum, down_sum = sums = [
        Reduce(g, g, dp * blocks[i][1], land, c, *blocks[i], SENT[i], LANES[i], p, q)
        for i, (g, land, c, p, q) in enumerate(
            [
                (r.gqkv, (r.g1, 0, True), r.c0, r.t0, r.u0),
                (r.gproj, (r.g1, shapes[0][0], True), r.c1, r.t1, r.u1),
                (r.g1, (r.w1, 0, False), r.c2, r.t2, r.u2),
                (r.g2, (r.w2, 0, False), r.c3, r.t3, r.u3),
            ]
        )
    ]

    def free(k):
        pl.semaphore_signal(r.free_sem.at[k], inc=1, device_id=(1 - dp, row, col), device_id_type=MESH)

    early = Small(r.small, r.small_come, r.small_sem.at[0], r.small_sem.at[1], 12)
    mid = Small(r.mid, r.mid_come, r.mid_sem.at[0], r.mid_sem.at[1])

    def every(n, j, way):
        pl.when(lax.rem(j, n) == n - 1)(lambda: way.start(0, j // n))

    def middle(act, slope, gu, cot_t):
        m = types.SimpleNamespace(**r.__dict__, act=act, slope=slope, gu=gu, cot_t=cot_t)

        def arrived():
            for way in up_ways:
                way.whole()
            give.gone()

        hooks = (
            (1, lambda: down_ways[2].step(1)),
            (2, lambda: down_ways[0].step(2)),
            (6, lambda: down_ways[1].step(2)),
            (11, lambda: down_ways[2].step(2)),
        )
        mlp_first(m, n_row, n_col, hidden, arrived, hooks)
        mlp_second(m, hidden, lambda part: down_ways[part].whole())
        for way in gathers:
            way.finish()
        free(0)
        pick_start(lend2, r.pick)
        pl.semaphore_wait(r.free_sem.at[0], 1)
        up_weights(m, hidden, lambda j: every(UP_PIECES // SENT[2], j, up_sum))
        up_sum.step(0)
        up_sum.gone()
        mlp_branch(m, hidden)
        free(1)
        pl.semaphore_wait(r.free_sem.at[1], 1)
        down_weights(m, lambda j: every(DOWN_PIECES // SENT[3], j, down_sum))
        mlp_out(m)
        leave(4)
        early.start()
        down_sum.step(0)

    v = pltpu.VMEM
    wide = (TOK, hidden)
    pl.run_scoped(middle, v(wide, BF), v(wide, BF), v(wide, BF), v((D, TOK), BF))
    proj_weight_grad(r)
    proj_sum.start(0)
    lend2.wait()

    def all_parts(way, k):
        for part in range(way.parts):
            way.step(k, part)

    def ends(gw):
        e = types.SimpleNamespace(**r.__dict__, gw=gw, gmix=r.mixed, dqkv=r.w1)
        all_parts(up_sum, 1)
        back_prepare(e, n_row, n_col)
        proj_sum.step(0)
        back_mix(e)
        early.step(0)
        hooks = (
            (2, lambda: all_parts(down_sum, 1)),
            (12, lambda: all_parts(up_sum, 2)),
            (13, lambda: proj_sum.step(1)),
        )
        back_windows(e, n_row, n_col, hooks)
        back_weights(e, n_row, n_col, lambda part: qkv_sum.start(0, part))
        qkv_sum.step(0)
        all_parts(down_sum, 2)
        back_return(e, n_row, n_col)
        give2.start()
        proj_sum.step(2)
        r.home2[pl.ds(0, TOK), :] = r.ret[pl.ds(0, TOK), :]
        all_parts(qkv_sum, 1)
        norm_sums(e, n_row, n_col)
        mid.start()
        early.step(1)
        for part in range(PARTS):
            up_sum.result(r.o2, part)
        leave(2)
        all_parts(qkv_sum, 2)
        mid.step(0)
        give2.arrive()
        back_last(e, n_row, n_col)
        leave(5)
        early.step(2)
        leave(6)
        mid.step(1)
        for part in range(PARTS):
            down_sum.result(r.o3, part)
        leave(3)
        proj_sum.result(r.o1)
        leave(1)
        mid.step(2)
        leave(7)
        give2.gone()
        for part in range(PARTS):
            qkv_sum.result(r.o0, part)
        leave(0)
        for way in (qkv_sum, proj_sum, down_sum):
            way.gone()
        for way in sums:
            way.finish()

    pl.run_scoped(ends, v((4 * SLOT, D), BF))
    for n in range(len(outs)):
        leaving(n).wait()


def split_ins(tensors, *names):
    return {k: (tensors[k], vmem()) for k in names}


def as_out(buffer):
    return (jax.ShapeDtypeStruct(buffer.shape, buffer.dtype), vmem())


def window_buffers(n_row):
    v = pltpu.VMEM
    late = 16 * (TILE * n_row - WIN * n_row)
    return dict(
        xw=v((4 * SLOT, D), BF),
        qkv=v((4 * SLOT, 3 * D), BF),
        probs0=v((2 * HEADS, 16 * WIN, SLOT), BF),
        probs1=v((2 * HEADS, late, SLOT), BF),
        mixed=v((4 * SLOT, D), BF),
        table=v((256, 128), BF),
        ret=v((FIELD, D), BF),
        shift=v((1, D), F32),
    )


def mlp_buffers(hidden):
    v = pltpu.VMEM
    return dict(
        mixed_own=v((TOK, D), BF),
        attended=v((TOK, D), BF),
        n2=v((TOK, D), BF),
        acc=v((TOK, D), F32),
        up_bias=v((hidden // D, D), F32),
        up_sum=v((1, hidden), F32),
        grad_middle=v((TOK, D), F32),
    )


def block_call(n_row, n_col, shapes, tensors, shards):
    hidden = shapes[2][0]
    sd, v = jax.ShapeDtypeStruct, pltpu.VMEM
    blocks = blocks_of(shapes)
    arrays = tensors | {"s" + str(i): w for i, w in enumerate(shards)}
    results = {"o" + str(i): v(b, F32) for i, b in enumerate(blocks)}
    results |= dict(output=v((TOK, D), BF), input_grad=v((TOK, D), BF), small=v((16, D), F32), mid=v((16, D), F32))
    there = "_"
    ins = {k + there: (t, hbm()) for k, t in arrays.items()}
    outs = {k + there: (sd(t.shape, t.dtype), hbm()) for k, t in results.items()}
    wqkv, wproj, w1, w2 = [v(s, BF) for s in shapes]
    come = [v((15 * b, h), BF) for b, h in blocks]
    field = v((FIELD, D), BF)
    scratch = dict(
        **window_buffers(n_row),
        **mlp_buffers(hidden),
        wqkv=wqkv,
        wproj=wproj,
        w1=w1,
        w2=w2,
        gqkv=wqkv,
        gproj=wproj,
        g1=w1,
        g2=w2,
        c0=come[0],
        c1=come[1],
        c2=come[2],
        c3=come[3],
        field=field,
        home=field,
        picked=v((PICKED, D), BF),
        gtab=v((2, 128, 128), F32),
        small_come=v((7, 16, D), F32),
        mid_come=v((7, 16, D), F32),
        **{k: v(t.shape, t.dtype) for k, t in arrays.items()},
        **results,
        load_sem=dma(len(arrays)),
        leave_sem=dma(len(results)),
        local_sem=dma(len(GATHERS)),
        gather_sem=dma(2, len(GATHERS), Gather.SEMS),
        lend_sem=dma(4, 3),
        give_sem=dma(4, 3),
        small_sem=dma(2, 7),
        mid_sem=dma(2, 7),
        free_sem=pltpu.SemaphoreType.REGULAR((2,)),
    )
    for i in range(4):
        count = SENT[i] + 7 * LANES[i]
        scratch |= {"t" + str(i): dma(count), "u" + str(i): dma(count)}

    def body(r):
        given = [(k, r.__dict__[k + there]) for k in arrays]
        taken = [(k, r.__dict__[k + there]) for k in results]
        block_body(n_row, n_col, shapes, hidden, given, taken, r)

    done = named_call(
        body, ins, outs, scratch, "block", vmem_limit_bytes=63 * MIB, collective_id=0, has_side_effects=True
    )
    return types.SimpleNamespace(**{k: done.__dict__[k + there] for k in results})


def plain_block(n_row, n_col, shapes, tensors, weights, field):
    hidden = shapes[2][0]
    sd, v = jax.ShapeDtypeStruct, pltpu.VMEM
    wqkv, wproj, w1, w2 = [(w, vmem()) for w in weights]
    limit = dict(vmem_limit_bytes=60 * MIB)

    def given(value, *names):
        return {k: (getattr(value, k), vmem()) for k in names}

    names = ("query_bias", "value_bias", "rel_rows", "rel_cols", "masks", "places", "marks")
    windows = window_buffers(n_row)
    outs = {k: as_out(windows.pop(k)) for k in ("qkv", "xw", "probs0", "probs1", "ret")}

    def attend_body(r):
        prepare(r)
        for w in range(4):
            cut_windows(r.field, r.xw, n_row, n_col, w)
        attend_part(r, n_row, n_col, (), lambda part: None)

    ins = split_ins(tensors, *names) | dict(field=(field, vmem()), wqkv=wqkv)
    one = named_call(attend_body, ins, outs, windows, "attend", **limit)
    home = (return_xla(one.ret, n_row, n_col), vmem())
    names = ("tokens", "cot", "proj_bias", "ln2_gain", "ln2_bias", "fc1_bias", "fc2_bias")
    buffers = mlp_buffers(hidden)
    outs = dict(grad_middle=as_out(buffers.pop("grad_middle")), gfield=(sd((FIELD, D), BF), vmem()))
    outs |= {k: (sd(s, BF), vmem()) for k, s in zip(("gproj", "g1", "g2"), shapes[1:])}
    outs |= dict(output=(sd((TOK, D), BF), vmem()), small=(sd((16, D), F32), vmem()))
    wide = (TOK, hidden)
    buffers |= dict(act=v(wide, BF), slope=v(wide, BF), gu=v(wide, BF), cot_t=v((D, TOK), BF))

    def mlp_body(r):
        r.gfield[...] = jnp.zeros_like(r.gfield)
        mlp_first(r, n_row, n_col, hidden, lambda: None, ())
        mlp_second(r, hidden, lambda part: None)
        up_weights(r, hidden, lambda j: None)
        mlp_branch(r, hidden)
        down_weights(r, lambda j: None)
        mlp_out(r)
        proj_weight_grad(r)

    ins = split_ins(tensors, *names) | dict(home=home, wproj=wproj, w1=w1, w2=w2)
    two = named_call(mlp_body, ins, outs, buffers, "mlp", **limit)
    gfield = (lend_xla(two.gfield[:TOK], n_row, n_col), vmem())
    ins = split_ins(tensors, "rel_rows", "rel_cols", "masks", "places_back", "marks_back", "ln1_gain", "ln1_bias")
    ins |= given(one, "qkv", "xw", "probs0", "probs1") | dict(wqkv=wqkv, wproj=wproj, gfield=gfield)
    outs = dict(
        gqkv=(sd(shapes[0], BF), vmem()),
        ret=(sd((FIELD, D), BF), vmem()),
        mid=(sd((16, D), F32), vmem()),
    )
    rows = v((4 * SLOT, D), BF)
    scratch = dict(gw=rows, gmix=rows, dqkv=v((12 * SLOT, D), BF))
    scratch |= dict(table=v((256, 128), BF), gtab=v((2, 128, 128), F32))

    def windows_body(r):
        back_prepare(r, n_row, n_col)
        back_mix(r)
        back_windows(r, n_row, n_col, ())
        back_weights(r, n_row, n_col, lambda n: None)
        back_return(r, n_row, n_col)
        norm_sums(r, n_row, n_col)

    three = named_call(windows_body, ins, outs, scratch, "windows", **limit)
    home = (return_xla(three.ret, n_row, n_col), vmem())
    ins = split_ins(tensors, "tokens", "ln1_gain", "ln1_bias") | dict(home2=home) | given(two, "grad_middle")
    outs = dict(input_grad=(sd((TOK, D), BF), vmem()))
    four = named_call(lambda r: back_last(r, n_row, n_col), ins, outs, dict(acc=v((TOK, D), F32)), "ends", **limit)
    grads = []
    for g in (three.gqkv, two.gproj, two.g1, two.g2):
        g = lax.psum_scatter(g, AXES, scatter_dimension=0, tiled=True)
        grads.append(lax.psum_scatter(g, "dp", scatter_dimension=1, tiled=True))
    line = jnp.arange(16)[:, None] == 12
    local = lax.psum(two.small, AXES)
    small = jnp.where(line, local, lax.psum(jnp.where(line, 0.0, local), "dp"))
    return grads, two.output, four.input_grad, small, lax.psum(three.mid, ("dp", *AXES))


def last_body(count, r):
    for i in range(4):
        r.__dict__["t" + str(i)][...] = r.__dict__["s" + str(i)][...].astype(F32)
    r.output_out[...] = r.output[...]
    r.input_grad_out[...] = r.input_grad[...]
    lines = ((r.mid, 10), (r.mid, 11), (r.mid, 8), (r.mid, 9), (r.small, 4), (r.small, 5), (r.small, 6), (r.small, 7))
    for i, (ref, line) in enumerate(lines):
        r.__dict__["v" + str(i)][...] = ref[line : line + 1, :].reshape(D)
    r.up[...] = jnp.concatenate([r.small[8 + i : 9 + i, :] for i in range(r.up.shape[0] // D)], 1).reshape(-1)
    tables = jnp.concatenate([r.mid[0:8, 128 * t : 128 * t + 128] for t in range(4)], 0)
    r.rows[...] = tables[0 : 2 * WIN - 1, :HEAD]
    r.cols[...] = pltpu.roll(tables, HEAD, 1)[0 : 2 * WIN - 1, :HEAD]
    r.stats[...] = jnp.sqrt(r.small[12:13, :5] / count)


def last_call(count, hidden, sums, output, input_grad, small, mid):
    sd = jax.ShapeDtypeStruct
    ins = {"s" + str(i): (s, vmem()) for i, s in enumerate(sums)}
    ins |= dict(output=(output, vmem()), input_grad=(input_grad, vmem()), small=(small, vmem()))
    ins |= dict(mid=(mid, vmem()))
    outs = {"t" + str(i): (sd(s.shape, F32), vmem()) for i, s in enumerate(sums)}
    outs |= dict(output_out=(sd((TOK, D), BF), vmem()), input_grad_out=(sd((TOK, D), BF), vmem()))
    outs |= {"v" + str(i): (sd((D,), F32), vmem()) for i in range(8)}
    outs |= dict(
        up=(sd((hidden,), F32), vmem()),
        rows=(sd((2 * WIN - 1, HEAD), F32), vmem()),
        cols=(sd((2 * WIN - 1, HEAD), F32), vmem()),
        stats=(sd((1, 5), F32), vmem()),
    )
    return named_call(functools.partial(last_body, count), ins, outs, {}, "last", vmem_limit_bytes=63 * MIB)


def on_device(
    n_dp, n_row, n_col,
    tokens, ln1_gain, ln1_bias, qkv_weight, query_bias, value_bias, rel_rows, rel_cols,
    proj_weight, proj_bias, ln2_gain, ln2_bias, fc1_weight, fc1_bias, fc2_weight, fc2_bias, cotangent,
):
    direct = (n_dp, n_row, n_col) == (2, 4, 4)
    tok = tokens.reshape(TOK, D)
    mask_values = np.zeros((16, 128), np.float32)
    mask_values[0, :64] = 1.0
    mask_values[1, 64:] = 1.0
    shared = dict(
        tokens=tok,
        cot=cotangent.reshape(TOK, D),
        ln1_gain=ln1_gain,
        ln1_bias=ln1_bias,
        rel_rows=rel_rows,
        rel_cols=rel_cols,
        masks=jnp.asarray(mask_values, BF),
    )
    tensors = shared | dict(
        query_bias=query_bias,
        value_bias=value_bias,
        proj_bias=proj_bias,
        ln2_gain=ln2_gain,
        ln2_bias=ln2_bias,
        fc1_bias=fc1_bias,
        fc2_bias=fc2_bias,
        places=jnp.asarray(table_places(False), BF),
        marks=jnp.asarray(key_marks(False), BF),
        places_back=jnp.asarray(table_places(True), BF),
        marks_back=jnp.asarray(key_marks(True), BF),
    )
    shards = (qkv_weight, proj_weight, fc1_weight, fc2_weight)
    shapes = [(s.shape[1] * n_row * n_col, s.shape[0] * n_dp) for s in shards]
    if direct:
        tensors |= dict(pick=jnp.asarray(pick_rows(), BF))
        done = block_call(n_row, n_col, shapes, tensors, [s.T for s in shards])
        sums = (done.o0, done.o1, done.o2, done.o3)
        rest = (done.output, done.input_grad, done.small, done.mid)
    else:
        weights = []
        for s in shards:
            s = lax.all_gather(s, AXES, axis=1, tiled=True)
            weights.append(lax.all_gather(s, "dp", axis=0, tiled=True).T)
        normed = norm(tok.astype(F32), ln1_gain.astype(F32), ln1_bias.astype(F32))[0].astype(BF)
        field = lend_xla(normed, n_row, n_col)
        sums, *rest = plain_block(n_row, n_col, shapes, tensors, weights, field)
    out = last_call(TOK * n_row * n_col * D, shapes[2][0], sums, *rest)
    return (
        out.output_out.reshape(tokens.shape),
        out.input_grad_out.reshape(tokens.shape),
        out.v0,
        out.v1,
        out.t0.T,
        out.v2,
        out.v3,
        out.rows,
        out.cols,
        out.t1.T,
        out.v4,
        out.v5,
        out.v6,
        out.t2.T,
        out.up,
        out.t3.T,
        out.v7,
        out.stats,
    )


def solution(mesh):
    tile = P("dp", "row", "col", None)
    weight = P("dp", AXES)
    sizes = [mesh.shape[a] for a in ("dp", "row", "col")]
    ins = [tile] + [P()] * 16
    for i in (3, 8, 12, 14):
        ins[i] = weight
    ins[16] = tile
    outs = [tile, tile] + [P()] * 16
    for i in (4, 9, 13, 15):
        outs[i] = weight
    outs[17] = P("dp", None)
    return jax.shard_map(
        functools.partial(on_device, *sizes),
        mesh=mesh,
        in_specs=tuple(ins),
        out_specs=tuple(outs),
        check_vma=False,
    )
```
